32 devices in a mesh: dp: 32 (over z, y, x, core).
Axes of the slice: x: 2, y: 2, z: 4, core: 2. Of those that a mesh axis runs over, the one named last changes fastest.
Arguments:
- tokens: bfloat16 [8192, 2048], P('dp'), may hold values from -6 to 6
- cotangent: bfloat16 [8192, 2048], P('dp'), may hold values from -6 to 6
- caption_len: int32 [64], P('dp'), may hold values from 1 to 64
- attn_weight: float32 [2048, 4, 2048], P('dp'), may hold values from -0.125 to 0.125
- up_weight: float32 [2048, 8192], P('dp'), may hold values from -0.125 to 0.125
- down_weight: float32 [2048, 8192], P('dp'), may hold values from -0.0625 to 0.0625
- small_norms: float32 [6, 2048], P(None, 'dp'), may hold values from -2 to 2, as said below
- wide_norms: float32 [2, 8192], P(None, 'dp'), may hold values from -2 to 2, as said below
- attn_row: float32 [4, 2048], P(None, 'dp'), as said below
- attn_col: float32 [4, 2048], replicated, as said below
- up_row: float32 [2048], P('dp'), as said below
- up_col: float32 [8192], replicated, as said below
- down_row: float32 [2048], P('dp'), as said below
- down_col: float32 [8192], replicated, as said below
- small_moment: float32 [6, 2048], P(None, 'dp'), as said below
- wide_moment: float32 [2, 8192], P(None, 'dp'), as said below
Outputs:
- block_out: bfloat16 [8192, 2048], P('dp')
- input_grad: float32 [8192, 2048], P('dp')
- attn_grad: float32 [2048, 4, 2048], P('dp')
- up_grad: float32 [2048, 8192], P('dp')
- down_grad: float32 [2048, 8192], P('dp')
- attn_row_new: float32 [4, 2048], P(None, 'dp')
- attn_col_new: float32 [4, 2048], replicated
- up_row_new: float32 [2048], P('dp')
- up_col_new: float32 [8192], replicated
- down_row_new: float32 [2048], P('dp')
- down_col_new: float32 [8192], replicated
- attn_new: float32 [2048, 4, 2048], P('dp')
- up_new: float32 [2048, 8192], P('dp')
- down_new: float32 [2048, 8192], P('dp')
- attn_copy: bfloat16 [2048, 4, 2048], P('dp')
- up_copy: bfloat16 [2048, 8192], P('dp')
- down_copy: bfloat16 [2048, 8192], P('dp')
- small_grad: float32 [6, 2048], P(None, 'dp')
- wide_grad: float32 [2, 8192], P(None, 'dp')
- small_moment_new: float32 [6, 2048], P(None, 'dp')
- wide_moment_new: float32 [2, 8192], P(None, 'dp')
- small_new: float32 [6, 2048], P(None, 'dp')
- wide_new: float32 [2, 8192], P(None, 'dp')
The draws below stay inside these ranges and needn't reach their ends.
Inputs may be any that keep to these rules, and one draw needn't show every extreme that they name: `small_norms`: gains near one in even rows, biases of both signs in odd rows. `wide_norms`: gains near one in row 0, biases of both signs in row 1. `attn_row`: positive. `attn_col`: positive. `up_row`: positive. `up_col`: positive. `down_row`: positive. `down_col`: positive. `small_moment`: positive. `wide_moment`: positive.
All inputs are finite; a program needn't handle non-finite values.
Results may differ from the reference program's by a relative error of at most 0.012.
Values may be sent and summed in bfloat16 or wider, within the bound.
A program may use at most 704 MiB of HBM per device.

```python
import math
import jax
import jax.numpy as jnp
from jax import lax

D = 2048
FF = 8192
HEADS = 32
L = 128
IMG = 64
ROWS = 64
TOKENS = 8192


def live_tokens():
    return TOKENS * (L + IMG) / (2.0 * L)


def spread_factor(key, shape):
    return jnp.exp(jax.random.uniform(key, shape, minval=0.0, maxval=jnp.log(4.0)))


def norm_pairs(key, pair_count, full_width, low_gain, high_gain):
    gain_key, bias_key = jax.random.split(key)
    gains = jax.random.uniform(gain_key, (pair_count, full_width), minval=low_gain, maxval=high_gain)
    biases = jnp.clip(0.5 * jax.random.normal(bias_key, (pair_count, full_width)), -2.0, 2.0)
    return jnp.stack([gains, biases], axis=1).reshape(2 * pair_count, full_width)


def row_state(key, factors, row_count):
    row_ramp = 1.0 + 2.0 * jnp.arange(row_count, dtype=jnp.float32) / max(row_count - 1, 1)
    base_scale = jnp.asarray(factors, jnp.float32)[:, None] * live_tokens()
    return base_scale * row_ramp[None, :] * spread_factor(key, (len(factors), row_count)) / 2.0


def col_state(key, factors, col_count):
    base_scale = jnp.asarray(factors, jnp.float32)[:, None] * live_tokens()
    return base_scale * spread_factor(key, (len(factors), col_count))


def draw_small_norms(key, part):
    key = jax.random.fold_in(key, 3)
    return norm_pairs(key, 3, D, 0.75, 1.25)


def draw_wide_norms(key, part):
    key = jax.random.fold_in(key, 5)
    return norm_pairs(key, 1, FF, 0.75, 1.25)


def draw_attn_row(key, part):
    key = jax.random.fold_in(key, 7)
    return row_state(key, [0.05, 0.05, 0.25, 1.0], D)


def draw_attn_col(key, part):
    key = jax.random.fold_in(key, 11)
    return col_state(key, [0.05, 0.05, 0.25, 1.0], D)


def draw_up_row(key, part):
    key = jax.random.fold_in(key, 13)
    return row_state(key, [0.16], D)[0]


def draw_up_col(key, part):
    key = jax.random.fold_in(key, 17)
    return col_state(key, [0.16], FF)[0]


def draw_down_row(key, part):
    key = jax.random.fold_in(key, 19)
    return row_state(key, [1.0], D)[0]


def draw_down_col(key, part):
    key = jax.random.fold_in(key, 23)
    return col_state(key, [1.0], FF)[0]


def draw_small_moment(key, part):
    key = jax.random.fold_in(key, 29)
    return col_state(key, [0.5, 0.5, 0.5, 0.5, 0.5, 0.5], D)


def draw_wide_moment(key, part):
    key = jax.random.fold_in(key, 31)
    return col_state(key, [0.5, 0.5], FF)


def set_ends(values, stream_key, low, high):
    dims = values.shape
    place = [jax.random.randint(jax.random.fold_in(stream_key, axis), (), 0, dims[axis]) for axis in range(len(dims))]
    values = values.at[tuple(place)].set(low)
    longest = dims.index(max(dims))
    place[longest] = (place[longest] + 1) % dims[longest]
    return values.at[tuple(place)].set(high)


def levels(own_key, shape, cuts, smallest, high):
    loudness = 1.0
    for axis_at, blocks in cuts:
        draws = jax.random.uniform(jax.random.fold_in(jax.random.fold_in(own_key, 6), axis_at), (blocks,), jnp.float32, smallest / len(cuts), high / len(cuts))
        loudness = loudness * jnp.repeat(jnp.exp(draws), shape[axis_at] // blocks).reshape((-1,) + (1,) * (len(shape) - 1 - axis_at))
    return loudness


def bell_draw(stream_key, shape, deviation, limit, cuts=(), kind=jnp.bfloat16):
    entries = deviation * jax.random.normal(stream_key, shape, jnp.float32)
    if cuts:
        entries = entries * levels(stream_key, shape, cuts, -0.22, 0.18)
    return jnp.clip(entries, -limit, limit).astype(kind)


def setup_inputs(seed: int = 0) -> dict:
    arg_keys = jax.random.split(jax.random.key(seed), 17)
    return {
        "tokens": bell_draw(arg_keys[0], (TOKENS, D), 1.0, 6.0, ((0, 32),)),
        "cotangent": bell_draw(arg_keys[1], (TOKENS, D), 1.0, 6.0, ((0, 32),)),
        "caption_len": set_ends(jax.random.randint(arg_keys[2], (ROWS,), 1, L - IMG + 1), jax.random.fold_in(arg_keys[2], 1), 1, L - IMG).astype(jnp.int32),
        "attn_weight": bell_draw(arg_keys[3], (D, 4, D), D ** -0.5, 0.125, ((0, 32),), jnp.float32),
        "up_weight": bell_draw(arg_keys[4], (D, FF), D ** -0.5, 0.125, ((0, 32),), jnp.float32),
        "down_weight": bell_draw(arg_keys[5], (D, FF), FF ** -0.5, 0.0625, ((0, 32),), jnp.float32),
        "small_norms": draw_small_norms(jax.random.fold_in(arg_keys[16], 71), 0),
        "wide_norms": draw_wide_norms(jax.random.fold_in(arg_keys[16], 71), 0),
        "attn_row": draw_attn_row(jax.random.fold_in(arg_keys[16], 71), 0),
        "attn_col": draw_attn_col(jax.random.fold_in(arg_keys[16], 71), 0),
        "up_row": draw_up_row(jax.random.fold_in(arg_keys[16], 71), 0),
        "up_col": draw_up_col(jax.random.fold_in(arg_keys[16], 71), 0),
        "down_row": draw_down_row(jax.random.fold_in(arg_keys[16], 71), 0),
        "down_col": draw_down_col(jax.random.fold_in(arg_keys[16], 71), 0),
        "small_moment": draw_small_moment(jax.random.fold_in(arg_keys[16], 71), 0),
        "wide_moment": draw_wide_moment(jax.random.fold_in(arg_keys[16], 71), 0),
    }


EPS_NORM = 1e-05
EPS_SQUARE = 1e-30
EPS_SCALE = 0.001
DECAY_RATE = 0.5
CLIP_LEVEL = 0.5
LEARN_RATE = 0.8
SCALE_BASE = 512.0
MASK_FILL = -1e+30
HIGH_PREC = lax.Precision.HIGHEST

@jax.custom_vjp
def low(v):
    return lax.optimization_barrier(v.astype(jnp.bfloat16)).astype(jnp.float32)

@jax.custom_vjp
def low_back(v):
    return v

def low_keep(v):
    return (low(v), None)

def low_pass(kept, grad):
    return (grad,)

def back_keep(v):
    return (v, None)

def back_low(kept, grad):
    return (low(grad),)
low.defvjp(low_keep, low_pass)
low_back.defvjp(back_keep, back_low)

def layer_norm(values, gain_row, bias_row):
    center = values - lax.optimization_barrier(jnp.mean(values, axis=-1, keepdims=True))
    spread = lax.optimization_barrier(jnp.mean(center * center, axis=-1, keepdims=True))
    return center * lax.rsqrt(spread + EPS_NORM) * gain_row + bias_row

def xpos_tables(length, head_size):
    slot_pos = jnp.arange(length, dtype=jnp.float32)[:, None]
    pair_idx = jnp.arange(head_size // 2, dtype=jnp.float32)[None, :]
    theta = jnp.exp(-(2.0 * pair_idx / head_size) * jnp.log(10000.0))
    angle = slot_pos * theta
    zeta = (2.0 * pair_idx / head_size + 0.4) / 1.4
    power_table = jnp.exp(jnp.log(zeta) * slot_pos / SCALE_BASE)
    return (jnp.cos(angle), jnp.sin(angle), power_table)

def xpos_turn(values, cosine, sine_table, power_table):
    pairs = values.reshape(values.shape[:-1] + (values.shape[-1] // 2, 2))
    first_half = pairs[..., 0]
    second_half = pairs[..., 1]
    cos_b = cosine[:, None, :]
    sin_b = sine_table[:, None, :]
    pow_b = power_table[:, None, :]
    turned_first = (first_half * cos_b - second_half * sin_b) * pow_b
    turned_second = (second_half * cos_b + first_half * sin_b) * pow_b
    return jnp.stack([turned_first, turned_second], axis=-1).reshape(values.shape)

def block_rows(inputs, live_mask, weights):
    attn_low, up_low, down_low, small_low, wide_low = weights
    row_count = inputs.shape[0]
    head_size = D // HEADS
    cosine, sine_table, power_table = xpos_tables(L, head_size)
    normed = low(layer_norm(inputs, small_low[0], small_low[1]))
    projected = low_back(jnp.einsum('rpd,dje->rpje', normed, attn_low[:, :3, :], precision=HIGH_PREC))
    head_shape = (row_count, L, HEADS, head_size)
    queries = low(xpos_turn(projected[:, :, 0].reshape(head_shape), cosine, sine_table, power_table))
    keys_low = low(xpos_turn(projected[:, :, 1].reshape(head_shape), cosine, sine_table, 1.0 / power_table))
    values_low = low(projected[:, :, 2].reshape(head_shape))
    raw_scores = low_back(jnp.einsum('rphe,rshe->rhps', queries, keys_low, precision=HIGH_PREC))
    slot_index = jnp.arange(L)
    allowed = (slot_index[None, :] <= slot_index[:, None])[None, None] & (live_mask[:, None, None, :] > 0)
    scores = jnp.where(allowed, raw_scores / math.sqrt(head_size), MASK_FILL)
    row_peak = lax.optimization_barrier(jnp.max(scores, axis=-1, keepdims=True))
    exp_terms = jnp.exp(scores - row_peak)
    attn_probs = exp_terms / lax.optimization_barrier(jnp.sum(exp_terms, axis=-1, keepdims=True))
    attn_mixed = low_back(jnp.einsum('rhps,rshe->rphe', low(attn_probs), values_low, precision=HIGH_PREC).reshape(row_count, L, D))
    context = low(layer_norm(attn_mixed, small_low[2], small_low[3]))
    hidden = inputs + low_back(jnp.einsum('rpd,de->rpe', context, attn_low[:, 3, :], precision=HIGH_PREC))
    ffn_in = low(layer_norm(hidden, small_low[4], small_low[5]))
    upward = low_back(jnp.einsum('rpd,df->rpf', ffn_in, up_low, precision=HIGH_PREC))
    activated = jax.nn.gelu(upward, approximate=False)
    ffn_mid = low(layer_norm(activated, wide_low[0], wide_low[1]))
    return hidden + low_back(jnp.einsum('rpf,df->rpd', ffn_mid, down_low, precision=HIGH_PREC))

def factored(grad_rows, weight_rows, row_old, col_old):
    squares = grad_rows * grad_rows + EPS_SQUARE
    row_new = DECAY_RATE * row_old + (1.0 - DECAY_RATE) * lax.optimization_barrier(jnp.mean(squares, axis=2)).T
    col_new = DECAY_RATE * col_old + (1.0 - DECAY_RATE) * lax.optimization_barrier(jnp.mean(squares, axis=0))
    row_mean = lax.optimization_barrier(jnp.mean(row_new, axis=1))
    scaled = grad_rows * lax.rsqrt(row_new.T[:, :, None] / row_mean[None, :, None]) * lax.rsqrt(col_new[None])
    upd_rms = jnp.sqrt(lax.optimization_barrier(jnp.mean(scaled * scaled, axis=(0, 2))))
    clipped = scaled / jnp.maximum(1.0, upd_rms / CLIP_LEVEL)[None, :, None]
    weight_rms = jnp.sqrt(lax.optimization_barrier(jnp.mean(weight_rows * weight_rows, axis=(0, 2))))
    new_rows = weight_rows - LEARN_RATE * jnp.maximum(EPS_SCALE, weight_rms)[None, :, None] * clipped
    return (row_new, col_new, new_rows)

def unfactored(grad_rows, param_rows, moment_old):
    moment_new = DECAY_RATE * moment_old + (1.0 - DECAY_RATE) * (grad_rows * grad_rows + EPS_SQUARE)
    scaled = grad_rows * lax.rsqrt(moment_new)
    upd_rms = jnp.sqrt(lax.optimization_barrier(jnp.mean(scaled * scaled, axis=1, keepdims=True)))
    weight_rms = jnp.sqrt(lax.optimization_barrier(jnp.mean(param_rows * param_rows, axis=1, keepdims=True)))
    new_rows = param_rows - LEARN_RATE * jnp.maximum(EPS_SCALE, weight_rms) * scaled / jnp.maximum(1.0, upd_rms / CLIP_LEVEL)
    return (moment_new, new_rows)

def reference(tokens, cotangent, caption_len, attn_weight, up_weight, down_weight, small_norms, wide_norms, attn_row, attn_col, up_row, up_col, down_row, down_col, small_moment, wide_moment):
    row_total = caption_len.shape[0]
    slot_index = jnp.arange(L).astype(jnp.int32)
    live_mask = (slot_index[None, :] < IMG + caption_len[:, None]).astype(jnp.float32)
    inputs = tokens.astype(jnp.float32).reshape(row_total, L, D)
    group_rows = math.gcd(row_total, max(1, 4096 // L))
    run_block = jax.checkpoint(block_rows)

    def forward(inputs_f, attn_f, up_f, down_f, small_f, wide_f):
        weights = (low(attn_f), low(up_f), low(down_f), low(small_f), low(wide_f))

        def scan_step(scan_carry, pair_in):
            return (scan_carry, run_block(pair_in[0], pair_in[1], weights))
        grouped = inputs_f.reshape(row_total // group_rows, group_rows, L, D)
        mask_groups = live_mask.reshape(row_total // group_rows, group_rows, L)
        unused, results = lax.scan(scan_step, jnp.zeros((), jnp.float32), (grouped, mask_groups))
        return results.reshape(row_total, L, D)
    output, pullback = jax.vjp(forward, inputs, attn_weight, up_weight, down_weight, small_norms, wide_norms)
    back_seed = cotangent.astype(jnp.float32).reshape(row_total, L, D) * live_mask[:, :, None]
    grad_in, attn_grad, up_grad, down_grad, small_grad, wide_grad = pullback(back_seed)
    attn_row_new, attn_col_new, attn_new = factored(attn_grad, attn_weight, attn_row, attn_col)
    up_row_new, up_col_new, up_new = factored(up_grad[:, None, :], up_weight[:, None, :], up_row[None], up_col[None])
    down_row_new, down_col_new, down_new = factored(down_grad[:, None, :], down_weight[:, None, :], down_row[None], down_col[None])
    small_moment_new, small_new = unfactored(small_grad, small_norms, small_moment)
    wide_moment_new, wide_new = unfactored(wide_grad, wide_norms, wide_moment)
    up_new = up_new[:, 0, :]
    down_new = down_new[:, 0, :]
    return (output.reshape(row_total * L, D).astype(jnp.bfloat16), grad_in.reshape(row_total * L, D), attn_grad, up_grad, down_grad, attn_row_new, attn_col_new, up_row_new[0], up_col_new[0], down_row_new[0], down_col_new[0], attn_new, up_new, down_new, attn_new.astype(jnp.bfloat16), up_new.astype(jnp.bfloat16), down_new.astype(jnp.bfloat16), small_grad, wide_grad, small_moment_new, wide_moment_new, small_new, wide_new)
```

```python
from functools import partial
import math

import jax
import jax.numpy as jnp
from jax import lax
from jax.experimental import pallas as pl
from jax.experimental.pallas import tpu as pltpu
from jax.sharding import PartitionSpec as P

D = 2048
FF = 8192
HEADS = 32
L = 128
IMG = 64
SHARE = 4
FF_CHUNKS = 2


EPS_NORM = 1e-05
EPS_SQUARE = 1e-30
EPS_SCALE = 0.001
DECAY_RATE = 0.5
CLIP_LEVEL = 0.5
LEARN_RATE = 0.8
SCALE_BASE = 512.0
MASK_FILL = -1e30

BF = jnp.bfloat16
F32 = jnp.float32


def dot_f32(left, right, left_dim, right_dim):
    return lax.dot_general(
        left, right, (((left_dim,), (right_dim,)), ((), ())), preferred_element_type=F32
    )


def swap(value, mask):
    count = lax.axis_size("dp")
    return lax.ppermute(value, "dp", [(i, i ^ mask) for i in range(count)])


def sum_all(value, masks=None):
    if masks is None:
        masks = [1, 2] + group_masks()[::-1]
    for mask in masks:
        value = value + swap(value, mask)
    return value


def group_masks():
    count = lax.axis_size("dp")
    masks = []
    mask = 2 * SHARE
    while mask < count:
        masks.append(mask)
        mask *= 2
    if count > SHARE:
        masks.append(SHARE)
    return masks


def group_offsets():
    offsets = [0]
    for mask in group_masks():
        offsets = offsets + [item ^ (mask // SHARE) for item in offsets]
    return offsets


def take_block(value, index, width, axis):
    return lax.dynamic_slice_in_dim(value, index * width, width, axis)


def to_gathered_order(value, group):
    offsets = group_offsets()
    width = value.shape[1] // len(offsets)
    return jnp.concatenate([take_block(value, group ^ off, width, 1) for off in offsets], axis=1)


def from_gathered_order(value, group):
    offsets = group_offsets()
    count = len(offsets)
    bits = count.bit_length() - 1
    width = value.shape[1] // count
    blocks = []
    for block in range(count):
        place = group ^ block
        if bits:
            place = (place >> 1) | ((place & 1) << (bits - 1))
        blocks.append(take_block(value, place, width, 1))
    return jnp.concatenate(blocks, axis=1)


def in_own_order(pieces, member):
    low_bit = (member & 1) > 0
    high_bit = (member & 2) > 0
    first = [
        jnp.where(low_bit, pieces[i ^ 1], pieces[i]) for i in range(SHARE)
    ]
    return [jnp.where(high_bit, first[i ^ 2], first[i]) for i in range(SHARE)]


def after(values, deps):
    held = lax.optimization_barrier((list(values), list(deps)))
    return held[0]


def columns_to_members(part, member):
    pieces = [part(member)] + [swap(part(member ^ j), j) for j in range(1, SHARE)]
    return jnp.concatenate(in_own_order(pieces, member), axis=0)


def rows_to_members(block, member):
    height = block.shape[0] // SHARE
    pieces = [take_block(block, member, height, 0)] + [
        swap(take_block(block, member ^ j, height, 0), j) for j in range(1, SHARE)
    ]
    return in_own_order(pieces, member)


def gather_groups(blocks):
    masks = group_masks()
    blocks = list(blocks)
    arrived = []
    late = []
    for stage in range(len(blocks) + len(masks) - 1):
        active = [
            (stage - depth, mask)
            for depth, mask in enumerate(masks)
            if 0 <= stage - depth < len(blocks)
        ]
        ready = after([blocks[k] for k, mask in active], arrived)
        late = arrived
        arrived = [swap(value, mask) for value, (k, mask) in zip(ready, active)]
        for (k, mask), value, got in zip(active, ready, arrived):
            blocks[k] = jnp.concatenate([value, got], axis=0)
    return blocks, late


def reduce_groups(makers, order):
    masks = group_masks()[::-1]
    if not masks:
        return [maker(0, D) for maker in makers]
    out = []
    for maker in makers:
        half = D // 2
        send = maker(half, D).astype(BF)
        kept = None
        for mask in masks:
            (send,) = after([send], order[mask])
            got = swap(send, mask)
            order[mask] = [got]
            if kept is None:
                kept = maker(0, half)
            else:
                kept = kept[:half] + last[:half].astype(F32)
            if mask == masks[-1]:
                out.append(kept + got.astype(F32))
            else:
                half //= 2
                send = (kept[half:] + got[half:].astype(F32)).astype(BF)
                last = got
    return out


def share_tokens(own):
    pair = jnp.concatenate([own, swap(own, 2)], axis=0)
    height = own.shape[0]
    other = swap(pair, 1)
    return jnp.concatenate(
        [pair[:height], other[:height], pair[height:], other[height:]], axis=0
    )


def sum_to_owner(terms):
    height = terms.shape[0] // SHARE
    blocks = [terms[j * height : (j + 1) * height] for j in range(SHARE)]
    got = swap(jnp.concatenate([blocks[3], blocks[1]], axis=0).astype(BF), 1)
    far = blocks[2] + got[:height].astype(F32)
    near = blocks[0] + got[height:].astype(F32)
    return near + swap(far.astype(BF), 2).astype(F32)


def member_stats(stats):
    out = [stats]
    for j in range(1, SHARE):
        got = swap(stats, j)
        out.append(jnp.stack([got[:, i ^ j] for i in range(SHARE)], axis=1))
    return out


def norm_stats(values):
    mean = jnp.mean(values, axis=-1, keepdims=True)
    center = values - mean
    rstd = lax.rsqrt(jnp.mean(center * center, axis=-1, keepdims=True) + EPS_NORM)
    return center * rstd, rstd


def norm_back(unit, rstd, gain, upstream):
    scaled = upstream * gain
    lean = jnp.mean(scaled, axis=-1, keepdims=True)
    slope = jnp.mean(scaled * unit, axis=-1, keepdims=True)
    return (
        rstd * (scaled - lean - unit * slope),
        jnp.sum(upstream * unit, axis=0),
        jnp.sum(upstream, axis=0),
    )


def xpos_tables(head_size, head_count):
    slot_pos = jnp.arange(L, dtype=F32)[:, None]
    pair_idx = jnp.arange(head_size // 2, dtype=F32)[None, :]
    theta = jnp.exp(-(2.0 * pair_idx / head_size) * jnp.log(10000.0))
    angle = slot_pos * theta
    zeta = (2.0 * pair_idx / head_size + 0.4) / 1.4
    power_table = jnp.exp(jnp.log(zeta) * slot_pos / SCALE_BASE)

    def widen(table):
        return jnp.tile(jnp.repeat(table, 2, axis=1), (1, head_count))

    cosine, sine, power = widen(jnp.cos(angle)), widen(jnp.sin(angle)), widen(power_table)
    return cosine * power, sine * power, cosine / power, sine / power


def quarter_turn(values):
    width = values.shape[1]
    lane = lax.broadcasted_iota(jnp.int32, values.shape, 1)
    return jnp.where(
        lane % 2 == 0, -pltpu.roll(values, width - 1, 1), pltpu.roll(values, 1, 1)
    )


def masked_probs(query, key, caption, head_size):
    scores = dot_f32(query, key, 1, 1) * (1.0 / math.sqrt(head_size))
    row = lax.broadcasted_iota(jnp.int32, scores.shape, 0)
    col = lax.broadcasted_iota(jnp.int32, scores.shape, 1)
    scores = jnp.where((col <= row) & (col < IMG + caption), scores, MASK_FILL)
    terms = jnp.exp(scores - jnp.max(scores, axis=-1, keepdims=True))
    return terms / jnp.sum(terms, axis=-1, keepdims=True)


def attention_kernel(head_size, cap, q_in, k_in, v_in, cq, sq, ck, sk, q_out, k_out, v_out, o_out):
    caption = cap[pl.program_id(0)]
    q_all = q_in[...]
    k_all = k_in[...]
    q_low = (q_all * cq[...] + quarter_turn(q_all) * sq[...]).astype(BF)
    k_low = (k_all * ck[...] + quarter_turn(k_all) * sk[...]).astype(BF)
    v_low = v_in[...].astype(BF)
    q_out[...] = q_low
    k_out[...] = k_low
    v_out[...] = v_low
    mixed = []
    for head in range(q_low.shape[1] // head_size):
        at = slice(head * head_size, (head + 1) * head_size)
        probs = masked_probs(q_low[:, at], k_low[:, at], caption, head_size).astype(BF)
        mixed.append(dot_f32(probs, v_low[:, at], 1, 0))
    o_out[...] = jnp.concatenate(mixed, axis=1).astype(BF)


def attention_back_kernel(
    head_size, cap, q_in, k_in, v_in, g_in, cq, sq, ck, sk, gq_out, gk_out, gv_out
):
    caption = cap[pl.program_id(0)]
    q_low, k_low, v_low, g_low = q_in[...], k_in[...], v_in[...], g_in[...]
    grads_q, grads_k, grads_v = [], [], []
    for head in range(q_low.shape[1] // head_size):
        at = slice(head * head_size, (head + 1) * head_size)
        probs = masked_probs(q_low[:, at], k_low[:, at], caption, head_size)
        grads_v.append(dot_f32(probs.astype(BF), g_low[:, at], 0, 0))
        prob_grad = dot_f32(g_low[:, at], v_low[:, at], 1, 1)
        score_grad = probs * (prob_grad - jnp.sum(probs * prob_grad, axis=-1, keepdims=True))
        score_low = (score_grad * (1.0 / math.sqrt(head_size))).astype(BF)
        grads_q.append(dot_f32(score_low, k_low[:, at], 1, 0))
        grads_k.append(dot_f32(score_low, q_low[:, at], 0, 0))
    grad_q = jnp.concatenate(grads_q, axis=1)
    grad_k = jnp.concatenate(grads_k, axis=1)
    gq_out[...] = (grad_q * cq[...] - quarter_turn(grad_q) * sq[...]).astype(BF)
    gk_out[...] = (grad_k * ck[...] - quarter_turn(grad_k) * sk[...]).astype(BF)
    gv_out[...] = jnp.concatenate(grads_v, axis=1).astype(BF)


def attention_call(kernel, captions, arrays, tables, outputs, width, name):
    row_count = captions.shape[0]
    by_row = pl.BlockSpec((L, width), lambda row, cap: (row, 0))
    table = pl.BlockSpec((L, width), lambda row, cap: (0, 0))
    size = row_count * L * width
    return pl.pallas_call(
        kernel,
        grid_spec=pltpu.PrefetchScalarGridSpec(
            num_scalar_prefetch=1,
            grid=(row_count,),
            in_specs=[by_row] * len(arrays) + [table] * 4,
            out_specs=[by_row] * outputs,
        ),
        out_shape=[jax.ShapeDtypeStruct((row_count * L, width), BF)] * outputs,
        compiler_params=pltpu.CompilerParams(vmem_limit_bytes=32 * 1024 * 1024),
        cost_estimate=pl.CostEstimate(
            flops=12 * size * L, bytes_accessed=16 * size, transcendentals=size * 2
        ),
        name=name,
    )(captions, *arrays, *tables)


def gelu_parts(value):
    cdf = 0.5 * (1.0 + lax.erf(value * math.sqrt(0.5)))
    density = jnp.exp(-0.5 * value * value) * (1.0 / math.sqrt(2.0 * math.pi))
    return cdf, density


def first_stats(grad, weight, row_old):
    squares = grad * grad
    row_new = DECAY_RATE * row_old + (1.0 - DECAY_RATE) * (
        jnp.mean(squares, axis=1) + EPS_SQUARE
    )
    return (
        row_new,
        jnp.sum(squares, axis=0),
        jnp.sum(squares / row_new[:, None], axis=0),
        jnp.sum(row_new),
        jnp.sum(weight * weight),
    )


def column_state(col_old, col_sums):
    return DECAY_RATE * col_old + (1.0 - DECAY_RATE) * (col_sums / D + EPS_SQUARE)


def updated(grad, weight, row_new, col_new, weighted, row_sum, weight_square):
    size = D * weight.shape[1]
    row_mean = row_sum / D
    upd_rms = jnp.sqrt(row_mean * jnp.sum(weighted / col_new) / size)
    weight_rms = jnp.sqrt(weight_square / size)
    step = LEARN_RATE * jnp.maximum(EPS_SCALE, weight_rms) / jnp.maximum(1.0, upd_rms / CLIP_LEVEL)
    row_scale = lax.rsqrt(row_new / row_mean) * step
    return weight - grad * row_scale[:, None] * lax.rsqrt(col_new)[None, :]


def vector_stats(grad_rows, param_rows, moment_old):
    moment_new = DECAY_RATE * moment_old + (1.0 - DECAY_RATE) * (grad_rows * grad_rows + EPS_SQUARE)
    scaled = grad_rows * lax.rsqrt(moment_new)
    return (
        moment_new,
        scaled,
        jnp.sum(scaled * scaled, axis=1),
        jnp.sum(param_rows * param_rows, axis=1),
    )


def vector_finish(scaled, param_rows, upd_square, weight_square, full_width):
    upd_rms = jnp.sqrt(upd_square / full_width)[:, None]
    weight_rms = jnp.sqrt(weight_square / full_width)[:, None]
    return param_rows - LEARN_RATE * jnp.maximum(EPS_SCALE, weight_rms) * scaled / jnp.maximum(
        1.0, upd_rms / CLIP_LEVEL
    )


def pack_rows(parts, width):
    rows, layout, at = [], [], 0
    for part in parts:
        flat = part.reshape(-1)
        count = -(-flat.shape[0] // width)
        flat = jnp.pad(flat, (0, count * width - flat.shape[0]))
        rows.append(flat.reshape(count, width))
        layout.append((at, count, part.shape))
        at += count
    def unpack(packed):
        return [
            packed[start : start + count].reshape(-1)[: math.prod(shape)].reshape(shape)
            for start, count, shape in layout
        ]
    return jnp.concatenate(rows, axis=0), unpack


def per_device(
    tokens,
    cotangent,
    caption_len,
    attn_weight,
    up_weight,
    down_weight,
    small_norms,
    wide_norms,
    attn_row,
    attn_col,
    up_row,
    up_col,
    down_row,
    down_col,
    small_moment,
    wide_moment,
):
    count = lax.axis_size("dp")
    me = lax.axis_index("dp")
    member = me % SHARE
    group = me // SHARE
    head_size = D // HEADS
    width = D // SHARE
    ff_width = FF // SHARE
    piece = ff_width // FF_CHUNKS
    own = tokens.shape[0]
    own_rows = caption_len.shape[0]
    local_rows = attn_weight.shape[0]

    norm_pack = jnp.concatenate(
        [
            small_norms.astype(BF).reshape(-1),
            wide_norms.astype(BF).reshape(-1),
            caption_len.astype(BF),
        ]
    )
    pack_width = norm_pack.shape[0]
    spread = jnp.zeros((count, pack_width), BF)
    spread = lax.dynamic_update_slice(spread, norm_pack[None], (me, 0))
    norm_all = sum_all(spread, group_masks() + [1, 2])
    small_width = D // count
    wide_width = FF // count
    small_vals = (
        norm_all[:, : 6 * small_width].reshape(count, 6, small_width).transpose(1, 0, 2)
    ).reshape(6, D).astype(F32)
    wide_vals = (
        norm_all[:, 6 * small_width : 6 * small_width + 2 * wide_width]
        .reshape(count, 2, wide_width)
        .transpose(1, 0, 2)
    ).reshape(2, FF).astype(F32)
    wide_own = take_block(wide_vals, member, ff_width, 1)
    captions = jnp.concatenate(
        [
            lax.dynamic_slice(
                norm_all, (me ^ j, pack_width - own_rows), (1, own_rows)
            ).reshape(own_rows)
            for j in range(SHARE)
        ]
    ).astype(jnp.int32)

    attn_low = [attn_weight[:, j].astype(BF) for j in range(4)]
    up_low = up_weight.astype(BF)
    down_low = down_weight.astype(BF)

    def attn_part(index):
        return jnp.concatenate(
            [take_block(attn_low[j], index, width, 1) for j in (2, 3, 0, 1)], axis=1
        )

    def ffn_part(index):
        return jnp.concatenate(
            [take_block(low, index, ff_width, 1) for low in (up_low, down_low)], axis=1
        )

    attn_rows = columns_to_members(attn_part, member)
    up_low, down_low = after([up_low, down_low], [attn_rows, norm_all])
    ffn_rows = columns_to_members(ffn_part, member)
    full, gather_late = gather_groups(
        [attn_rows[:, : 2 * width], attn_rows[:, 2 * width :]]
        + [ffn_rows[:, k * piece : (k + 1) * piece] for k in range(2 * FF_CHUNKS)]
    )
    value_out, query_key = full[:2]
    attn_full = [query_key[:, :width], query_key[:, width:], value_out[:, :width]]
    up_full, down_full = full[2 : 2 + FF_CHUNKS], full[2 + FF_CHUNKS :]

    inputs = tokens.astype(F32)
    unit_one, rstd_one = norm_stats(inputs)
    normed = (unit_one * small_vals[0] + small_vals[1]).astype(BF)
    normed_all = share_tokens(to_gathered_order(normed, group))
    slot_index = jnp.arange(L)
    live_mask = (slot_index[None, :] < IMG + caption_len[:, None]).astype(F32).reshape(own)
    back_out = cotangent.astype(F32) * live_mask[:, None]
    (back_low,) = after([back_out.astype(BF)], [normed_all])
    back_all = share_tokens(to_gathered_order(back_low, group))

    tables = xpos_tables(head_size, width // head_size)
    projected = [dot_f32(normed_all, attn_full[j], 1, 0) for j in range(3)]
    queries, keys_low, values_low, mixed_part = attention_call(
        partial(attention_kernel, head_size), captions, projected, tables, 4, width, "attention"
    )
    mixed_pieces = [mixed_part[:own]] + [
        swap(mixed_part[j * own : (j + 1) * own], j) for j in range(1, SHARE)
    ]
    attn_mixed = jnp.concatenate(in_own_order(mixed_pieces, member), axis=1).astype(F32)
    unit_two, rstd_two = norm_stats(attn_mixed)
    context = (unit_two * small_vals[2] + small_vals[3]).astype(BF)
    context_turned = to_gathered_order(context, group)
    out_own = value_out[:, width:]
    out_far = swap(out_own, 2)
    out_pair = swap(jnp.concatenate([out_own, out_far], axis=1), 1)
    out_full = jnp.concatenate(
        in_own_order([out_own, out_pair[:, :width], out_far, out_pair[:, width:]], member), axis=1
    )
    hidden = inputs + dot_f32(context_turned, out_full, 1, 0)

    unit_three, rstd_three = norm_stats(hidden)
    ffn_in = (unit_three * small_vals[4] + small_vals[5]).astype(BF)
    ffn_all = share_tokens(to_gathered_order(ffn_in, group))
    (context_turned,) = after([context_turned], [ffn_all])
    context_all = share_tokens(context_turned)
    all_tokens = SHARE * own
    upward = [dot_f32(ffn_all, up_full[k], 1, 0) for k in range(FF_CHUNKS)]
    activated = [value * gelu_parts(value)[0] for value in upward]
    mean_own = sum(jnp.sum(value, axis=1) for value in activated) / ff_width
    square_own = sum(
        jnp.sum((value - mean_own[:, None]) ** 2, axis=1) for value in activated
    )
    stats = member_stats(
        jnp.stack([mean_own, square_own]).reshape(2, SHARE, own)
    )
    mean = sum(item[0] for item in stats) / SHARE
    square = sum(item[1] + ff_width * (item[0] - mean) ** 2 for item in stats)
    rstd = lax.rsqrt(square / FF + EPS_NORM).reshape(all_tokens, 1)
    mean = mean.reshape(all_tokens, 1)
    unit = [(value - mean) * rstd for value in activated]
    gain = [wide_own[0, k * piece : (k + 1) * piece] for k in range(FF_CHUNKS)]
    bias = [wide_own[1, k * piece : (k + 1) * piece] for k in range(FF_CHUNKS)]
    ffn_mid = [(unit[k] * gain[k] + bias[k]).astype(BF) for k in range(FF_CHUNKS)]

    def weight_grad(left, right):
        return lambda start, stop: dot_f32(left[:, start:stop], right, 0, 0)

    order = {mask: gather_late for mask in group_masks()}
    down_grads = reduce_groups([weight_grad(back_all, ffn_mid[k]) for k in range(FF_CHUNKS)], order)

    mid_grad = [dot_f32(back_all, down_full[k], 1, 0) for k in range(FF_CHUNKS)]
    lean_own = sum(jnp.sum(mid_grad[k] * gain[k], axis=1) for k in range(FF_CHUNKS))
    slope_own = sum(jnp.sum(mid_grad[k] * gain[k] * unit[k], axis=1) for k in range(FF_CHUNKS))
    both = sum(member_stats(jnp.stack([lean_own, slope_own]).reshape(2, SHARE, own)))
    both = both.reshape(2, all_tokens, 1) / FF
    up_grad_low = []
    for k in range(FF_CHUNKS):
        act_grad = rstd * (mid_grad[k] * gain[k] - both[0] - unit[k] * both[1])
        cdf, density = gelu_parts(upward[k])
        up_grad_low.append((act_grad * (cdf + upward[k] * density)).astype(BF))
    wide_terms = jnp.stack(
        [
            jnp.concatenate([jnp.sum(mid_grad[k] * unit[k], axis=0) for k in range(FF_CHUNKS)]),
            jnp.concatenate([jnp.sum(mid_grad[k], axis=0) for k in range(FF_CHUNKS)]),
        ]
    )
    ffn_in_terms = sum(dot_f32(up_grad_low[k], up_full[k], 1, 1) for k in range(FF_CHUNKS))
    ffn_in_grad = from_gathered_order(sum_to_owner(ffn_in_terms), group)
    up_grads = reduce_groups([weight_grad(ffn_all, up_grad_low[k]) for k in range(FF_CHUNKS)], order)
    hidden_part, gain_three, bias_three = norm_back(unit_three, rstd_three, small_vals[4], ffn_in_grad)
    hidden_grad = back_out + hidden_part
    hidden_low = hidden_grad.astype(BF)
    mid_again = after(ffn_mid, [ffn_in_terms])
    block_terms = sum(dot_f32(mid_again[k], down_full[k], 1, 1) for k in range(FF_CHUNKS))
    (block_terms,) = after([block_terms], [hidden_low])
    block_out = (hidden + from_gathered_order(sum_to_owner(block_terms), group)).astype(BF)

    context_grad = from_gathered_order(dot_f32(hidden_low, out_full, 1, 1), group)
    mixed_grad, gain_two, bias_two = norm_back(unit_two, rstd_two, small_vals[2], context_grad)

    def columns_of_tokens(value):
        return jnp.concatenate(
            [take_block(value, member, width, 1)]
            + [swap(take_block(value, member ^ j, width, 1), j) for j in range(1, SHARE)],
            axis=0,
        )

    mixed_low = columns_of_tokens(mixed_grad.astype(BF))
    proj_grad = attention_call(
        partial(attention_back_kernel, head_size),
        captions,
        [queries, keys_low, values_low, mixed_low],
        tables,
        3,
        width,
        "attention_back",
    )
    hidden_columns = columns_of_tokens(after([hidden_low], [mixed_low])[0])
    attn_grads = reduce_groups(
        [weight_grad(context_all, hidden_columns)]
        + [weight_grad(normed_all, proj_grad[j]) for j in range(3)],
        order,
    )
    attn_grads = attn_grads[1:] + attn_grads[:1]
    normed_grad = from_gathered_order(
        sum_to_owner(sum(dot_f32(proj_grad[j], attn_full[j], 1, 1) for j in range(3))), group
    )
    input_part, gain_one, bias_one = norm_back(unit_one, rstd_one, small_vals[0], normed_grad)
    input_grad = hidden_grad + input_part

    def own_rows_of(blocks):
        joined = jnp.concatenate([block.astype(BF) for block in blocks], axis=1)
        return rows_to_members(joined, member)

    attn_quarters = own_rows_of(attn_grads)
    attn_grad = [
        jnp.concatenate(
            [part[:, j * width : (j + 1) * width] for part in attn_quarters], axis=1
        ).astype(F32)
        for j in range(4)
    ]
    up_grad = jnp.concatenate(own_rows_of(up_grads), axis=1).astype(F32)
    down_grad = jnp.concatenate(own_rows_of(down_grads), axis=1).astype(F32)

    norm_terms = sum_all(
        jnp.concatenate(
            [
                lax.dynamic_update_slice(
                    jnp.zeros((2, SHARE, ff_width), F32),
                    wide_terms[:, None, :],
                    (0, member, 0),
                ).reshape(2 * SHARE * ff_width // D, D),
                jnp.stack([gain_one, bias_one, gain_two, bias_two, gain_three, bias_three]),
            ],
            axis=0,
        )
    )
    wide_grad = take_block(norm_terms[:-6].reshape(2, FF), me, wide_width, 1)
    small_grad = take_block(norm_terms[-6:], me, small_width, 1)

    wide_moment_new, wide_scaled, wide_usq, wide_wsq = vector_stats(
        wide_grad, wide_norms, wide_moment
    )
    small_moment_new, small_scaled, small_usq, small_wsq = vector_stats(
        small_grad, small_norms, small_moment
    )
    attn_old = [attn_weight[:, j] for j in range(4)]
    up_stats = first_stats(up_grad, up_weight, up_row)
    down_stats = first_stats(down_grad, down_weight, down_row)
    packed, unpack = pack_rows(
        [
            up_stats[1],
            down_stats[1],
            up_stats[2],
            down_stats[2],
            jnp.concatenate(
                [jnp.stack(up_stats[3:] + down_stats[3:]), wide_usq, wide_wsq, small_usq, small_wsq]
            ),
        ],
        D,
    )
    up_cols, down_cols, up_weighted, down_weighted, totals = unpack(sum_all(packed))
    up_col_new = column_state(up_col, up_cols)
    down_col_new = column_state(down_col, down_cols)
    up_new = updated(
        up_grad, up_weight, up_stats[0], up_col_new, up_weighted, totals[0], totals[1]
    )
    down_new = updated(
        down_grad, down_weight, down_stats[0], down_col_new, down_weighted, totals[2], totals[3]
    )
    wide_new = vector_finish(wide_scaled, wide_norms, totals[4:6], totals[6:8], FF)
    small_new = vector_finish(small_scaled, small_norms, totals[8:14], totals[14:20], D)

    attn_stats = [first_stats(attn_grad[j], attn_old[j], attn_row[j]) for j in range(4)]
    packed, unpack = pack_rows(
        [item[1] for item in attn_stats]
        + [item[2] for item in attn_stats]
        + [jnp.stack([item[k] for k in (3, 4) for item in attn_stats])],
        D,
    )
    summed = unpack(sum_all(packed))
    attn_col_new = jnp.stack([column_state(attn_col[j], summed[j]) for j in range(4)])
    attn_new = jnp.stack(
        [
            updated(
                attn_grad[j],
                attn_old[j],
                attn_stats[j][0],
                attn_col_new[j],
                summed[4 + j],
                summed[8][j],
                summed[8][4 + j],
            )
            for j in range(4)
        ],
        axis=1,
    )
    attn_row_new = jnp.stack([item[0] for item in attn_stats])
    return (
        block_out,
        input_grad,
        jnp.stack(attn_grad, axis=1),
        up_grad,
        down_grad,
        attn_row_new,
        attn_col_new,
        up_stats[0],
        up_col_new,
        down_stats[0],
        down_col_new,
        attn_new,
        up_new,
        down_new,
        attn_new.astype(BF),
        up_new.astype(BF),
        down_new.astype(BF),
        small_grad,
        wide_grad,
        small_moment_new,
        wide_moment_new,
        small_new,
        wide_new,
    )


def solution(mesh):
    placed = (
        P("dp", None),
        P("dp", None),
        P("dp"),
        P("dp", None, None),
        P("dp", None),
        P("dp", None),
        P(None, "dp"),
        P(None, "dp"),
        P(None, "dp"),
        P(),
        P("dp"),
        P(),
        P("dp"),
        P(),
        P(None, "dp"),
        P(None, "dp"),
    )
    return jax.shard_map(
        per_device,
        mesh=mesh,
        in_specs=placed,
        out_specs=(
            P("dp", None),
            P("dp", None),
            P("dp", None, None),
            P("dp", None),
            P("dp", None),
            P(None, "dp"),
            P(),
            P("dp"),
            P(),
            P("dp"),
            P(),
            P("dp", None, None),
            P("dp", None),
            P("dp", None),
            P("dp", None, None),
            P("dp", None),
            P("dp", None),
            P(None, "dp"),
            P(None, "dp"),
            P(None, "dp"),
            P(None, "dp"),
            P(None, "dp"),
            P(None, "dp"),
        ),
        check_vma=False,
    )
```

```python
from functools import partial
import math

import jax
import jax.numpy as jnp
from jax import lax
from jax.experimental import pallas as pl
from jax.experimental.pallas import tpu as pltpu
from jax.sharding import PartitionSpec as P

D = 2048
FF = 8192
HEADS = 32
L = 128
IMG = 64
SHARE = 4
FF_CHUNKS = 2


EPS_NORM = 1e-05
EPS_SQUARE = 1e-30
EPS_SCALE = 0.001
DECAY_RATE = 0.5
CLIP_LEVEL = 0.5
LEARN_RATE = 0.8
SCALE_BASE = 512.0
MASK_FILL = -1e30

BF = jnp.bfloat16
F32 = jnp.float32


def dot_f32(left, right, left_dim, right_dim):
    return lax.dot_general(
        left, right, (((left_dim,), (right_dim,)), ((), ())), preferred_element_type=F32
    )


def swap(value, mask):
    count = lax.axis_size("dp")
    return lax.ppermute(value, "dp", [(i, i ^ mask) for i in range(count)])


def sum_all(value, masks=None):
    if masks is None:
        masks = [1, 2] + group_masks()[::-1]
    for mask in masks:
        value = value + swap(value, mask)
    return value


def group_masks():
    count = lax.axis_size("dp")
    masks = []
    mask = 2 * SHARE
    while mask < count:
        masks.append(mask)
        mask *= 2
    if count > SHARE:
        masks.append(SHARE)
    return masks


def group_offsets():
    offsets = [0]
    for mask in group_masks():
        offsets = offsets + [item ^ (mask // SHARE) for item in offsets]
    return offsets


def take_block(value, index, width, axis):
    return lax.dynamic_slice_in_dim(value, index * width, width, axis)


def to_gathered_order(value, group):
    offsets = group_offsets()
    width = value.shape[1] // len(offsets)
    return jnp.concatenate([take_block(value, group ^ off, width, 1) for off in offsets], axis=1)


def from_gathered_order(value, group):
    offsets = group_offsets()
    count = len(offsets)
    bits = count.bit_length() - 1
    width = value.shape[1] // count
    blocks = []
    for block in range(count):
        place = group ^ block
        if bits:
            place = (place >> 1) | ((place & 1) << (bits - 1))
        blocks.append(take_block(value, place, width, 1))
    return jnp.concatenate(blocks, axis=1)


def in_own_order(pieces, member):
    low_bit = (member & 1) > 0
    high_bit = (member & 2) > 0
    first = [
        jnp.where(low_bit, pieces[i ^ 1], pieces[i]) for i in range(SHARE)
    ]
    return [jnp.where(high_bit, first[i ^ 2], first[i]) for i in range(SHARE)]


def after(values, deps):
    held = lax.optimization_barrier((list(values), list(deps)))
    return held[0]


def columns_to_members(part, member):
    pieces = [part(member)] + [swap(part(member ^ j), j) for j in range(1, SHARE)]
    return jnp.concatenate(in_own_order(pieces, member), axis=0)


def gather_groups(blocks):
    masks = group_masks()
    blocks = list(blocks)
    arrived = []
    late = []
    for stage in range(len(blocks) + len(masks) - 1):
        active = [
            (stage - depth, mask)
            for depth, mask in enumerate(masks)
            if 0 <= stage - depth < len(blocks)
        ]
        ready = after([blocks[k] for k, mask in active], arrived)
        late = arrived
        arrived = [swap(value, mask) for value, (k, mask) in zip(ready, active)]
        for (k, mask), value, got in zip(active, ready, arrived):
            blocks[k] = jnp.concatenate([value, got], axis=0)
    return blocks, late


def share_tokens(own):
    pair = jnp.concatenate([own, swap(own, 2)], axis=0)
    height = own.shape[0]
    other = swap(pair, 1)
    return jnp.concatenate(
        [pair[:height], other[:height], pair[height:], other[height:]], axis=0
    )


def member_stats(stats):
    out = [stats]
    for j in range(1, SHARE):
        got = swap(stats, j)
        out.append(jnp.stack([got[:, i ^ j] for i in range(SHARE)], axis=1))
    return out


def norm_stats(values):
    mean = jnp.mean(values, axis=-1, keepdims=True)
    center = values - mean
    rstd = lax.rsqrt(jnp.mean(center * center, axis=-1, keepdims=True) + EPS_NORM)
    return center * rstd, rstd


def norm_back(unit, rstd, gain, upstream):
    scaled = upstream * gain
    lean = jnp.mean(scaled, axis=-1, keepdims=True)
    slope = jnp.mean(scaled * unit, axis=-1, keepdims=True)
    return (
        rstd * (scaled - lean - unit * slope),
        jnp.sum(upstream * unit, axis=0),
        jnp.sum(upstream, axis=0),
    )


def xpos_tables(head_size, head_count):
    slot_pos = jnp.arange(L, dtype=F32)[:, None]
    pair_idx = jnp.arange(head_size // 2, dtype=F32)[None, :]
    theta = jnp.exp(-(2.0 * pair_idx / head_size) * jnp.log(10000.0))
    angle = slot_pos * theta
    zeta = (2.0 * pair_idx / head_size + 0.4) / 1.4
    power_table = jnp.exp(jnp.log(zeta) * slot_pos / SCALE_BASE)

    def widen(table):
        return jnp.tile(jnp.repeat(table, 2, axis=1), (1, head_count))

    cosine, sine, power = widen(jnp.cos(angle)), widen(jnp.sin(angle)), widen(power_table)
    return cosine * power, sine * power, cosine / power, sine / power


def quarter_turn(values):
    width = values.shape[1]
    lane = lax.broadcasted_iota(jnp.int32, values.shape, 1)
    return jnp.where(
        lane % 2 == 0, -pltpu.roll(values, width - 1, 1), pltpu.roll(values, 1, 1)
    )


def masked_probs(query, key, caption, head_size):
    scores = dot_f32(query, key, 1, 1) * (1.0 / math.sqrt(head_size))
    row = lax.broadcasted_iota(jnp.int32, scores.shape, 0)
    col = lax.broadcasted_iota(jnp.int32, scores.shape, 1)
    scores = jnp.where((col <= row) & (col < IMG + caption), scores, MASK_FILL)
    terms = jnp.exp(scores - jnp.max(scores, axis=-1, keepdims=True))
    return terms / jnp.sum(terms, axis=-1, keepdims=True)


def attention_kernel(head_size, cap, q_in, k_in, v_in, cq, sq, ck, sk, q_out, k_out, v_out, o_out):
    caption = cap[pl.program_id(0)]
    q_all = q_in[...]
    k_all = k_in[...]
    q_low = (q_all * cq[...] + quarter_turn(q_all) * sq[...]).astype(BF)
    k_low = (k_all * ck[...] + quarter_turn(k_all) * sk[...]).astype(BF)
    v_low = v_in[...].astype(BF)
    q_out[...] = q_low
    k_out[...] = k_low
    v_out[...] = v_low
    mixed = []
    for head in range(q_low.shape[1] // head_size):
        at = slice(head * head_size, (head + 1) * head_size)
        probs = masked_probs(q_low[:, at], k_low[:, at], caption, head_size).astype(BF)
        mixed.append(dot_f32(probs, v_low[:, at], 1, 0))
    o_out[...] = jnp.concatenate(mixed, axis=1).astype(BF)


def attention_back_block(head_size, caption, q_low, k_low, v_low, g_low, tables):
    cq, sq, ck, sk = tables
    grads_q, grads_k, grads_v = [], [], []
    for head in range(q_low.shape[1] // head_size):
        at = slice(head * head_size, (head + 1) * head_size)
        probs = masked_probs(q_low[:, at], k_low[:, at], caption, head_size)
        grads_v.append(dot_f32(probs.astype(BF), g_low[:, at], 0, 0))
        prob_grad = dot_f32(g_low[:, at], v_low[:, at], 1, 1)
        score_grad = probs * (prob_grad - jnp.sum(probs * prob_grad, axis=-1, keepdims=True))
        score_low = (score_grad * (1.0 / math.sqrt(head_size))).astype(BF)
        grads_q.append(dot_f32(score_low, k_low[:, at], 1, 0))
        grads_k.append(dot_f32(score_low, q_low[:, at], 0, 0))
    grad_q = jnp.concatenate(grads_q, axis=1)
    grad_k = jnp.concatenate(grads_k, axis=1)
    return (
        (grad_q * cq - quarter_turn(grad_q) * sq).astype(BF),
        (grad_k * ck - quarter_turn(grad_k) * sk).astype(BF),
        jnp.concatenate(grads_v, axis=1).astype(BF),
    )


def attention_call(kernel, captions, arrays, tables, outputs, width, name):
    row_count = captions.shape[0]
    by_row = pl.BlockSpec((L, width), lambda row, cap: (row, 0))
    table = pl.BlockSpec((L, width), lambda row, cap: (0, 0))
    size = row_count * L * width
    return pl.pallas_call(
        kernel,
        grid_spec=pltpu.PrefetchScalarGridSpec(
            num_scalar_prefetch=1,
            grid=(row_count,),
            in_specs=[by_row] * len(arrays) + [table] * 4,
            out_specs=[by_row] * outputs,
        ),
        out_shape=[jax.ShapeDtypeStruct((row_count * L, width), BF)] * outputs,
        compiler_params=pltpu.CompilerParams(vmem_limit_bytes=32 * 1024 * 1024),
        cost_estimate=pl.CostEstimate(
            flops=12 * size * L, bytes_accessed=16 * size, transcendentals=size * 2
        ),
        name=name,
    )(captions, *arrays, *tables)


MESH = pl.DeviceIdType.MESH
KERNEL_VMEM = 62 * 1024 * 1024


def flipped(index, mask):
    bit = 1
    while bit <= mask:
        if mask & bit:
            index = index + bit - 2 * bit * ((index // bit) % 2)
        bit *= 2
    return index


def partner_masks():
    return list(range(1, SHARE)) + group_masks()


class Wire:
    def __init__(self):
        self.me = lax.axis_index("dp")
        self.member = self.me % SHARE

    def meet(self):
        barrier = pltpu.get_barrier_semaphore()
        masks = partner_masks()
        for mask in masks:
            pl.semaphore_signal(
                barrier, inc=1, device_id=(flipped(self.me, mask),), device_id_type=MESH
            )
        pl.semaphore_wait(barrier, len(masks))

    def copy(self, source, target, send_sem, recv_sem, mask):
        return pltpu.make_async_remote_copy(
            src_ref=source,
            dst_ref=target,
            send_sem=send_sem,
            recv_sem=recv_sem,
            device_id=(flipped(self.me, mask),),
            device_id_type=MESH,
        )


def row_tiles(rows, body, tile=256):
    tile = min(tile, rows)

    @pl.loop(0, rows // tile)
    def _(index):
        body(pl.multiple_of(index * tile, tile), tile)


class Reducer:
    @staticmethod
    def scratch(count, cols):
        stages = len(group_masks())
        halves = [D >> (stage + 1) for stage in range(stages)]
        block = D >> stages
        return (
            [pltpu.VMEM((2, half, cols), BF) for half in halves]
            + [pltpu.VMEM((count, half, cols), BF) for half in halves]
            + [
                pltpu.VMEM((min(stages, count), D // 2, cols), F32),
                pltpu.VMEM((2, block, cols), BF),
                pltpu.SemaphoreType.DMA((count, stages)),
                pltpu.SemaphoreType.DMA((count, stages)),
                pltpu.SemaphoreType.DMA((count, SHARE)),
                pltpu.SemaphoreType.DMA((count, SHARE)),
            ]
        )

    @staticmethod
    def out_shape(count, cols):
        block = D >> len(group_masks())
        return jax.ShapeDtypeStruct((SHARE, count, block // SHARE, cols), BF)

    def __init__(self, wire, count, terms, out, refs):
        self.wire, self.count, self.terms, self.out = wire, count, terms, out
        self.masks = group_masks()[::-1]
        self.stages = len(self.masks)
        self.slots = min(self.stages, count)
        self.sends, refs = refs[: self.stages], refs[self.stages :]
        self.recvs, refs = refs[: self.stages], refs[self.stages :]
        self.kept, self.done, self.send_sem, self.recv_sem, self.out_send, self.out_recv = refs
        self.block = D >> self.stages

    def copy(self, chunk, stage):
        return self.wire.copy(
            self.sends[stage].at[chunk % 2],
            self.recvs[stage].at[chunk],
            self.send_sem.at[chunk, stage],
            self.recv_sem.at[chunk, stage],
            self.masks[stage],
        )

    def start(self, chunk):
        if chunk >= self.count:
            return
        if chunk >= 2:
            self.copy(chunk - 2, 0).wait_send()
        lhs, rhs, cols = self.terms[chunk]
        half = D // 2

        def body(row, tile):
            value = dot_f32(lhs[pl.ds(half + row, tile), :], rhs[:, cols], 1, 0)
            self.sends[0][chunk % 2, pl.ds(row, tile), :] = value.astype(BF)

        row_tiles(half, body)
        self.copy(chunk, 0).start()

    def keep(self, chunk):
        if chunk >= self.count:
            return
        lhs, rhs, cols = self.terms[chunk]

        def body(row, tile):
            self.kept[chunk % self.slots, pl.ds(row, tile), :] = dot_f32(
                lhs[pl.ds(row, tile), :], rhs[:, cols], 1, 0
            )

        row_tiles(D // 2, body)

    def step(self, chunk, stage):
        if not 0 <= chunk < self.count:
            return
        self.copy(chunk, stage - 1).wait_recv()
        if chunk >= 2:
            self.copy(chunk - 2, stage).wait_send()
        half = D >> (stage + 1)
        kept, got, send = self.kept, self.recvs[stage - 1], self.sends[stage]
        slot = chunk % self.slots

        def out_half(row, tile):
            at = pl.ds(half + row, tile)
            send[chunk % 2, pl.ds(row, tile), :] = (
                kept[slot, at, :] + got[chunk, at, :].astype(F32)
            ).astype(BF)

        def own_half(row, tile):
            at = pl.ds(row, tile)
            kept[slot, at, :] = kept[slot, at, :] + got[chunk, at, :].astype(F32)

        row_tiles(half, out_half)
        self.copy(chunk, stage).start()
        row_tiles(half, own_half)

    def give(self, chunk):
        part = self.block // SHARE
        slot = chunk % 2
        copies = []
        for j in range(1, SHARE):
            to = flipped(self.wire.member, j)
            copies.append(
                self.wire.copy(
                    self.done.at[slot, pl.ds(pl.multiple_of(to * part, part), part), :],
                    self.out.at[j, chunk],
                    self.out_send.at[chunk, j],
                    self.out_recv.at[chunk, j],
                    j,
                )
            )
        own = pltpu.make_async_copy(
            self.done.at[slot, pl.ds(pl.multiple_of(self.wire.member * part, part), part), :],
            self.out.at[0, chunk],
            self.out_send.at[chunk, 0],
        )
        return own, copies

    def given(self, chunk):
        own, copies = self.give(chunk)
        own.wait()
        for item in copies:
            item.wait_send()

    def finish(self, chunk):
        if not 0 <= chunk < self.count:
            return
        self.copy(chunk, self.stages - 1).wait_recv()
        if chunk >= 2:
            self.given(chunk - 2)
        got = self.recvs[self.stages - 1]
        slot = chunk % self.slots

        def body(row, tile):
            at = pl.ds(row, tile)
            self.done[chunk % 2, at, :] = (
                self.kept[slot, at, :] + got[chunk, at, :].astype(F32)
            ).astype(BF)

        row_tiles(self.block, body)
        own, copies = self.give(chunk)
        own.start()
        for item in copies:
            item.start()

    def tick(self, at):
        for stage in range(1, self.stages):
            self.step(at - stage + 1, stage)
            if stage == 1:
                self.start(at + 2)
        if self.stages == 1:
            self.start(at + 2)
        self.finish(at - self.stages + 1)
        self.keep(at + 1)

    def ticks(self):
        return self.count + self.stages - 1

    def close(self):
        for chunk in range(max(0, self.count - 2), self.count):
            for stage in range(self.stages):
                self.copy(chunk, stage).wait_send()
            self.given(chunk)
        for chunk in range(self.count):
            for item in self.give(chunk)[1]:
                item.wait_recv()


class OwnerSum:
    @staticmethod
    def scratch(own):
        return [
            pltpu.VMEM((2 * own, D), BF),
            pltpu.VMEM((own, D), BF),
            pltpu.SemaphoreType.DMA((4,)),
        ]

    def __init__(self, wire, own, send, kept, refs):
        self.wire, self.own, self.send, self.kept = wire, own, send, kept
        self.near, self.far, self.sems = refs

    def core_copy(self):
        return self.wire.copy(
            self.send.at[pl.ds(0, 2 * self.own), :],
            self.near,
            self.sems.at[0],
            self.sems.at[1],
            1,
        )

    def far_copy(self):
        return self.wire.copy(
            self.send.at[pl.ds(2 * self.own, self.own), :],
            self.far,
            self.sems.at[2],
            self.sems.at[3],
            2,
        )

    def first(self, term):
        for place, block in enumerate((3, 1)):

            def body(row, tile, place=place, block=block):
                self.send[pl.ds(place * self.own + row, tile), :] = term(block, row, tile).astype(BF)

            row_tiles(self.own, body)
        self.core_copy().start()

    def second(self, term):
        for place, block in enumerate((2, 0)):

            def body(row, tile, place=place, block=block):
                self.kept[pl.ds((1 - place) * self.own + row, tile), :] = term(block, row, tile)

            row_tiles(self.own, body)

    def third(self):
        self.core_copy().wait_recv()
        own = self.own

        def far(row, tile):
            self.send[pl.ds(2 * own + row, tile), :] = (
                self.kept[pl.ds(own + row, tile), :] + self.near[pl.ds(row, tile), :].astype(F32)
            ).astype(BF)

        def near(row, tile):
            at = pl.ds(row, tile)
            self.kept[at, :] = self.kept[at, :] + self.near[pl.ds(own + row, tile), :].astype(F32)

        row_tiles(own, far)
        self.far_copy().start()
        row_tiles(own, near)

    def last(self):
        self.far_copy().wait_recv()

        def body(row, tile):
            at = pl.ds(row, tile)
            self.kept[at, :] = self.kept[at, :] + self.far[at, :].astype(F32)

        row_tiles(self.own, body)
        self.core_copy().wait_send()
        self.far_copy().wait_send()


REDUCE_CHUNKS = 4


def ffn_back_kernel(own, back, back_t, mid, down, up, unit_in, slope_in, gain, rstd, *refs):
    width = mid.shape[1]
    tokens = SHARE * own
    cols = width // REDUCE_CHUNKS
    pieces = len(down)
    out, up_low_out, wide_out, sum_out = refs[:4]
    refs = refs[4:]
    wire = Wire()
    count = len(Reducer.scratch(REDUCE_CHUNKS, cols))
    reducer_refs, refs = refs[:count], refs[count:]
    sum_refs, refs = refs[:3], refs[3:]
    (
        back_v, back_tv, mid_v, weight, unit, slope, grad, sums, stat_send, stat_recv,
        load_sem, stat_sems, store_sem,
    ) = refs

    def weight_copies(parts, first):
        step = width // pieces
        return [
            pltpu.make_async_copy(
                part, weight.at[:, pl.ds(k * step, step)], load_sem.at[first + k]
            )
            for k, part in enumerate(parts)
        ]

    loads = [
        pltpu.make_async_copy(source, target, load_sem.at[k])
        for k, (source, target) in enumerate(
            [(back_t, back_tv), (mid, mid_v), (back, back_v), (unit_in, unit), (slope_in, slope)]
        )
    ]
    down_loads = weight_copies(down, 5)
    up_loads = weight_copies(up, 5 + pieces)
    for item in loads[:3] + down_loads + loads[3:]:
        item.start()
    wire.meet()
    reducer = Reducer(
        wire,
        REDUCE_CHUNKS,
        [(back_tv, mid_v, pl.ds(c * cols, cols)) for c in range(REDUCE_CHUNKS)],
        out,
        reducer_refs,
    )
    loads[0].wait()
    loads[1].wait()
    reducer.start(0)
    reducer.start(1)
    reducer.keep(0)

    wide_out[...] = jnp.zeros_like(wide_out)
    sums[...] = jnp.zeros_like(sums)

    def token_tiles(body):
        row_tiles(tokens, body, own)

    def first_pass(k):
        at_cols = pl.ds(k * cols, cols)

        def body(row, tile):
            at = pl.ds(row, tile)
            value = dot_f32(back_v[at, :], weight[:, at_cols], 1, 0)
            grad[at, at_cols] = value
            part = unit[at, at_cols].astype(F32)
            scaled = value * gain[:, at_cols]
            lane = lax.broadcasted_iota(jnp.int32, (tile, sums.shape[1]), 1)
            sums[at, :] += jnp.where(
                lane == 0,
                jnp.sum(scaled, axis=1, keepdims=True),
                jnp.sum(scaled * part, axis=1, keepdims=True),
            )
            wide_out[0:1, at_cols] += jnp.sum(value * part, axis=0, keepdims=True)
            wide_out[1:2, at_cols] += jnp.sum(value, axis=0, keepdims=True)

        token_tiles(body)

    loads[2].wait()
    for item in down_loads:
        item.wait()
    loads[3].wait()
    loads[4].wait()
    first_pass(0)
    first_pass(1)
    reducer.tick(0)
    first_pass(2)
    first_pass(3)
    for item in up_loads:
        item.start()

    stats = [
        wire.copy(
            stat_send, stat_recv.at[j - 1], stat_sems.at[0, j - 1], stat_sems.at[1, j - 1], j
        )
        for j in range(1, SHARE)
    ]
    for j in range(SHARE):
        stat_send[j] = sums[pl.ds(j * own, own), :].T[0:8, :]
    for item in stats:
        item.start()
    reducer.tick(1)
    for item in stats:
        item.wait_recv()
    for j in range(SHARE):
        total = stat_send[j]
        for k in range(1, SHARE):
            total = total + stat_recv[k - 1, j ^ k]
        total = total * (1.0 / (SHARE * width))
        sums[pl.ds(j * own, own), :] = jnp.concatenate([total] * (sums.shape[1] // 8), axis=0).T
    for item in stats:
        item.wait_send()

    def second_pass(k):
        at_cols = pl.ds(k * cols, cols)

        def body(row, tile):
            at = pl.ds(row, tile)
            act_grad = rstd[at, 0:1] * (
                grad[at, at_cols] * gain[:, at_cols]
                - sums[at, 0:1]
                - unit[at, at_cols].astype(F32) * sums[at, 1:2]
            )
            unit[at, at_cols] = (act_grad * slope[at, at_cols].astype(F32)).astype(BF)

        token_tiles(body)

    second_pass(0)
    second_pass(1)
    second_pass(2)
    second_pass(3)
    store = pltpu.make_async_copy(unit, up_low_out, store_sem.at[0])
    store.start()
    reducer.tick(2)
    for item in up_loads:
        item.wait()

    def term(block, row, tile):
        return dot_f32(unit[pl.ds(block * own + row, tile), :], weight[...], 1, 1)

    owner = OwnerSum(wire, own, slope, grad, sum_refs)
    owner.first(term)
    owner.second(term)
    reducer.tick(3)
    owner.third()
    for at in range(4, reducer.ticks()):
        reducer.tick(at)
    owner.last()
    result = pltpu.make_async_copy(grad.at[pl.ds(0, own), :], sum_out, store_sem.at[1])
    result.start()
    reducer.close()
    store.wait()
    result.wait()


def ffn_back(back, mid, down, up, unit, slope, gain, rstd):
    tokens, width = mid.shape
    own = tokens // SHARE
    cols = width // REDUCE_CHUNKS
    lanes = 128
    any_spec = pl.BlockSpec(memory_space=pl.ANY)
    vmem = pl.BlockSpec(memory_space=pltpu.VMEM)
    pieces = len(down)

    def kernel(back, back_t, mid, *refs):
        down, up, refs = refs[:pieces], refs[pieces : 2 * pieces], refs[2 * pieces :]
        ffn_back_kernel(own, back, back_t, mid, down, up, *refs)

    return pl.pallas_call(
        kernel,
        in_specs=[any_spec] * (5 + 2 * pieces) + [vmem] * 2,
        out_specs=[any_spec, any_spec, vmem, any_spec],
        out_shape=[
            Reducer.out_shape(REDUCE_CHUNKS, cols),
            jax.ShapeDtypeStruct((tokens, width), BF),
            jax.ShapeDtypeStruct((8, width), F32),
            jax.ShapeDtypeStruct((own, D), F32),
        ],
        scratch_shapes=Reducer.scratch(REDUCE_CHUNKS, cols)
        + OwnerSum.scratch(own)
        + [
            pltpu.VMEM((tokens, D), BF),
            pltpu.VMEM((D, tokens), BF),
            pltpu.VMEM((tokens, width), BF),
            pltpu.VMEM((D, width), BF),
            pltpu.VMEM((tokens, width), BF),
            pltpu.VMEM((tokens, width), BF),
            pltpu.VMEM((tokens, width), F32),
            pltpu.VMEM((tokens, lanes), F32),
            pltpu.VMEM((SHARE, 8, own), F32),
            pltpu.VMEM((SHARE - 1, SHARE, 8, own), F32),
            pltpu.SemaphoreType.DMA((5 + 2 * pieces,)),
            pltpu.SemaphoreType.DMA((2, SHARE - 1)),
            pltpu.SemaphoreType.DMA((2,)),
        ],
        compiler_params=pltpu.CompilerParams(
            collective_id=1, has_side_effects=True, vmem_limit_bytes=KERNEL_VMEM
        ),
        name="ffn_back",
    )(
        back,
        back.T,
        mid,
        *down,
        *up,
        unit,
        slope,
        gain[None],
        jnp.broadcast_to(rstd, (tokens, lanes)),
    )


def attention_back_kernel(
    head_size, own, left_t, right, q_in, k_in, v_in, mixed, hidden, cap, cq, sq, ck, sk, *refs
):
    width = q_in.shape[1]
    cols = right.shape[1] // REDUCE_CHUNKS
    out, q_out, k_out, v_out, hidden_out = refs[:5]
    refs = refs[5:]
    wire = Wire()
    count = len(Reducer.scratch(REDUCE_CHUNKS, cols))
    reducer_refs, refs = refs[:count], refs[count:]
    left_v, right_v, q_v, k_v, v_v, mixed_cols, hidden_cols, load_sem, turn_sem = refs
    loads = [
        pltpu.make_async_copy(source, target, load_sem.at[k])
        for k, (source, target) in enumerate(
            [(left_t, left_v), (right, right_v), (q_in, q_v), (k_in, k_v), (v_in, v_v)]
        )
    ]
    for item in loads:
        item.start()
    wire.meet()

    def turn(source, target, sems):
        copies = []
        for j in range(1, SHARE):
            to = pl.multiple_of(flipped(wire.member, j) * width, width)
            copies.append(
                wire.copy(
                    source.at[:, pl.ds(to, width)],
                    target.at[pl.ds(j * own, own), :],
                    sems.at[0, j],
                    sems.at[1, j],
                    j,
                )
            )
        here = pl.multiple_of(wire.member * width, width)
        local = pltpu.make_async_copy(
            source.at[:, pl.ds(here, width)], target.at[pl.ds(0, own), :], sems.at[0, 0]
        )
        for item in copies + [local]:
            item.start()
        return copies, local

    def turned(copies, local):
        local.wait()
        for item in copies:
            item.wait_recv()

    mixed_turn = turn(mixed, mixed_cols, turn_sem.at[0])
    reducer = Reducer(
        wire,
        REDUCE_CHUNKS,
        [(left_v, right_v, pl.ds(c * cols, cols)) for c in range(REDUCE_CHUNKS)],
        out,
        reducer_refs,
    )
    loads[0].wait()
    loads[1].wait()
    reducer.start(0)
    reducer.start(1)
    hidden_turn = turn(hidden, hidden_cols, turn_sem.at[1])
    reducer.keep(0)
    turned(*mixed_turn)
    for item in loads[2:]:
        item.wait()
    row_count = SHARE * own // L

    def rows(first, last):
        @pl.loop(first, last)
        def _(row):
            at = pl.ds(pl.multiple_of(row * L, L), L)
            got = attention_back_block(
                head_size,
                cap[row],
                q_v[at, :],
                k_v[at, :],
                v_v[at, :],
                mixed_cols[at, :],
                (cq[...], sq[...], ck[...], sk[...]),
            )
            q_v[at, :], k_v[at, :], v_v[at, :] = got

    rows(0, row_count // 2)
    reducer.tick(0)
    rows(row_count // 2, row_count)
    stores = [
        pltpu.make_async_copy(source, target, load_sem.at[k])
        for k, (source, target) in enumerate([(q_v, q_out), (k_v, k_out), (v_v, v_out)])
    ]
    for item in stores:
        item.start()
    reducer.tick(1)
    turned(*hidden_turn)
    stores.append(pltpu.make_async_copy(hidden_cols, hidden_out, load_sem.at[3]))
    stores[-1].start()
    for at in range(2, reducer.ticks()):
        reducer.tick(at)
    reducer.close()
    for item in stores:
        item.wait()
    for item in mixed_turn[0] + hidden_turn[0]:
        item.wait_send()


def attention_back(left, right, queries, keys, values, mixed, hidden, captions, tables):
    tokens, width = queries.shape
    own = tokens // SHARE
    cols = right.shape[1] // REDUCE_CHUNKS
    any_spec = pl.BlockSpec(memory_space=pl.ANY)
    vmem = pl.BlockSpec(memory_space=pltpu.VMEM)
    part = jax.ShapeDtypeStruct((tokens, width), BF)
    return pl.pallas_call(
        partial(attention_back_kernel, D // HEADS, own),
        in_specs=[any_spec] * 5
        + [vmem] * 2
        + [pl.BlockSpec(memory_space=pltpu.SMEM)]
        + [vmem] * 4,
        out_specs=[any_spec] * 5,
        out_shape=[Reducer.out_shape(REDUCE_CHUNKS, cols)] + [part] * 4,
        scratch_shapes=Reducer.scratch(REDUCE_CHUNKS, cols)
        + [pltpu.VMEM((D, tokens), BF), pltpu.VMEM(right.shape, BF)]
        + [pltpu.VMEM((tokens, width), BF)] * 5
        + [pltpu.SemaphoreType.DMA((5,)), pltpu.SemaphoreType.DMA((2, 2, SHARE))],
        compiler_params=pltpu.CompilerParams(
            collective_id=2, has_side_effects=True, vmem_limit_bytes=KERNEL_VMEM
        ),
        name="attention_back",
    )(left.T, right, queries, keys, values, mixed, hidden, captions, *tables)


def project_back_kernel(own, normed_t, context_t, *refs):
    parts, refs = refs[:4], refs[4:]
    mid, query_key, value_out, refs = refs[0], refs[1], refs[2], refs[3:]
    pieces = FF_CHUNKS
    down, refs = refs[:pieces], refs[pieces:]
    out, grad_out, block_out = refs[:3]
    refs = refs[3:]
    width = parts[0].shape[1]
    wire = Wire()
    count = len(Reducer.scratch(SHARE, width))
    reducer_refs, refs = refs[:count], refs[count:]
    grad_refs, refs = refs[:3], refs[3:]
    block_refs, refs = refs[:3], refs[3:]
    normed_v, context_v, parts_v, mid_v, weight, send, kept, load_sem, store_sem = refs
    loads = [
        pltpu.make_async_copy(source, target, load_sem.at[k])
        for k, (source, target) in enumerate(
            [
                (context_t, context_v),
                (parts[0], parts_v.at[0]),
                (normed_t, normed_v),
                (parts[1], parts_v.at[1]),
                (parts[2], parts_v.at[2]),
                (parts[3], parts_v.at[3]),
                (query_key, weight.at[:, pl.ds(0, 2 * width)]),
                (value_out.at[:, pl.ds(0, width)], weight.at[:, pl.ds(2 * width, width)]),
                (mid, mid_v),
            ]
        )
    ]
    for item in loads:
        item.start()
    wire.meet()
    every = pl.ds(0, width)
    reducer = Reducer(
        wire,
        SHARE,
        [(context_v, parts_v.at[0], every)]
        + [(normed_v, parts_v.at[k], every) for k in range(1, 4)],
        out,
        reducer_refs,
    )
    loads[0].wait()
    loads[1].wait()
    reducer.start(0)
    loads[2].wait()
    loads[3].wait()
    reducer.start(1)
    reducer.keep(0)
    for item in loads[4:]:
        item.wait()

    def grad_term(block, row, tile):
        at = pl.ds(block * own + row, tile)
        return sum(
            dot_f32(parts_v[1 + k, at, :], weight[:, pl.ds(k * width, width)], 1, 1)
            for k in range(3)
        )

    grad_sum = OwnerSum(wire, own, send, kept, grad_refs)
    grad_sum.first(grad_term)
    grad_sum.second(grad_term)
    step = mid.shape[1] // pieces
    down_loads = [
        pltpu.make_async_copy(part, weight.at[:, pl.ds(k * step, step)], load_sem.at[9 + k])
        for k, part in enumerate(down)
    ]
    for item in down_loads:
        item.start()
    reducer.tick(0)
    grad_sum.third()
    for item in down_loads:
        item.wait()
    reducer.tick(1)
    grad_sum.last()
    grad_store = pltpu.make_async_copy(kept.at[pl.ds(0, own), :], grad_out, store_sem.at[0])
    grad_store.start()

    def block_term(block, row, tile):
        at = pl.ds(block * own + row, tile)
        return dot_f32(mid_v[at, :], weight[...], 1, 1)

    block_sum = OwnerSum(wire, own, send, kept, block_refs)
    block_sum.first(block_term)
    reducer.tick(2)
    grad_store.wait()
    block_sum.second(block_term)
    block_sum.third()
    for at in range(3, reducer.ticks()):
        reducer.tick(at)
    block_sum.last()
    block_store = pltpu.make_async_copy(kept.at[pl.ds(0, own), :], block_out, store_sem.at[1])
    block_store.start()
    reducer.close()
    block_store.wait()


def project_back(normed, context, parts, mid, query_key, value_out, down):
    tokens, width = parts[0].shape
    own = tokens // SHARE
    any_spec = pl.BlockSpec(memory_space=pl.ANY)
    part = jax.ShapeDtypeStruct((own, D), F32)
    return pl.pallas_call(
        partial(project_back_kernel, own),
        in_specs=[any_spec] * (9 + len(down)),
        out_specs=[any_spec] * 3,
        out_shape=[Reducer.out_shape(SHARE, width), part, part],
        scratch_shapes=Reducer.scratch(SHARE, width)
        + OwnerSum.scratch(own)
        + OwnerSum.scratch(own)
        + [
            pltpu.VMEM((D, tokens), BF),
            pltpu.VMEM((D, tokens), BF),
            pltpu.VMEM((4, tokens, width), BF),
            pltpu.VMEM(mid.shape, BF),
            pltpu.VMEM((D, mid.shape[1]), BF),
            pltpu.VMEM((3 * own, D), BF),
            pltpu.VMEM((2 * own, D), F32),
            pltpu.SemaphoreType.DMA((9 + len(down),)),
            pltpu.SemaphoreType.DMA((2,)),
        ],
        compiler_params=pltpu.CompilerParams(
            collective_id=3, has_side_effects=True, vmem_limit_bytes=KERNEL_VMEM
        ),
        name="project_back",
    )(normed.T, context.T, *parts, mid, query_key, value_out, *down)


def gelu_parts(value):
    cdf = 0.5 * (1.0 + lax.erf(value * math.sqrt(0.5)))
    density = jnp.exp(-0.5 * value * value) * (1.0 / math.sqrt(2.0 * math.pi))
    return cdf, density


def first_stats(grad, weight, row_old):
    squares = grad * grad
    row_new = DECAY_RATE * row_old + (1.0 - DECAY_RATE) * (
        jnp.mean(squares, axis=1) + EPS_SQUARE
    )
    return (
        row_new,
        jnp.sum(squares, axis=0),
        jnp.sum(squares / row_new[:, None], axis=0),
        jnp.sum(row_new),
        jnp.sum(weight * weight),
    )


def column_state(col_old, col_sums):
    return DECAY_RATE * col_old + (1.0 - DECAY_RATE) * (col_sums / D + EPS_SQUARE)


def updated(grad, weight, row_new, col_new, weighted, row_sum, weight_square):
    size = D * weight.shape[1]
    row_mean = row_sum / D
    upd_rms = jnp.sqrt(row_mean * jnp.sum(weighted / col_new) / size)
    weight_rms = jnp.sqrt(weight_square / size)
    step = LEARN_RATE * jnp.maximum(EPS_SCALE, weight_rms) / jnp.maximum(1.0, upd_rms / CLIP_LEVEL)
    row_scale = lax.rsqrt(row_new / row_mean) * step
    return weight - grad * row_scale[:, None] * lax.rsqrt(col_new)[None, :]


def vector_stats(grad_rows, param_rows, moment_old):
    moment_new = DECAY_RATE * moment_old + (1.0 - DECAY_RATE) * (grad_rows * grad_rows + EPS_SQUARE)
    scaled = grad_rows * lax.rsqrt(moment_new)
    return (
        moment_new,
        scaled,
        jnp.sum(scaled * scaled, axis=1),
        jnp.sum(param_rows * param_rows, axis=1),
    )


def vector_finish(scaled, param_rows, upd_square, weight_square, full_width):
    upd_rms = jnp.sqrt(upd_square / full_width)[:, None]
    weight_rms = jnp.sqrt(weight_square / full_width)[:, None]
    return param_rows - LEARN_RATE * jnp.maximum(EPS_SCALE, weight_rms) * scaled / jnp.maximum(
        1.0, upd_rms / CLIP_LEVEL
    )


def pack_rows(parts, width):
    rows, layout, at = [], [], 0
    for part in parts:
        flat = part.reshape(-1)
        count = -(-flat.shape[0] // width)
        flat = jnp.pad(flat, (0, count * width - flat.shape[0]))
        rows.append(flat.reshape(count, width))
        layout.append((at, count, part.shape))
        at += count
    def unpack(packed):
        return [
            packed[start : start + count].reshape(-1)[: math.prod(shape)].reshape(shape)
            for start, count, shape in layout
        ]
    return jnp.concatenate(rows, axis=0), unpack


def per_device(
    tokens,
    cotangent,
    caption_len,
    attn_weight,
    up_weight,
    down_weight,
    small_norms,
    wide_norms,
    attn_row,
    attn_col,
    up_row,
    up_col,
    down_row,
    down_col,
    small_moment,
    wide_moment,
):
    count = lax.axis_size("dp")
    me = lax.axis_index("dp")
    member = me % SHARE
    group = me // SHARE
    head_size = D // HEADS
    width = D // SHARE
    ff_width = FF // SHARE
    piece = ff_width // FF_CHUNKS
    own = tokens.shape[0]
    own_rows = caption_len.shape[0]
    local_rows = attn_weight.shape[0]

    norm_pack = jnp.concatenate(
        [
            small_norms.astype(BF).reshape(-1),
            wide_norms.astype(BF).reshape(-1),
            caption_len.astype(BF),
        ]
    )
    pack_width = norm_pack.shape[0]
    spread = jnp.zeros((count, pack_width), BF)
    spread = lax.dynamic_update_slice(spread, norm_pack[None], (me, 0))
    norm_all = sum_all(spread, group_masks() + [1, 2])
    small_width = D // count
    wide_width = FF // count
    small_vals = (
        norm_all[:, : 6 * small_width].reshape(count, 6, small_width).transpose(1, 0, 2)
    ).reshape(6, D).astype(F32)
    wide_vals = (
        norm_all[:, 6 * small_width : 6 * small_width + 2 * wide_width]
        .reshape(count, 2, wide_width)
        .transpose(1, 0, 2)
    ).reshape(2, FF).astype(F32)
    wide_own = take_block(wide_vals, member, ff_width, 1)
    captions = jnp.concatenate(
        [
            lax.dynamic_slice(
                norm_all, (me ^ j, pack_width - own_rows), (1, own_rows)
            ).reshape(own_rows)
            for j in range(SHARE)
        ]
    ).astype(jnp.int32)

    attn_low = [attn_weight[:, j].astype(BF) for j in range(4)]
    up_low = up_weight.astype(BF)
    down_low = down_weight.astype(BF)

    def attn_part(index):
        return jnp.concatenate(
            [take_block(attn_low[j], index, width, 1) for j in (2, 3, 0, 1)], axis=1
        )

    def ffn_part(index):
        return jnp.concatenate(
            [take_block(low, index, ff_width, 1) for low in (up_low, down_low)], axis=1
        )

    attn_rows = columns_to_members(attn_part, member)
    up_low, down_low = after([up_low, down_low], [attn_rows, norm_all])
    ffn_rows = columns_to_members(ffn_part, member)
    full, gather_late = gather_groups(
        [attn_rows[:, : 2 * width], attn_rows[:, 2 * width :]]
        + [ffn_rows[:, k * piece : (k + 1) * piece] for k in range(2 * FF_CHUNKS)]
    )
    value_out, query_key = full[:2]
    attn_full = [query_key[:, :width], query_key[:, width:], value_out[:, :width]]
    up_full, down_full = full[2 : 2 + FF_CHUNKS], full[2 + FF_CHUNKS :]

    inputs = tokens.astype(F32)
    unit_one, rstd_one = norm_stats(inputs)
    normed = (unit_one * small_vals[0] + small_vals[1]).astype(BF)
    normed_all = share_tokens(to_gathered_order(normed, group))
    slot_index = jnp.arange(L)
    live_mask = (slot_index[None, :] < IMG + caption_len[:, None]).astype(F32).reshape(own)
    back_out = cotangent.astype(F32) * live_mask[:, None]
    (back_low,) = after([back_out.astype(BF)], [normed_all])
    back_all = share_tokens(to_gathered_order(back_low, group))

    tables = xpos_tables(head_size, width // head_size)
    projected = [dot_f32(normed_all, attn_full[j], 1, 0) for j in range(3)]
    queries, keys_low, values_low, mixed_part = attention_call(
        partial(attention_kernel, head_size), captions, projected, tables, 4, width, "attention"
    )
    mixed_pieces = [mixed_part[:own]] + [
        swap(mixed_part[j * own : (j + 1) * own], j) for j in range(1, SHARE)
    ]
    attn_mixed = jnp.concatenate(in_own_order(mixed_pieces, member), axis=1).astype(F32)
    unit_two, rstd_two = norm_stats(attn_mixed)
    context = (unit_two * small_vals[2] + small_vals[3]).astype(BF)
    context_turned = to_gathered_order(context, group)
    out_own = value_out[:, width:]
    out_far = swap(out_own, 2)
    out_pair = swap(jnp.concatenate([out_own, out_far], axis=1), 1)
    out_full = jnp.concatenate(
        in_own_order([out_own, out_pair[:, :width], out_far, out_pair[:, width:]], member), axis=1
    )
    hidden = inputs + dot_f32(context_turned, out_full, 1, 0)

    unit_three, rstd_three = norm_stats(hidden)
    ffn_in = (unit_three * small_vals[4] + small_vals[5]).astype(BF)
    ffn_all = share_tokens(to_gathered_order(ffn_in, group))
    (context_turned,) = after([context_turned], [ffn_all])
    context_all = share_tokens(context_turned)
    all_tokens = SHARE * own
    upward = [dot_f32(ffn_all, up_full[k], 1, 0) for k in range(FF_CHUNKS)]
    activated = [value * gelu_parts(value)[0] for value in upward]
    mean_own = sum(jnp.sum(value, axis=1) for value in activated) / ff_width
    square_own = sum(
        jnp.sum((value - mean_own[:, None]) ** 2, axis=1) for value in activated
    )
    stats = member_stats(
        jnp.stack([mean_own, square_own]).reshape(2, SHARE, own)
    )
    mean = sum(item[0] for item in stats) / SHARE
    square = sum(item[1] + ff_width * (item[0] - mean) ** 2 for item in stats)
    rstd = lax.rsqrt(square / FF + EPS_NORM).reshape(all_tokens, 1)
    mean = mean.reshape(all_tokens, 1)
    unit = [(value - mean) * rstd for value in activated]
    gain = [wide_own[0, k * piece : (k + 1) * piece] for k in range(FF_CHUNKS)]
    bias = [wide_own[1, k * piece : (k + 1) * piece] for k in range(FF_CHUNKS)]
    ffn_mid = [(unit[k] * gain[k] + bias[k]).astype(BF) for k in range(FF_CHUNKS)]


    slopes = []
    for value in upward:
        cdf, density = gelu_parts(value)
        slopes.append((cdf + value * density).astype(BF))
    ffn_mid = jnp.concatenate(ffn_mid, axis=1)
    down_rows, up_grad_low, wide_terms, ffn_in_grad = ffn_back(
        back_all,
        ffn_mid,
        down_full,
        up_full,
        jnp.concatenate([value.astype(BF) for value in unit], axis=1),
        jnp.concatenate(slopes, axis=1),
        wide_own[0],
        rstd,
    )
    wide_terms = wide_terms[:2]
    ffn_in_grad = from_gathered_order(ffn_in_grad, group)
    hidden_part, gain_three, bias_three = norm_back(unit_three, rstd_three, small_vals[4], ffn_in_grad)
    hidden_grad = back_out + hidden_part
    hidden_low = hidden_grad.astype(BF)

    context_grad = from_gathered_order(dot_f32(hidden_low, out_full, 1, 1), group)
    mixed_grad, gain_two, bias_two = norm_back(unit_two, rstd_two, small_vals[2], context_grad)

    up_rows, grad_q, grad_k, grad_v, hidden_cols = attention_back(
        ffn_all,
        up_grad_low,
        queries,
        keys_low,
        values_low,
        mixed_grad.astype(BF),
        hidden_low,
        captions,
        tables,
    )
    attn_rows_out, normed_grad, block_sum = project_back(
        normed_all,
        context_all,
        [hidden_cols, grad_q, grad_k, grad_v],
        ffn_mid,
        query_key,
        value_out,
        down_full,
    )
    normed_grad = from_gathered_order(normed_grad, group)
    block_out = (hidden + from_gathered_order(block_sum, group)).astype(BF)
    input_part, gain_one, bias_one = norm_back(unit_one, rstd_one, small_vals[0], normed_grad)
    input_grad = hidden_grad + input_part

    def joined(rows):
        quarters = [
            jnp.concatenate([rows[j, c] for c in range(REDUCE_CHUNKS)], axis=1)
            for j in range(SHARE)
        ]
        return jnp.concatenate(in_own_order(quarters, member), axis=1).astype(F32)

    attn_grad = [
        jnp.concatenate(
            in_own_order([attn_rows_out[j, c] for j in range(SHARE)], member), axis=1
        ).astype(F32)
        for c in (1, 2, 3, 0)
    ]
    up_grad = joined(up_rows)
    down_grad = joined(down_rows)

    norm_terms = sum_all(
        jnp.concatenate(
            [
                lax.dynamic_update_slice(
                    jnp.zeros((2, SHARE, ff_width), F32),
                    wide_terms[:, None, :],
                    (0, member, 0),
                ).reshape(2 * SHARE * ff_width // D, D),
                jnp.stack([gain_one, bias_one, gain_two, bias_two, gain_three, bias_three]),
            ],
            axis=0,
        )
    )
    wide_grad = take_block(norm_terms[:-6].reshape(2, FF), me, wide_width, 1)
    small_grad = take_block(norm_terms[-6:], me, small_width, 1)

    wide_moment_new, wide_scaled, wide_usq, wide_wsq = vector_stats(
        wide_grad, wide_norms, wide_moment
    )
    small_moment_new, small_scaled, small_usq, small_wsq = vector_stats(
        small_grad, small_norms, small_moment
    )
    attn_old = [attn_weight[:, j] for j in range(4)]
    up_stats = first_stats(up_grad, up_weight, up_row)
    down_stats = first_stats(down_grad, down_weight, down_row)
    packed, unpack = pack_rows(
        [
            up_stats[1],
            down_stats[1],
            up_stats[2],
            down_stats[2],
            jnp.concatenate(
                [jnp.stack(up_stats[3:] + down_stats[3:]), wide_usq, wide_wsq, small_usq, small_wsq]
            ),
        ],
        D,
    )
    up_cols, down_cols, up_weighted, down_weighted, totals = unpack(sum_all(packed))
    up_col_new = column_state(up_col, up_cols)
    down_col_new = column_state(down_col, down_cols)
    up_new = updated(
        up_grad, up_weight, up_stats[0], up_col_new, up_weighted, totals[0], totals[1]
    )
    down_new = updated(
        down_grad, down_weight, down_stats[0], down_col_new, down_weighted, totals[2], totals[3]
    )
    wide_new = vector_finish(wide_scaled, wide_norms, totals[4:6], totals[6:8], FF)
    small_new = vector_finish(small_scaled, small_norms, totals[8:14], totals[14:20], D)

    attn_stats = [first_stats(attn_grad[j], attn_old[j], attn_row[j]) for j in range(4)]
    packed, unpack = pack_rows(
        [item[1] for item in attn_stats]
        + [item[2] for item in attn_stats]
        + [jnp.stack([item[k] for k in (3, 4) for item in attn_stats])],
        D,
    )
    summed = unpack(sum_all(packed))
    attn_col_new = jnp.stack([column_state(attn_col[j], summed[j]) for j in range(4)])
    attn_new = jnp.stack(
        [
            updated(
                attn_grad[j],
                attn_old[j],
                attn_stats[j][0],
                attn_col_new[j],
                summed[4 + j],
                summed[8][j],
                summed[8][4 + j],
            )
            for j in range(4)
        ],
        axis=1,
    )
    attn_row_new = jnp.stack([item[0] for item in attn_stats])
    return (
        block_out,
        input_grad,
        jnp.stack(attn_grad, axis=1),
        up_grad,
        down_grad,
        attn_row_new,
        attn_col_new,
        up_stats[0],
        up_col_new,
        down_stats[0],
        down_col_new,
        attn_new,
        up_new,
        down_new,
        attn_new.astype(BF),
        up_new.astype(BF),
        down_new.astype(BF),
        small_grad,
        wide_grad,
        small_moment_new,
        wide_moment_new,
        small_new,
        wide_new,
    )


def solution(mesh):
    placed = (
        P("dp", None),
        P("dp", None),
        P("dp"),
        P("dp", None, None),
        P("dp", None),
        P("dp", None),
        P(None, "dp"),
        P(None, "dp"),
        P(None, "dp"),
        P(),
        P("dp"),
        P(),
        P("dp"),
        P(),
        P(None, "dp"),
        P(None, "dp"),
    )
    return jax.shard_map(
        per_device,
        mesh=mesh,
        in_specs=placed,
        out_specs=(
            P("dp", None),
            P("dp", None),
            P("dp", None, None),
            P("dp", None),
            P("dp", None),
            P(None, "dp"),
            P(),
            P("dp"),
            P(),
            P("dp"),
            P(),
            P("dp", None, None),
            P("dp", None),
            P("dp", None),
            P("dp", None, None),
            P("dp", None),
            P("dp", None),
            P(None, "dp"),
            P(None, "dp"),
            P(None, "dp"),
            P(None, "dp"),
            P(None, "dp"),
            P(None, "dp"),
        ),
        check_vma=False,
    )
```

```python
from functools import partial
import math

import jax
import jax.numpy as jnp
from jax import lax
from jax.experimental import pallas as pl
from jax.experimental.pallas import tpu as pltpu
from jax.sharding import PartitionSpec as P

D = 2048
FF = 8192
HEADS = 32
L = 128
IMG = 64
SHARE = 4


EPS_NORM = 1e-05
EPS_SQUARE = 1e-30
EPS_SCALE = 0.001
DECAY_RATE = 0.5
CLIP_LEVEL = 0.5
LEARN_RATE = 0.8
SCALE_BASE = 512.0
MASK_FILL = -1e30

BF = jnp.bfloat16
F32 = jnp.float32


def dot_f32(left, right, left_dim, right_dim):
    return lax.dot_general(
        left, right, (((left_dim,), (right_dim,)), ((), ())), preferred_element_type=F32
    )


def group_masks():
    count = lax.axis_size("dp")
    masks = []
    mask = 2 * SHARE
    while mask < count:
        masks.append(mask)
        mask *= 2
    if count > SHARE:
        masks.append(SHARE)
    return masks


def take_block(value, index, width, axis):
    return lax.dynamic_slice_in_dim(value, index * width, width, axis)


def norm_stats(values):
    mean = jnp.mean(values, axis=-1, keepdims=True)
    center = values - mean
    rstd = lax.rsqrt(jnp.mean(center * center, axis=-1, keepdims=True) + EPS_NORM)
    return center * rstd, rstd


def norm_back(unit, rstd, gain, upstream):
    scaled = upstream * gain
    lean = jnp.mean(scaled, axis=-1, keepdims=True)
    slope = jnp.mean(scaled * unit, axis=-1, keepdims=True)
    return (
        rstd * (scaled - lean - unit * slope),
        jnp.sum(upstream * unit, axis=0),
        jnp.sum(upstream, axis=0),
    )


def xpos_tables(head_size, head_count):
    slot_pos = jnp.arange(L, dtype=F32)[:, None]
    pair_idx = jnp.arange(head_size // 2, dtype=F32)[None, :]
    theta = jnp.exp(-(2.0 * pair_idx / head_size) * jnp.log(10000.0))
    angle = slot_pos * theta
    zeta = (2.0 * pair_idx / head_size + 0.4) / 1.4
    power_table = jnp.exp(jnp.log(zeta) * slot_pos / SCALE_BASE)

    def widen(table):
        return jnp.tile(jnp.repeat(table, 2, axis=1), (1, head_count))

    cosine, sine, power = widen(jnp.cos(angle)), widen(jnp.sin(angle)), widen(power_table)
    return cosine * power, sine * power, cosine / power, sine / power


def quarter_turn(values):
    width = values.shape[1]
    lane = lax.broadcasted_iota(jnp.int32, values.shape, 1)
    return jnp.where(
        lane % 2 == 0, -pltpu.roll(values, width - 1, 1), pltpu.roll(values, 1, 1)
    )


def masked_probs(query, key, caption, head_size):
    scores = dot_f32(query, key, 1, 1) * (1.0 / math.sqrt(head_size))
    row = lax.broadcasted_iota(jnp.int32, scores.shape, 0)
    col = lax.broadcasted_iota(jnp.int32, scores.shape, 1)
    scores = jnp.where((col <= row) & (col < IMG + caption), scores, MASK_FILL)
    terms = jnp.exp(scores - jnp.max(scores, axis=-1, keepdims=True))
    return terms / jnp.sum(terms, axis=-1, keepdims=True)


def attention_back_block(head_size, caption, q_low, k_low, v_low, g_low, tables):
    cq, sq, ck, sk = tables
    grads_q, grads_k, grads_v = [], [], []
    for head in range(q_low.shape[1] // head_size):
        at = slice(head * head_size, (head + 1) * head_size)
        probs = masked_probs(q_low[:, at], k_low[:, at], caption, head_size)
        grads_v.append(dot_f32(probs.astype(BF), g_low[:, at], 0, 0))
        prob_grad = dot_f32(g_low[:, at], v_low[:, at], 1, 1)
        score_grad = probs * (prob_grad - jnp.sum(probs * prob_grad, axis=-1, keepdims=True))
        score_low = (score_grad * (1.0 / math.sqrt(head_size))).astype(BF)
        grads_q.append(dot_f32(score_low, k_low[:, at], 1, 0))
        grads_k.append(dot_f32(score_low, q_low[:, at], 0, 0))
    grad_q = jnp.concatenate(grads_q, axis=1)
    grad_k = jnp.concatenate(grads_k, axis=1)
    return (
        (grad_q * cq - quarter_turn(grad_q) * sq).astype(BF),
        (grad_k * ck - quarter_turn(grad_k) * sk).astype(BF),
        jnp.concatenate(grads_v, axis=1).astype(BF),
    )


MESH = pl.DeviceIdType.MESH
KERNEL_VMEM = 62 * 1024 * 1024


def flipped(index, mask):
    bit = 1
    while bit <= mask:
        if mask & bit:
            index = index + bit - 2 * bit * ((index // bit) % 2)
        bit *= 2
    return index


def partner_masks():
    return list(range(1, SHARE)) + group_masks()


class Wire:
    def __init__(self):
        self.me = lax.axis_index("dp")
        self.member = self.me % SHARE

    def meet(self):
        barrier = pltpu.get_barrier_semaphore()
        masks = partner_masks()
        for mask in masks:
            pl.semaphore_signal(
                barrier, inc=1, device_id=(flipped(self.me, mask),), device_id_type=MESH
            )
        pl.semaphore_wait(barrier, len(masks))

    def copy(self, source, target, send_sem, recv_sem, mask):
        return pltpu.make_async_remote_copy(
            src_ref=source,
            dst_ref=target,
            send_sem=send_sem,
            recv_sem=recv_sem,
            device_id=(flipped(self.me, mask),),
            device_id_type=MESH,
        )


def row_tiles(rows, body, tile=256):
    tile = min(tile, rows)

    @pl.loop(0, rows // tile)
    def _(index):
        body(pl.multiple_of(index * tile, tile), tile)


class Reducer:
    @staticmethod
    def scratch(count, cols):
        stages = len(group_masks())
        halves = [D >> (stage + 1) for stage in range(stages)]
        block = D >> stages
        return (
            [pltpu.VMEM((2, half, cols), BF) for half in halves]
            + [pltpu.VMEM((count, half, cols), BF) for half in halves]
            + [
                pltpu.VMEM((min(stages, count), D // 2, cols), F32),
                pltpu.VMEM((2, block, cols), BF),
                pltpu.SemaphoreType.DMA((count, stages)),
                pltpu.SemaphoreType.DMA((count, stages)),
                pltpu.SemaphoreType.DMA((count, SHARE)),
                pltpu.SemaphoreType.DMA((count, SHARE)),
            ]
        )

    @staticmethod
    def out_shape(count, cols):
        block = D >> len(group_masks())
        return jax.ShapeDtypeStruct((SHARE, count, block // SHARE, cols), BF)

    def __init__(self, wire, count, terms, out, refs):
        self.wire, self.count, self.terms, self.out = wire, count, terms, out
        self.masks = group_masks()[::-1]
        self.stages = len(self.masks)
        self.slots = min(self.stages, count)
        self.sends, refs = refs[: self.stages], refs[self.stages :]
        self.recvs, refs = refs[: self.stages], refs[self.stages :]
        self.kept, self.done, self.send_sem, self.recv_sem, self.out_send, self.out_recv = refs
        self.block = D >> self.stages
        self.low = (wire.me // SHARE) % 2

    def half_bit(self, stage):
        return (self.wire.me // self.masks[stage]) % 2

    def lhs_row(self, row, tile, low):
        block = row // self.block
        return pl.multiple_of((2 * block + low) * self.block + row % self.block, tile)

    def copy(self, chunk, stage):
        return self.wire.copy(
            self.sends[stage].at[chunk % 2],
            self.recvs[stage].at[chunk],
            self.send_sem.at[chunk, stage],
            self.recv_sem.at[chunk, stage],
            self.masks[stage],
        )

    def start(self, chunk):
        if chunk >= self.count:
            return
        if chunk >= 2:
            self.copy(chunk - 2, 0).wait_send()
        lhs, rhs, cols = self.terms[chunk]
        half = D // 2

        def body(row, tile):
            at = pl.ds(self.lhs_row(row, tile, 1 - self.low), tile)
            self.sends[0][chunk % 2, pl.ds(row, tile), :] = dot_f32(
                lhs[at, :], rhs[:, cols], 1, 0
            ).astype(BF)

        row_tiles(half, body, self.block)
        self.copy(chunk, 0).start()

    def keep(self, chunk):
        if chunk >= self.count:
            return
        lhs, rhs, cols = self.terms[chunk]

        def body(row, tile):
            at = pl.ds(self.lhs_row(row, tile, self.low), tile)
            self.kept[chunk % self.slots, pl.ds(row, tile), :] = dot_f32(
                lhs[at, :], rhs[:, cols], 1, 0
            )

        row_tiles(D // 2, body, self.block)

    def step(self, chunk, stage):
        if not 0 <= chunk < self.count:
            return
        self.copy(chunk, stage - 1).wait_recv()
        if chunk >= 2:
            self.copy(chunk - 2, stage).wait_send()
        half = D >> (stage + 1)
        kept, got, send = self.kept, self.recvs[stage - 1], self.sends[stage]
        slot = chunk % self.slots

        bit = self.half_bit(stage)

        def out_half(row, tile):
            at = pl.ds(pl.multiple_of((1 - bit) * half + row, tile), tile)
            send[chunk % 2, pl.ds(row, tile), :] = (
                kept[slot, at, :] + got[chunk, at, :].astype(F32)
            ).astype(BF)

        def own_half(row, tile):
            at = pl.ds(pl.multiple_of(bit * half + row, tile), tile)
            kept[slot, pl.ds(row, tile), :] = kept[slot, at, :] + got[chunk, at, :].astype(F32)

        row_tiles(half, out_half)
        self.copy(chunk, stage).start()
        row_tiles(half, own_half)

    def give(self, chunk):
        part = self.block // SHARE
        slot = chunk % 2
        copies = []
        for j in range(1, SHARE):
            to = flipped(self.wire.member, j)
            copies.append(
                self.wire.copy(
                    self.done.at[slot, pl.ds(pl.multiple_of(to * part, part), part), :],
                    self.out.at[j, chunk],
                    self.out_send.at[chunk, j],
                    self.out_recv.at[chunk, j],
                    j,
                )
            )
        own = pltpu.make_async_copy(
            self.done.at[slot, pl.ds(pl.multiple_of(self.wire.member * part, part), part), :],
            self.out.at[0, chunk],
            self.out_send.at[chunk, 0],
        )
        return own, copies

    def given(self, chunk):
        own, copies = self.give(chunk)
        own.wait()
        for item in copies:
            item.wait_send()

    def finish(self, chunk):
        if not 0 <= chunk < self.count:
            return
        self.copy(chunk, self.stages - 1).wait_recv()
        if chunk >= 2:
            self.given(chunk - 2)
        got = self.recvs[self.stages - 1]
        slot = chunk % self.slots

        def body(row, tile):
            at = pl.ds(row, tile)
            self.done[chunk % 2, at, :] = (
                self.kept[slot, at, :] + got[chunk, at, :].astype(F32)
            ).astype(BF)

        row_tiles(self.block, body)
        own, copies = self.give(chunk)
        own.start()
        for item in copies:
            item.start()

    def tick(self, at):
        for stage in range(1, self.stages):
            self.step(at - stage + 1, stage)
            if stage == 1:
                self.start(at + 2)
        if self.stages == 1:
            self.start(at + 2)
        self.finish(at - self.stages + 1)
        self.keep(at + 1)

    def ticks(self):
        return self.count + self.stages - 1

    def close(self):
        for chunk in range(max(0, self.count - 2), self.count):
            for stage in range(self.stages):
                self.copy(chunk, stage).wait_send()
            self.given(chunk)
        for chunk in range(self.count):
            for item in self.give(chunk)[1]:
                item.wait_recv()


class OwnerSum:
    @staticmethod
    def scratch(own):
        return [
            pltpu.VMEM((2 * own, D), BF),
            pltpu.VMEM((own, D), BF),
            pltpu.SemaphoreType.DMA((4,)),
        ]

    def __init__(self, wire, own, send, kept, refs):
        self.wire, self.own, self.send, self.kept = wire, own, send, kept
        self.near, self.far, self.sems = refs

    def core_copy(self):
        return self.wire.copy(
            self.send.at[pl.ds(0, 2 * self.own), :],
            self.near,
            self.sems.at[0],
            self.sems.at[1],
            1,
        )

    def far_copy(self):
        return self.wire.copy(
            self.send.at[pl.ds(2 * self.own, self.own), :],
            self.far,
            self.sems.at[2],
            self.sems.at[3],
            2,
        )

    def first(self, term):
        for place, block in enumerate((3, 1)):

            def body(row, tile, place=place, block=block):
                self.send[pl.ds(place * self.own + row, tile), :] = term(block, row, tile).astype(BF)

            row_tiles(self.own, body)
        self.core_copy().start()

    def second(self, term):
        for place, block in enumerate((2, 0)):

            def body(row, tile, place=place, block=block):
                self.kept[pl.ds((1 - place) * self.own + row, tile), :] = term(block, row, tile)

            row_tiles(self.own, body)

    def third(self):
        self.core_copy().wait_recv()
        own = self.own

        def far(row, tile):
            self.send[pl.ds(2 * own + row, tile), :] = (
                self.kept[pl.ds(own + row, tile), :] + self.near[pl.ds(row, tile), :].astype(F32)
            ).astype(BF)

        def near(row, tile):
            at = pl.ds(row, tile)
            self.kept[at, :] = self.kept[at, :] + self.near[pl.ds(own + row, tile), :].astype(F32)

        row_tiles(own, far)
        self.far_copy().start()
        row_tiles(own, near)

    def last(self):
        self.far_copy().wait_recv()

        def body(row, tile):
            at = pl.ds(row, tile)
            self.kept[at, :] = self.kept[at, :] + self.far[at, :].astype(F32)

        row_tiles(self.own, body)
        self.core_copy().wait_send()
        self.far_copy().wait_send()


REDUCE_CHUNKS = 4


def ffn_back_kernel(own, back, back_t, mid, down, up, unit_in, slope_in, gain, rstd, *refs):
    width = mid.shape[1]
    tokens = SHARE * own
    cols = width // REDUCE_CHUNKS
    pieces = len(down)
    out, up_low_out, wide_out, sum_out = refs[:4]
    refs = refs[4:]
    wire = Wire()
    count = len(Reducer.scratch(REDUCE_CHUNKS, cols))
    reducer_refs, refs = refs[:count], refs[count:]
    sum_refs, refs = refs[:3], refs[3:]
    (
        back_v, back_tv, mid_v, weight, unit, slope, grad, sums, stat_send, stat_recv,
        load_sem, stat_sems, store_sem,
    ) = refs

    def weight_copies(parts, first):
        step = width // pieces
        return [
            pltpu.make_async_copy(
                part, weight.at[:, pl.ds(k * step, step)], load_sem.at[first + k]
            )
            for k, part in enumerate(parts)
        ]

    loads = [
        pltpu.make_async_copy(source, target, load_sem.at[k])
        for k, (source, target) in enumerate(
            [(back_t, back_tv), (mid, mid_v), (back, back_v), (unit_in, unit), (slope_in, slope)]
        )
    ]
    down_loads = weight_copies(down, 5)
    up_loads = weight_copies(up, 5 + pieces)
    for item in loads[:3] + down_loads + loads[3:]:
        item.start()
    wire.meet()
    reducer = Reducer(
        wire,
        REDUCE_CHUNKS,
        [(back_tv, mid_v, pl.ds(c * cols, cols)) for c in range(REDUCE_CHUNKS)],
        out,
        reducer_refs,
    )
    loads[0].wait()
    loads[1].wait()
    reducer.start(0)
    reducer.start(1)
    reducer.keep(0)

    wide_out[...] = jnp.zeros_like(wide_out)
    sums[...] = jnp.zeros_like(sums)

    def token_tiles(body):
        row_tiles(tokens, body, own)

    def first_pass(k):
        at_cols = pl.ds(k * cols, cols)

        def body(row, tile):
            at = pl.ds(row, tile)
            value = dot_f32(back_v[at, :], weight[:, at_cols], 1, 0)
            grad[at, at_cols] = value
            part = unit[at, at_cols].astype(F32)
            scaled = value * gain[:, at_cols]
            lane = lax.broadcasted_iota(jnp.int32, (tile, sums.shape[1]), 1)
            sums[at, :] += jnp.where(
                lane == 0,
                jnp.sum(scaled, axis=1, keepdims=True),
                jnp.sum(scaled * part, axis=1, keepdims=True),
            )
            wide_out[0:1, at_cols] += jnp.sum(value * part, axis=0, keepdims=True)
            wide_out[1:2, at_cols] += jnp.sum(value, axis=0, keepdims=True)

        token_tiles(body)

    loads[2].wait()
    for item in down_loads:
        item.wait()
    loads[3].wait()
    loads[4].wait()
    first_pass(0)
    first_pass(1)
    reducer.tick(0)
    first_pass(2)
    first_pass(3)
    for item in up_loads:
        item.start()

    stats = [
        wire.copy(
            stat_send, stat_recv.at[j - 1], stat_sems.at[0, j - 1], stat_sems.at[1, j - 1], j
        )
        for j in range(1, SHARE)
    ]
    for j in range(SHARE):
        stat_send[j] = sums[pl.ds(j * own, own), :].T[0:8, :]
    for item in stats:
        item.start()
    reducer.tick(1)
    for item in stats:
        item.wait_recv()
    for j in range(SHARE):
        total = stat_send[j]
        for k in range(1, SHARE):
            total = total + stat_recv[k - 1, j ^ k]
        total = total * (1.0 / (SHARE * width))
        sums[pl.ds(j * own, own), :] = jnp.concatenate([total] * (sums.shape[1] // 8), axis=0).T
    for item in stats:
        item.wait_send()

    def second_pass(k):
        at_cols = pl.ds(k * cols, cols)

        def body(row, tile):
            at = pl.ds(row, tile)
            act_grad = rstd[at, 0:1] * (
                grad[at, at_cols] * gain[:, at_cols]
                - sums[at, 0:1]
                - unit[at, at_cols].astype(F32) * sums[at, 1:2]
            )
            unit[at, at_cols] = (act_grad * slope[at, at_cols].astype(F32)).astype(BF)

        token_tiles(body)

    second_pass(0)
    second_pass(1)
    second_pass(2)
    second_pass(3)
    store = pltpu.make_async_copy(unit, up_low_out, store_sem.at[0])
    store.start()
    reducer.tick(2)
    for item in up_loads:
        item.wait()

    def term(block, row, tile):
        return dot_f32(unit[pl.ds(block * own + row, tile), :], weight[...], 1, 1)

    owner = OwnerSum(wire, own, slope, grad, sum_refs)
    owner.first(term)
    owner.second(term)
    reducer.tick(3)
    owner.third()
    for at in range(4, reducer.ticks()):
        reducer.tick(at)
    owner.last()
    result = pltpu.make_async_copy(grad.at[pl.ds(0, own), :], sum_out, store_sem.at[1])
    result.start()
    reducer.close()
    store.wait()
    result.wait()


def ffn_back(back, mid, down, up, unit, slope, gain, rstd):
    tokens, width = mid.shape
    own = tokens // SHARE
    cols = width // REDUCE_CHUNKS
    lanes = 128
    any_spec = pl.BlockSpec(memory_space=pl.ANY)
    vmem = pl.BlockSpec(memory_space=pltpu.VMEM)
    pieces = len(down)

    def kernel(back, back_t, mid, *refs):
        down, up, refs = refs[:pieces], refs[pieces : 2 * pieces], refs[2 * pieces :]
        ffn_back_kernel(own, back, back_t, mid, down, up, *refs)

    return pl.pallas_call(
        kernel,
        in_specs=[any_spec] * (5 + 2 * pieces) + [vmem] * 2,
        out_specs=[any_spec, any_spec, vmem, any_spec],
        out_shape=[
            Reducer.out_shape(REDUCE_CHUNKS, cols),
            jax.ShapeDtypeStruct((tokens, width), BF),
            jax.ShapeDtypeStruct((8, width), F32),
            jax.ShapeDtypeStruct((own, D), F32),
        ],
        scratch_shapes=Reducer.scratch(REDUCE_CHUNKS, cols)
        + OwnerSum.scratch(own)
        + [
            pltpu.VMEM((tokens, D), BF),
            pltpu.VMEM((D, tokens), BF),
            pltpu.VMEM((tokens, width), BF),
            pltpu.VMEM((D, width), BF),
            pltpu.VMEM((tokens, width), BF),
            pltpu.VMEM((tokens, width), BF),
            pltpu.VMEM((tokens, width), F32),
            pltpu.VMEM((tokens, lanes), F32),
            pltpu.VMEM((SHARE, 8, own), F32),
            pltpu.VMEM((SHARE - 1, SHARE, 8, own), F32),
            pltpu.SemaphoreType.DMA((5 + 2 * pieces,)),
            pltpu.SemaphoreType.DMA((2, SHARE - 1)),
            pltpu.SemaphoreType.DMA((2,)),
        ],
        compiler_params=pltpu.CompilerParams(
            collective_id=1, has_side_effects=True, vmem_limit_bytes=KERNEL_VMEM
        ),
        name="ffn_back",
    )(
        back,
        back.T,
        mid,
        *down,
        *up,
        unit,
        slope,
        gain[None],
        rstd,
    )


def attention_back_kernel(
    head_size, own, left_t, right, q_in, k_in, v_in, mixed, hidden, cap, cq, sq, ck, sk, *refs
):
    width = q_in.shape[1]
    cols = right.shape[1] // REDUCE_CHUNKS
    out, q_out, k_out, v_out, hidden_out = refs[:5]
    refs = refs[5:]
    wire = Wire()
    count = len(Reducer.scratch(REDUCE_CHUNKS, cols))
    reducer_refs, refs = refs[:count], refs[count:]
    left_v, right_v, q_v, k_v, v_v, mixed_cols, hidden_cols, load_sem, turn_sem = refs
    loads = [
        pltpu.make_async_copy(source, target, load_sem.at[k])
        for k, (source, target) in enumerate(
            [(left_t, left_v), (right, right_v), (q_in, q_v), (k_in, k_v), (v_in, v_v)]
        )
    ]
    for item in loads:
        item.start()
    wire.meet()

    def turn(source, target, sems):
        copies = []
        for j in range(1, SHARE):
            to = pl.multiple_of(flipped(wire.member, j) * width, width)
            copies.append(
                wire.copy(
                    source.at[:, pl.ds(to, width)],
                    target.at[pl.ds(j * own, own), :],
                    sems.at[0, j],
                    sems.at[1, j],
                    j,
                )
            )
        here = pl.multiple_of(wire.member * width, width)
        local = pltpu.make_async_copy(
            source.at[:, pl.ds(here, width)], target.at[pl.ds(0, own), :], sems.at[0, 0]
        )
        for item in copies + [local]:
            item.start()
        return copies, local

    def turned(copies, local):
        local.wait()
        for item in copies:
            item.wait_recv()

    mixed_turn = turn(mixed, mixed_cols, turn_sem.at[0])
    reducer = Reducer(
        wire,
        REDUCE_CHUNKS,
        [(left_v, right_v, pl.ds(c * cols, cols)) for c in range(REDUCE_CHUNKS)],
        out,
        reducer_refs,
    )
    loads[0].wait()
    loads[1].wait()
    reducer.start(0)
    reducer.start(1)
    hidden_turn = turn(hidden, hidden_cols, turn_sem.at[1])
    reducer.keep(0)
    turned(*mixed_turn)
    for item in loads[2:]:
        item.wait()
    row_count = SHARE * own // L

    def rows(first, last):
        @pl.loop(first, last)
        def _(row):
            at = pl.ds(pl.multiple_of(row * L, L), L)
            got = attention_back_block(
                head_size,
                cap[row],
                q_v[at, :],
                k_v[at, :],
                v_v[at, :],
                mixed_cols[at, :],
                (cq[...], sq[...], ck[...], sk[...]),
            )
            q_v[at, :], k_v[at, :], v_v[at, :] = got

    rows(0, row_count // 2)
    reducer.tick(0)
    rows(row_count // 2, row_count)
    stores = [
        pltpu.make_async_copy(source, target, load_sem.at[k])
        for k, (source, target) in enumerate([(q_v, q_out), (k_v, k_out), (v_v, v_out)])
    ]
    for item in stores:
        item.start()
    reducer.tick(1)
    turned(*hidden_turn)
    stores.append(pltpu.make_async_copy(hidden_cols, hidden_out, load_sem.at[3]))
    stores[-1].start()
    for at in range(2, reducer.ticks()):
        reducer.tick(at)
    reducer.close()
    for item in stores:
        item.wait()
    for item in mixed_turn[0] + hidden_turn[0]:
        item.wait_send()


def attention_back(left, right, queries, keys, values, mixed, hidden, captions, tables):
    tokens, width = queries.shape
    own = tokens // SHARE
    cols = right.shape[1] // REDUCE_CHUNKS
    any_spec = pl.BlockSpec(memory_space=pl.ANY)
    vmem = pl.BlockSpec(memory_space=pltpu.VMEM)
    part = jax.ShapeDtypeStruct((tokens, width), BF)
    return pl.pallas_call(
        partial(attention_back_kernel, D // HEADS, own),
        in_specs=[any_spec] * 5
        + [vmem] * 2
        + [pl.BlockSpec(memory_space=pltpu.SMEM)]
        + [vmem] * 4,
        out_specs=[any_spec] * 5,
        out_shape=[Reducer.out_shape(REDUCE_CHUNKS, cols)] + [part] * 4,
        scratch_shapes=Reducer.scratch(REDUCE_CHUNKS, cols)
        + [pltpu.VMEM((D, tokens), BF), pltpu.VMEM(right.shape, BF)]
        + [pltpu.VMEM((tokens, width), BF)] * 5
        + [pltpu.SemaphoreType.DMA((5,)), pltpu.SemaphoreType.DMA((2, 2, SHARE))],
        compiler_params=pltpu.CompilerParams(
            collective_id=2, has_side_effects=True, vmem_limit_bytes=KERNEL_VMEM
        ),
        name="attention_back",
    )(left.T, right, queries, keys, values, mixed, hidden, captions, *tables)


def project_back_kernel(own, normed_t, context_t, *refs):
    parts, refs = refs[:4], refs[4:]
    mid, weights, refs = refs[0], refs[1:4], refs[4:]
    pieces = REDUCE_CHUNKS
    down, refs = refs[:pieces], refs[pieces:]
    out, grad_out, block_out = refs[:3]
    refs = refs[3:]
    width = parts[0].shape[1]
    wire = Wire()
    count = len(Reducer.scratch(SHARE, width))
    reducer_refs, refs = refs[:count], refs[count:]
    grad_refs, refs = refs[:3], refs[3:]
    block_refs, refs = refs[:3], refs[3:]
    normed_v, context_v, parts_v, mid_v, weight, send, kept, load_sem, store_sem = refs
    loads = [
        pltpu.make_async_copy(source, target, load_sem.at[k])
        for k, (source, target) in enumerate(
            [
                (context_t, context_v),
                (parts[0], parts_v.at[0]),
                (normed_t, normed_v),
                (parts[1], parts_v.at[1]),
                (parts[2], parts_v.at[2]),
                (parts[3], parts_v.at[3]),
                (mid, mid_v),
            ]
            + [(item, weight.at[:, pl.ds(k * width, width)]) for k, item in enumerate(weights)]
        )
    ]
    for item in loads:
        item.start()
    wire.meet()
    every = pl.ds(0, width)
    reducer = Reducer(
        wire,
        SHARE,
        [(context_v, parts_v.at[0], every)]
        + [(normed_v, parts_v.at[k], every) for k in range(1, 4)],
        out,
        reducer_refs,
    )
    loads[0].wait()
    loads[1].wait()
    reducer.start(0)
    loads[2].wait()
    loads[3].wait()
    reducer.start(1)
    reducer.keep(0)
    for item in loads[4:]:
        item.wait()

    def grad_term(block, row, tile):
        at = pl.ds(block * own + row, tile)
        return sum(
            dot_f32(parts_v[1 + k, at, :], weight[:, pl.ds(k * width, width)], 1, 1)
            for k in range(3)
        )

    grad_sum = OwnerSum(wire, own, send, kept, grad_refs)
    grad_sum.first(grad_term)
    grad_sum.second(grad_term)
    step = mid.shape[1] // pieces
    down_loads = [
        pltpu.make_async_copy(part, weight.at[:, pl.ds(k * step, step)], load_sem.at[10 + k])
        for k, part in enumerate(down)
    ]
    for item in down_loads:
        item.start()
    reducer.tick(0)
    grad_sum.third()
    for item in down_loads:
        item.wait()
    reducer.tick(1)
    grad_sum.last()
    grad_store = pltpu.make_async_copy(kept.at[pl.ds(0, own), :], grad_out, store_sem.at[0])
    grad_store.start()

    def block_term(block, row, tile):
        at = pl.ds(block * own + row, tile)
        return dot_f32(mid_v[at, :], weight[...], 1, 1)

    block_sum = OwnerSum(wire, own, send, kept, block_refs)
    block_sum.first(block_term)
    reducer.tick(2)
    grad_store.wait()
    block_sum.second(block_term)
    block_sum.third()
    for at in range(3, reducer.ticks()):
        reducer.tick(at)
    block_sum.last()
    block_store = pltpu.make_async_copy(kept.at[pl.ds(0, own), :], block_out, store_sem.at[1])
    block_store.start()
    reducer.close()
    block_store.wait()


def project_back(normed, context, parts, mid, weights, down):
    tokens, width = parts[0].shape
    own = tokens // SHARE
    any_spec = pl.BlockSpec(memory_space=pl.ANY)
    part = jax.ShapeDtypeStruct((own, D), F32)
    return pl.pallas_call(
        partial(project_back_kernel, own),
        in_specs=[any_spec] * (10 + len(down)),
        out_specs=[any_spec] * 3,
        out_shape=[Reducer.out_shape(SHARE, width), part, part],
        scratch_shapes=Reducer.scratch(SHARE, width)
        + OwnerSum.scratch(own)
        + OwnerSum.scratch(own)
        + [
            pltpu.VMEM((D, tokens), BF),
            pltpu.VMEM((D, tokens), BF),
            pltpu.VMEM((4, tokens, width), BF),
            pltpu.VMEM(mid.shape, BF),
            pltpu.VMEM((D, mid.shape[1]), BF),
            pltpu.VMEM((3 * own, D), BF),
            pltpu.VMEM((2 * own, D), F32),
            pltpu.SemaphoreType.DMA((10 + len(down),)),
            pltpu.SemaphoreType.DMA((2,)),
        ],
        compiler_params=pltpu.CompilerParams(
            collective_id=3, has_side_effects=True, vmem_limit_bytes=KERNEL_VMEM
        ),
        name="project_back",
    )(normed.T, context.T, *parts, mid, *weights, *down)


def sum_over_devices(wire, total, whole, got, send_sem, recv_sem):
    rows, cols = total.shape
    row, col = 0, 0
    regions = []
    for stage in range(len(got)):
        mask = 1 << stage
        bit = (wire.me // mask) % 2
        regions.append((row, col, rows, cols))
        if rows > 8:
            rows //= 2
            away = (pl.multiple_of(row + (1 - bit) * rows, 8), col)
            row = pl.multiple_of(row + bit * rows, 8)
        else:
            cols //= 2
            away = (row, pl.multiple_of(col + (1 - bit) * cols, 128))
            col = pl.multiple_of(col + bit * cols, 128)
        copy = wire.copy(
            total.at[pl.ds(away[0], rows), pl.ds(away[1], cols)],
            got[stage],
            send_sem.at[0, stage],
            recv_sem.at[0, stage],
            mask,
        )
        copy.start()
        copy.wait()
        total[pl.ds(row, rows), pl.ds(col, cols)] += got[stage][...]
    whole[pl.ds(row, rows), pl.ds(col, cols)] = total[pl.ds(row, rows), pl.ds(col, cols)]
    for stage in reversed(range(len(got))):
        part = whole.at[pl.ds(row, rows), pl.ds(col, cols)]
        copy = wire.copy(part, part, send_sem.at[1, stage], recv_sem.at[1, stage], 1 << stage)
        copy.start()
        copy.wait()
        row, col, rows, cols = regions[stage]


WIDE = FF // D
SUM_COLS, SUM_WEIGHTED = 0, 2 * WIDE + 4
SUM_NORMS = 2 * SUM_WEIGHTED
SUM_MOMENTS = SUM_NORMS + 2 * WIDE + 6
SUM_SCALARS = SUM_MOMENTS + 2 * WIDE + 6
SUM_ROWS = 64


def update_matrices(step, width, places):
    matrices = []
    for index in range(2):
        pieces = [
            (index * WIDE + t, c * step, t * D + c * step, t, places[index][c])
            for t in range(SHARE)
            for c in range(REDUCE_CHUNKS)
        ]
        matrices.append((index, FF, pieces, step))
    for j in range(4):
        pieces = [(2 * WIDE + j, t * width, t * width, t, places[2][j]) for t in range(SHARE)]
        matrices.append((2 + j, D, pieces, width))
    return matrices


def matrix_cols(refs, index, col, size):
    if index < 2:
        return refs[index][:, pl.ds(col, size)]
    return refs[2][:, index - 2, pl.ds(col, size)]


def put_matrix_cols(refs, index, col, size, value):
    if index < 2:
        refs[index][:, pl.ds(col, size)] = value
    else:
        refs[2][:, index - 2, pl.ds(col, size)] = value


def update_sums_kernel(
    places, sources, up_old, down_old, attn_old, row_old, wide_terms, small_terms, moments,
    vector_squares, *refs
):
    row_new, whole, total = refs[:3]
    got, send_sem, recv_sem = refs[3:-2], refs[-2], refs[-1]
    wire = Wire()
    barrier = pltpu.get_barrier_semaphore()
    for stage in range(len(got)):
        pl.semaphore_signal(
            barrier, inc=1, device_id=(flipped(wire.me, 1 << stage),), device_id_type=MESH
        )
    width = sources[0].shape[3]
    old = (up_old, down_old, attn_old)

    def piece_of(member, place):
        return sources[place[0]][flipped(wire.member, member), place[1]].astype(F32)

    total[...] = jnp.zeros_like(total)
    lane = lax.broadcasted_iota(jnp.int32, (1, 128), 1)
    scalars = vector_squares[0:1, :]
    row_lane = lax.broadcasted_iota(jnp.int32, row_new.shape, 1)
    row_all = jnp.zeros(row_new.shape, F32)
    for index, size, pieces, tile in update_matrices(width, width, places):
        row_sum = jnp.zeros((row_new.shape[0], 1), F32)
        square = jnp.zeros((1, 1), F32)
        for at, sum_col, col, member, place in pieces:
            value = piece_of(member, place)
            squares = value * value
            row_sum += jnp.sum(squares, axis=1, keepdims=True)
            total[SUM_COLS + at : SUM_COLS + at + 1, sum_col : sum_col + tile] = jnp.sum(
                squares, axis=0, keepdims=True
            )
            weight = matrix_cols(old, index, col, tile)
            square += jnp.sum(weight * weight, keepdims=True)
        moment = DECAY_RATE * row_old[:, index : index + 1] + (1.0 - DECAY_RATE) * (
            row_sum * (1.0 / size) + EPS_SQUARE
        )
        row_all = jnp.where(row_lane == index, moment, row_all)
        inverse = 1.0 / moment
        for at, sum_col, col, member, place in pieces:
            value = piece_of(member, place)
            total[SUM_WEIGHTED + at : SUM_WEIGHTED + at + 1, sum_col : sum_col + tile] = jnp.sum(
                value * value * inverse, axis=0, keepdims=True
            )
        scalars = jnp.where(lane == index, jnp.sum(moment, keepdims=True), scalars)
        scalars = jnp.where(lane == 6 + index, square, scalars)
    row_new[...] = row_all
    for r in range(2):
        for t in range(SHARE):
            at = SUM_NORMS + r * WIDE + t
            total[at : at + 1, :] = jnp.where(wire.member == t, wide_terms[r : r + 1, :], 0.0)
    total[SUM_NORMS + 2 * WIDE : SUM_MOMENTS, :] = small_terms[...]
    total[SUM_MOMENTS:SUM_SCALARS, :] = moments[...]
    total[SUM_SCALARS : SUM_SCALARS + 1, 0:128] = scalars

    pl.semaphore_wait(barrier, len(got))
    sum_over_devices(wire, total, whole, got, send_sem, recv_sem)


def update_kernel(
    places, sources, up_old, down_old, attn_old, row_new, col_old, whole, up_grad, down_grad,
    attn_grad, up_new, down_new, attn_new, up_copy, down_copy, attn_copy, col_new, vectors, scale
):
    mine = lax.axis_index("dp") % SHARE
    width = sources[0].shape[3]
    old, grad = (up_old, down_old, attn_old), (up_grad, down_grad, attn_grad)
    new, low = (up_new, down_new, attn_new), (up_copy, down_copy, attn_copy)
    columns = DECAY_RATE * col_old[...] + (1.0 - DECAY_RATE) * (
        whole[SUM_COLS:SUM_WEIGHTED, :] * (1.0 / D) + EPS_SQUARE
    )
    col_new[...] = columns
    scale[...] = lax.rsqrt(columns)
    ratio = whole[SUM_WEIGHTED:SUM_NORMS, :] / columns

    def scalar(index):
        return whole[SUM_SCALARS : SUM_SCALARS + 1, index : index + 1]

    def step_size(square, weight_square, size):
        upd_rms = jnp.sqrt(square * (1.0 / size))
        weight_rms = jnp.sqrt(weight_square * (1.0 / size))
        return (
            LEARN_RATE
            * jnp.maximum(EPS_SCALE, weight_rms)
            / jnp.maximum(1.0, upd_rms * (1.0 / CLIP_LEVEL))
        )

    for index, size, pieces, tile in update_matrices(width, width, places):
        first, last = pieces[0][0], pieces[-1][0] + 1
        row_mean = scalar(index) * (1.0 / D)
        square = row_mean * jnp.sum(ratio[first:last, :], keepdims=True)
        factor = step_size(square, scalar(6 + index), D * size)
        row_scale = lax.rsqrt(row_new[:, index : index + 1] / row_mean) * factor
        for at, sum_col, col, member, place in pieces:
            value = sources[place[0]][flipped(mine, member), place[1]].astype(F32)
            put_matrix_cols(grad, index, col, tile, value)
            value = matrix_cols(old, index, col, tile) - value * row_scale * scale[
                at : at + 1, sum_col : sum_col + tile
            ]
            put_matrix_cols(new, index, col, tile, value)
            put_matrix_cols(low, index, col, tile, value.astype(BF))

    count = 2 * WIDE + 6
    grads = whole[SUM_NORMS:SUM_MOMENTS, :]
    moment = DECAY_RATE * whole[SUM_MOMENTS:SUM_SCALARS, :] + (1.0 - DECAY_RATE) * (
        grads * grads + EPS_SQUARE
    )
    scaled = grads * lax.rsqrt(moment)
    vectors[0:count, :] = grads
    vectors[count : 2 * count, :] = moment
    spans = [(r * WIDE, (r + 1) * WIDE) for r in range(2)]
    spans += [(2 * WIDE + r, 2 * WIDE + r + 1) for r in range(6)]
    for r, (first, last) in enumerate(spans):
        part = scaled[first:last, :]
        size = (last - first) * D
        factor = step_size(jnp.sum(part * part, keepdims=True), scalar(12 + r), size)
        vectors[2 * count + first : 2 * count + last, :] = part * factor


def update(places, sources, weights, row_old, col_old, wide_terms, small_terms, moments, squares):
    count = lax.axis_size("dp")
    stages = count.bit_length() - 1
    rows = weights[0].shape[0]
    parts = []
    size = [SUM_ROWS, D]
    for _ in range(stages):
        size[0 if size[0] > 8 else 1] //= 2
        parts.append(pltpu.VMEM(tuple(size), F32))
    vmem = pl.BlockSpec(memory_space=pltpu.VMEM)
    number = len(sources)
    whole_shape = jax.ShapeDtypeStruct((SUM_ROWS, D), F32)

    def sums_kernel(*refs):
        update_sums_kernel(places, refs[:number], *refs[number:])

    def kernel(*refs):
        update_kernel(places, refs[:number], *refs[number:])

    row_new, whole = pl.pallas_call(
        sums_kernel,
        in_specs=[vmem] * (number + 8),
        out_specs=[vmem] * 2,
        out_shape=[jax.ShapeDtypeStruct((rows, 128), F32), whole_shape],
        scratch_shapes=[pltpu.VMEM((SUM_ROWS, D), F32)]
        + parts
        + [pltpu.SemaphoreType.DMA((2, stages)), pltpu.SemaphoreType.DMA((2, stages))],
        compiler_params=pltpu.CompilerParams(
            collective_id=4, has_side_effects=True, vmem_limit_bytes=KERNEL_VMEM
        ),
        name="update_sums",
    )(*sources, *weights, row_old, wide_terms, small_terms, moments, squares)
    shapes = [jax.ShapeDtypeStruct(item.shape, kind) for kind in (F32, F32, BF) for item in weights]
    shapes += [
        jax.ShapeDtypeStruct((SUM_WEIGHTED, D), F32),
        jax.ShapeDtypeStruct((3 * (2 * WIDE + 6), D), F32),
    ]
    results = pl.pallas_call(
        kernel,
        in_specs=[vmem] * (number + 6),
        out_specs=[vmem] * len(shapes),
        out_shape=shapes,
        scratch_shapes=[pltpu.VMEM((SUM_WEIGHTED, D), F32)],
        compiler_params=pltpu.CompilerParams(vmem_limit_bytes=KERNEL_VMEM),
        name="update",
    )(*sources, *weights, row_new, col_old, whole)
    return row_new, results


class Share:
    def __init__(self, wire, source, target, sems):
        self.wire, self.source, self.target, self.sems = wire, source, target, sems

    def copies(self):
        parts = [
            (self.source, self.target.at[2], 2),
            (self.source, self.target.at[1], 1),
            (self.target.at[2], self.target.at[3], 1),
        ]
        return [
            self.wire.copy(source, target, self.sems.at[0, k], self.sems.at[1, k], mask)
            for k, (source, target, mask) in enumerate(parts)
        ]

    def start(self):
        far, near, unused = self.copies()
        far.start()
        near.start()

    def forward(self):
        far, unused, last = self.copies()
        far.wait_recv()
        last.start()

    def done(self):
        unused, near, last = self.copies()
        near.wait_recv()
        last.wait_recv()

    def close(self):
        for item in self.copies():
            item.wait_send()


def normalized(value):
    center = value - jnp.mean(value, axis=-1, keepdims=True)
    return center * lax.rsqrt(jnp.mean(center * center, axis=-1, keepdims=True) + EPS_NORM)


def attention_block(head_size, caption, q_low, k_low, v_low):
    mixed = []
    for head in range(q_low.shape[1] // head_size):
        at = slice(head * head_size, (head + 1) * head_size)
        probs = masked_probs(q_low[:, at], k_low[:, at], caption, head_size).astype(BF)
        mixed.append(dot_f32(probs, v_low[:, at], 1, 0))
    return jnp.concatenate(mixed, axis=1).astype(BF)


def vector_rows(count):
    wide = FF // count
    return max(1, wide // 128), min(wide, 128)


GATHERED = 4 + 2 * REDUCE_CHUNKS


def forward_kernel(
    own, tokens, cotangent, live, attn_in, up_in, down_in, vectors, cq, sq, ck, sk, *refs
):
    gathered, refs = refs[:GATHERED], refs[GATHERED:]
    (
        out_full, normed_out, back_all, context_all, ffn_out, mid_out, unit_out, slope_out,
        q_out, k_out, v_out, mixed_out, hidden_out, small, wide, rstd_out, captions,
    ) = refs[:17]
    (
        attn_v, up_v, down_v, pieces, normed, back_v, weight, q_v, k_v, v_v, mixed, mixed_own,
        context, ffn, act, unit, mid, slope, norms, sums, stat_send, stat_recv, load_sem,
        piece_sems, gather_sems, norm_sems, share_sems, turn_sems, stat_sems, weight_sem, store_sem,
    ) = refs[17:]
    wire = Wire()
    count = lax.axis_size("dp")
    member, group = wire.member, wire.me // SHARE
    low, high = group % 2, group // 2
    masks = group_masks()
    width = q_v.shape[1]
    step = width
    ff_width = act.shape[1]
    local = attn_v.shape[0]
    head_size = D // HEADS
    rows_each = L

    loads = [
        pltpu.make_async_copy(source, target, load_sem.at[k])
        for k, (source, target) in enumerate(
            [(attn_in, attn_v), (up_in, up_v), (down_in, down_v)]
        )
    ]
    for item in loads:
        item.start()
    norms[wire.me] = vectors[...].astype(BF).astype(F32)
    wire.meet()

    def piece_copies(chunk):
        place = gathered[chunk].at[high, low, pl.ds(pl.multiple_of(member * local, local), local), :]
        here = pltpu.make_async_copy(pieces.at[0, chunk], place, piece_sems.at[0, chunk, 0])
        away = [
            wire.copy(
                pieces.at[j, chunk], place, piece_sems.at[0, chunk, j], piece_sems.at[1, chunk, j], j
            )
            for j in range(1, SHARE)
        ]
        return here, away

    def send_pieces(chunk):
        for j in range(SHARE):
            to = flipped(member, j)
            if chunk < 4:
                value = attn_v[:, chunk, pl.ds(pl.multiple_of(to * width, width), width)]
            else:
                source = up_v if chunk < 4 + REDUCE_CHUNKS else down_v
                k = (chunk - 4) % REDUCE_CHUNKS
                value = source[:, pl.ds(pl.multiple_of(to * ff_width + k * step, step), step)]
            pieces[j, chunk] = value.astype(BF)
        here, away = piece_copies(chunk)
        here.start()
        for item in away:
            item.start()

    def gather_copy(chunk, stage):
        buf = gathered[chunk]
        if stage == len(masks) - 1:
            part = buf.at[:, low]
        else:
            size = 1 << stage
            part = buf.at[pl.ds((high // size) * size, size), low]
        return wire.copy(
            part,
            part,
            gather_sems.at[0, chunk, stage],
            gather_sems.at[1, chunk, stage],
            masks[stage],
        )

    def begin(chunk):
        if chunk >= GATHERED:
            return
        here, away = piece_copies(chunk)
        here.wait()
        for item in away:
            item.wait_recv()
        gather_copy(chunk, 0).start()

    def follow(chunk, stage):
        if not 0 <= chunk < GATHERED:
            return
        gather_copy(chunk, stage - 1).wait_recv()
        gather_copy(chunk, stage).start()

    stages = len(masks)

    def advance(at):
        begin(at)
        for stage in range(1, stages):
            follow(at - stage, stage)

    def tick(chunk):
        advance(chunk + stages)
        gather_copy(chunk, stages - 1).wait_recv()

    norm_stages = count.bit_length() - 1

    def norm_copy(stage):
        size = 1 << stage
        part = norms.at[pl.ds((wire.me // size) * size, size)]
        return wire.copy(part, part, norm_sems.at[0, stage], norm_sems.at[1, stage], size)

    norm_copy(0).start()
    loads[0].wait()
    for chunk in range(4):
        send_pieces(chunk)
    for stage in range(1, norm_stages):
        norm_copy(stage - 1).wait_recv()
        norm_copy(stage).start()
    advance(0)
    norm_copy(norm_stages - 1).wait_recv()
    small_cols = D // count
    join = max(1, 128 // small_cols)
    small[...] = jnp.concatenate(
        [
            jnp.concatenate([norms[p * join + i][0:8, 0:small_cols] for i in range(join)], axis=1)
            for p in range(count // join)
        ],
        axis=1,
    )
    wide[...] = jnp.zeros_like(wide)
    per_row, row_cols = vector_rows(count)
    per_quarter = count // SHARE
    for r in range(2):
        got = [
            norms[member * per_quarter + i][8 + r * per_row + k : 9 + r * per_row + k, 0:row_cols]
            for i in range(per_quarter)
            for k in range(per_row)
        ]
        wide[r : r + 1, :] = jnp.concatenate(got, axis=1)
    row_count = SHARE * own // rows_each
    own_count = own // rows_each
    lane = lax.broadcasted_iota(jnp.int32, (8, 128), 1)
    sub = lax.broadcasted_iota(jnp.int32, (8, 128), 0)
    table = jnp.zeros((8, 128), F32)
    for row in range(row_count):
        j, i = row // own_count, row % own_count
        at = 8 + 2 * per_row
        value = norms[flipped(wire.me, j)][at : at + 1, i : i + 1]
        table = jnp.where((sub == row % 8) & (lane == row // 8), value, table)
    captions[...] = table

    def norm_rows(read, at_gain, write, tile=64):
        def body(row, tile):
            at = pl.ds(row, tile)
            scaled = normalized(read(at)) * small[at_gain : at_gain + 1, :]
            write(at, scaled + small[at_gain + 1 : at_gain + 2, :])

        row_tiles(own, body, tile)

    def write_normed(at, value):
        normed[0, at, :] = value.astype(BF)

    norm_rows(lambda at: tokens[at, :].astype(F32), 0, write_normed)
    share_normed = Share(wire, normed.at[0], normed, share_sems.at[0])
    share_normed.start()
    advance(1)

    def back_rows(row, tile):
        at = pl.ds(row, tile)
        back_v[at, :] = (cotangent[at, :].astype(F32) * live[at, 0:1]).astype(BF)

    row_tiles(own, back_rows, 64)
    back_here = pltpu.make_async_copy(back_v, back_all.at[0], store_sem.at[0])
    back_here.start()
    for item in loads[1:]:
        item.wait()
    for chunk in range(4, 4 + REDUCE_CHUNKS):
        send_pieces(chunk)
    for at in range(2, stages):
        advance(at)
    share_normed.forward()
    share_back = Share(wire, back_v, back_all, share_sems.at[1])
    share_back.start()
    for chunk in range(4 + REDUCE_CHUNKS, GATHERED):
        send_pieces(chunk)

    def fetch(source, slot):
        return pltpu.make_async_copy(source, weight.at[slot], weight_sem.at[slot])

    def block_of(chunk):
        return gathered[chunk]

    def weights_of(slot):
        return weight[slot].reshape(D, step)

    def project(slot, target, cosine, sine):
        @pl.loop(0, SHARE)
        def _(j):
            value = dot_f32(normed[j], weights_of(slot), 1, 0)
            for i in range(own_count):
                part = value[i * rows_each : (i + 1) * rows_each]
                if cosine is not None:
                    part = part * cosine[...] + quarter_turn(part) * sine[...]
                at = pl.ds(pl.multiple_of(j * own + i * rows_each, rows_each), rows_each)
                target[at, :] = part.astype(BF)

    tick(0)
    fetch(block_of(0), 0).start()
    share_normed.done()
    fetch(block_of(0), 0).wait()
    project(0, q_v, cq, sq)
    normed_store = pltpu.make_async_copy(normed, normed_out, store_sem.at[1])
    normed_store.start()
    tick(1)
    fetch(block_of(1), 1).start()
    fetch(block_of(1), 1).wait()
    project(1, k_v, ck, sk)
    tick(2)
    fetch(block_of(2), 0).start()
    fetch(block_of(2), 0).wait()
    project(0, v_v, None, None)

    def attend_loop(first, last):
        @pl.loop(first, last)
        def _(row):
            at = pl.ds(pl.multiple_of(row * rows_each, rows_each), rows_each)
            caption = captions[pl.ds(row, 1), 0:1]
            mixed[at, :] = attention_block(
                head_size, caption, q_v[at, :], k_v[at, :], v_v[at, :]
            )

    attend_loop(0, row_count // 2)
    tick(3)
    share_back.forward()

    def out_copies():
        mine = out_full.at[member]
        far = flipped(member, 2)
        parts = [
            (gathered[3], mine, 2),
            (gathered[3], mine, 1),
            (out_full.at[far], out_full.at[far], 1),
        ]
        return [
            wire.copy(source, target, share_sems.at[4, 0, k], share_sems.at[4, 1, k], mask)
            for k, (source, target, mask) in enumerate(parts)
        ]

    out_here = pltpu.make_async_copy(gathered[3], out_full.at[member], store_sem.at[2])
    out_here.start()
    out_moves = out_copies()
    out_moves[0].start()
    out_moves[1].start()
    attend_loop(row_count // 2, row_count)

    def mixed_copies():
        here = pltpu.make_async_copy(
            mixed.at[pl.ds(0, own), :], mixed_own.at[member], turn_sems.at[0, 0]
        )
        away = [
            wire.copy(
                mixed.at[pl.ds(j * own, own), :],
                mixed_own.at[member],
                turn_sems.at[0, j],
                turn_sems.at[1, j],
                j,
            )
            for j in range(1, SHARE)
        ]
        return here, away

    mixed_here, mixed_away = mixed_copies()
    mixed_here.start()
    for item in mixed_away:
        item.start()
    stores = [
        pltpu.make_async_copy(source, target, store_sem.at[3 + k])
        for k, (source, target) in enumerate([(q_v, q_out), (k_v, k_out), (v_v, v_out)])
    ]
    for item in stores:
        item.start()
    tick(4)
    mixed_here.wait()
    for item in mixed_away:
        item.wait_recv()

    def write_context(at, value):
        context[at, :] = value.astype(BF)

    norm_rows(
        lambda at: jnp.concatenate(
            [mixed_own[t, at, :].astype(F32) for t in range(SHARE)], axis=1
        ),
        2,
        write_context,
    )
    stores.append(pltpu.make_async_copy(mixed_own, mixed_out, store_sem.at[6]))
    stores[-1].start()
    tick(5)
    out_moves[0].wait_recv()
    out_moves[2].start()
    tick(6)
    out_here.wait()
    out_moves[1].wait_recv()
    out_moves[2].wait_recv()
    fetch(out_full.at[0], 0).start()
    for t in range(SHARE):
        fetch(out_full.at[t], t % 2).wait()
        if t + 1 < SHARE:
            fetch(out_full.at[t + 1], (t + 1) % 2).start()
        at = pl.ds(t * width, width)
        hidden_out[:, at] = tokens[:, at].astype(F32) + dot_f32(
            context[...], weights_of(t % 2), 1, 0
        )

    def write_ffn(at, value):
        ffn[0, at, :] = value.astype(BF)

    norm_rows(lambda at: hidden_out[at, :], 4, write_ffn)
    share_ffn = Share(wire, ffn.at[0], ffn, share_sems.at[2])
    share_ffn.start()
    context_here = pltpu.make_async_copy(context, context_all.at[0], store_sem.at[7])
    context_here.start()
    share_context = Share(wire, context, context_all, share_sems.at[3])
    tick(7)
    share_ffn.forward()
    share_context.start()
    fetch(block_of(4), 0).start()
    share_ffn.done()
    stores.append(pltpu.make_async_copy(ffn, ffn_out, store_sem.at[8]))
    stores[-1].start()
    sums[...] = jnp.zeros_like(sums)

    def widen(k):
        slot = k % 2
        fetch(block_of(4 + k), slot).wait()
        if k + 1 < REDUCE_CHUNKS:
            fetch(block_of(5 + k), 1 - slot).start()
        at_cols = pl.ds(k * step, step)

        @pl.loop(0, SHARE)
        def _(j):
            at = pl.ds(pl.multiple_of(j * own, own), own)
            value = dot_f32(ffn[j], weights_of(slot), 1, 0)
            cdf, density = gelu_parts(value)
            active = value * cdf
            act[at, at_cols] = active
            slope[at, at_cols] = (cdf + value * density).astype(BF)
            sums[at, :] += jnp.broadcast_to(
                jnp.sum(active, axis=1, keepdims=True), (own, sums.shape[1])
            )

    widen(0)
    widen(1)
    tick(8)
    widen(2)
    widen(3)
    share_context.forward()

    def spread_body(row, tile):
        at = pl.ds(row, tile)
        mean = sums[at, 0:1] * (1.0 / ff_width)
        square = jnp.zeros((tile, 1), F32)
        for k in range(REDUCE_CHUNKS):
            center = act[at, pl.ds(k * step, step)] - mean
            square += jnp.sum(center * center, axis=1, keepdims=True)
        lane = lax.broadcasted_iota(jnp.int32, (tile, sums.shape[1]), 1)
        sums[at, :] = jnp.where(lane == 0, mean, square)

    row_tiles(SHARE * own, spread_body)
    for j in range(SHARE):
        stat_send[j] = sums[pl.ds(j * own, own), :].T[0:8, :]
    stats = [
        wire.copy(
            stat_send, stat_recv.at[j - 1], stat_sems.at[0, j - 1], stat_sems.at[1, j - 1], j
        )
        for j in range(1, SHARE)
    ]
    for item in stats:
        item.start()
    stores.append(pltpu.make_async_copy(slope, slope_out, store_sem.at[9]))
    stores[-1].start()
    tick(9)
    for item in stats:
        item.wait_recv()
    for j in range(SHARE):
        parts = [stat_send[j]] + [stat_recv[k - 1, j ^ k] for k in range(1, SHARE)]
        mean = sum(part[0:1, :] for part in parts) * (1.0 / SHARE)
        square = sum(
            part[1:2, :] + ff_width * (part[0:1, :] - mean) ** 2 for part in parts
        )
        rstd = lax.rsqrt(square * (1.0 / (SHARE * ff_width)) + EPS_NORM)
        sub_all = lax.broadcasted_iota(jnp.int32, (128, own), 0)
        both = jnp.where(sub_all == 0, mean, rstd).T
        sums[pl.ds(j * own, own), :] = both
    rstd_out[...] = jnp.broadcast_to(sums[:, 1:2], rstd_out.shape)

    def finish(k):
        at_cols = pl.ds(k * step, step)

        @pl.loop(0, SHARE)
        def _(j):
            at = pl.ds(pl.multiple_of(j * own, own), own)
            value = (act[at, at_cols] - sums[at, 0:1]) * sums[at, 1:2]
            unit[at, at_cols] = value.astype(BF)
            mid[at, at_cols] = (value * wide[0:1, at_cols] + wide[1:2, at_cols]).astype(BF)

    finish(0)
    finish(1)
    tick(10)
    finish(2)
    finish(3)
    stores += [
        pltpu.make_async_copy(unit, unit_out, store_sem.at[10]),
        pltpu.make_async_copy(mid, mid_out, store_sem.at[11]),
    ]
    for item in stores[-2:]:
        item.start()
    share_context.done()
    share_back.done()
    for chunk in range(11, GATHERED):
        tick(chunk)
    for item in stores + [back_here, normed_store, context_here]:
        item.wait()
    for chunk in range(GATHERED):
        for item in piece_copies(chunk)[1]:
            item.wait_send()
        for stage in range(len(masks)):
            gather_copy(chunk, stage).wait_send()
    for stage in range(norm_stages):
        norm_copy(stage).wait_send()
    for item in [share_normed, share_back, share_context, share_ffn]:
        item.close()
    for item in out_moves + mixed_away + stats:
        item.wait_send()


def forward(tokens, cotangent, live, attn_weight, up_weight, down_weight, vectors, tables):
    count = lax.axis_size("dp")
    own = tokens.shape[0]
    all_tokens = SHARE * own
    width, ff_width = D // SHARE, FF // SHARE
    groups = count // SHARE
    local = D // count
    chunk = (groups // 2, 2, D // groups, width)
    stages = len(group_masks())
    any_spec = pl.BlockSpec(memory_space=pl.ANY)
    vmem = pl.BlockSpec(memory_space=pltpu.VMEM)
    shared = jax.ShapeDtypeStruct((SHARE, own, D), BF)
    wide = jax.ShapeDtypeStruct((all_tokens, ff_width), BF)
    part = jax.ShapeDtypeStruct((all_tokens, width), BF)
    norm_stages = count.bit_length() - 1
    return pl.pallas_call(
        partial(forward_kernel, own),
        in_specs=[vmem] * 3 + [any_spec] * 3 + [vmem] * 5,
        out_specs=[any_spec] * (GATHERED + 12) + [vmem] * 5,
        out_shape=[jax.ShapeDtypeStruct(chunk, BF)] * GATHERED
        + [jax.ShapeDtypeStruct((SHARE,) + chunk, BF)]
        + [shared] * 4
        + [wide] * 3
        + [part] * 3
        + [
            jax.ShapeDtypeStruct((SHARE, own, width), BF),
            jax.ShapeDtypeStruct((own, D), F32),
            jax.ShapeDtypeStruct((8, D), F32),
            jax.ShapeDtypeStruct((8, ff_width), F32),
            jax.ShapeDtypeStruct((all_tokens, 128), F32),
            jax.ShapeDtypeStruct((8, 128), F32),
        ],
        scratch_shapes=[
            pltpu.VMEM((local, 4, D), F32),
            pltpu.VMEM((local, FF), F32),
            pltpu.VMEM((local, FF), F32),
            pltpu.VMEM((SHARE, GATHERED, local, width), BF),
            pltpu.VMEM((SHARE, own, D), BF),
            pltpu.VMEM((own, D), BF),
            pltpu.VMEM((2,) + chunk, BF),
            pltpu.VMEM((all_tokens, width), BF),
            pltpu.VMEM((all_tokens, width), BF),
            pltpu.VMEM((all_tokens, width), BF),
            pltpu.VMEM((all_tokens, width), BF),
            pltpu.VMEM((SHARE, own, width), BF),
            pltpu.VMEM((own, D), BF),
            pltpu.VMEM((SHARE, own, D), BF),
            pltpu.VMEM((all_tokens, ff_width), F32),
            pltpu.VMEM((all_tokens, ff_width), BF),
            pltpu.VMEM((all_tokens, ff_width), BF),
            pltpu.VMEM((all_tokens, ff_width), BF),
            pltpu.VMEM((count, 16, 128), F32),
            pltpu.VMEM((all_tokens, 128), F32),
            pltpu.VMEM((SHARE, 8, own), F32),
            pltpu.VMEM((SHARE - 1, SHARE, 8, own), F32),
            pltpu.SemaphoreType.DMA((3,)),
            pltpu.SemaphoreType.DMA((2, GATHERED, SHARE)),
            pltpu.SemaphoreType.DMA((2, GATHERED, stages)),
            pltpu.SemaphoreType.DMA((2, norm_stages)),
            pltpu.SemaphoreType.DMA((5, 2, 3)),
            pltpu.SemaphoreType.DMA((2, SHARE)),
            pltpu.SemaphoreType.DMA((2, SHARE - 1)),
            pltpu.SemaphoreType.DMA((2,)),
            pltpu.SemaphoreType.DMA((12,)),
        ],
        compiler_params=pltpu.CompilerParams(
            collective_id=5, has_side_effects=True, vmem_limit_bytes=KERNEL_VMEM
        ),
        name="forward",
    )(tokens, cotangent, live, attn_weight, up_weight, down_weight, vectors, *tables)


def gelu_parts(value):
    cdf = 0.5 * (1.0 + lax.erf(value * math.sqrt(0.5)))
    density = jnp.exp(-0.5 * value * value) * (1.0 / math.sqrt(2.0 * math.pi))
    return cdf, density


def per_device(
    tokens,
    cotangent,
    caption_len,
    attn_weight,
    up_weight,
    down_weight,
    small_norms,
    wide_norms,
    attn_row,
    attn_col,
    up_row,
    up_col,
    down_row,
    down_col,
    small_moment,
    wide_moment,
):
    count = lax.axis_size("dp")
    me = lax.axis_index("dp")
    head_size = D // HEADS
    width = D // SHARE
    own = tokens.shape[0]
    own_rows = caption_len.shape[0]

    small_width = D // count
    wide_width = FF // count
    per_row, row_cols = vector_rows(count)
    vectors = jnp.concatenate(
        [
            jnp.pad(small_norms, ((0, 2), (0, 128 - small_width))),
            jnp.pad(
                wide_norms.reshape(2 * per_row, row_cols),
                ((0, 0), (0, 128 - row_cols)),
            ),
            jnp.pad(caption_len.astype(F32), (0, 128 - own_rows))[None],
            jnp.zeros((7 - 2 * per_row, 128), F32),
        ],
        axis=0,
    )
    slot_index = jnp.arange(L)
    live_mask = (slot_index[None, :] < IMG + caption_len[:, None]).astype(F32).reshape(own)
    tables = xpos_tables(head_size, width // head_size)
    results = forward(
        tokens,
        cotangent,
        jnp.broadcast_to(live_mask[:, None], (own, 128)),
        attn_weight,
        up_weight,
        down_weight,
        vectors,
        tables,
    )
    full = [item.reshape(D, width) for item in results[:GATHERED]]
    query_full, key_full, value_full = full[:3]
    up_full, down_full = full[4 : 4 + REDUCE_CHUNKS], full[4 + REDUCE_CHUNKS :]
    (
        out_full, normed_all, back_all, context_all, ffn_all, ffn_mid, unit, slope, queries,
        keys_low, values_low, mixed_own, hidden, small_vals, wide_own, rstd, captions,
    ) = results[GATHERED:]
    all_tokens = SHARE * own
    out_full = out_full.reshape(SHARE, D, width)
    normed_all, back_all, context_all, ffn_all = [
        item.reshape(all_tokens, D) for item in (normed_all, back_all, context_all, ffn_all)
    ]
    captions = captions[:, 0].astype(jnp.int32)
    inputs = tokens.astype(F32)
    back_out = cotangent.astype(F32) * live_mask[:, None]
    unit_one, rstd_one = norm_stats(inputs)
    attn_mixed = jnp.concatenate([mixed_own[t] for t in range(SHARE)], axis=1).astype(F32)
    unit_two, rstd_two = norm_stats(attn_mixed)
    unit_three, rstd_three = norm_stats(hidden)

    down_rows, up_grad_low, wide_terms, ffn_in_grad = ffn_back(
        back_all, ffn_mid, down_full, up_full, unit, slope, wide_own[0], rstd
    )
    hidden_part, gain_three, bias_three = norm_back(unit_three, rstd_three, small_vals[4], ffn_in_grad)
    hidden_grad = back_out + hidden_part
    hidden_low = hidden_grad.astype(BF)

    context_grad = sum(
        dot_f32(hidden_low[:, t * width : (t + 1) * width], out_full[t], 1, 1)
        for t in range(SHARE)
    )
    mixed_grad, gain_two, bias_two = norm_back(unit_two, rstd_two, small_vals[2], context_grad)

    up_rows, grad_q, grad_k, grad_v, hidden_cols = attention_back(
        ffn_all,
        up_grad_low,
        queries,
        keys_low,
        values_low,
        mixed_grad.astype(BF),
        hidden_low,
        captions,
        tables,
    )
    attn_rows_out, normed_grad, block_sum = project_back(
        normed_all,
        context_all,
        [hidden_cols, grad_q, grad_k, grad_v],
        ffn_mid,
        [query_full, key_full, value_full],
        down_full,
    )
    block_out = (hidden + block_sum).astype(BF)
    input_part, gain_one, bias_one = norm_back(unit_one, rstd_one, small_vals[0], normed_grad)
    input_grad = hidden_grad + input_part

    def spread_columns(value, whole):
        return lax.dynamic_update_slice(
            jnp.zeros((value.shape[0], whole), F32), value, (0, me * value.shape[1])
        ).reshape(-1, D)

    moments = jnp.concatenate(
        [spread_columns(wide_moment, FF), spread_columns(small_moment, D)], axis=0
    )
    vector_squares = jnp.pad(
        jnp.concatenate([jnp.sum(item * item, axis=1) for item in (wide_norms, small_norms)]),
        (12, 128 - 20),
    )[None]
    row_old = jnp.pad(
        jnp.stack([up_row, down_row] + [attn_row[j] for j in range(4)], axis=1), ((0, 0), (0, 122))
    )
    col_old = jnp.concatenate([up_col.reshape(-1, D), down_col.reshape(-1, D), attn_col], axis=0)
    every = range(REDUCE_CHUNKS)
    row_new, results = update(
        [[(0, c) for c in every], [(1, c) for c in every], [(2, c) for c in (1, 2, 3, 0)]],
        [up_rows, down_rows, attn_rows_out],
        [up_weight, down_weight, attn_weight],
        row_old,
        col_old,
        wide_terms,
        jnp.stack([gain_one, bias_one, gain_two, bias_two, gain_three, bias_three]),
        moments,
        vector_squares,
    )
    (
        up_grad, down_grad, attn_grad, up_new, down_new, attn_new, up_copy, down_copy, attn_copy,
        col_new, vectors,
    ) = results
    vectors = vectors.reshape(3, -1, D)
    wide_parts = take_block(vectors[:, : 2 * WIDE].reshape(6, FF), me, wide_width, 1)
    wide_parts = wide_parts.reshape(3, 2, wide_width)
    small_parts = take_block(vectors[:, 2 * WIDE :].reshape(18, D), me, small_width, 1)
    small_parts = small_parts.reshape(3, 6, small_width)
    return (
        block_out,
        input_grad,
        attn_grad,
        up_grad,
        down_grad,
        row_new[:, 2:6].T,
        col_new[2 * WIDE :],
        row_new[:, 0],
        col_new[:WIDE].reshape(FF),
        row_new[:, 1],
        col_new[WIDE : 2 * WIDE].reshape(FF),
        attn_new,
        up_new,
        down_new,
        attn_copy,
        up_copy,
        down_copy,
        small_parts[0],
        wide_parts[0],
        small_parts[1],
        wide_parts[1],
        small_norms - small_parts[2],
        wide_norms - wide_parts[2],
    )


def solution(mesh):
    placed = (
        P("dp", None),
        P("dp", None),
        P("dp"),
        P("dp", None, None),
        P("dp", None),
        P("dp", None),
        P(None, "dp"),
        P(None, "dp"),
        P(None, "dp"),
        P(),
        P("dp"),
        P(),
        P("dp"),
        P(),
        P(None, "dp"),
        P(None, "dp"),
    )
    return jax.shard_map(
        per_device,
        mesh=mesh,
        in_specs=placed,
        out_specs=(
            P("dp", None),
            P("dp", None),
            P("dp", None, None),
            P("dp", None),
            P("dp", None),
            P(None, "dp"),
            P(),
            P("dp"),
            P(),
            P("dp"),
            P(),
            P("dp", None, None),
            P("dp", None),
            P("dp", None),
            P("dp", None, None),
            P("dp", None),
            P("dp", None),
            P(None, "dp"),
            P(None, "dp"),
            P(None, "dp"),
            P(None, "dp"),
            P(None, "dp"),
            P(None, "dp"),
        ),
        check_vma=False,
    )
```

```python
from functools import partial
import math

import jax
import jax.numpy as jnp
from jax import lax
from jax.experimental import pallas as pl
from jax.experimental.pallas import tpu as pltpu
from jax.sharding import PartitionSpec as P

D = 2048
FF = 8192
HEADS = 32
L = 128
IMG = 64
SHARE = 4


EPS_NORM = 1e-05
EPS_SQUARE = 1e-30
EPS_SCALE = 0.001
DECAY_RATE = 0.5
CLIP_LEVEL = 0.5
LEARN_RATE = 0.8
SCALE_BASE = 512.0
MASK_FILL = -1e30

BF = jnp.bfloat16
F32 = jnp.float32


def dot_f32(left, right, left_dim, right_dim):
    return lax.dot_general(
        left, right, (((left_dim,), (right_dim,)), ((), ())), preferred_element_type=F32
    )


def group_masks():
    count = lax.axis_size("dp")
    masks = []
    mask = 2 * SHARE
    while mask < count:
        masks.append(mask)
        mask *= 2
    if count > SHARE:
        masks.append(SHARE)
    return masks


def take_block(value, index, width, axis):
    return lax.dynamic_slice_in_dim(value, index * width, width, axis)


def norm_stats(values):
    mean = jnp.mean(values, axis=-1, keepdims=True)
    center = values - mean
    rstd = lax.rsqrt(jnp.mean(center * center, axis=-1, keepdims=True) + EPS_NORM)
    return center * rstd, rstd


def norm_back(unit, rstd, gain, upstream):
    scaled = upstream * gain
    lean = jnp.mean(scaled, axis=-1, keepdims=True)
    slope = jnp.mean(scaled * unit, axis=-1, keepdims=True)
    return (
        rstd * (scaled - lean - unit * slope),
        jnp.sum(upstream * unit, axis=0),
        jnp.sum(upstream, axis=0),
    )


def xpos_tables(head_size, head_count):
    slot_pos = jnp.arange(L, dtype=F32)[:, None]
    pair_idx = jnp.arange(head_size // 2, dtype=F32)[None, :]
    theta = jnp.exp(-(2.0 * pair_idx / head_size) * jnp.log(10000.0))
    angle = slot_pos * theta
    zeta = (2.0 * pair_idx / head_size + 0.4) / 1.4
    power_table = jnp.exp(jnp.log(zeta) * slot_pos / SCALE_BASE)

    def widen(table):
        return jnp.tile(jnp.repeat(table, 2, axis=1), (1, head_count))

    cosine, sine, power = widen(jnp.cos(angle)), widen(jnp.sin(angle)), widen(power_table)
    return cosine * power, sine * power, cosine / power, sine / power


def quarter_turn(values):
    width = values.shape[1]
    lane = lax.broadcasted_iota(jnp.int32, values.shape, 1)
    return jnp.where(
        lane % 2 == 0, -pltpu.roll(values, width - 1, 1), pltpu.roll(values, 1, 1)
    )


def masked_probs(query, key, caption, head_size):
    scores = dot_f32(query, key, 1, 1) * (1.0 / math.sqrt(head_size))
    row = lax.broadcasted_iota(jnp.int32, scores.shape, 0)
    col = lax.broadcasted_iota(jnp.int32, scores.shape, 1)
    scores = jnp.where((col <= row) & (col < IMG + caption), scores, MASK_FILL)
    terms = jnp.exp(scores - jnp.max(scores, axis=-1, keepdims=True))
    return terms / jnp.sum(terms, axis=-1, keepdims=True)


def attention_back_block(head_size, caption, q_low, k_low, v_low, g_low, tables):
    cq, sq, ck, sk = tables
    grads_q, grads_k, grads_v = [], [], []
    for head in range(q_low.shape[1] // head_size):
        at = slice(head * head_size, (head + 1) * head_size)
        probs = masked_probs(q_low[:, at], k_low[:, at], caption, head_size)
        grads_v.append(dot_f32(probs.astype(BF), g_low[:, at], 0, 0))
        prob_grad = dot_f32(g_low[:, at], v_low[:, at], 1, 1)
        score_grad = probs * (prob_grad - jnp.sum(probs * prob_grad, axis=-1, keepdims=True))
        score_low = (score_grad * (1.0 / math.sqrt(head_size))).astype(BF)
        grads_q.append(dot_f32(score_low, k_low[:, at], 1, 0))
        grads_k.append(dot_f32(score_low, q_low[:, at], 0, 0))
    grad_q = jnp.concatenate(grads_q, axis=1)
    grad_k = jnp.concatenate(grads_k, axis=1)
    return (
        (grad_q * cq - quarter_turn(grad_q) * sq).astype(BF),
        (grad_k * ck - quarter_turn(grad_k) * sk).astype(BF),
        jnp.concatenate(grads_v, axis=1).astype(BF),
    )


MESH = pl.DeviceIdType.MESH
KERNEL_VMEM = 62 * 1024 * 1024


def flipped(index, mask):
    bit = 1
    while bit <= mask:
        if mask & bit:
            index = index + bit - 2 * bit * ((index // bit) % 2)
        bit *= 2
    return index


def partner_masks():
    return list(range(1, SHARE)) + group_masks()


class Wire:
    def __init__(self):
        self.me = lax.axis_index("dp")
        self.member = self.me % SHARE

    def meet(self, more=()):
        barrier = pltpu.get_barrier_semaphore()
        masks = partner_masks() + list(more)
        for mask in masks:
            pl.semaphore_signal(
                barrier, inc=1, device_id=(flipped(self.me, mask),), device_id_type=MESH
            )
        pl.semaphore_wait(barrier, len(masks))

    def copy(self, source, target, send_sem, recv_sem, mask):
        return pltpu.make_async_remote_copy(
            src_ref=source,
            dst_ref=target,
            send_sem=send_sem,
            recv_sem=recv_sem,
            device_id=(flipped(self.me, mask),),
            device_id_type=MESH,
        )


def row_tiles(rows, body, tile=256):
    tile = min(tile, rows)

    @pl.loop(0, rows // tile)
    def _(index):
        body(pl.multiple_of(index * tile, tile), tile)


class Reducer:
    @staticmethod
    def plan(count, resumed, stopped):
        stages = len(group_masks())
        carried = min(2, stages - 1)
        resume, stop = [0] * count, [stages] * count
        if resumed:
            resume = list(range(carried, 0, -1)) + [0] * count
        stop = [stages] * len(resume)
        if stopped:
            stop[len(stop) - carried :] = range(carried, 0, -1)
        return resume, stop

    @staticmethod
    def carry_shapes(cols):
        carried = min(2, len(group_masks()) - 1)
        return [jax.ShapeDtypeStruct((D >> at, cols), F32) for at in range(carried, 0, -1)]

    @staticmethod
    def scratch(plan, cols):
        resume, stop = plan
        stages = len(group_masks())
        halves = [D >> (stage + 1) for stage in range(stages)]
        block = D >> stages
        count = len(resume)
        used = [
            sum(first <= stage < last for first, last in zip(resume, stop))
            for stage in range(stages)
        ]
        return (
            [pltpu.VMEM((2, half, cols), BF) for half in halves]
            + [pltpu.VMEM((number, half, cols), BF) for number, half in zip(used, halves)]
            + [
                pltpu.VMEM((min(stages, count), D // 2, cols), F32),
                pltpu.VMEM((2, block, cols), BF),
                pltpu.SemaphoreType.DMA((count, stages)),
                pltpu.SemaphoreType.DMA((count, stages)),
                pltpu.SemaphoreType.DMA((count, SHARE)),
                pltpu.SemaphoreType.DMA((count, SHARE)),
                pltpu.SemaphoreType.DMA((count,)),
            ]
        )

    @staticmethod
    def out_shape(plan, cols):
        stages = len(group_masks())
        block = D >> stages
        finished = sum(last == stages for last in plan[1])
        return jax.ShapeDtypeStruct((SHARE, finished, block // SHARE, cols), BF)

    def __init__(self, wire, plan, terms, out, refs, carry_in=(), carry_out=()):
        self.wire, self.out = wire, out
        self.resume, self.stop = plan
        self.count = len(self.resume)
        self.terms = [None] * (self.count - len(terms)) + list(terms)
        self.carry_in, self.carry_out = carry_in, carry_out
        self.masks = group_masks()[::-1]
        self.stages = len(self.masks)
        self.slots = min(self.stages, self.count)
        self.sends, refs = refs[: self.stages], refs[self.stages :]
        self.recvs, refs = refs[: self.stages], refs[self.stages :]
        (
            self.kept, self.done, self.send_sem, self.recv_sem, self.out_send, self.out_recv,
            self.carry_sem,
        ) = refs
        self.block = D >> self.stages
        self.low = (wire.me // SHARE) % 2

    def goes(self, chunk, stage):
        return 0 <= chunk < self.count and self.resume[chunk] <= stage < self.stop[chunk]

    def got(self, chunk, stage):
        first = min(c for c in range(self.count) if self.goes(c, stage))
        return self.recvs[stage].at[chunk - first]

    def finishes(self, chunk):
        return 0 <= chunk < self.count and self.stop[chunk] == self.stages

    def carry_load(self, chunk):
        ref = self.carry_in[chunk]
        return pltpu.make_async_copy(
            ref,
            self.kept.at[chunk % self.slots, pl.ds(0, ref.shape[0]), :],
            self.carry_sem.at[chunk],
        )

    def carry_store(self, chunk):
        ref = self.carry_out[chunk - (self.count - len(self.carry_out))]
        return pltpu.make_async_copy(
            self.kept.at[chunk % self.slots, pl.ds(0, ref.shape[0]), :],
            ref,
            self.carry_sem.at[chunk],
        )

    def load(self):
        for chunk in range(len(self.carry_in)):
            self.carry_load(chunk).start()

    def half_bit(self, stage):
        return (self.wire.me // self.masks[stage]) % 2

    def lhs_row(self, row, tile, low):
        block = row // self.block
        return pl.multiple_of((2 * block + low) * self.block + row % self.block, tile)

    def copy(self, chunk, stage):
        return self.wire.copy(
            self.sends[stage].at[chunk % 2],
            self.got(chunk, stage),
            self.send_sem.at[chunk, stage],
            self.recv_sem.at[chunk, stage],
            self.masks[stage],
        )

    def start(self, chunk):
        if not self.goes(chunk, 0):
            return
        if self.goes(chunk - 2, 0):
            self.copy(chunk - 2, 0).wait_send()
        lhs, rhs, cols = self.terms[chunk]
        half = D // 2

        def body(row, tile):
            at = pl.ds(self.lhs_row(row, tile, 1 - self.low), tile)
            self.sends[0][chunk % 2, pl.ds(row, tile), :] = dot_f32(
                lhs[at, :], rhs[:, cols], 1, 0
            ).astype(BF)

        row_tiles(half, body, self.block)
        self.copy(chunk, 0).start()

    def keep(self, chunk):
        if not self.goes(chunk, 0):
            return
        lhs, rhs, cols = self.terms[chunk]

        def body(row, tile):
            at = pl.ds(self.lhs_row(row, tile, self.low), tile)
            self.kept[chunk % self.slots, pl.ds(row, tile), :] = dot_f32(
                lhs[at, :], rhs[:, cols], 1, 0
            )

        row_tiles(D // 2, body, self.block)

    def step(self, chunk, stage):
        if not 0 <= chunk < self.count or not self.resume[chunk] <= stage <= self.stop[chunk]:
            return
        half = D >> (stage + 1)
        kept = self.kept
        slot = chunk % self.slots
        got = None
        if stage > self.resume[chunk]:
            self.copy(chunk, stage - 1).wait_recv()
            got = self.got(chunk, stage - 1)
        else:
            self.carry_load(chunk).wait()

        def value(at):
            if got is None:
                return kept[slot, at, :]
            return kept[slot, at, :] + got[at, :].astype(F32)

        if stage == self.stop[chunk]:

            def whole(row, tile):
                at = pl.ds(row, tile)
                kept[slot, at, :] = value(at)

            row_tiles(2 * half, whole)
            self.carry_store(chunk).start()
            return
        if self.goes(chunk - 2, stage):
            self.copy(chunk - 2, stage).wait_send()
        send = self.sends[stage]
        bit = self.half_bit(stage)

        def out_half(row, tile):
            at = pl.ds(pl.multiple_of((1 - bit) * half + row, tile), tile)
            send[chunk % 2, pl.ds(row, tile), :] = value(at).astype(BF)

        def own_half(row, tile):
            at = pl.ds(pl.multiple_of(bit * half + row, tile), tile)
            kept[slot, pl.ds(row, tile), :] = value(at)

        row_tiles(half, out_half)
        self.copy(chunk, stage).start()
        row_tiles(half, own_half)

    def place(self, chunk):
        return sum(self.finishes(c) for c in range(chunk))

    def give(self, chunk):
        part = self.block // SHARE
        slot = chunk % 2
        copies = []
        for j in range(1, SHARE):
            to = flipped(self.wire.member, j)
            copies.append(
                self.wire.copy(
                    self.done.at[slot, pl.ds(pl.multiple_of(to * part, part), part), :],
                    self.out.at[j, self.place(chunk)],
                    self.out_send.at[chunk, j],
                    self.out_recv.at[chunk, j],
                    j,
                )
            )
        own = pltpu.make_async_copy(
            self.done.at[slot, pl.ds(pl.multiple_of(self.wire.member * part, part), part), :],
            self.out.at[0, self.place(chunk)],
            self.out_send.at[chunk, 0],
        )
        return own, copies

    def given(self, chunk):
        own, copies = self.give(chunk)
        own.wait()
        for item in copies:
            item.wait_send()

    def finish(self, chunk):
        if not self.finishes(chunk):
            return
        self.copy(chunk, self.stages - 1).wait_recv()
        if self.finishes(chunk - 2):
            self.given(chunk - 2)
        got = self.got(chunk, self.stages - 1)
        slot = chunk % self.slots

        def body(row, tile):
            at = pl.ds(row, tile)
            self.done[chunk % 2, at, :] = (
                self.kept[slot, at, :] + got[at, :].astype(F32)
            ).astype(BF)

        row_tiles(self.block, body)
        own, copies = self.give(chunk)
        own.start()
        for item in copies:
            item.start()

    def tick(self, at):
        for stage in range(1, self.stages):
            self.step(at - stage + 1, stage)
            if stage == 1:
                self.start(at + 2)
        if self.stages == 1:
            self.start(at + 2)
        self.finish(at - self.stages + 1)
        self.keep(at + 1)

    def ticks(self):
        return self.count + self.stages - 1

    def close(self):
        for stage in range(self.stages):
            for chunk in [c for c in range(self.count) if self.goes(c, stage)][-2:]:
                self.copy(chunk, stage).wait_send()
        finished = [c for c in range(self.count) if self.finishes(c)]
        for chunk in finished[-2:]:
            self.given(chunk)
        for chunk in finished:
            for item in self.give(chunk)[1]:
                item.wait_recv()
        for chunk in range(self.count - len(self.carry_out), self.count):
            self.carry_store(chunk).wait()


class OwnerSum:
    @staticmethod
    def scratch(own):
        return [
            pltpu.VMEM((2 * own, D), BF),
            pltpu.VMEM((own, D), BF),
            pltpu.SemaphoreType.DMA((4,)),
        ]

    def __init__(self, wire, own, send, kept, refs):
        self.wire, self.own, self.send, self.kept = wire, own, send, kept
        self.near, self.far, self.sems = refs

    def core_copy(self):
        return self.wire.copy(
            self.send.at[pl.ds(0, 2 * self.own), :],
            self.near,
            self.sems.at[0],
            self.sems.at[1],
            1,
        )

    def far_copy(self):
        return self.wire.copy(
            self.send.at[pl.ds(2 * self.own, self.own), :],
            self.far,
            self.sems.at[2],
            self.sems.at[3],
            2,
        )

    def first(self, term):
        for place, block in enumerate((3, 1)):

            def body(row, tile, place=place, block=block):
                self.send[pl.ds(place * self.own + row, tile), :] = term(block, row, tile).astype(BF)

            row_tiles(self.own, body)
        self.core_copy().start()

    def second(self, term):
        for place, block in enumerate((2, 0)):

            def body(row, tile, place=place, block=block):
                self.kept[pl.ds((1 - place) * self.own + row, tile), :] = term(block, row, tile)

            row_tiles(self.own, body)

    def third(self):
        self.core_copy().wait_recv()
        own = self.own

        def far(row, tile):
            self.send[pl.ds(2 * own + row, tile), :] = (
                self.kept[pl.ds(own + row, tile), :] + self.near[pl.ds(row, tile), :].astype(F32)
            ).astype(BF)

        def near(row, tile):
            at = pl.ds(row, tile)
            self.kept[at, :] = self.kept[at, :] + self.near[pl.ds(own + row, tile), :].astype(F32)

        row_tiles(own, far)
        self.far_copy().start()
        row_tiles(own, near)

    def last(self):
        self.far_copy().wait_recv()

        def body(row, tile):
            at = pl.ds(row, tile)
            self.kept[at, :] = self.kept[at, :] + self.far[at, :].astype(F32)

        row_tiles(self.own, body)
        self.core_copy().wait_send()
        self.far_copy().wait_send()


REDUCE_CHUNKS = 4


def ffn_back_kernel(own, back, back_t, mid, down, up, unit_in, slope_in, gain, rstd, *refs):
    width = mid.shape[1]
    tokens = SHARE * own
    cols = width // REDUCE_CHUNKS
    pieces = len(down)
    out, up_low_out, wide_out, sum_out = refs[:4]
    refs = refs[4:]
    plan = Reducer.plan(REDUCE_CHUNKS, False, True)
    carried = len(Reducer.carry_shapes(cols))
    carry_out, refs = refs[:carried], refs[carried:]
    wire = Wire()
    count = len(Reducer.scratch(plan, cols))
    reducer_refs, refs = refs[:count], refs[count:]
    sum_refs, refs = refs[:3], refs[3:]
    (
        back_v, back_tv, mid_v, weight, unit, slope, grad, sums, stat_send, stat_recv,
        load_sem, stat_sems, store_sem,
    ) = refs

    def weight_copies(parts, first):
        step = width // pieces
        return [
            pltpu.make_async_copy(
                part, weight.at[:, pl.ds(k * step, step)], load_sem.at[first + k]
            )
            for k, part in enumerate(parts)
        ]

    loads = [
        pltpu.make_async_copy(source, target, load_sem.at[k])
        for k, (source, target) in enumerate(
            [(back_t, back_tv), (mid, mid_v), (back, back_v), (unit_in, unit), (slope_in, slope)]
        )
    ]
    down_loads = weight_copies(down, 5)
    up_loads = weight_copies(up, 5 + pieces)
    for item in loads[:3] + down_loads + loads[3:]:
        item.start()
    wire.meet()
    reducer = Reducer(
        wire,
        plan,
        [(back_tv, mid_v, pl.ds(c * cols, cols)) for c in range(REDUCE_CHUNKS)],
        out,
        reducer_refs,
        carry_out=carry_out,
    )
    loads[0].wait()
    loads[1].wait()
    reducer.start(0)
    reducer.start(1)
    reducer.keep(0)

    wide_out[...] = jnp.zeros_like(wide_out)
    sums[...] = jnp.zeros_like(sums)

    def token_tiles(body):
        row_tiles(tokens, body, own)

    def first_pass(k):
        at_cols = pl.ds(k * cols, cols)

        def body(row, tile):
            at = pl.ds(row, tile)
            value = dot_f32(back_v[at, :], weight[:, at_cols], 1, 0)
            grad[at, at_cols] = value
            part = unit[at, at_cols].astype(F32)
            scaled = value * gain[:, at_cols]
            lane = lax.broadcasted_iota(jnp.int32, (tile, sums.shape[1]), 1)
            sums[at, :] += jnp.where(
                lane == 0,
                jnp.sum(scaled, axis=1, keepdims=True),
                jnp.sum(scaled * part, axis=1, keepdims=True),
            )
            wide_out[0:1, at_cols] += jnp.sum(value * part, axis=0, keepdims=True)
            wide_out[1:2, at_cols] += jnp.sum(value, axis=0, keepdims=True)

        token_tiles(body)

    loads[2].wait()
    for item in down_loads:
        item.wait()
    loads[3].wait()
    loads[4].wait()
    for k in range(REDUCE_CHUNKS):
        first_pass(k)
    for item in up_loads:
        item.start()

    stats = [
        wire.copy(
            stat_send, stat_recv.at[j - 1], stat_sems.at[0, j - 1], stat_sems.at[1, j - 1], j
        )
        for j in range(1, SHARE)
    ]
    for j in range(SHARE):
        stat_send[j] = sums[pl.ds(j * own, own), :].T[0:8, :]
    for item in stats:
        item.start()
    reducer.tick(0)
    for item in stats:
        item.wait_recv()
    for j in range(SHARE):
        total = stat_send[j]
        for k in range(1, SHARE):
            total = total + stat_recv[k - 1, j ^ k]
        total = total * (1.0 / (SHARE * width))
        sums[pl.ds(j * own, own), :] = jnp.concatenate([total] * (sums.shape[1] // 8), axis=0).T
    for item in stats:
        item.wait_send()

    def second_pass(k):
        at_cols = pl.ds(k * cols, cols)

        def body(row, tile):
            at = pl.ds(row, tile)
            act_grad = rstd[at, 0:1] * (
                grad[at, at_cols] * gain[:, at_cols]
                - sums[at, 0:1]
                - unit[at, at_cols].astype(F32) * sums[at, 1:2]
            )
            unit[at, at_cols] = (act_grad * slope[at, at_cols].astype(F32)).astype(BF)

        token_tiles(body)

    for k in range(REDUCE_CHUNKS):
        second_pass(k)
    store = pltpu.make_async_copy(unit, up_low_out, store_sem.at[0])
    store.start()
    reducer.tick(1)
    for item in up_loads:
        item.wait()

    def term(block, row, tile):
        return dot_f32(unit[pl.ds(block * own + row, tile), :], weight[...], 1, 1)

    owner = OwnerSum(wire, own, slope, grad, sum_refs)
    owner.first(term)
    owner.second(term)
    owner.third()
    for at in range(2, reducer.ticks()):
        reducer.tick(at)
    owner.last()
    result = pltpu.make_async_copy(grad.at[pl.ds(0, own), :], sum_out, store_sem.at[1])
    result.start()
    reducer.close()
    store.wait()
    result.wait()


def ffn_back(back, back_t, mid, down, up, unit, slope, gain, rstd):
    tokens, width = mid.shape
    own = tokens // SHARE
    cols = width // REDUCE_CHUNKS
    lanes = 128
    any_spec = pl.BlockSpec(memory_space=pl.ANY)
    vmem = pl.BlockSpec(memory_space=pltpu.VMEM)
    pieces = len(down)
    plan = Reducer.plan(REDUCE_CHUNKS, False, True)
    carry = Reducer.carry_shapes(cols)

    def kernel(back, back_t, mid, *refs):
        down, up, refs = refs[:pieces], refs[pieces : 2 * pieces], refs[2 * pieces :]
        ffn_back_kernel(own, back, back_t, mid, down, up, *refs)

    return pl.pallas_call(
        kernel,
        in_specs=[any_spec] * (5 + 2 * pieces) + [vmem] * 2,
        out_specs=[any_spec, any_spec, vmem, any_spec] + [any_spec] * len(carry),
        out_shape=[
            Reducer.out_shape(plan, cols),
            jax.ShapeDtypeStruct((tokens, width), BF),
            jax.ShapeDtypeStruct((8, width), F32),
            jax.ShapeDtypeStruct((own, D), F32),
        ]
        + carry,
        scratch_shapes=Reducer.scratch(plan, cols)
        + OwnerSum.scratch(own)
        + [
            pltpu.VMEM((tokens, D), BF),
            pltpu.VMEM((D, tokens), BF),
            pltpu.VMEM((tokens, width), BF),
            pltpu.VMEM((D, width), BF),
            pltpu.VMEM((tokens, width), BF),
            pltpu.VMEM((tokens, width), BF),
            pltpu.VMEM((tokens, width), F32),
            pltpu.VMEM((tokens, lanes), F32),
            pltpu.VMEM((SHARE, 8, own), F32),
            pltpu.VMEM((SHARE - 1, SHARE, 8, own), F32),
            pltpu.SemaphoreType.DMA((5 + 2 * pieces,)),
            pltpu.SemaphoreType.DMA((2, SHARE - 1)),
            pltpu.SemaphoreType.DMA((2,)),
        ],
        compiler_params=pltpu.CompilerParams(
            collective_id=1, has_side_effects=True, vmem_limit_bytes=KERNEL_VMEM
        ),
        name="ffn_back",
    )(
        back,
        back_t,
        mid,
        *down,
        *up,
        unit,
        slope,
        gain[None],
        rstd,
    )


def attention_back_kernel(
    head_size, own, left_t, right, q_in, k_in, v_in, mixed, hidden, cap, cq, sq, ck, sk, *refs
):
    width = q_in.shape[1]
    cols = right.shape[1] // REDUCE_CHUNKS
    plan = Reducer.plan(REDUCE_CHUNKS, True, True)
    carried = len(Reducer.carry_shapes(cols))
    carry_in, refs = refs[:carried], refs[carried:]
    out, q_out, k_out, v_out, hidden_out = refs[:5]
    refs = refs[5:]
    carry_out, refs = refs[:carried], refs[carried:]
    wire = Wire()
    count = len(Reducer.scratch(plan, cols))
    reducer_refs, refs = refs[:count], refs[count:]
    left_v, right_v, q_v, k_v, v_v, mixed_cols, hidden_cols, load_sem, turn_sem = refs
    loads = [
        pltpu.make_async_copy(source, target, load_sem.at[k])
        for k, (source, target) in enumerate(
            [(left_t, left_v), (right, right_v), (q_in, q_v), (k_in, k_v), (v_in, v_v)]
        )
    ]
    for item in loads:
        item.start()
    wire.meet()

    def turn(source, target, sems):
        copies = []
        for j in range(1, SHARE):
            to = pl.multiple_of(flipped(wire.member, j) * width, width)
            copies.append(
                wire.copy(
                    source.at[:, pl.ds(to, width)],
                    target.at[pl.ds(j * own, own), :],
                    sems.at[0, j],
                    sems.at[1, j],
                    j,
                )
            )
        here = pl.multiple_of(wire.member * width, width)
        local = pltpu.make_async_copy(
            source.at[:, pl.ds(here, width)], target.at[pl.ds(0, own), :], sems.at[0, 0]
        )
        for item in copies + [local]:
            item.start()
        return copies, local

    def turned(copies, local):
        local.wait()
        for item in copies:
            item.wait_recv()

    mixed_turn = turn(mixed, mixed_cols, turn_sem.at[0])
    reducer = Reducer(
        wire,
        plan,
        [(left_v, right_v, pl.ds(c * cols, cols)) for c in range(REDUCE_CHUNKS)],
        out,
        reducer_refs,
        carry_in,
        carry_out,
    )
    reducer.load()
    loads[0].wait()
    loads[1].wait()
    for at in range(carried):
        reducer.tick(at)
    hidden_turn = turn(hidden, hidden_cols, turn_sem.at[1])
    turned(*mixed_turn)
    for item in loads[2:]:
        item.wait()
    row_count = SHARE * own // L

    def rows(first, last):
        @pl.loop(first, last)
        def _(row):
            at = pl.ds(pl.multiple_of(row * L, L), L)
            got = attention_back_block(
                head_size,
                cap[row],
                q_v[at, :],
                k_v[at, :],
                v_v[at, :],
                mixed_cols[at, :],
                (cq[...], sq[...], ck[...], sk[...]),
            )
            q_v[at, :], k_v[at, :], v_v[at, :] = got

    rows(0, row_count // 2)
    reducer.tick(carried)
    rows(row_count // 2, row_count)
    stores = [
        pltpu.make_async_copy(source, target, load_sem.at[k])
        for k, (source, target) in enumerate([(q_v, q_out), (k_v, k_out), (v_v, v_out)])
    ]
    for item in stores:
        item.start()
    reducer.tick(carried + 1)
    turned(*hidden_turn)
    stores.append(pltpu.make_async_copy(hidden_cols, hidden_out, load_sem.at[3]))
    stores[-1].start()
    for at in range(carried + 2, reducer.ticks()):
        reducer.tick(at)
    reducer.close()
    for item in stores:
        item.wait()
    for item in mixed_turn[0] + hidden_turn[0]:
        item.wait_send()


def attention_back(
    left_t, right, queries, keys, values, mixed, hidden, captions, tables, carry_in
):
    tokens, width = queries.shape
    own = tokens // SHARE
    cols = right.shape[1] // REDUCE_CHUNKS
    any_spec = pl.BlockSpec(memory_space=pl.ANY)
    vmem = pl.BlockSpec(memory_space=pltpu.VMEM)
    part = jax.ShapeDtypeStruct((tokens, width), BF)
    plan = Reducer.plan(REDUCE_CHUNKS, True, True)
    carry = Reducer.carry_shapes(cols)
    return pl.pallas_call(
        partial(attention_back_kernel, D // HEADS, own),
        in_specs=[any_spec] * 5
        + [vmem] * 2
        + [pl.BlockSpec(memory_space=pltpu.SMEM)]
        + [vmem] * 4
        + [any_spec] * len(carry),
        out_specs=[any_spec] * (5 + len(carry)),
        out_shape=[Reducer.out_shape(plan, cols)] + [part] * 4 + carry,
        scratch_shapes=Reducer.scratch(plan, cols)
        + [pltpu.VMEM((D, tokens), BF), pltpu.VMEM(right.shape, BF)]
        + [pltpu.VMEM((tokens, width), BF)] * 5
        + [pltpu.SemaphoreType.DMA((5,)), pltpu.SemaphoreType.DMA((2, 2, SHARE))],
        compiler_params=pltpu.CompilerParams(
            collective_id=2, has_side_effects=True, vmem_limit_bytes=KERNEL_VMEM
        ),
        name="attention_back",
    )(left_t, right, queries, keys, values, mixed, hidden, captions, *tables, *carry_in)


def project_back_kernel(own, normed_t, context_t, *refs):
    parts, refs = refs[:4], refs[4:]
    mid, weights, refs = refs[0], refs[1:4], refs[4:]
    pieces = REDUCE_CHUNKS
    down, refs = refs[:pieces], refs[pieces:]
    width = parts[0].shape[1]
    plan = Reducer.plan(SHARE, True, False)
    carried = len(Reducer.carry_shapes(width))
    carry_in, refs = refs[:carried], refs[carried:]
    out, grad_out, block_out = refs[:3]
    refs = refs[3:]
    wire = Wire()
    count = len(Reducer.scratch(plan, width))
    reducer_refs, refs = refs[:count], refs[count:]
    grad_refs, refs = refs[:3], refs[3:]
    block_refs, refs = refs[:3], refs[3:]
    normed_v, context_v, parts_v, mid_v, weight, send, kept, load_sem, store_sem = refs
    loads = [
        pltpu.make_async_copy(source, target, load_sem.at[k])
        for k, (source, target) in enumerate(
            [
                (context_t, context_v),
                (parts[0], parts_v.at[0]),
                (normed_t, normed_v),
                (parts[1], parts_v.at[1]),
                (parts[2], parts_v.at[2]),
                (parts[3], parts_v.at[3]),
                (mid, mid_v),
            ]
            + [(item, weight.at[:, pl.ds(k * width, width)]) for k, item in enumerate(weights)]
        )
    ]
    for item in loads:
        item.start()
    wire.meet()
    every = pl.ds(0, width)
    reducer = Reducer(
        wire,
        plan,
        [(context_v, parts_v.at[0], every)]
        + [(normed_v, parts_v.at[k], every) for k in range(1, 4)],
        out,
        reducer_refs,
        carry_in,
    )
    reducer.load()
    loads[0].wait()
    loads[1].wait()
    reducer.tick(0)
    loads[2].wait()
    loads[3].wait()
    for at in range(1, carried):
        reducer.tick(at)
    for item in loads[4:]:
        item.wait()

    def grad_term(block, row, tile):
        at = pl.ds(block * own + row, tile)
        return sum(
            dot_f32(parts_v[1 + k, at, :], weight[:, pl.ds(k * width, width)], 1, 1)
            for k in range(3)
        )

    grad_sum = OwnerSum(wire, own, send, kept, grad_refs)
    grad_sum.first(grad_term)
    grad_sum.second(grad_term)
    step = mid.shape[1] // pieces
    down_loads = [
        pltpu.make_async_copy(part, weight.at[:, pl.ds(k * step, step)], load_sem.at[10 + k])
        for k, part in enumerate(down)
    ]
    for item in down_loads:
        item.start()
    reducer.tick(carried)
    grad_sum.third()
    for item in down_loads:
        item.wait()
    reducer.tick(carried + 1)
    grad_sum.last()
    grad_store = pltpu.make_async_copy(kept.at[pl.ds(0, own), :], grad_out, store_sem.at[0])
    grad_store.start()

    def block_term(block, row, tile):
        at = pl.ds(block * own + row, tile)
        return dot_f32(mid_v[at, :], weight[...], 1, 1)

    block_sum = OwnerSum(wire, own, send, kept, block_refs)
    block_sum.first(block_term)
    reducer.tick(carried + 2)
    grad_store.wait()
    block_sum.second(block_term)
    block_sum.third()
    for at in range(carried + 3, reducer.ticks()):
        reducer.tick(at)
    block_sum.last()
    block_store = pltpu.make_async_copy(kept.at[pl.ds(0, own), :], block_out, store_sem.at[1])
    block_store.start()
    reducer.close()
    block_store.wait()


def project_back(normed_t, context_t, parts, mid, weights, down, carry_in):
    tokens, width = parts[0].shape
    own = tokens // SHARE
    any_spec = pl.BlockSpec(memory_space=pl.ANY)
    part = jax.ShapeDtypeStruct((own, D), F32)
    plan = Reducer.plan(SHARE, True, False)
    return pl.pallas_call(
        partial(project_back_kernel, own),
        in_specs=[any_spec] * (10 + len(down) + len(carry_in)),
        out_specs=[any_spec] * 3,
        out_shape=[Reducer.out_shape(plan, width), part, part],
        scratch_shapes=Reducer.scratch(plan, width)
        + OwnerSum.scratch(own)
        + OwnerSum.scratch(own)
        + [
            pltpu.VMEM((D, tokens), BF),
            pltpu.VMEM((D, tokens), BF),
            pltpu.VMEM((4, tokens, width), BF),
            pltpu.VMEM(mid.shape, BF),
            pltpu.VMEM((D, mid.shape[1]), BF),
            pltpu.VMEM((3 * own, D), BF),
            pltpu.VMEM((2 * own, D), F32),
            pltpu.SemaphoreType.DMA((10 + len(down),)),
            pltpu.SemaphoreType.DMA((2,)),
        ],
        compiler_params=pltpu.CompilerParams(
            collective_id=3, has_side_effects=True, vmem_limit_bytes=KERNEL_VMEM
        ),
        name="project_back",
    )(normed_t, context_t, *parts, mid, *weights, *down, *carry_in)


def sum_over_devices(wire, total, whole, got, send_sem, recv_sem):
    rows, cols = total.shape
    row, col = 0, 0
    regions = []
    for stage in range(len(got)):
        mask = 1 << stage
        bit = (wire.me // mask) % 2
        regions.append((row, col, rows, cols))
        if rows > 8:
            rows //= 2
            away = (pl.multiple_of(row + (1 - bit) * rows, 8), col)
            row = pl.multiple_of(row + bit * rows, 8)
        else:
            cols //= 2
            away = (row, pl.multiple_of(col + (1 - bit) * cols, 128))
            col = pl.multiple_of(col + bit * cols, 128)
        copy = wire.copy(
            total.at[pl.ds(away[0], rows), pl.ds(away[1], cols)],
            got[stage],
            send_sem.at[0, stage],
            recv_sem.at[0, stage],
            mask,
        )
        copy.start()
        copy.wait()
        total[pl.ds(row, rows), pl.ds(col, cols)] += got[stage][...]
    whole[pl.ds(row, rows), pl.ds(col, cols)] = total[pl.ds(row, rows), pl.ds(col, cols)]
    for stage in reversed(range(len(got))):
        part = whole.at[pl.ds(row, rows), pl.ds(col, cols)]
        copy = wire.copy(part, part, send_sem.at[1, stage], recv_sem.at[1, stage], 1 << stage)
        copy.start()
        copy.wait()
        row, col, rows, cols = regions[stage]


WIDE = FF // D
SUM_COLS, SUM_WEIGHTED = 0, 2 * WIDE + 4
SUM_NORMS = 2 * SUM_WEIGHTED
SUM_MOMENTS = SUM_NORMS + 2 * WIDE + 6
SUM_SCALARS = SUM_MOMENTS + 2 * WIDE + 6
SUM_ROWS = 64


def update_matrices(step, width, places):
    matrices = []
    for index in range(2):
        pieces = [
            (index * WIDE + t, c * step, t * D + c * step, t, places[index][c])
            for t in range(SHARE)
            for c in range(REDUCE_CHUNKS)
        ]
        matrices.append((index, FF, pieces, step))
    for j in range(4):
        pieces = [(2 * WIDE + j, t * width, t * width, t, places[2][j]) for t in range(SHARE)]
        matrices.append((2 + j, D, pieces, width))
    return matrices


def matrix_cols(refs, index, col, size):
    if index < 2:
        return refs[index][:, pl.ds(col, size)]
    return refs[2][:, index - 2, pl.ds(col, size)]


def put_matrix_cols(refs, index, col, size, value):
    if index < 2:
        refs[index][:, pl.ds(col, size)] = value
    else:
        refs[2][:, index - 2, pl.ds(col, size)] = value


def update_sums_kernel(
    places, sources, up_old, down_old, attn_old, row_old, wide_terms, small_terms, moments,
    vector_squares, *refs
):
    row_new, whole, total = refs[:3]
    got, send_sem, recv_sem = refs[3:-2], refs[-2], refs[-1]
    wire = Wire()
    barrier = pltpu.get_barrier_semaphore()
    for stage in range(len(got)):
        pl.semaphore_signal(
            barrier, inc=1, device_id=(flipped(wire.me, 1 << stage),), device_id_type=MESH
        )
    width = sources[0].shape[3]
    old = (up_old, down_old, attn_old)

    def piece_of(member, place):
        return sources[place[0]][flipped(wire.member, member), place[1]].astype(F32)

    total[...] = jnp.zeros_like(total)
    lane = lax.broadcasted_iota(jnp.int32, (1, 128), 1)
    scalars = vector_squares[0:1, :]
    row_lane = lax.broadcasted_iota(jnp.int32, row_new.shape, 1)
    row_all = jnp.zeros(row_new.shape, F32)
    for index, size, pieces, tile in update_matrices(width, width, places):
        row_sum = jnp.zeros((row_new.shape[0], 1), F32)
        square = jnp.zeros((1, 1), F32)
        for at, sum_col, col, member, place in pieces:
            value = piece_of(member, place)
            squares = value * value
            row_sum += jnp.sum(squares, axis=1, keepdims=True)
            total[SUM_COLS + at : SUM_COLS + at + 1, sum_col : sum_col + tile] = jnp.sum(
                squares, axis=0, keepdims=True
            )
            weight = matrix_cols(old, index, col, tile)
            square += jnp.sum(weight * weight, keepdims=True)
        moment = DECAY_RATE * row_old[:, index : index + 1] + (1.0 - DECAY_RATE) * (
            row_sum * (1.0 / size) + EPS_SQUARE
        )
        row_all = jnp.where(row_lane == index, moment, row_all)
        inverse = 1.0 / moment
        for at, sum_col, col, member, place in pieces:
            value = piece_of(member, place)
            total[SUM_WEIGHTED + at : SUM_WEIGHTED + at + 1, sum_col : sum_col + tile] = jnp.sum(
                value * value * inverse, axis=0, keepdims=True
            )
        scalars = jnp.where(lane == index, jnp.sum(moment, keepdims=True), scalars)
        scalars = jnp.where(lane == 6 + index, square, scalars)
    row_new[...] = row_all
    for r in range(2):
        for t in range(SHARE):
            at = SUM_NORMS + r * WIDE + t
            total[at : at + 1, :] = jnp.where(wire.member == t, wide_terms[r : r + 1, :], 0.0)
    total[SUM_NORMS + 2 * WIDE : SUM_MOMENTS, :] = small_terms[...]
    total[SUM_MOMENTS:SUM_SCALARS, :] = moments[...]
    total[SUM_SCALARS : SUM_SCALARS + 1, 0:128] = scalars

    pl.semaphore_wait(barrier, len(got))
    sum_over_devices(wire, total, whole, got, send_sem, recv_sem)


def update_kernel(
    places, sources, up_old, down_old, attn_old, row_new, col_old, whole, up_grad, down_grad,
    attn_grad, up_new, down_new, attn_new, up_copy, down_copy, attn_copy, col_new, vectors, scale
):
    mine = lax.axis_index("dp") % SHARE
    width = sources[0].shape[3]
    old, grad = (up_old, down_old, attn_old), (up_grad, down_grad, attn_grad)
    new, low = (up_new, down_new, attn_new), (up_copy, down_copy, attn_copy)
    columns = DECAY_RATE * col_old[...] + (1.0 - DECAY_RATE) * (
        whole[SUM_COLS:SUM_WEIGHTED, :] * (1.0 / D) + EPS_SQUARE
    )
    col_new[...] = columns
    scale[...] = lax.rsqrt(columns)
    ratio = whole[SUM_WEIGHTED:SUM_NORMS, :] / columns

    def scalar(index):
        return whole[SUM_SCALARS : SUM_SCALARS + 1, index : index + 1]

    def step_size(square, weight_square, size):
        upd_rms = jnp.sqrt(square * (1.0 / size))
        weight_rms = jnp.sqrt(weight_square * (1.0 / size))
        return (
            LEARN_RATE
            * jnp.maximum(EPS_SCALE, weight_rms)
            / jnp.maximum(1.0, upd_rms * (1.0 / CLIP_LEVEL))
        )

    for index, size, pieces, tile in update_matrices(width, width, places):
        first, last = pieces[0][0], pieces[-1][0] + 1
        row_mean = scalar(index) * (1.0 / D)
        square = row_mean * jnp.sum(ratio[first:last, :], keepdims=True)
        factor = step_size(square, scalar(6 + index), D * size)
        row_scale = lax.rsqrt(row_new[:, index : index + 1] / row_mean) * factor
        for at, sum_col, col, member, place in pieces:
            value = sources[place[0]][flipped(mine, member), place[1]].astype(F32)
            put_matrix_cols(grad, index, col, tile, value)
            value = matrix_cols(old, index, col, tile) - value * row_scale * scale[
                at : at + 1, sum_col : sum_col + tile
            ]
            put_matrix_cols(new, index, col, tile, value)
            put_matrix_cols(low, index, col, tile, value.astype(BF))

    count = 2 * WIDE + 6
    grads = whole[SUM_NORMS:SUM_MOMENTS, :]
    moment = DECAY_RATE * whole[SUM_MOMENTS:SUM_SCALARS, :] + (1.0 - DECAY_RATE) * (
        grads * grads + EPS_SQUARE
    )
    scaled = grads * lax.rsqrt(moment)
    vectors[0:count, :] = grads
    vectors[count : 2 * count, :] = moment
    spans = [(r * WIDE, (r + 1) * WIDE) for r in range(2)]
    spans += [(2 * WIDE + r, 2 * WIDE + r + 1) for r in range(6)]
    for r, (first, last) in enumerate(spans):
        part = scaled[first:last, :]
        size = (last - first) * D
        factor = step_size(jnp.sum(part * part, keepdims=True), scalar(12 + r), size)
        vectors[2 * count + first : 2 * count + last, :] = part * factor


def update(places, sources, weights, row_old, col_old, wide_terms, small_terms, moments, squares):
    count = lax.axis_size("dp")
    stages = count.bit_length() - 1
    rows = weights[0].shape[0]
    parts = []
    size = [SUM_ROWS, D]
    for _ in range(stages):
        size[0 if size[0] > 8 else 1] //= 2
        parts.append(pltpu.VMEM(tuple(size), F32))
    vmem = pl.BlockSpec(memory_space=pltpu.VMEM)
    number = len(sources)
    whole_shape = jax.ShapeDtypeStruct((SUM_ROWS, D), F32)

    def sums_kernel(*refs):
        update_sums_kernel(places, refs[:number], *refs[number:])

    def kernel(*refs):
        update_kernel(places, refs[:number], *refs[number:])

    row_new, whole = pl.pallas_call(
        sums_kernel,
        in_specs=[vmem] * (number + 8),
        out_specs=[vmem] * 2,
        out_shape=[jax.ShapeDtypeStruct((rows, 128), F32), whole_shape],
        scratch_shapes=[pltpu.VMEM((SUM_ROWS, D), F32)]
        + parts
        + [pltpu.SemaphoreType.DMA((2, stages)), pltpu.SemaphoreType.DMA((2, stages))],
        compiler_params=pltpu.CompilerParams(
            collective_id=4, has_side_effects=True, vmem_limit_bytes=KERNEL_VMEM
        ),
        name="update_sums",
    )(*sources, *weights, row_old, wide_terms, small_terms, moments, squares)
    shapes = [jax.ShapeDtypeStruct(item.shape, kind) for kind in (F32, F32, BF) for item in weights]
    shapes += [
        jax.ShapeDtypeStruct((SUM_WEIGHTED, D), F32),
        jax.ShapeDtypeStruct((3 * (2 * WIDE + 6), D), F32),
    ]
    results = pl.pallas_call(
        kernel,
        in_specs=[vmem] * (number + 6),
        out_specs=[vmem] * len(shapes),
        out_shape=shapes,
        scratch_shapes=[pltpu.VMEM((SUM_WEIGHTED, D), F32)],
        compiler_params=pltpu.CompilerParams(vmem_limit_bytes=KERNEL_VMEM),
        name="update",
    )(*sources, *weights, row_new, col_old, whole)
    return row_new, results


class Share:
    def __init__(self, wire, source, target, sems):
        self.wire, self.source, self.target, self.sems = wire, source, target, sems

    def copies(self):
        parts = [
            (self.source, self.target.at[2], 2),
            (self.source, self.target.at[1], 1),
            (self.target.at[2], self.target.at[3], 1),
        ]
        return [
            self.wire.copy(source, target, self.sems.at[0, k], self.sems.at[1, k], mask)
            for k, (source, target, mask) in enumerate(parts)
        ]

    def start(self):
        far, near, unused = self.copies()
        far.start()
        near.start()

    def forward(self):
        far, unused, last = self.copies()
        far.wait_recv()
        last.start()

    def done(self):
        unused, near, last = self.copies()
        near.wait_recv()
        last.wait_recv()

    def close(self):
        for item in self.copies():
            item.wait_send()


def normalized(value):
    center = value - jnp.mean(value, axis=-1, keepdims=True)
    return center * lax.rsqrt(jnp.mean(center * center, axis=-1, keepdims=True) + EPS_NORM)


def attention_block(head_size, caption, q_low, k_low, v_low):
    mixed = []
    for head in range(q_low.shape[1] // head_size):
        at = slice(head * head_size, (head + 1) * head_size)
        probs = masked_probs(q_low[:, at], k_low[:, at], caption, head_size).astype(BF)
        mixed.append(dot_f32(probs, v_low[:, at], 1, 0))
    return jnp.concatenate(mixed, axis=1).astype(BF)


def vector_rows(count):
    wide = FF // count
    return max(1, wide // 128), min(wide, 128)


GATHERED = 4 + 2 * REDUCE_CHUNKS


def forward_kernel(
    own, tokens, cotangent, live, attn_in, up_in, down_in, vectors, cq, sq, ck, sk, *refs
):
    gathered, refs = refs[:GATHERED], refs[GATHERED:]
    (
        out_full, normed_out, back_out, back_t_out, context_out, ffn_out, mid_out, unit_out,
        slope_out, q_out, k_out, v_out, mixed_out, hidden_out, small, wide, rstd_out, captions,
    ) = refs[:18]
    (
        attn_v, up_v, down_v, pieces, normed, back_v, weight, q_v, k_v, v_v, mixed, mixed_own,
        context, ffn, act, unit, mid, slope, norms, sums, stat_send, stat_recv, load_sem,
        piece_sems, gather_sems, norm_sems, share_sems, turn_sems, stat_sems, weight_sem, store_sem,
        turned, turned_sem,
    ) = refs[18:]
    wire = Wire()
    count = lax.axis_size("dp")
    member, group = wire.member, wire.me // SHARE
    low, high = group % 2, group // 2
    masks = group_masks()
    width = q_v.shape[1]
    step = width
    ff_width = act.shape[1]
    local = attn_v.shape[0]
    head_size = D // HEADS
    rows_each = L

    loads = [
        pltpu.make_async_copy(source, target, load_sem.at[k])
        for k, (source, target) in enumerate(
            [(attn_in, attn_v), (up_in, up_v), (down_in, down_v)]
        )
    ]
    for item in loads:
        item.start()
    norms[wire.me] = vectors[...].astype(BF).astype(F32)
    chain = count == 8 * SHARE
    wire.meet([6 * SHARE] if chain else [])

    def piece_copies(chunk):
        place = gathered[chunk].at[high, low, pl.ds(pl.multiple_of(member * local, local), local), :]
        here = pltpu.make_async_copy(pieces.at[0, chunk], place, piece_sems.at[0, chunk, 0])
        away = [
            wire.copy(
                pieces.at[j, chunk], place, piece_sems.at[0, chunk, j], piece_sems.at[1, chunk, j], j
            )
            for j in range(1, SHARE)
        ]
        return here, away

    def send_pieces(chunk):
        for j in range(SHARE):
            to = flipped(member, j)
            if chunk < 4:
                value = attn_v[:, chunk, pl.ds(pl.multiple_of(to * width, width), width)]
            else:
                source = up_v if chunk < 4 + REDUCE_CHUNKS else down_v
                k = (chunk - 4) % REDUCE_CHUNKS
                value = source[:, pl.ds(pl.multiple_of(to * ff_width + k * step, step), step)]
            pieces[j, chunk] = value.astype(BF)
        here, away = piece_copies(chunk)
        here.start()
        for item in away:
            item.start()

    always = None
    nearby = flipped(wire.me, 1)

    def doubling(chunk):
        buf = gathered[chunk]
        route = []
        for stage, mask in enumerate(masks):
            if stage == len(masks) - 1:
                part = buf.at[:, low]
            else:
                size = 1 << stage
                part = buf.at[pl.ds((high // size) * size, size), low]
            to = flipped(wire.me, mask)
            route.append(([(always, part, to, stage)], [(always, part, stage)]))
        return route

    def chained(chunk):
        buf = gathered[chunk]
        y_first = chunk % 6 == 5
        neighbour = 2 * SHARE

        def part(z):
            return buf.at[z] if y_first else buf.at[z, low]

        hops = []
        for hop in range(1, 4):
            hops.append(
                (
                    [
                        (
                            jnp.logical_and(high >= hop - 1, high < 3),
                            part(high - hop + 1),
                            wire.me + neighbour,
                            hop - 1,
                        ),
                        (
                            jnp.logical_and(high <= 4 - hop, high > 0),
                            part(high + hop - 1),
                            wire.me - neighbour,
                            hop + 2,
                        ),
                    ],
                    [
                        (high >= hop, part(high - hop), hop - 1),
                        (high <= 3 - hop, part(high + hop), hop + 2),
                    ],
                )
            )
        own_part = buf.at[high, low] if y_first else buf.at[:, low]
        across = ([(always, own_part, flipped(wire.me, SHARE), 6)], [(always, own_part, 6)])
        return [across] + hops if y_first else hops + [across]

    route_of = chained if chain else doubling
    stages = 4 if chain else len(masks)
    ahead = stages + 1 if chain else stages

    def where(condition, action):
        if condition is always:
            action()
        else:
            pl.when(condition)(action)

    def moved(chunk, part, to, index):
        return pltpu.make_async_remote_copy(
            src_ref=part,
            dst_ref=part,
            send_sem=gather_sems.at[0, chunk, index],
            recv_sem=gather_sems.at[1, chunk, index],
            device_id=(to,),
            device_id_type=MESH,
        )

    def expect(chunk, stage):
        for condition, part, index in route_of(chunk)[stage][1]:
            where(condition, lambda: moved(chunk, part, nearby, index).wait_recv())

    def launch(chunk, stage):
        if not 0 <= chunk < GATHERED:
            return
        if stage == 0:
            here, away = piece_copies(chunk)
            here.wait()
            for item in away:
                item.wait_recv()
        else:
            expect(chunk, stage - 1)
        for condition, part, to, index in route_of(chunk)[stage][0]:
            where(condition, lambda: moved(chunk, part, to, index).start())

    def advance(at):
        for stage in range(stages):
            launch(at - stage, stage)

    def tick(chunk):
        advance(chunk + ahead)
        expect(chunk, stages - 1)

    norm_stages = count.bit_length() - 1

    def norm_copy(stage):
        size = 1 << stage
        part = norms.at[pl.ds((wire.me // size) * size, size)]
        return wire.copy(part, part, norm_sems.at[0, stage], norm_sems.at[1, stage], size)

    norm_copy(0).start()
    loads[0].wait()
    for chunk in range(4):
        send_pieces(chunk)
    for stage in range(1, norm_stages):
        norm_copy(stage - 1).wait_recv()
        norm_copy(stage).start()
        if stage == 2:
            advance(0)
    norm_copy(norm_stages - 1).wait_recv()
    advance(1)
    small_cols = D // count
    join = max(1, 128 // small_cols)
    small[...] = jnp.concatenate(
        [
            jnp.concatenate([norms[p * join + i][0:8, 0:small_cols] for i in range(join)], axis=1)
            for p in range(count // join)
        ],
        axis=1,
    )
    wide[...] = jnp.zeros_like(wide)
    per_row, row_cols = vector_rows(count)
    per_quarter = count // SHARE
    for r in range(2):
        got = [
            norms[member * per_quarter + i][8 + r * per_row + k : 9 + r * per_row + k, 0:row_cols]
            for i in range(per_quarter)
            for k in range(per_row)
        ]
        wide[r : r + 1, :] = jnp.concatenate(got, axis=1)
    row_count = SHARE * own // rows_each
    own_count = own // rows_each
    lane = lax.broadcasted_iota(jnp.int32, (8, 128), 1)
    sub = lax.broadcasted_iota(jnp.int32, (8, 128), 0)
    table = jnp.zeros((8, 128), F32)
    for row in range(row_count):
        j, i = row // own_count, row % own_count
        at = 8 + 2 * per_row
        value = norms[flipped(wire.me, j)][at : at + 1, i : i + 1]
        table = jnp.where((sub == row % 8) & (lane == row // 8), value, table)
    captions[...] = table

    def norm_rows(read, at_gain, write, tile=64):
        def body(row, tile):
            at = pl.ds(row, tile)
            scaled = normalized(read(at)) * small[at_gain : at_gain + 1, :]
            write(at, scaled + small[at_gain + 1 : at_gain + 2, :])

        row_tiles(own, body, tile)

    def write_normed(at, value):
        normed[0, at, :] = value.astype(BF)

    norm_rows(lambda at: tokens[at, :].astype(F32), 0, write_normed)
    share_normed = Share(wire, normed.at[0], normed, share_sems.at[0])
    share_normed.start()
    advance(2)

    def back_rows(row, tile):
        at = pl.ds(row, tile)
        back_v[at, :] = (cotangent[at, :].astype(F32) * live[at, 0:1]).astype(BF)

    row_tiles(own, back_rows, 64)
    back_here = pltpu.make_async_copy(back_v, mid.at[0], store_sem.at[0])
    back_here.start()

    def store_turned(source, target):
        tile = turned.shape[1]

        def copy(row, slot):
            return pltpu.make_async_copy(
                turned.at[slot], target.at[pl.ds(row, tile), :], turned_sem.at[slot]
            )

        @pl.loop(0, D // tile // 2)
        def _(pair):
            for slot in range(2):
                row = pl.multiple_of((2 * pair + slot) * tile, tile)

                @pl.when(pair > 0)
                def _():
                    copy(row, slot).wait()

                for j in range(SHARE):
                    turned[slot, :, pl.ds(j * own, own)] = source[j, :, pl.ds(row, tile)].T
                copy(row, slot).start()

        for slot in range(2):
            copy(0, slot).wait()

    for item in loads[1:]:
        item.wait()
    for chunk in range(4, 4 + REDUCE_CHUNKS):
        send_pieces(chunk)
    for at in range(3, ahead):
        advance(at)
    share_normed.forward()
    share_back = Share(wire, back_v, mid, share_sems.at[1])
    share_back.start()
    for chunk in range(4 + REDUCE_CHUNKS, GATHERED):
        send_pieces(chunk)

    def fetch(source, slot):
        return pltpu.make_async_copy(source, weight.at[slot], weight_sem.at[slot])

    def block_of(chunk):
        return gathered[chunk]

    def weights_of(slot):
        return weight[slot].reshape(D, step)

    def project(slot, target, cosine, sine):
        @pl.loop(0, SHARE)
        def _(j):
            value = dot_f32(normed[j], weights_of(slot), 1, 0)
            for i in range(own_count):
                part = value[i * rows_each : (i + 1) * rows_each]
                if cosine is not None:
                    part = part * cosine[...] + quarter_turn(part) * sine[...]
                at = pl.ds(pl.multiple_of(j * own + i * rows_each, rows_each), rows_each)
                target[at, :] = part.astype(BF)

    tick(0)
    fetch(block_of(0), 0).start()
    share_normed.done()
    fetch(block_of(0), 0).wait()
    project(0, q_v, cq, sq)
    store_turned(normed, normed_out)
    tick(1)
    fetch(block_of(1), 1).start()
    fetch(block_of(1), 1).wait()
    project(1, k_v, ck, sk)
    share_back.forward()
    tick(2)
    fetch(block_of(2), 0).start()
    fetch(block_of(2), 0).wait()
    project(0, v_v, None, None)

    def attend_loop(first, last):
        @pl.loop(first, last)
        def _(row):
            at = pl.ds(pl.multiple_of(row * rows_each, rows_each), rows_each)
            caption = captions[pl.ds(row, 1), 0:1]
            mixed[at, :] = attention_block(
                head_size, caption, q_v[at, :], k_v[at, :], v_v[at, :]
            )

    attend_loop(0, row_count // 2)
    tick(3)

    def out_copies():
        mine = out_full.at[member]
        far = flipped(member, 2)
        parts = [
            (gathered[3], mine, 2),
            (gathered[3], mine, 1),
            (out_full.at[far], out_full.at[far], 1),
        ]
        return [
            wire.copy(source, target, share_sems.at[4, 0, k], share_sems.at[4, 1, k], mask)
            for k, (source, target, mask) in enumerate(parts)
        ]

    out_here = pltpu.make_async_copy(gathered[3], out_full.at[member], store_sem.at[2])
    out_here.start()
    out_moves = out_copies()
    out_moves[0].start()
    out_moves[1].start()
    attend_loop(row_count // 2, row_count)

    def mixed_copies():
        here = pltpu.make_async_copy(
            mixed.at[pl.ds(0, own), :], mixed_own.at[member], turn_sems.at[0, 0]
        )
        away = [
            wire.copy(
                mixed.at[pl.ds(j * own, own), :],
                mixed_own.at[member],
                turn_sems.at[0, j],
                turn_sems.at[1, j],
                j,
            )
            for j in range(1, SHARE)
        ]
        return here, away

    mixed_here, mixed_away = mixed_copies()
    mixed_here.start()
    for item in mixed_away:
        item.start()
    stores = [
        pltpu.make_async_copy(source, target, store_sem.at[3 + k])
        for k, (source, target) in enumerate([(q_v, q_out), (k_v, k_out), (v_v, v_out)])
    ]
    for item in stores:
        item.start()
    tick(4)
    mixed_here.wait()
    for item in mixed_away:
        item.wait_recv()

    def write_context(at, value):
        context[at, :] = value.astype(BF)

    norm_rows(
        lambda at: jnp.concatenate(
            [mixed_own[t, at, :].astype(F32) for t in range(SHARE)], axis=1
        ),
        2,
        write_context,
    )
    stores.append(pltpu.make_async_copy(mixed_own, mixed_out, store_sem.at[6]))
    stores[-1].start()
    context_here = pltpu.make_async_copy(context, unit.at[0], store_sem.at[7])
    context_here.start()
    back_here.wait()
    share_back.done()
    back_store = pltpu.make_async_copy(mid, back_out, store_sem.at[1])
    back_store.start()
    store_turned(mid, back_t_out)
    tick(5)
    out_moves[0].wait_recv()
    out_moves[2].start()
    share_context = Share(wire, context, unit, share_sems.at[3])
    share_context.start()
    tick(6)
    out_here.wait()
    out_moves[1].wait_recv()
    out_moves[2].wait_recv()
    fetch(out_full.at[0], 0).start()
    for t in range(SHARE):
        fetch(out_full.at[t], t % 2).wait()
        if t + 1 < SHARE:
            fetch(out_full.at[t + 1], (t + 1) % 2).start()
        at = pl.ds(t * width, width)
        hidden_out[:, at] = tokens[:, at].astype(F32) + dot_f32(
            context[...], weights_of(t % 2), 1, 0
        )

    def write_ffn(at, value):
        ffn[0, at, :] = value.astype(BF)

    norm_rows(lambda at: hidden_out[at, :], 4, write_ffn)
    share_ffn = Share(wire, ffn.at[0], ffn, share_sems.at[2])
    share_ffn.start()
    share_context.forward()
    context_here.wait()
    share_context.done()
    store_turned(unit, context_out)
    tick(7)
    share_ffn.forward()
    fetch(block_of(4), 0).start()
    share_ffn.done()
    sums[...] = jnp.zeros_like(sums)

    def widen(k):
        slot = k % 2
        fetch(block_of(4 + k), slot).wait()
        if k + 1 < REDUCE_CHUNKS:
            fetch(block_of(5 + k), 1 - slot).start()
        at_cols = pl.ds(k * step, step)

        @pl.loop(0, SHARE)
        def _(j):
            at = pl.ds(pl.multiple_of(j * own, own), own)
            value = dot_f32(ffn[j], weights_of(slot), 1, 0)
            cdf, density = gelu_parts(value)
            active = value * cdf
            act[at, at_cols] = active
            slope[at, at_cols] = (cdf + value * density).astype(BF)
            sums[at, :] += jnp.broadcast_to(
                jnp.sum(active, axis=1, keepdims=True), (own, sums.shape[1])
            )

    widen(0)
    widen(1)
    tick(8)
    widen(2)
    widen(3)

    def spread_body(row, tile):
        at = pl.ds(row, tile)
        mean = sums[at, 0:1] * (1.0 / ff_width)
        square = jnp.zeros((tile, 1), F32)
        for k in range(REDUCE_CHUNKS):
            center = act[at, pl.ds(k * step, step)] - mean
            square += jnp.sum(center * center, axis=1, keepdims=True)
        lane = lax.broadcasted_iota(jnp.int32, (tile, sums.shape[1]), 1)
        sums[at, :] = jnp.where(lane == 0, mean, square)

    row_tiles(SHARE * own, spread_body)
    for j in range(SHARE):
        stat_send[j] = sums[pl.ds(j * own, own), :].T[0:8, :]
    stats = [
        wire.copy(
            stat_send, stat_recv.at[j - 1], stat_sems.at[0, j - 1], stat_sems.at[1, j - 1], j
        )
        for j in range(1, SHARE)
    ]
    for item in stats:
        item.start()
    stores.append(pltpu.make_async_copy(slope, slope_out, store_sem.at[9]))
    stores[-1].start()
    back_store.wait()
    share_back.close()
    share_context.close()
    tick(9)
    for item in stats:
        item.wait_recv()
    for j in range(SHARE):
        parts = [stat_send[j]] + [stat_recv[k - 1, j ^ k] for k in range(1, SHARE)]
        mean = sum(part[0:1, :] for part in parts) * (1.0 / SHARE)
        square = sum(
            part[1:2, :] + ff_width * (part[0:1, :] - mean) ** 2 for part in parts
        )
        rstd = lax.rsqrt(square * (1.0 / (SHARE * ff_width)) + EPS_NORM)
        sub_all = lax.broadcasted_iota(jnp.int32, (128, own), 0)
        both = jnp.where(sub_all == 0, mean, rstd).T
        sums[pl.ds(j * own, own), :] = both
    rstd_out[...] = jnp.broadcast_to(sums[:, 1:2], rstd_out.shape)

    def finish(k):
        at_cols = pl.ds(k * step, step)

        @pl.loop(0, SHARE)
        def _(j):
            at = pl.ds(pl.multiple_of(j * own, own), own)
            value = (act[at, at_cols] - sums[at, 0:1]) * sums[at, 1:2]
            unit[j, :, at_cols] = value.astype(BF)
            mid[j, :, at_cols] = (value * wide[0:1, at_cols] + wide[1:2, at_cols]).astype(BF)

    finish(0)
    finish(1)
    tick(10)
    finish(2)
    finish(3)
    stores += [
        pltpu.make_async_copy(unit, unit_out, store_sem.at[10]),
        pltpu.make_async_copy(mid, mid_out, store_sem.at[11]),
    ]
    for item in stores[-2:]:
        item.start()
    store_turned(ffn, ffn_out)
    for chunk in range(11, GATHERED):
        tick(chunk)
    for item in stores:
        item.wait()
    for chunk in range(GATHERED):
        for item in piece_copies(chunk)[1]:
            item.wait_send()
        for starts, unused in route_of(chunk):
            for condition, part, to, index in starts:
                where(condition, lambda: moved(chunk, part, to, index).wait_send())
    for stage in range(norm_stages):
        norm_copy(stage).wait_send()
    for item in [share_normed, share_ffn]:
        item.close()
    for item in out_moves + mixed_away + stats:
        item.wait_send()


def forward(tokens, cotangent, live, attn_weight, up_weight, down_weight, vectors, tables):
    count = lax.axis_size("dp")
    own = tokens.shape[0]
    all_tokens = SHARE * own
    width, ff_width = D // SHARE, FF // SHARE
    groups = count // SHARE
    local = D // count
    chunk = (groups // 2, 2, D // groups, width)
    stages = len(group_masks())
    any_spec = pl.BlockSpec(memory_space=pl.ANY)
    vmem = pl.BlockSpec(memory_space=pltpu.VMEM)
    shared = jax.ShapeDtypeStruct((SHARE, own, D), BF)
    across = jax.ShapeDtypeStruct((D, all_tokens), BF)
    wide = jax.ShapeDtypeStruct((SHARE, own, ff_width), BF)
    flat = jax.ShapeDtypeStruct((all_tokens, ff_width), BF)
    part = jax.ShapeDtypeStruct((all_tokens, width), BF)
    norm_stages = count.bit_length() - 1
    return pl.pallas_call(
        partial(forward_kernel, own),
        in_specs=[vmem] * 3 + [any_spec] * 3 + [vmem] * 5,
        out_specs=[any_spec] * (GATHERED + 13) + [vmem] * 5,
        out_shape=[jax.ShapeDtypeStruct(chunk, BF)] * GATHERED
        + [jax.ShapeDtypeStruct((SHARE,) + chunk, BF)]
        + [across, shared, across, across, across]
        + [wide, wide, flat]
        + [part] * 3
        + [
            jax.ShapeDtypeStruct((SHARE, own, width), BF),
            jax.ShapeDtypeStruct((own, D), F32),
            jax.ShapeDtypeStruct((8, D), F32),
            jax.ShapeDtypeStruct((8, ff_width), F32),
            jax.ShapeDtypeStruct((all_tokens, 128), F32),
            jax.ShapeDtypeStruct((8, 128), F32),
        ],
        scratch_shapes=[
            pltpu.VMEM((local, 4, D), F32),
            pltpu.VMEM((local, FF), F32),
            pltpu.VMEM((local, FF), F32),
            pltpu.VMEM((SHARE, GATHERED, local, width), BF),
            pltpu.VMEM((SHARE, own, D), BF),
            pltpu.VMEM((own, D), BF),
            pltpu.VMEM((2,) + chunk, BF),
            pltpu.VMEM((all_tokens, width), BF),
            pltpu.VMEM((all_tokens, width), BF),
            pltpu.VMEM((all_tokens, width), BF),
            pltpu.VMEM((all_tokens, width), BF),
            pltpu.VMEM((SHARE, own, width), BF),
            pltpu.VMEM((own, D), BF),
            pltpu.VMEM((SHARE, own, D), BF),
            pltpu.VMEM((all_tokens, ff_width), F32),
            pltpu.VMEM((SHARE, own, ff_width), BF),
            pltpu.VMEM((SHARE, own, ff_width), BF),
            pltpu.VMEM((all_tokens, ff_width), BF),
            pltpu.VMEM((count, 16, 128), F32),
            pltpu.VMEM((all_tokens, 128), F32),
            pltpu.VMEM((SHARE, 8, own), F32),
            pltpu.VMEM((SHARE - 1, SHARE, 8, own), F32),
            pltpu.SemaphoreType.DMA((3,)),
            pltpu.SemaphoreType.DMA((2, GATHERED, SHARE)),
            pltpu.SemaphoreType.DMA((2, GATHERED, max(stages, 7))),
            pltpu.SemaphoreType.DMA((2, norm_stages)),
            pltpu.SemaphoreType.DMA((5, 2, 3)),
            pltpu.SemaphoreType.DMA((2, SHARE)),
            pltpu.SemaphoreType.DMA((2, SHARE - 1)),
            pltpu.SemaphoreType.DMA((2,)),
            pltpu.SemaphoreType.DMA((12,)),
            pltpu.VMEM((2, 256, all_tokens), BF),
            pltpu.SemaphoreType.DMA((2,)),
        ],
        compiler_params=pltpu.CompilerParams(
            collective_id=5, has_side_effects=True, vmem_limit_bytes=KERNEL_VMEM
        ),
        name="forward",
    )(tokens, cotangent, live, attn_weight, up_weight, down_weight, vectors, *tables)


def gelu_parts(value):
    cdf = 0.5 * (1.0 + lax.erf(value * math.sqrt(0.5)))
    density = jnp.exp(-0.5 * value * value) * (1.0 / math.sqrt(2.0 * math.pi))
    return cdf, density


def per_device(
    tokens,
    cotangent,
    caption_len,
    attn_weight,
    up_weight,
    down_weight,
    small_norms,
    wide_norms,
    attn_row,
    attn_col,
    up_row,
    up_col,
    down_row,
    down_col,
    small_moment,
    wide_moment,
):
    count = lax.axis_size("dp")
    me = lax.axis_index("dp")
    head_size = D // HEADS
    width = D // SHARE
    own = tokens.shape[0]
    own_rows = caption_len.shape[0]

    small_width = D // count
    wide_width = FF // count
    per_row, row_cols = vector_rows(count)
    vectors = jnp.concatenate(
        [
            jnp.pad(small_norms, ((0, 2), (0, 128 - small_width))),
            jnp.pad(
                wide_norms.reshape(2 * per_row, row_cols),
                ((0, 0), (0, 128 - row_cols)),
            ),
            jnp.pad(caption_len.astype(F32), (0, 128 - own_rows))[None],
            jnp.zeros((7 - 2 * per_row, 128), F32),
        ],
        axis=0,
    )
    slot_index = jnp.arange(L)
    live_mask = (slot_index[None, :] < IMG + caption_len[:, None]).astype(F32).reshape(own)
    tables = xpos_tables(head_size, width // head_size)
    results = forward(
        tokens,
        cotangent,
        jnp.broadcast_to(live_mask[:, None], (own, 128)),
        attn_weight,
        up_weight,
        down_weight,
        vectors,
        tables,
    )
    full = [item.reshape(D, width) for item in results[:GATHERED]]
    query_full, key_full, value_full = full[:3]
    up_full, down_full = full[4 : 4 + REDUCE_CHUNKS], full[4 + REDUCE_CHUNKS :]
    (
        out_full, normed_turned, back_all, back_turned, context_turned, ffn_turned, ffn_mid, unit,
        slope, queries, keys_low, values_low, mixed_own, hidden, small_vals, wide_own, rstd, captions,
    ) = results[GATHERED:]
    all_tokens = SHARE * own
    out_full = out_full.reshape(SHARE, D, width)
    back_all = back_all.reshape(all_tokens, D)
    ffn_mid, unit = ffn_mid.reshape(all_tokens, -1), unit.reshape(all_tokens, -1)
    captions = captions[:, 0].astype(jnp.int32)
    inputs = tokens.astype(F32)
    back_out = cotangent.astype(F32) * live_mask[:, None]
    unit_one, rstd_one = norm_stats(inputs)
    attn_mixed = jnp.concatenate([mixed_own[t] for t in range(SHARE)], axis=1).astype(F32)
    unit_two, rstd_two = norm_stats(attn_mixed)
    unit_three, rstd_three = norm_stats(hidden)

    down_rows, up_grad_low, wide_terms, ffn_in_grad, *carry = ffn_back(
        back_all, back_turned, ffn_mid, down_full, up_full, unit, slope, wide_own[0], rstd
    )
    hidden_part, gain_three, bias_three = norm_back(unit_three, rstd_three, small_vals[4], ffn_in_grad)
    hidden_grad = back_out + hidden_part
    hidden_low = hidden_grad.astype(BF)

    context_grad = sum(
        dot_f32(hidden_low[:, t * width : (t + 1) * width], out_full[t], 1, 1)
        for t in range(SHARE)
    )
    mixed_grad, gain_two, bias_two = norm_back(unit_two, rstd_two, small_vals[2], context_grad)

    up_rows, grad_q, grad_k, grad_v, hidden_cols, *carry = attention_back(
        ffn_turned,
        up_grad_low,
        queries,
        keys_low,
        values_low,
        mixed_grad.astype(BF),
        hidden_low,
        captions,
        tables,
        carry,
    )
    attn_rows_out, normed_grad, block_sum = project_back(
        normed_turned,
        context_turned,
        [hidden_cols, grad_q, grad_k, grad_v],
        ffn_mid,
        [query_full, key_full, value_full],
        down_full,
        carry,
    )
    block_out = (hidden + block_sum).astype(BF)
    input_part, gain_one, bias_one = norm_back(unit_one, rstd_one, small_vals[0], normed_grad)
    input_grad = hidden_grad + input_part

    def spread_columns(value, whole):
        return lax.dynamic_update_slice(
            jnp.zeros((value.shape[0], whole), F32), value, (0, me * value.shape[1])
        ).reshape(-1, D)

    moments = jnp.concatenate(
        [spread_columns(wide_moment, FF), spread_columns(small_moment, D)], axis=0
    )
    vector_squares = jnp.pad(
        jnp.concatenate([jnp.sum(item * item, axis=1) for item in (wide_norms, small_norms)]),
        (12, 128 - 20),
    )[None]
    row_old = jnp.pad(
        jnp.stack([up_row, down_row] + [attn_row[j] for j in range(4)], axis=1), ((0, 0), (0, 122))
    )
    col_old = jnp.concatenate([up_col.reshape(-1, D), down_col.reshape(-1, D), attn_col], axis=0)
    sources = [down_rows, up_rows, attn_rows_out]
    finished = [(k, c) for k, item in enumerate(sources) for c in range(item.shape[1])]
    down_places = finished[:REDUCE_CHUNKS]
    up_places = finished[REDUCE_CHUNKS : 2 * REDUCE_CHUNKS]
    attn_places = [finished[2 * REDUCE_CHUNKS + c] for c in (1, 2, 3, 0)]
    row_new, results = update(
        [up_places, down_places, attn_places],
        sources,
        [up_weight, down_weight, attn_weight],
        row_old,
        col_old,
        wide_terms,
        jnp.stack([gain_one, bias_one, gain_two, bias_two, gain_three, bias_three]),
        moments,
        vector_squares,
    )
    (
        up_grad, down_grad, attn_grad, up_new, down_new, attn_new, up_copy, down_copy, attn_copy,
        col_new, vectors,
    ) = results
    vectors = vectors.reshape(3, -1, D)
    wide_parts = take_block(vectors[:, : 2 * WIDE].reshape(6, FF), me, wide_width, 1)
    wide_parts = wide_parts.reshape(3, 2, wide_width)
    small_parts = take_block(vectors[:, 2 * WIDE :].reshape(18, D), me, small_width, 1)
    small_parts = small_parts.reshape(3, 6, small_width)
    return (
        block_out,
        input_grad,
        attn_grad,
        up_grad,
        down_grad,
        row_new[:, 2:6].T,
        col_new[2 * WIDE :],
        row_new[:, 0],
        col_new[:WIDE].reshape(FF),
        row_new[:, 1],
        col_new[WIDE : 2 * WIDE].reshape(FF),
        attn_new,
        up_new,
        down_new,
        attn_copy,
        up_copy,
        down_copy,
        small_parts[0],
        wide_parts[0],
        small_parts[1],
        wide_parts[1],
        small_norms - small_parts[2],
        wide_norms - wide_parts[2],
    )


def solution(mesh):
    placed = (
        P("dp", None),
        P("dp", None),
        P("dp"),
        P("dp", None, None),
        P("dp", None),
        P("dp", None),
        P(None, "dp"),
        P(None, "dp"),
        P(None, "dp"),
        P(),
        P("dp"),
        P(),
        P("dp"),
        P(),
        P(None, "dp"),
        P(None, "dp"),
    )
    return jax.shard_map(
        per_device,
        mesh=mesh,
        in_specs=placed,
        out_specs=(
            P("dp", None),
            P("dp", None),
            P("dp", None, None),
            P("dp", None),
            P("dp", None),
            P(None, "dp"),
            P(),
            P("dp"),
            P(),
            P("dp"),
            P(),
            P("dp", None, None),
            P("dp", None),
            P("dp", None),
            P("dp", None, None),
            P("dp", None),
            P("dp", None),
            P(None, "dp"),
            P(None, "dp"),
            P(None, "dp"),
            P(None, "dp"),
            P(None, "dp"),
            P(None, "dp"),
        ),
        check_vma=False,
    )
```

```python
from functools import partial
import math

import jax
import jax.numpy as jnp
from jax import lax
from jax.experimental import pallas as pl
from jax.experimental.pallas import tpu as pltpu
from jax.sharding import PartitionSpec as P

D = 2048
FF = 8192
HEADS = 32
L = 128
IMG = 64
SHARE = 4


EPS_NORM = 1e-05
EPS_SQUARE = 1e-30
EPS_SCALE = 0.001
DECAY_RATE = 0.5
CLIP_LEVEL = 0.5
LEARN_RATE = 0.8
SCALE_BASE = 512.0
MASK_FILL = -1e30

BF = jnp.bfloat16
F32 = jnp.float32


def dot_f32(left, right, left_dim, right_dim):
    return lax.dot_general(
        left, right, (((left_dim,), (right_dim,)), ((), ())), preferred_element_type=F32
    )


def group_masks():
    count = lax.axis_size("dp")
    masks = []
    mask = 2 * SHARE
    while mask < count:
        masks.append(mask)
        mask *= 2
    if count > SHARE:
        masks.append(SHARE)
    return masks


def take_block(value, index, width, axis):
    return lax.dynamic_slice_in_dim(value, index * width, width, axis)


def norm_stats(values):
    mean = jnp.mean(values, axis=-1, keepdims=True)
    center = values - mean
    rstd = lax.rsqrt(jnp.mean(center * center, axis=-1, keepdims=True) + EPS_NORM)
    return center * rstd, rstd


def norm_back(unit, rstd, gain, upstream):
    scaled = upstream * gain
    lean = jnp.mean(scaled, axis=-1, keepdims=True)
    slope = jnp.mean(scaled * unit, axis=-1, keepdims=True)
    return (
        rstd * (scaled - lean - unit * slope),
        jnp.sum(upstream * unit, axis=0),
        jnp.sum(upstream, axis=0),
    )


def xpos_tables(head_size, head_count):
    slot_pos = jnp.arange(L, dtype=F32)[:, None]
    pair_idx = jnp.arange(head_size // 2, dtype=F32)[None, :]
    theta = jnp.exp(-(2.0 * pair_idx / head_size) * jnp.log(10000.0))
    angle = slot_pos * theta
    zeta = (2.0 * pair_idx / head_size + 0.4) / 1.4
    power_table = jnp.exp(jnp.log(zeta) * slot_pos / SCALE_BASE)

    def widen(table):
        return jnp.tile(jnp.repeat(table, 2, axis=1), (1, head_count))

    cosine, sine, power = widen(jnp.cos(angle)), widen(jnp.sin(angle)), widen(power_table)
    return cosine * power, sine * power, cosine / power, sine / power


def quarter_turn(values):
    width = values.shape[1]
    lane = lax.broadcasted_iota(jnp.int32, values.shape, 1)
    return jnp.where(
        lane % 2 == 0, -pltpu.roll(values, width - 1, 1), pltpu.roll(values, 1, 1)
    )


def masked_probs(query, key, caption, head_size):
    scores = dot_f32(query, key, 1, 1) * (1.0 / math.sqrt(head_size))
    row = lax.broadcasted_iota(jnp.int32, scores.shape, 0)
    col = lax.broadcasted_iota(jnp.int32, scores.shape, 1)
    scores = jnp.where((col <= row) & (col < IMG + caption), scores, MASK_FILL)
    terms = jnp.exp(scores - jnp.max(scores, axis=-1, keepdims=True))
    return terms / jnp.sum(terms, axis=-1, keepdims=True)


def attention_back_block(head_size, caption, q_low, k_low, v_low, g_low, tables):
    cq, sq, ck, sk = tables
    grads_q, grads_k, grads_v = [], [], []
    for head in range(q_low.shape[1] // head_size):
        at = slice(head * head_size, (head + 1) * head_size)
        probs = masked_probs(q_low[:, at], k_low[:, at], caption, head_size)
        grads_v.append(dot_f32(probs.astype(BF), g_low[:, at], 0, 0))
        prob_grad = dot_f32(g_low[:, at], v_low[:, at], 1, 1)
        score_grad = probs * (prob_grad - jnp.sum(probs * prob_grad, axis=-1, keepdims=True))
        score_low = (score_grad * (1.0 / math.sqrt(head_size))).astype(BF)
        grads_q.append(dot_f32(score_low, k_low[:, at], 1, 0))
        grads_k.append(dot_f32(score_low, q_low[:, at], 0, 0))
    grad_q = jnp.concatenate(grads_q, axis=1)
    grad_k = jnp.concatenate(grads_k, axis=1)
    return (
        (grad_q * cq - quarter_turn(grad_q) * sq).astype(BF),
        (grad_k * ck - quarter_turn(grad_k) * sk).astype(BF),
        jnp.concatenate(grads_v, axis=1).astype(BF),
    )


MESH = pl.DeviceIdType.MESH
KERNEL_VMEM = 62 * 1024 * 1024


def flipped(index, mask):
    bit = 1
    while bit <= mask:
        if mask & bit:
            index = index + bit - 2 * bit * ((index // bit) % 2)
        bit *= 2
    return index


def partner_masks():
    return list(range(1, SHARE)) + group_masks()


class Wire:
    def __init__(self):
        self.me = lax.axis_index("dp")
        self.member = self.me % SHARE

    def meet(self, more=()):
        barrier = pltpu.get_barrier_semaphore()
        masks = partner_masks() + list(more)
        for mask in masks:
            pl.semaphore_signal(
                barrier, inc=1, device_id=(flipped(self.me, mask),), device_id_type=MESH
            )
        pl.semaphore_wait(barrier, len(masks))

    def copy(self, source, target, send_sem, recv_sem, mask):
        return pltpu.make_async_remote_copy(
            src_ref=source,
            dst_ref=target,
            send_sem=send_sem,
            recv_sem=recv_sem,
            device_id=(flipped(self.me, mask),),
            device_id_type=MESH,
        )


def row_tiles(rows, body, tile=256):
    tile = min(tile, rows)

    @pl.loop(0, rows // tile)
    def _(index):
        body(pl.multiple_of(index * tile, tile), tile)


class Reducer:
    @staticmethod
    def plan(count, resumed, stopped):
        stages = len(group_masks())
        carried = min(2, stages - 1)
        resume, stop = [0] * count, [stages] * count
        if resumed:
            resume = list(range(carried, 0, -1)) + [0] * count
        stop = [stages] * len(resume)
        if stopped:
            stop[len(stop) - carried :] = range(carried, 0, -1)
        return resume, stop

    @staticmethod
    def carry_shapes(cols):
        carried = min(2, len(group_masks()) - 1)
        return [jax.ShapeDtypeStruct((D >> at, cols), F32) for at in range(carried, 0, -1)]

    @staticmethod
    def scratch(plan, cols):
        resume, stop = plan
        stages = len(group_masks())
        halves = [D >> (stage + 1) for stage in range(stages)]
        block = D >> stages
        count = len(resume)
        used = [
            sum(first <= stage < last for first, last in zip(resume, stop))
            for stage in range(stages)
        ]
        return (
            [
                pltpu.VMEM((2 if stage else REDUCE_AHEAD, half, cols), BF)
                for stage, half in enumerate(halves)
            ]
            + [pltpu.VMEM((number, half, cols), BF) for number, half in zip(used, halves)]
            + [
                pltpu.VMEM((min(stages, count), D // 2, cols), F32),
                pltpu.VMEM((2, block, cols), BF),
                pltpu.SemaphoreType.DMA((count, stages)),
                pltpu.SemaphoreType.DMA((count, stages)),
                pltpu.SemaphoreType.DMA((count, SHARE)),
                pltpu.SemaphoreType.DMA((count, SHARE)),
                pltpu.SemaphoreType.DMA((count,)),
            ]
        )

    @staticmethod
    def out_shape(plan, cols):
        stages = len(group_masks())
        block = D >> stages
        finished = sum(last == stages for last in plan[1])
        return jax.ShapeDtypeStruct((SHARE, finished, block // SHARE, cols), BF)

    def __init__(self, wire, plan, terms, out, refs, carry_in=(), carry_out=()):
        self.wire, self.out = wire, out
        self.resume, self.stop = plan
        self.count = len(self.resume)
        self.terms = [None] * (self.count - len(terms)) + list(terms)
        self.carry_in, self.carry_out = carry_in, carry_out
        self.masks = group_masks()[::-1]
        self.stages = len(self.masks)
        self.slots = min(self.stages, self.count)
        self.sends, refs = refs[: self.stages], refs[self.stages :]
        self.recvs, refs = refs[: self.stages], refs[self.stages :]
        (
            self.kept, self.done, self.send_sem, self.recv_sem, self.out_send, self.out_recv,
            self.carry_sem,
        ) = refs
        self.block = D >> self.stages
        self.low = (wire.me // SHARE) % 2

    def goes(self, chunk, stage):
        return 0 <= chunk < self.count and self.resume[chunk] <= stage < self.stop[chunk]

    def got(self, chunk, stage):
        first = min(c for c in range(self.count) if self.goes(c, stage))
        return self.recvs[stage].at[chunk - first]

    def finishes(self, chunk):
        return 0 <= chunk < self.count and self.stop[chunk] == self.stages

    def carry_load(self, chunk):
        ref = self.carry_in[chunk]
        return pltpu.make_async_copy(
            ref,
            self.kept.at[chunk % self.slots, pl.ds(0, ref.shape[0]), :],
            self.carry_sem.at[chunk],
        )

    def carry_store(self, chunk):
        ref = self.carry_out[chunk - (self.count - len(self.carry_out))]
        return pltpu.make_async_copy(
            self.kept.at[chunk % self.slots, pl.ds(0, ref.shape[0]), :],
            ref,
            self.carry_sem.at[chunk],
        )

    def load(self):
        for chunk in range(len(self.carry_in)):
            self.carry_load(chunk).start()

    def begin(self):
        first = self.resume.index(0)
        for chunk in range(first, first + REDUCE_AHEAD):
            self.start(chunk)
            if chunk == first:
                for at in range(first):
                    self.tick(at, start=False)
        if first == 0:
            self.keep(0)

    def half_bit(self, stage):
        return (self.wire.me // self.masks[stage]) % 2

    def lhs_row(self, row, tile, low):
        block = row // self.block
        return pl.multiple_of((2 * block + low) * self.block + row % self.block, tile)

    def copy(self, chunk, stage):
        return self.wire.copy(
            self.sends[stage].at[chunk % self.sends[stage].shape[0]],
            self.got(chunk, stage),
            self.send_sem.at[chunk, stage],
            self.recv_sem.at[chunk, stage],
            self.masks[stage],
        )

    def start(self, chunk):
        if not self.goes(chunk, 0):
            return
        slot = chunk % REDUCE_AHEAD
        if self.goes(chunk - REDUCE_AHEAD, 0):
            self.copy(chunk - REDUCE_AHEAD, 0).wait_send()
        lhs, rhs, cols = self.terms[chunk]
        half = D // 2

        def body(row, tile):
            at = pl.ds(self.lhs_row(row, tile, 1 - self.low), tile)
            self.sends[0][slot, pl.ds(row, tile), :] = dot_f32(
                lhs[at, :], rhs[:, cols], 1, 0
            ).astype(BF)

        row_tiles(half, body, self.block)
        self.copy(chunk, 0).start()

    def keep(self, chunk):
        if not self.goes(chunk, 0):
            return
        lhs, rhs, cols = self.terms[chunk]

        def body(row, tile):
            at = pl.ds(self.lhs_row(row, tile, self.low), tile)
            self.kept[chunk % self.slots, pl.ds(row, tile), :] = dot_f32(
                lhs[at, :], rhs[:, cols], 1, 0
            )

        row_tiles(D // 2, body, self.block)

    def step(self, chunk, stage):
        if not 0 <= chunk < self.count or not self.resume[chunk] <= stage <= self.stop[chunk]:
            return
        half = D >> (stage + 1)
        kept = self.kept
        slot = chunk % self.slots
        got = None
        if stage > self.resume[chunk]:
            self.copy(chunk, stage - 1).wait_recv()
            got = self.got(chunk, stage - 1)
        else:
            self.carry_load(chunk).wait()

        def value(at):
            if got is None:
                return kept[slot, at, :]
            return kept[slot, at, :] + got[at, :].astype(F32)

        if stage == self.stop[chunk]:

            def whole(row, tile):
                at = pl.ds(row, tile)
                kept[slot, at, :] = value(at)

            row_tiles(2 * half, whole)
            self.carry_store(chunk).start()
            return
        if self.goes(chunk - 2, stage):
            self.copy(chunk - 2, stage).wait_send()
        send = self.sends[stage]
        bit = self.half_bit(stage)

        def out_half(row, tile):
            at = pl.ds(pl.multiple_of((1 - bit) * half + row, tile), tile)
            send[chunk % 2, pl.ds(row, tile), :] = value(at).astype(BF)

        def own_half(row, tile):
            at = pl.ds(pl.multiple_of(bit * half + row, tile), tile)
            kept[slot, pl.ds(row, tile), :] = value(at)

        row_tiles(half, out_half)
        self.copy(chunk, stage).start()
        row_tiles(half, own_half)

    def place(self, chunk):
        return sum(self.finishes(c) for c in range(chunk))

    def give(self, chunk):
        part = self.block // SHARE
        slot = chunk % 2
        copies = []
        for j in range(1, SHARE):
            to = flipped(self.wire.member, j)
            copies.append(
                self.wire.copy(
                    self.done.at[slot, pl.ds(pl.multiple_of(to * part, part), part), :],
                    self.out.at[j, self.place(chunk)],
                    self.out_send.at[chunk, j],
                    self.out_recv.at[chunk, j],
                    j,
                )
            )
        own = pltpu.make_async_copy(
            self.done.at[slot, pl.ds(pl.multiple_of(self.wire.member * part, part), part), :],
            self.out.at[0, self.place(chunk)],
            self.out_send.at[chunk, 0],
        )
        return own, copies

    def given(self, chunk):
        own, copies = self.give(chunk)
        own.wait()
        for item in copies:
            item.wait_send()

    def finish(self, chunk):
        if not self.finishes(chunk):
            return
        self.copy(chunk, self.stages - 1).wait_recv()
        if self.finishes(chunk - 2):
            self.given(chunk - 2)
        got = self.got(chunk, self.stages - 1)
        slot = chunk % self.slots

        def body(row, tile):
            at = pl.ds(row, tile)
            self.done[chunk % 2, at, :] = (
                self.kept[slot, at, :] + got[at, :].astype(F32)
            ).astype(BF)

        row_tiles(self.block, body)
        own, copies = self.give(chunk)
        own.start()
        for item in copies:
            item.start()

    def tick(self, at, start=True):
        for stage in range(1, self.stages):
            self.step(at - stage + 1, stage)
            if stage == 1 and start:
                self.start(at + REDUCE_AHEAD)
        if self.stages == 1:
            self.start(at + REDUCE_AHEAD)
        self.finish(at - self.stages + 1)
        self.keep(at + 1)

    def ticks(self):
        return self.count + self.stages - 1

    def close(self):
        for stage in range(self.stages):
            slots = self.sends[stage].shape[0]
            for chunk in [c for c in range(self.count) if self.goes(c, stage)][-slots:]:
                self.copy(chunk, stage).wait_send()
        finished = [c for c in range(self.count) if self.finishes(c)]
        for chunk in finished[-2:]:
            self.given(chunk)
        for chunk in finished:
            for item in self.give(chunk)[1]:
                item.wait_recv()
        for chunk in range(self.count - len(self.carry_out), self.count):
            self.carry_store(chunk).wait()


class OwnerSum:
    @staticmethod
    def scratch(own):
        return [
            pltpu.VMEM((2 * own, D), BF),
            pltpu.VMEM((own, D), BF),
            pltpu.SemaphoreType.DMA((4,)),
        ]

    def __init__(self, wire, own, send, kept, refs):
        self.wire, self.own, self.send, self.kept = wire, own, send, kept
        self.near, self.far, self.sems = refs

    def core_copy(self):
        return self.wire.copy(
            self.send.at[pl.ds(0, 2 * self.own), :],
            self.near,
            self.sems.at[0],
            self.sems.at[1],
            1,
        )

    def far_copy(self):
        return self.wire.copy(
            self.send.at[pl.ds(2 * self.own, self.own), :],
            self.far,
            self.sems.at[2],
            self.sems.at[3],
            2,
        )

    def first(self, term):
        for place, block in enumerate((3, 1)):

            def body(row, tile, place=place, block=block):
                self.send[pl.ds(place * self.own + row, tile), :] = term(block, row, tile).astype(BF)

            row_tiles(self.own, body)
        self.core_copy().start()

    def second(self, term):
        for place, block in enumerate((2, 0)):

            def body(row, tile, place=place, block=block):
                self.kept[pl.ds((1 - place) * self.own + row, tile), :] = term(block, row, tile)

            row_tiles(self.own, body)

    def third(self):
        self.core_copy().wait_recv()
        own = self.own

        def far(row, tile):
            self.send[pl.ds(2 * own + row, tile), :] = (
                self.kept[pl.ds(own + row, tile), :] + self.near[pl.ds(row, tile), :].astype(F32)
            ).astype(BF)

        def near(row, tile):
            at = pl.ds(row, tile)
            self.kept[at, :] = self.kept[at, :] + self.near[pl.ds(own + row, tile), :].astype(F32)

        row_tiles(own, far)
        self.far_copy().start()
        row_tiles(own, near)

    def last(self):
        self.far_copy().wait_recv()

        def body(row, tile):
            at = pl.ds(row, tile)
            self.kept[at, :] = self.kept[at, :] + self.far[at, :].astype(F32)

        row_tiles(self.own, body)
        self.core_copy().wait_send()
        self.far_copy().wait_send()


REDUCE_CHUNKS = 4
REDUCE_COLS = 256
REDUCE_AHEAD = 4


def ffn_back_kernel(own, back, back_t, mid, down, up, unit_in, slope_in, gain, rstd, *refs):
    width = mid.shape[1]
    tokens = SHARE * own
    cols = width // REDUCE_CHUNKS
    chunks = width // REDUCE_COLS
    pieces = len(down)
    out, up_low_out, wide_out, sum_out = refs[:4]
    refs = refs[4:]
    plan = Reducer.plan(chunks, False, True)
    carried = len(Reducer.carry_shapes(REDUCE_COLS))
    carry_out, refs = refs[:carried], refs[carried:]
    wire = Wire()
    count = len(Reducer.scratch(plan, REDUCE_COLS))
    reducer_refs, refs = refs[:count], refs[count:]
    sum_refs, refs = refs[:3], refs[3:]
    (
        back_v, back_tv, mid_v, weight, unit, slope, grad, sums, stat_send, stat_recv,
        load_sem, stat_sems, store_sem,
    ) = refs

    def weight_copies(parts, first):
        step = width // pieces
        return [
            pltpu.make_async_copy(
                part, weight.at[:, pl.ds(k * step, step)], load_sem.at[first + k]
            )
            for k, part in enumerate(parts)
        ]

    loads = [
        pltpu.make_async_copy(source, target, load_sem.at[k])
        for k, (source, target) in enumerate(
            [(back_t, back_tv), (mid, mid_v), (back, back_v), (unit_in, unit), (slope_in, slope)]
        )
    ]
    down_loads = weight_copies(down, 5)
    up_loads = weight_copies(up, 5 + pieces)
    for item in loads[:3] + down_loads + loads[3:]:
        item.start()
    wire.meet()
    reducer = Reducer(
        wire,
        plan,
        [(back_tv, mid_v, pl.ds(c * REDUCE_COLS, REDUCE_COLS)) for c in range(chunks)],
        out,
        reducer_refs,
        carry_out=carry_out,
    )
    loads[0].wait()
    loads[1].wait()
    reducer.begin()

    wide_out[...] = jnp.zeros_like(wide_out)
    sums[...] = jnp.zeros_like(sums)

    def token_tiles(body):
        row_tiles(tokens, body, own)

    def first_pass(k):
        at_cols = pl.ds(k * cols, cols)

        def body(row, tile):
            at = pl.ds(row, tile)
            value = dot_f32(back_v[at, :], weight[:, at_cols], 1, 0)
            grad[at, at_cols] = value
            part = unit[at, at_cols].astype(F32)
            scaled = value * gain[:, at_cols]
            lane = lax.broadcasted_iota(jnp.int32, (tile, sums.shape[1]), 1)
            sums[at, :] += jnp.where(
                lane == 0,
                jnp.sum(scaled, axis=1, keepdims=True),
                jnp.sum(scaled * part, axis=1, keepdims=True),
            )
            wide_out[0:1, at_cols] += jnp.sum(value * part, axis=0, keepdims=True)
            wide_out[1:2, at_cols] += jnp.sum(value, axis=0, keepdims=True)

        token_tiles(body)

    loads[2].wait()
    for item in down_loads:
        item.wait()
    loads[3].wait()
    loads[4].wait()
    for k in range(REDUCE_CHUNKS):
        first_pass(k)
    for item in up_loads:
        item.start()

    stats = [
        wire.copy(
            stat_send, stat_recv.at[j - 1], stat_sems.at[0, j - 1], stat_sems.at[1, j - 1], j
        )
        for j in range(1, SHARE)
    ]
    for j in range(SHARE):
        stat_send[j] = sums[pl.ds(j * own, own), :].T[0:8, :]
    for item in stats:
        item.start()
    reducer.tick(0)
    reducer.tick(1)
    for item in stats:
        item.wait_recv()
    for j in range(SHARE):
        total = stat_send[j]
        for k in range(1, SHARE):
            total = total + stat_recv[k - 1, j ^ k]
        total = total * (1.0 / (SHARE * width))
        sums[pl.ds(j * own, own), :] = jnp.concatenate([total] * (sums.shape[1] // 8), axis=0).T
    for item in stats:
        item.wait_send()

    def second_pass(k):
        at_cols = pl.ds(k * cols, cols)

        def body(row, tile):
            at = pl.ds(row, tile)
            act_grad = rstd[at, 0:1] * (
                grad[at, at_cols] * gain[:, at_cols]
                - sums[at, 0:1]
                - unit[at, at_cols].astype(F32) * sums[at, 1:2]
            )
            unit[at, at_cols] = (act_grad * slope[at, at_cols].astype(F32)).astype(BF)

        token_tiles(body)

    for k in range(REDUCE_CHUNKS):
        second_pass(k)
    store = pltpu.make_async_copy(unit, up_low_out, store_sem.at[0])
    store.start()
    reducer.tick(2)
    reducer.tick(3)
    for item in up_loads:
        item.wait()

    def term(block, row, tile):
        return dot_f32(unit[pl.ds(block * own + row, tile), :], weight[...], 1, 1)

    owner = OwnerSum(wire, own, slope, grad, sum_refs)
    owner.first(term)
    owner.second(term)
    owner.third()
    for at in range(4, reducer.ticks()):
        reducer.tick(at)
    owner.last()
    result = pltpu.make_async_copy(grad.at[pl.ds(0, own), :], sum_out, store_sem.at[1])
    result.start()
    reducer.close()
    store.wait()
    result.wait()


def ffn_back(back, back_t, mid, down, up, unit, slope, gain, rstd):
    tokens, width = mid.shape
    own = tokens // SHARE
    cols = REDUCE_COLS
    lanes = 128
    any_spec = pl.BlockSpec(memory_space=pl.ANY)
    vmem = pl.BlockSpec(memory_space=pltpu.VMEM)
    pieces = len(down)
    plan = Reducer.plan(width // cols, False, True)
    carry = Reducer.carry_shapes(cols)

    def kernel(back, back_t, mid, *refs):
        down, up, refs = refs[:pieces], refs[pieces : 2 * pieces], refs[2 * pieces :]
        ffn_back_kernel(own, back, back_t, mid, down, up, *refs)

    return pl.pallas_call(
        kernel,
        in_specs=[any_spec] * (5 + 2 * pieces) + [vmem] * 2,
        out_specs=[any_spec, any_spec, vmem, any_spec] + [any_spec] * len(carry),
        out_shape=[
            Reducer.out_shape(plan, cols),
            jax.ShapeDtypeStruct((tokens, width), BF),
            jax.ShapeDtypeStruct((8, width), F32),
            jax.ShapeDtypeStruct((own, D), F32),
        ]
        + carry,
        scratch_shapes=Reducer.scratch(plan, cols)
        + OwnerSum.scratch(own)
        + [
            pltpu.VMEM((tokens, D), BF),
            pltpu.VMEM((D, tokens), BF),
            pltpu.VMEM((tokens, width), BF),
            pltpu.VMEM((D, width), BF),
            pltpu.VMEM((tokens, width), BF),
            pltpu.VMEM((tokens, width), BF),
            pltpu.VMEM((tokens, width), F32),
            pltpu.VMEM((tokens, lanes), F32),
            pltpu.VMEM((SHARE, 8, own), F32),
            pltpu.VMEM((SHARE - 1, SHARE, 8, own), F32),
            pltpu.SemaphoreType.DMA((5 + 2 * pieces,)),
            pltpu.SemaphoreType.DMA((2, SHARE - 1)),
            pltpu.SemaphoreType.DMA((2,)),
        ],
        compiler_params=pltpu.CompilerParams(
            collective_id=1, has_side_effects=True, vmem_limit_bytes=KERNEL_VMEM
        ),
        name="ffn_back",
    )(
        back,
        back_t,
        mid,
        *down,
        *up,
        unit,
        slope,
        gain[None],
        rstd,
    )


def attention_back_kernel(
    head_size, own, left_t, right, q_in, k_in, v_in, ffn_grad, hidden, back, mixed_in, out_full,
    small, cap, cq, sq, ck, sk, *refs
):
    width = q_in.shape[1]
    chunks = right.shape[1] // REDUCE_COLS
    plan = Reducer.plan(chunks, True, True)
    carried = len(Reducer.carry_shapes(REDUCE_COLS))
    carry_in, refs = refs[:carried], refs[carried:]
    out, q_out, k_out, v_out, hidden_out, grad_out, norm_out = refs[:7]
    refs = refs[7:]
    carry_out, refs = refs[:carried], refs[carried:]
    wire = Wire()
    count = len(Reducer.scratch(plan, REDUCE_COLS))
    reducer_refs, refs = refs[:count], refs[count:]
    (
        left_v, right_v, q_v, k_v, v_v, mixed_cols, hidden_cols, grad, state, back_v, mixed_v,
        weight, low, mixed, load_sem, turn_sem, weight_sem, store_sem,
    ) = refs
    loads = [
        pltpu.make_async_copy(source, target, load_sem.at[k])
        for k, (source, target) in enumerate(
            [
                (left_t, left_v),
                (right, right_v),
                (ffn_grad, grad),
                (hidden, state),
                (back.at[pl.ds(0, own), :], back_v),
                (mixed_in, mixed_v),
                (q_in, q_v),
                (k_in, k_v),
                (v_in, v_v),
            ]
        )
    ]
    for item in loads:
        item.start()
    wire.meet()
    reducer = Reducer(
        wire,
        plan,
        [(left_v, right_v, pl.ds(c * REDUCE_COLS, REDUCE_COLS)) for c in range(chunks)],
        out,
        reducer_refs,
        carry_in,
        carry_out,
    )
    reducer.load()
    loads[0].wait()
    loads[1].wait()
    reducer.begin()

    def fetch(t):
        return pltpu.make_async_copy(out_full.at[t], weight.at[t % 2], weight_sem.at[t % 2])

    fetch(0).start()
    for item in loads[2:6]:
        item.wait()
    norm_out[...] = jnp.zeros_like(norm_out)

    def norm_back_rows(value, upstream, gain_row):
        center = value - jnp.mean(value, axis=-1, keepdims=True)
        rstd = lax.rsqrt(jnp.mean(center * center, axis=-1, keepdims=True) + EPS_NORM)
        unit = center * rstd
        scaled = upstream * small[gain_row : gain_row + 1, :]
        lean = jnp.mean(scaled, axis=-1, keepdims=True)
        slope = jnp.mean(scaled * unit, axis=-1, keepdims=True)
        norm_out[gain_row : gain_row + 1, :] += jnp.sum(upstream * unit, axis=0, keepdims=True)
        norm_out[gain_row + 1 : gain_row + 2, :] += jnp.sum(upstream, axis=0, keepdims=True)
        return rstd * (scaled - lean - unit * slope)

    def hidden_rows(row, tile):
        at = pl.ds(row, tile)
        value = back_v[at, :].astype(F32) + norm_back_rows(state[at, :], grad[at, :], 4)
        grad[at, :] = value
        low[at, :] = value.astype(BF)

    row_tiles(own, hidden_rows, 64)
    grad_store = pltpu.make_async_copy(grad, grad_out, store_sem.at[0])
    grad_store.start()

    def turn(source, target, sems):
        copies = []
        for j in range(1, SHARE):
            to = pl.multiple_of(flipped(wire.member, j) * width, width)
            copies.append(
                wire.copy(
                    source.at[:, pl.ds(to, width)],
                    target.at[pl.ds(j * own, own), :],
                    sems.at[0, j],
                    sems.at[1, j],
                    j,
                )
            )
        here = pl.multiple_of(wire.member * width, width)
        local = pltpu.make_async_copy(
            source.at[:, pl.ds(here, width)], target.at[pl.ds(0, own), :], sems.at[0, 0]
        )
        for item in copies + [local]:
            item.start()
        return copies, local

    def turned(copies, local):
        local.wait()
        for item in copies:
            item.wait_recv()

    for t in range(SHARE):
        fetch(t).wait()
        if t + 1 < SHARE:
            fetch(t + 1).start()
        part = dot_f32(
            low[:, pl.ds(t * width, width)], weight[t % 2].reshape(D, width), 1, 1
        )
        state[...] = part if t == 0 else state[...] + part

    reducer.tick(carried)

    def mixed_rows(row, tile):
        at = pl.ds(row, tile)
        value = jnp.concatenate([mixed_v[t, at, :].astype(F32) for t in range(SHARE)], axis=1)
        mixed[at, :] = norm_back_rows(value, state[at, :], 2).astype(BF)

    row_tiles(own, mixed_rows, 64)
    mixed_turn = turn(mixed, mixed_cols, turn_sem.at[0])
    hidden_turn = turn(low, hidden_cols, turn_sem.at[1])
    reducer.tick(carried + 1)
    turned(*mixed_turn)
    for item in loads[6:]:
        item.wait()
    row_count = SHARE * own // L

    def rows(first, last):
        @pl.loop(first, last)
        def _(row):
            at = pl.ds(pl.multiple_of(row * L, L), L)
            got = attention_back_block(
                head_size,
                cap[row],
                q_v[at, :],
                k_v[at, :],
                v_v[at, :],
                mixed_cols[at, :],
                (cq[...], sq[...], ck[...], sk[...]),
            )
            q_v[at, :], k_v[at, :], v_v[at, :] = got

    parts = 4
    for part in range(parts):
        rows(part * row_count // parts, (part + 1) * row_count // parts)
        if part < parts - 1:
            reducer.tick(carried + 2 + part)
    stores = [
        pltpu.make_async_copy(source, target, load_sem.at[k])
        for k, (source, target) in enumerate([(q_v, q_out), (k_v, k_out), (v_v, v_out)])
    ]
    for item in stores:
        item.start()
    turned(*hidden_turn)
    stores.append(pltpu.make_async_copy(hidden_cols, hidden_out, load_sem.at[3]))
    stores[-1].start()
    for at in range(carried + 1 + parts, reducer.ticks()):
        reducer.tick(at)
    reducer.close()
    for item in stores + [grad_store]:
        item.wait()
    for item in mixed_turn[0] + hidden_turn[0]:
        item.wait_send()


def attention_back(
    left_t, right, queries, keys, values, ffn_grad, hidden, back, mixed, out_full, small, captions,
    tables, carry_in,
):
    tokens, width = queries.shape
    own = tokens // SHARE
    cols = REDUCE_COLS
    any_spec = pl.BlockSpec(memory_space=pl.ANY)
    vmem = pl.BlockSpec(memory_space=pltpu.VMEM)
    part = jax.ShapeDtypeStruct((tokens, width), BF)
    plan = Reducer.plan(right.shape[1] // cols, True, True)
    carry = Reducer.carry_shapes(cols)
    return pl.pallas_call(
        partial(attention_back_kernel, D // HEADS, own),
        in_specs=[any_spec] * 10
        + [vmem]
        + [pl.BlockSpec(memory_space=pltpu.SMEM)]
        + [vmem] * 4
        + [any_spec] * len(carry),
        out_specs=[any_spec] * 6 + [vmem] + [any_spec] * len(carry),
        out_shape=[Reducer.out_shape(plan, cols)]
        + [part] * 4
        + [jax.ShapeDtypeStruct((own, D), F32), jax.ShapeDtypeStruct((8, D), F32)]
        + carry,
        scratch_shapes=Reducer.scratch(plan, cols)
        + [pltpu.VMEM((D, tokens), BF), pltpu.VMEM(right.shape, BF)]
        + [pltpu.VMEM((tokens, width), BF)] * 5
        + [pltpu.VMEM((own, D), F32)] * 2
        + [
            pltpu.VMEM((own, D), BF),
            pltpu.VMEM(mixed.shape, BF),
            pltpu.VMEM((2,) + out_full.shape[1:], BF),
            pltpu.VMEM((own, D), BF),
            pltpu.VMEM((own, D), BF),
            pltpu.SemaphoreType.DMA((9,)),
            pltpu.SemaphoreType.DMA((2, 2, SHARE)),
            pltpu.SemaphoreType.DMA((2,)),
            pltpu.SemaphoreType.DMA((1,)),
        ],
        compiler_params=pltpu.CompilerParams(
            collective_id=2, has_side_effects=True, vmem_limit_bytes=KERNEL_VMEM
        ),
        name="attention_back",
    )(
        left_t,
        right,
        queries,
        keys,
        values,
        ffn_grad,
        hidden,
        back,
        mixed,
        out_full,
        small,
        captions,
        *tables,
        *carry_in,
    )


def project_back_kernel(own, normed_t, context_t, *refs):
    parts, refs = refs[:4], refs[4:]
    mid, weights, refs = refs[0], refs[1:4], refs[4:]
    pieces = REDUCE_CHUNKS
    down, refs = refs[:pieces], refs[pieces:]
    width = parts[0].shape[1]
    split = width // REDUCE_COLS
    plan = Reducer.plan(4 * split, True, False)
    carried = len(Reducer.carry_shapes(REDUCE_COLS))
    carry_in, refs = refs[:carried], refs[carried:]
    out, grad_out, block_out = refs[:3]
    refs = refs[3:]
    wire = Wire()
    count = len(Reducer.scratch(plan, REDUCE_COLS))
    reducer_refs, refs = refs[:count], refs[count:]
    grad_refs, refs = refs[:3], refs[3:]
    block_refs, refs = refs[:3], refs[3:]
    normed_v, context_v, parts_v, mid_v, weight, send, kept, load_sem, store_sem = refs
    loads = [
        pltpu.make_async_copy(source, target, load_sem.at[k])
        for k, (source, target) in enumerate(
            [
                (context_t, context_v),
                (parts[0], parts_v.at[0]),
                (normed_t, normed_v),
                (parts[1], parts_v.at[1]),
                (parts[2], parts_v.at[2]),
                (parts[3], parts_v.at[3]),
                (mid, mid_v),
            ]
            + [(item, weight.at[:, pl.ds(k * width, width)]) for k, item in enumerate(weights)]
        )
    ]
    for item in loads:
        item.start()
    wire.meet()
    reducer = Reducer(
        wire,
        plan,
        [
            (normed_v if k else context_v, parts_v.at[k], pl.ds(c * REDUCE_COLS, REDUCE_COLS))
            for k in range(4)
            for c in range(split)
        ],
        out,
        reducer_refs,
        carry_in,
    )
    reducer.load()
    for item in loads[:4]:
        item.wait()
    reducer.begin()
    for item in loads[4:]:
        item.wait()

    def grad_term(block, row, tile):
        at = pl.ds(block * own + row, tile)
        return sum(
            dot_f32(parts_v[1 + k, at, :], weight[:, pl.ds(k * width, width)], 1, 1)
            for k in range(3)
        )

    grad_sum = OwnerSum(wire, own, send, kept, grad_refs)
    grad_sum.first(grad_term)
    grad_sum.second(grad_term)
    step = mid.shape[1] // pieces
    down_loads = [
        pltpu.make_async_copy(part, weight.at[:, pl.ds(k * step, step)], load_sem.at[10 + k])
        for k, part in enumerate(down)
    ]
    for item in down_loads:
        item.start()
    reducer.tick(carried)
    reducer.tick(carried + 1)
    grad_sum.third()
    for item in down_loads:
        item.wait()
    reducer.tick(carried + 2)
    reducer.tick(carried + 3)
    grad_sum.last()
    grad_store = pltpu.make_async_copy(kept.at[pl.ds(0, own), :], grad_out, store_sem.at[0])
    grad_store.start()

    def block_term(block, row, tile):
        at = pl.ds(block * own + row, tile)
        return dot_f32(mid_v[at, :], weight[...], 1, 1)

    block_sum = OwnerSum(wire, own, send, kept, block_refs)
    block_sum.first(block_term)
    reducer.tick(carried + 4)
    grad_store.wait()
    block_sum.second(block_term)
    block_sum.third()
    for at in range(carried + 5, reducer.ticks()):
        reducer.tick(at)
    block_sum.last()
    block_store = pltpu.make_async_copy(kept.at[pl.ds(0, own), :], block_out, store_sem.at[1])
    block_store.start()
    reducer.close()
    block_store.wait()


def project_back(normed_t, context_t, parts, mid, weights, down, carry_in):
    tokens, width = parts[0].shape
    own = tokens // SHARE
    any_spec = pl.BlockSpec(memory_space=pl.ANY)
    part = jax.ShapeDtypeStruct((own, D), F32)
    plan = Reducer.plan(4 * width // REDUCE_COLS, True, False)
    return pl.pallas_call(
        partial(project_back_kernel, own),
        in_specs=[any_spec] * (10 + len(down) + len(carry_in)),
        out_specs=[any_spec] * 3,
        out_shape=[Reducer.out_shape(plan, REDUCE_COLS), part, part],
        scratch_shapes=Reducer.scratch(plan, REDUCE_COLS)
        + OwnerSum.scratch(own)
        + OwnerSum.scratch(own)
        + [
            pltpu.VMEM((D, tokens), BF),
            pltpu.VMEM((D, tokens), BF),
            pltpu.VMEM((4, tokens, width), BF),
            pltpu.VMEM(mid.shape, BF),
            pltpu.VMEM((D, mid.shape[1]), BF),
            pltpu.VMEM((3 * own, D), BF),
            pltpu.VMEM((2 * own, D), F32),
            pltpu.SemaphoreType.DMA((10 + len(down),)),
            pltpu.SemaphoreType.DMA((2,)),
        ],
        compiler_params=pltpu.CompilerParams(
            collective_id=3, has_side_effects=True, vmem_limit_bytes=KERNEL_VMEM
        ),
        name="project_back",
    )(normed_t, context_t, *parts, mid, *weights, *down, *carry_in)


def sum_over_devices(wire, total, whole, got, send_sem, recv_sem):
    rows, cols = total.shape
    row, col = 0, 0
    regions = []
    for stage in range(len(got)):
        mask = 1 << stage
        bit = (wire.me // mask) % 2
        regions.append((row, col, rows, cols))
        if rows > 8:
            rows //= 2
            away = (pl.multiple_of(row + (1 - bit) * rows, 8), col)
            row = pl.multiple_of(row + bit * rows, 8)
        else:
            cols //= 2
            away = (row, pl.multiple_of(col + (1 - bit) * cols, 128))
            col = pl.multiple_of(col + bit * cols, 128)
        copy = wire.copy(
            total.at[pl.ds(away[0], rows), pl.ds(away[1], cols)],
            got[stage],
            send_sem.at[0, stage],
            recv_sem.at[0, stage],
            mask,
        )
        copy.start()
        copy.wait()
        total[pl.ds(row, rows), pl.ds(col, cols)] += got[stage][...]
    whole[pl.ds(row, rows), pl.ds(col, cols)] = total[pl.ds(row, rows), pl.ds(col, cols)]
    for stage in reversed(range(len(got))):
        part = whole.at[pl.ds(row, rows), pl.ds(col, cols)]
        copy = wire.copy(part, part, send_sem.at[1, stage], recv_sem.at[1, stage], 1 << stage)
        copy.start()
        copy.wait()
        row, col, rows, cols = regions[stage]


WIDE = FF // D
SUM_COLS, SUM_WEIGHTED = 0, 2 * WIDE + 4
SUM_NORMS = 2 * SUM_WEIGHTED
SUM_MOMENTS = SUM_NORMS + 2 * WIDE + 6
SUM_SCALARS = SUM_MOMENTS + 2 * WIDE + 6
SUM_ROWS = 64


def update_matrices(places, tile):
    matrices = []
    for index in range(2):
        pieces = [
            (index * WIDE + t, c * tile, t * D + c * tile, t, place)
            for t in range(SHARE)
            for c, place in enumerate(places[index])
        ]
        matrices.append((index, FF, pieces, tile))
    for j in range(4):
        width = len(places[2 + j]) * tile
        pieces = [
            (2 * WIDE + j, t * width + c * tile, t * width + c * tile, t, place)
            for t in range(SHARE)
            for c, place in enumerate(places[2 + j])
        ]
        matrices.append((2 + j, D, pieces, tile))
    return matrices


def matrix_cols(refs, index, col, size):
    if index < 2:
        return refs[index][:, pl.ds(col, size)]
    return refs[2][:, index - 2, pl.ds(col, size)]


def put_matrix_cols(refs, index, col, size, value):
    if index < 2:
        refs[index][:, pl.ds(col, size)] = value
    else:
        refs[2][:, index - 2, pl.ds(col, size)] = value


def update_sums_kernel(
    places, sources, up_old, down_old, attn_old, row_old, wide_terms, small_terms, moments,
    vector_squares, *refs
):
    row_new, whole, total = refs[:3]
    got, send_sem, recv_sem = refs[3:-2], refs[-2], refs[-1]
    wire = Wire()
    barrier = pltpu.get_barrier_semaphore()
    for stage in range(len(got)):
        pl.semaphore_signal(
            barrier, inc=1, device_id=(flipped(wire.me, 1 << stage),), device_id_type=MESH
        )
    width = sources[0].shape[3]
    old = (up_old, down_old, attn_old)

    def piece_of(member, place):
        return sources[place[0]][flipped(wire.member, member), place[1]].astype(F32)

    total[...] = jnp.zeros_like(total)
    lane = lax.broadcasted_iota(jnp.int32, (1, 128), 1)
    scalars = vector_squares[0:1, :]
    row_lane = lax.broadcasted_iota(jnp.int32, row_new.shape, 1)
    row_all = jnp.zeros(row_new.shape, F32)
    for index, size, pieces, tile in update_matrices(places, width):
        row_sum = jnp.zeros((row_new.shape[0], 1), F32)
        square = jnp.zeros((1, 1), F32)
        for at, sum_col, col, member, place in pieces:
            value = piece_of(member, place)
            squares = value * value
            row_sum += jnp.sum(squares, axis=1, keepdims=True)
            total[SUM_COLS + at : SUM_COLS + at + 1, sum_col : sum_col + tile] = jnp.sum(
                squares, axis=0, keepdims=True
            )
            weight = matrix_cols(old, index, col, tile)
            square += jnp.sum(weight * weight, keepdims=True)
        moment = DECAY_RATE * row_old[:, index : index + 1] + (1.0 - DECAY_RATE) * (
            row_sum * (1.0 / size) + EPS_SQUARE
        )
        row_all = jnp.where(row_lane == index, moment, row_all)
        inverse = 1.0 / moment
        for at, sum_col, col, member, place in pieces:
            value = piece_of(member, place)
            total[SUM_WEIGHTED + at : SUM_WEIGHTED + at + 1, sum_col : sum_col + tile] = jnp.sum(
                value * value * inverse, axis=0, keepdims=True
            )
        scalars = jnp.where(lane == index, jnp.sum(moment, keepdims=True), scalars)
        scalars = jnp.where(lane == 6 + index, square, scalars)
    row_new[...] = row_all
    for r in range(2):
        for t in range(SHARE):
            at = SUM_NORMS + r * WIDE + t
            total[at : at + 1, :] = jnp.where(wire.member == t, wide_terms[r : r + 1, :], 0.0)
    total[SUM_NORMS + 2 * WIDE : SUM_MOMENTS, :] = small_terms[...]
    total[SUM_MOMENTS:SUM_SCALARS, :] = moments[...]
    total[SUM_SCALARS : SUM_SCALARS + 1, 0:128] = scalars

    pl.semaphore_wait(barrier, len(got))
    sum_over_devices(wire, total, whole, got, send_sem, recv_sem)


def update_kernel(
    places, sources, up_old, down_old, attn_old, row_new, col_old, whole, up_grad, down_grad,
    attn_grad, up_new, down_new, attn_new, up_copy, down_copy, attn_copy, col_new, vectors, scale
):
    mine = lax.axis_index("dp") % SHARE
    width = sources[0].shape[3]
    old, grad = (up_old, down_old, attn_old), (up_grad, down_grad, attn_grad)
    new, low = (up_new, down_new, attn_new), (up_copy, down_copy, attn_copy)
    columns = DECAY_RATE * col_old[...] + (1.0 - DECAY_RATE) * (
        whole[SUM_COLS:SUM_WEIGHTED, :] * (1.0 / D) + EPS_SQUARE
    )
    col_new[...] = columns
    scale[...] = lax.rsqrt(columns)
    ratio = whole[SUM_WEIGHTED:SUM_NORMS, :] / columns

    def scalar(index):
        return whole[SUM_SCALARS : SUM_SCALARS + 1, index : index + 1]

    def step_size(square, weight_square, size):
        upd_rms = jnp.sqrt(square * (1.0 / size))
        weight_rms = jnp.sqrt(weight_square * (1.0 / size))
        return (
            LEARN_RATE
            * jnp.maximum(EPS_SCALE, weight_rms)
            / jnp.maximum(1.0, upd_rms * (1.0 / CLIP_LEVEL))
        )

    for index, size, pieces, tile in update_matrices(places, width):
        first, last = pieces[0][0], pieces[-1][0] + 1
        row_mean = scalar(index) * (1.0 / D)
        square = row_mean * jnp.sum(ratio[first:last, :], keepdims=True)
        factor = step_size(square, scalar(6 + index), D * size)
        row_scale = lax.rsqrt(row_new[:, index : index + 1] / row_mean) * factor
        for at, sum_col, col, member, place in pieces:
            value = sources[place[0]][flipped(mine, member), place[1]].astype(F32)
            put_matrix_cols(grad, index, col, tile, value)
            value = matrix_cols(old, index, col, tile) - value * row_scale * scale[
                at : at + 1, sum_col : sum_col + tile
            ]
            put_matrix_cols(new, index, col, tile, value)
            put_matrix_cols(low, index, col, tile, value.astype(BF))

    count = 2 * WIDE + 6
    grads = whole[SUM_NORMS:SUM_MOMENTS, :]
    moment = DECAY_RATE * whole[SUM_MOMENTS:SUM_SCALARS, :] + (1.0 - DECAY_RATE) * (
        grads * grads + EPS_SQUARE
    )
    scaled = grads * lax.rsqrt(moment)
    vectors[0:count, :] = grads
    vectors[count : 2 * count, :] = moment
    spans = [(r * WIDE, (r + 1) * WIDE) for r in range(2)]
    spans += [(2 * WIDE + r, 2 * WIDE + r + 1) for r in range(6)]
    for r, (first, last) in enumerate(spans):
        part = scaled[first:last, :]
        size = (last - first) * D
        factor = step_size(jnp.sum(part * part, keepdims=True), scalar(12 + r), size)
        vectors[2 * count + first : 2 * count + last, :] = part * factor


def update(places, sources, weights, row_old, col_old, wide_terms, small_terms, moments, squares):
    count = lax.axis_size("dp")
    stages = count.bit_length() - 1
    rows = weights[0].shape[0]
    parts = []
    size = [SUM_ROWS, D]
    for _ in range(stages):
        size[0 if size[0] > 8 else 1] //= 2
        parts.append(pltpu.VMEM(tuple(size), F32))
    vmem = pl.BlockSpec(memory_space=pltpu.VMEM)
    number = len(sources)
    whole_shape = jax.ShapeDtypeStruct((SUM_ROWS, D), F32)

    def sums_kernel(*refs):
        update_sums_kernel(places, refs[:number], *refs[number:])

    def kernel(*refs):
        update_kernel(places, refs[:number], *refs[number:])

    row_new, whole = pl.pallas_call(
        sums_kernel,
        in_specs=[vmem] * (number + 8),
        out_specs=[vmem] * 2,
        out_shape=[jax.ShapeDtypeStruct((rows, 128), F32), whole_shape],
        scratch_shapes=[pltpu.VMEM((SUM_ROWS, D), F32)]
        + parts
        + [pltpu.SemaphoreType.DMA((2, stages)), pltpu.SemaphoreType.DMA((2, stages))],
        compiler_params=pltpu.CompilerParams(
            collective_id=4, has_side_effects=True, vmem_limit_bytes=KERNEL_VMEM
        ),
        name="update_sums",
    )(*sources, *weights, row_old, wide_terms, small_terms, moments, squares)
    shapes = [jax.ShapeDtypeStruct(item.shape, kind) for kind in (F32, F32, BF) for item in weights]
    shapes += [
        jax.ShapeDtypeStruct((SUM_WEIGHTED, D), F32),
        jax.ShapeDtypeStruct((3 * (2 * WIDE + 6), D), F32),
    ]
    results = pl.pallas_call(
        kernel,
        in_specs=[vmem] * (number + 6),
        out_specs=[vmem] * len(shapes),
        out_shape=shapes,
        scratch_shapes=[pltpu.VMEM((SUM_WEIGHTED, D), F32)],
        compiler_params=pltpu.CompilerParams(vmem_limit_bytes=KERNEL_VMEM),
        name="update",
    )(*sources, *weights, row_new, col_old, whole)
    return row_new, results


class Share:
    def __init__(self, wire, source, target, sems):
        self.wire, self.source, self.target, self.sems = wire, source, target, sems

    def copies(self):
        parts = [
            (self.source, self.target.at[2], 2),
            (self.source, self.target.at[1], 1),
            (self.target.at[2], self.target.at[3], 1),
        ]
        return [
            self.wire.copy(source, target, self.sems.at[0, k], self.sems.at[1, k], mask)
            for k, (source, target, mask) in enumerate(parts)
        ]

    def start(self):
        far, near, unused = self.copies()
        far.start()
        near.start()

    def forward(self):
        far, unused, last = self.copies()
        far.wait_recv()
        last.start()

    def done(self):
        unused, near, last = self.copies()
        near.wait_recv()
        last.wait_recv()

    def close(self):
        for item in self.copies():
            item.wait_send()


def normalized(value):
    center = value - jnp.mean(value, axis=-1, keepdims=True)
    return center * lax.rsqrt(jnp.mean(center * center, axis=-1, keepdims=True) + EPS_NORM)


def attention_block(head_size, caption, q_low, k_low, v_low):
    mixed = []
    for head in range(q_low.shape[1] // head_size):
        at = slice(head * head_size, (head + 1) * head_size)
        probs = masked_probs(q_low[:, at], k_low[:, at], caption, head_size).astype(BF)
        mixed.append(dot_f32(probs, v_low[:, at], 1, 0))
    return jnp.concatenate(mixed, axis=1).astype(BF)


def vector_rows(count):
    wide = FF // count
    return max(1, wide // 128), min(wide, 128)


GATHERED = 4 + 2 * REDUCE_CHUNKS


def forward_kernel(
    own, tokens, cotangent, live, attn_in, up_in, down_in, vectors, cq, sq, ck, sk, *refs
):
    gathered, refs = refs[:GATHERED], refs[GATHERED:]
    (
        out_full, normed_out, back_out, back_t_out, context_out, ffn_out, mid_out, unit_out,
        slope_out, q_out, k_out, v_out, mixed_out, hidden_out, small, wide, rstd_out, captions,
    ) = refs[:18]
    (
        attn_v, up_v, down_v, pieces, normed, back_v, weight, q_v, k_v, v_v, mixed, mixed_own,
        context, ffn, act, unit, mid, slope, norms, sums, stat_send, stat_recv, load_sem,
        piece_sems, gather_sems, norm_sems, share_sems, turn_sems, stat_sems, weight_sem, store_sem,
        turned, turned_sem,
    ) = refs[18:]
    wire = Wire()
    count = lax.axis_size("dp")
    member, group = wire.member, wire.me // SHARE
    low, high = group % 2, group // 2
    masks = group_masks()
    width = q_v.shape[1]
    step = width
    ff_width = act.shape[1]
    local = attn_v.shape[0]
    head_size = D // HEADS
    rows_each = L

    loads = [
        pltpu.make_async_copy(source, target, load_sem.at[k])
        for k, (source, target) in enumerate(
            [(attn_in, attn_v), (up_in, up_v), (down_in, down_v)]
        )
    ]
    for item in loads:
        item.start()
    norms[wire.me] = vectors[...].astype(BF).astype(F32)
    chain = count == 8 * SHARE
    wire.meet([6 * SHARE] if chain else [])

    def piece_copies(chunk):
        place = gathered[chunk].at[high, low, pl.ds(pl.multiple_of(member * local, local), local), :]
        here = pltpu.make_async_copy(pieces.at[0, chunk], place, piece_sems.at[0, chunk, 0])
        away = [
            wire.copy(
                pieces.at[j, chunk], place, piece_sems.at[0, chunk, j], piece_sems.at[1, chunk, j], j
            )
            for j in range(1, SHARE)
        ]
        return here, away

    def send_pieces(chunk):
        for j in range(SHARE):
            to = flipped(member, j)
            if chunk < 4:
                value = attn_v[:, chunk, pl.ds(pl.multiple_of(to * width, width), width)]
            else:
                source = up_v if chunk < 4 + REDUCE_CHUNKS else down_v
                k = (chunk - 4) % REDUCE_CHUNKS
                value = source[:, pl.ds(pl.multiple_of(to * ff_width + k * step, step), step)]
            pieces[j, chunk] = value.astype(BF)
        here, away = piece_copies(chunk)
        here.start()
        for item in away:
            item.start()

    always = None
    nearby = flipped(wire.me, 1)

    def doubling(chunk):
        buf = gathered[chunk]
        route = []
        for stage, mask in enumerate(masks):
            if stage == len(masks) - 1:
                part = buf.at[:, low]
            else:
                size = 1 << stage
                part = buf.at[pl.ds((high // size) * size, size), low]
            to = flipped(wire.me, mask)
            route.append(([(always, part, to, stage)], [(always, part, stage)]))
        return route

    def chained(chunk):
        buf = gathered[chunk]
        y_first = chunk % 6 == 5
        neighbour = 2 * SHARE

        def part(z):
            return buf.at[z] if y_first else buf.at[z, low]

        hops = []
        for hop in range(1, 4):
            hops.append(
                (
                    [
                        (
                            jnp.logical_and(high >= hop - 1, high < 3),
                            part(high - hop + 1),
                            wire.me + neighbour,
                            hop - 1,
                        ),
                        (
                            jnp.logical_and(high <= 4 - hop, high > 0),
                            part(high + hop - 1),
                            wire.me - neighbour,
                            hop + 2,
                        ),
                    ],
                    [
                        (high >= hop, part(high - hop), hop - 1),
                        (high <= 3 - hop, part(high + hop), hop + 2),
                    ],
                )
            )
        own_part = buf.at[high, low] if y_first else buf.at[:, low]
        across = ([(always, own_part, flipped(wire.me, SHARE), 6)], [(always, own_part, 6)])
        return [across] + hops if y_first else hops + [across]

    route_of = chained if chain else doubling
    stages = 4 if chain else len(masks)
    ahead = stages + 1 if chain else stages

    def where(condition, action):
        if condition is always:
            action()
        else:
            pl.when(condition)(action)

    def moved(chunk, part, to, index):
        return pltpu.make_async_remote_copy(
            src_ref=part,
            dst_ref=part,
            send_sem=gather_sems.at[0, chunk, index],
            recv_sem=gather_sems.at[1, chunk, index],
            device_id=(to,),
            device_id_type=MESH,
        )

    def expect(chunk, stage):
        for condition, part, index in route_of(chunk)[stage][1]:
            where(condition, lambda: moved(chunk, part, nearby, index).wait_recv())

    def launch(chunk, stage):
        if not 0 <= chunk < GATHERED:
            return
        if stage == 0:
            here, away = piece_copies(chunk)
            here.wait()
            for item in away:
                item.wait_recv()
        else:
            expect(chunk, stage - 1)
        for condition, part, to, index in route_of(chunk)[stage][0]:
            where(condition, lambda: moved(chunk, part, to, index).start())

    def advance(at):
        for stage in range(stages):
            launch(at - stage, stage)

    def tick(chunk):
        advance(chunk + ahead)
        expect(chunk, stages - 1)

    norm_stages = count.bit_length() - 1

    def norm_copy(stage):
        size = 1 << stage
        part = norms.at[pl.ds((wire.me // size) * size, size)]
        return wire.copy(part, part, norm_sems.at[0, stage], norm_sems.at[1, stage], size)

    norm_copy(0).start()
    loads[0].wait()
    for chunk in range(4):
        send_pieces(chunk)
    for stage in range(1, norm_stages):
        norm_copy(stage - 1).wait_recv()
        norm_copy(stage).start()
        if stage == 2:
            advance(0)
    norm_copy(norm_stages - 1).wait_recv()
    advance(1)
    small_cols = D // count
    join = max(1, 128 // small_cols)
    small[...] = jnp.concatenate(
        [
            jnp.concatenate([norms[p * join + i][0:8, 0:small_cols] for i in range(join)], axis=1)
            for p in range(count // join)
        ],
        axis=1,
    )
    wide[...] = jnp.zeros_like(wide)
    per_row, row_cols = vector_rows(count)
    per_quarter = count // SHARE
    for r in range(2):
        got = [
            norms[member * per_quarter + i][8 + r * per_row + k : 9 + r * per_row + k, 0:row_cols]
            for i in range(per_quarter)
            for k in range(per_row)
        ]
        wide[r : r + 1, :] = jnp.concatenate(got, axis=1)
    row_count = SHARE * own // rows_each
    own_count = own // rows_each
    lane = lax.broadcasted_iota(jnp.int32, (8, 128), 1)
    sub = lax.broadcasted_iota(jnp.int32, (8, 128), 0)
    table = jnp.zeros((8, 128), F32)
    for row in range(row_count):
        j, i = row // own_count, row % own_count
        at = 8 + 2 * per_row
        value = norms[flipped(wire.me, j)][at : at + 1, i : i + 1]
        table = jnp.where((sub == row % 8) & (lane == row // 8), value, table)
    captions[...] = table

    def norm_rows(read, at_gain, write, tile=64):
        def body(row, tile):
            at = pl.ds(row, tile)
            scaled = normalized(read(at)) * small[at_gain : at_gain + 1, :]
            write(at, scaled + small[at_gain + 1 : at_gain + 2, :])

        row_tiles(own, body, tile)

    def write_normed(at, value):
        normed[0, at, :] = value.astype(BF)

    norm_rows(lambda at: tokens[at, :].astype(F32), 0, write_normed)
    share_normed = Share(wire, normed.at[0], normed, share_sems.at[0])
    share_normed.start()
    advance(2)

    def back_rows(row, tile):
        at = pl.ds(row, tile)
        back_v[at, :] = (cotangent[at, :].astype(F32) * live[at, 0:1]).astype(BF)

    row_tiles(own, back_rows, 64)
    back_here = pltpu.make_async_copy(back_v, mid.at[0], store_sem.at[0])
    back_here.start()

    def store_turned(source, target):
        tile = turned.shape[1]

        def copy(row, slot):
            return pltpu.make_async_copy(
                turned.at[slot], target.at[pl.ds(row, tile), :], turned_sem.at[slot]
            )

        @pl.loop(0, D // tile // 2)
        def _(pair):
            for slot in range(2):
                row = pl.multiple_of((2 * pair + slot) * tile, tile)

                @pl.when(pair > 0)
                def _():
                    copy(row, slot).wait()

                for j in range(SHARE):
                    turned[slot, :, pl.ds(j * own, own)] = source[j, :, pl.ds(row, tile)].T
                copy(row, slot).start()

        for slot in range(2):
            copy(0, slot).wait()

    for item in loads[1:]:
        item.wait()
    for chunk in range(4, 4 + REDUCE_CHUNKS):
        send_pieces(chunk)
    for at in range(3, ahead):
        advance(at)
    share_normed.forward()
    share_back = Share(wire, back_v, mid, share_sems.at[1])
    share_back.start()
    for chunk in range(4 + REDUCE_CHUNKS, GATHERED):
        send_pieces(chunk)

    def fetch(source, slot):
        return pltpu.make_async_copy(source, weight.at[slot], weight_sem.at[slot])

    def block_of(chunk):
        return gathered[chunk]

    def weights_of(slot):
        return weight[slot].reshape(D, step)

    def project(slot, target, cosine, sine):
        @pl.loop(0, SHARE)
        def _(j):
            value = dot_f32(normed[j], weights_of(slot), 1, 0)
            for i in range(own_count):
                part = value[i * rows_each : (i + 1) * rows_each]
                if cosine is not None:
                    part = part * cosine[...] + quarter_turn(part) * sine[...]
                at = pl.ds(pl.multiple_of(j * own + i * rows_each, rows_each), rows_each)
                target[at, :] = part.astype(BF)

    tick(0)
    fetch(block_of(0), 0).start()
    share_normed.done()
    fetch(block_of(0), 0).wait()
    project(0, q_v, cq, sq)
    store_turned(normed, normed_out)
    tick(1)
    fetch(block_of(1), 1).start()
    fetch(block_of(1), 1).wait()
    project(1, k_v, ck, sk)
    share_back.forward()
    tick(2)
    fetch(block_of(2), 0).start()
    fetch(block_of(2), 0).wait()
    project(0, v_v, None, None)

    def attend_loop(first, last):
        @pl.loop(first, last)
        def _(row):
            at = pl.ds(pl.multiple_of(row * rows_each, rows_each), rows_each)
            caption = captions[pl.ds(row, 1), 0:1]
            mixed[at, :] = attention_block(
                head_size, caption, q_v[at, :], k_v[at, :], v_v[at, :]
            )

    attend_loop(0, row_count // 2)
    tick(3)

    def out_copies():
        mine = out_full.at[member]
        far = flipped(member, 2)
        parts = [
            (gathered[3], mine, 2),
            (gathered[3], mine, 1),
            (out_full.at[far], out_full.at[far], 1),
        ]
        return [
            wire.copy(source, target, share_sems.at[4, 0, k], share_sems.at[4, 1, k], mask)
            for k, (source, target, mask) in enumerate(parts)
        ]

    out_here = pltpu.make_async_copy(gathered[3], out_full.at[member], store_sem.at[2])
    out_here.start()
    out_moves = out_copies()
    out_moves[0].start()
    out_moves[1].start()
    attend_loop(row_count // 2, row_count)

    def mixed_copies():
        here = pltpu.make_async_copy(
            mixed.at[pl.ds(0, own), :], mixed_own.at[member], turn_sems.at[0, 0]
        )
        away = [
            wire.copy(
                mixed.at[pl.ds(j * own, own), :],
                mixed_own.at[member],
                turn_sems.at[0, j],
                turn_sems.at[1, j],
                j,
            )
            for j in range(1, SHARE)
        ]
        return here, away

    mixed_here, mixed_away = mixed_copies()
    mixed_here.start()
    for item in mixed_away:
        item.start()
    stores = [
        pltpu.make_async_copy(source, target, store_sem.at[3 + k])
        for k, (source, target) in enumerate([(q_v, q_out), (k_v, k_out), (v_v, v_out)])
    ]
    for item in stores:
        item.start()
    tick(4)
    mixed_here.wait()
    for item in mixed_away:
        item.wait_recv()

    def write_context(at, value):
        context[at, :] = value.astype(BF)

    norm_rows(
        lambda at: jnp.concatenate(
            [mixed_own[t, at, :].astype(F32) for t in range(SHARE)], axis=1
        ),
        2,
        write_context,
    )
    stores.append(pltpu.make_async_copy(mixed_own, mixed_out, store_sem.at[6]))
    stores[-1].start()
    context_here = pltpu.make_async_copy(context, unit.at[0], store_sem.at[7])
    context_here.start()
    back_here.wait()
    share_back.done()
    back_store = pltpu.make_async_copy(mid, back_out, store_sem.at[1])
    back_store.start()
    store_turned(mid, back_t_out)
    tick(5)
    out_moves[0].wait_recv()
    out_moves[2].start()
    share_context = Share(wire, context, unit, share_sems.at[3])
    share_context.start()
    tick(6)
    out_here.wait()
    out_moves[1].wait_recv()
    out_moves[2].wait_recv()
    fetch(out_full.at[0], 0).start()
    for t in range(SHARE):
        fetch(out_full.at[t], t % 2).wait()
        if t + 1 < SHARE:
            fetch(out_full.at[t + 1], (t + 1) % 2).start()
        at = pl.ds(t * width, width)
        hidden_out[:, at] = tokens[:, at].astype(F32) + dot_f32(
            context[...], weights_of(t % 2), 1, 0
        )

    def write_ffn(at, value):
        ffn[0, at, :] = value.astype(BF)

    norm_rows(lambda at: hidden_out[at, :], 4, write_ffn)
    share_ffn = Share(wire, ffn.at[0], ffn, share_sems.at[2])
    share_ffn.start()
    share_context.forward()
    context_here.wait()
    share_context.done()
    store_turned(unit, context_out)
    tick(7)
    share_ffn.forward()
    fetch(block_of(4), 0).start()
    share_ffn.done()
    sums[...] = jnp.zeros_like(sums)

    def widen(k):
        slot = k % 2
        fetch(block_of(4 + k), slot).wait()
        if k + 1 < REDUCE_CHUNKS:
            fetch(block_of(5 + k), 1 - slot).start()
        at_cols = pl.ds(k * step, step)

        @pl.loop(0, SHARE)
        def _(j):
            at = pl.ds(pl.multiple_of(j * own, own), own)
            value = dot_f32(ffn[j], weights_of(slot), 1, 0)
            cdf, density = gelu_parts(value)
            active = value * cdf
            act[at, at_cols] = active
            slope[at, at_cols] = (cdf + value * density).astype(BF)
            sums[at, :] += jnp.broadcast_to(
                jnp.sum(active, axis=1, keepdims=True), (own, sums.shape[1])
            )

    widen(0)
    widen(1)
    tick(8)
    widen(2)
    widen(3)

    def spread_body(row, tile):
        at = pl.ds(row, tile)
        mean = sums[at, 0:1] * (1.0 / ff_width)
        square = jnp.zeros((tile, 1), F32)
        for k in range(REDUCE_CHUNKS):
            center = act[at, pl.ds(k * step, step)] - mean
            square += jnp.sum(center * center, axis=1, keepdims=True)
        lane = lax.broadcasted_iota(jnp.int32, (tile, sums.shape[1]), 1)
        sums[at, :] = jnp.where(lane == 0, mean, square)

    row_tiles(SHARE * own, spread_body)
    for j in range(SHARE):
        stat_send[j] = sums[pl.ds(j * own, own), :].T[0:8, :]
    stats = [
        wire.copy(
            stat_send, stat_recv.at[j - 1], stat_sems.at[0, j - 1], stat_sems.at[1, j - 1], j
        )
        for j in range(1, SHARE)
    ]
    for item in stats:
        item.start()
    stores.append(pltpu.make_async_copy(slope, slope_out, store_sem.at[9]))
    stores[-1].start()
    back_store.wait()
    share_back.close()
    share_context.close()
    tick(9)
    for item in stats:
        item.wait_recv()
    for j in range(SHARE):
        parts = [stat_send[j]] + [stat_recv[k - 1, j ^ k] for k in range(1, SHARE)]
        mean = sum(part[0:1, :] for part in parts) * (1.0 / SHARE)
        square = sum(
            part[1:2, :] + ff_width * (part[0:1, :] - mean) ** 2 for part in parts
        )
        rstd = lax.rsqrt(square * (1.0 / (SHARE * ff_width)) + EPS_NORM)
        sub_all = lax.broadcasted_iota(jnp.int32, (128, own), 0)
        both = jnp.where(sub_all == 0, mean, rstd).T
        sums[pl.ds(j * own, own), :] = both
    rstd_out[...] = jnp.broadcast_to(sums[:, 1:2], rstd_out.shape)

    def finish(k):
        at_cols = pl.ds(k * step, step)

        @pl.loop(0, SHARE)
        def _(j):
            at = pl.ds(pl.multiple_of(j * own, own), own)
            value = (act[at, at_cols] - sums[at, 0:1]) * sums[at, 1:2]
            unit[j, :, at_cols] = value.astype(BF)
            mid[j, :, at_cols] = (value * wide[0:1, at_cols] + wide[1:2, at_cols]).astype(BF)

    finish(0)
    finish(1)
    tick(10)
    finish(2)
    finish(3)
    stores += [
        pltpu.make_async_copy(unit, unit_out, store_sem.at[10]),
        pltpu.make_async_copy(mid, mid_out, store_sem.at[11]),
    ]
    for item in stores[-2:]:
        item.start()
    store_turned(ffn, ffn_out)
    for chunk in range(11, GATHERED):
        tick(chunk)
    for item in stores:
        item.wait()
    for chunk in range(GATHERED):
        for item in piece_copies(chunk)[1]:
            item.wait_send()
        for starts, unused in route_of(chunk):
            for condition, part, to, index in starts:
                where(condition, lambda: moved(chunk, part, to, index).wait_send())
    for stage in range(norm_stages):
        norm_copy(stage).wait_send()
    for item in [share_normed, share_ffn]:
        item.close()
    for item in out_moves + mixed_away + stats:
        item.wait_send()


def forward(tokens, cotangent, live, attn_weight, up_weight, down_weight, vectors, tables):
    count = lax.axis_size("dp")
    own = tokens.shape[0]
    all_tokens = SHARE * own
    width, ff_width = D // SHARE, FF // SHARE
    groups = count // SHARE
    local = D // count
    chunk = (groups // 2, 2, D // groups, width)
    stages = len(group_masks())
    any_spec = pl.BlockSpec(memory_space=pl.ANY)
    vmem = pl.BlockSpec(memory_space=pltpu.VMEM)
    shared = jax.ShapeDtypeStruct((SHARE, own, D), BF)
    across = jax.ShapeDtypeStruct((D, all_tokens), BF)
    wide = jax.ShapeDtypeStruct((SHARE, own, ff_width), BF)
    flat = jax.ShapeDtypeStruct((all_tokens, ff_width), BF)
    part = jax.ShapeDtypeStruct((all_tokens, width), BF)
    norm_stages = count.bit_length() - 1
    return pl.pallas_call(
        partial(forward_kernel, own),
        in_specs=[vmem] * 3 + [any_spec] * 3 + [vmem] * 5,
        out_specs=[any_spec] * (GATHERED + 13) + [vmem] * 5,
        out_shape=[jax.ShapeDtypeStruct(chunk, BF)] * GATHERED
        + [jax.ShapeDtypeStruct((SHARE,) + chunk, BF)]
        + [across, shared, across, across, across]
        + [wide, wide, flat]
        + [part] * 3
        + [
            jax.ShapeDtypeStruct((SHARE, own, width), BF),
            jax.ShapeDtypeStruct((own, D), F32),
            jax.ShapeDtypeStruct((8, D), F32),
            jax.ShapeDtypeStruct((8, ff_width), F32),
            jax.ShapeDtypeStruct((all_tokens, 128), F32),
            jax.ShapeDtypeStruct((8, 128), F32),
        ],
        scratch_shapes=[
            pltpu.VMEM((local, 4, D), F32),
            pltpu.VMEM((local, FF), F32),
            pltpu.VMEM((local, FF), F32),
            pltpu.VMEM((SHARE, GATHERED, local, width), BF),
            pltpu.VMEM((SHARE, own, D), BF),
            pltpu.VMEM((own, D), BF),
            pltpu.VMEM((2,) + chunk, BF),
            pltpu.VMEM((all_tokens, width), BF),
            pltpu.VMEM((all_tokens, width), BF),
            pltpu.VMEM((all_tokens, width), BF),
            pltpu.VMEM((all_tokens, width), BF),
            pltpu.VMEM((SHARE, own, width), BF),
            pltpu.VMEM((own, D), BF),
            pltpu.VMEM((SHARE, own, D), BF),
            pltpu.VMEM((all_tokens, ff_width), F32),
            pltpu.VMEM((SHARE, own, ff_width), BF),
            pltpu.VMEM((SHARE, own, ff_width), BF),
            pltpu.VMEM((all_tokens, ff_width), BF),
            pltpu.VMEM((count, 16, 128), F32),
            pltpu.VMEM((all_tokens, 128), F32),
            pltpu.VMEM((SHARE, 8, own), F32),
            pltpu.VMEM((SHARE - 1, SHARE, 8, own), F32),
            pltpu.SemaphoreType.DMA((3,)),
            pltpu.SemaphoreType.DMA((2, GATHERED, SHARE)),
            pltpu.SemaphoreType.DMA((2, GATHERED, max(stages, 7))),
            pltpu.SemaphoreType.DMA((2, norm_stages)),
            pltpu.SemaphoreType.DMA((5, 2, 3)),
            pltpu.SemaphoreType.DMA((2, SHARE)),
            pltpu.SemaphoreType.DMA((2, SHARE - 1)),
            pltpu.SemaphoreType.DMA((2,)),
            pltpu.SemaphoreType.DMA((12,)),
            pltpu.VMEM((2, 256, all_tokens), BF),
            pltpu.SemaphoreType.DMA((2,)),
        ],
        compiler_params=pltpu.CompilerParams(
            collective_id=5, has_side_effects=True, vmem_limit_bytes=KERNEL_VMEM
        ),
        name="forward",
    )(tokens, cotangent, live, attn_weight, up_weight, down_weight, vectors, *tables)


def gelu_parts(value):
    cdf = 0.5 * (1.0 + lax.erf(value * math.sqrt(0.5)))
    density = jnp.exp(-0.5 * value * value) * (1.0 / math.sqrt(2.0 * math.pi))
    return cdf, density


def per_device(
    tokens,
    cotangent,
    caption_len,
    attn_weight,
    up_weight,
    down_weight,
    small_norms,
    wide_norms,
    attn_row,
    attn_col,
    up_row,
    up_col,
    down_row,
    down_col,
    small_moment,
    wide_moment,
):
    count = lax.axis_size("dp")
    me = lax.axis_index("dp")
    head_size = D // HEADS
    width = D // SHARE
    own = tokens.shape[0]
    own_rows = caption_len.shape[0]

    small_width = D // count
    wide_width = FF // count
    per_row, row_cols = vector_rows(count)
    vectors = jnp.concatenate(
        [
            jnp.pad(small_norms, ((0, 2), (0, 128 - small_width))),
            jnp.pad(
                wide_norms.reshape(2 * per_row, row_cols),
                ((0, 0), (0, 128 - row_cols)),
            ),
            jnp.pad(caption_len.astype(F32), (0, 128 - own_rows))[None],
            jnp.zeros((7 - 2 * per_row, 128), F32),
        ],
        axis=0,
    )
    slot_index = jnp.arange(L)
    live_mask = (slot_index[None, :] < IMG + caption_len[:, None]).astype(F32).reshape(own)
    tables = xpos_tables(head_size, width // head_size)
    results = forward(
        tokens,
        cotangent,
        jnp.broadcast_to(live_mask[:, None], (own, 128)),
        attn_weight,
        up_weight,
        down_weight,
        vectors,
        tables,
    )
    full = [item.reshape(D, width) for item in results[:GATHERED]]
    query_full, key_full, value_full = full[:3]
    up_full, down_full = full[4 : 4 + REDUCE_CHUNKS], full[4 + REDUCE_CHUNKS :]
    (
        out_full, normed_turned, back_all, back_turned, context_turned, ffn_turned, ffn_mid, unit,
        slope, queries, keys_low, values_low, mixed_own, hidden, small_vals, wide_own, rstd, captions,
    ) = results[GATHERED:]
    all_tokens = SHARE * own
    back_all = back_all.reshape(all_tokens, D)
    ffn_mid, unit = ffn_mid.reshape(all_tokens, -1), unit.reshape(all_tokens, -1)
    captions = captions[:, 0].astype(jnp.int32)
    inputs = tokens.astype(F32)
    unit_one, rstd_one = norm_stats(inputs)

    down_rows, up_grad_low, wide_terms, ffn_in_grad, *carry = ffn_back(
        back_all, back_turned, ffn_mid, down_full, up_full, unit, slope, wide_own[0], rstd
    )

    up_rows, grad_q, grad_k, grad_v, hidden_cols, hidden_grad, norm_grads, *carry = attention_back(
        ffn_turned,
        up_grad_low,
        queries,
        keys_low,
        values_low,
        ffn_in_grad,
        hidden,
        back_all,
        mixed_own,
        out_full,
        small_vals,
        captions,
        tables,
        carry,
    )
    attn_rows_out, normed_grad, block_sum = project_back(
        normed_turned,
        context_turned,
        [hidden_cols, grad_q, grad_k, grad_v],
        ffn_mid,
        [query_full, key_full, value_full],
        down_full,
        carry,
    )
    block_out = (hidden + block_sum).astype(BF)
    input_part, gain_one, bias_one = norm_back(unit_one, rstd_one, small_vals[0], normed_grad)
    input_grad = hidden_grad + input_part

    def spread_columns(value, whole):
        return lax.dynamic_update_slice(
            jnp.zeros((value.shape[0], whole), F32), value, (0, me * value.shape[1])
        ).reshape(-1, D)

    moments = jnp.concatenate(
        [spread_columns(wide_moment, FF), spread_columns(small_moment, D)], axis=0
    )
    vector_squares = jnp.pad(
        jnp.concatenate([jnp.sum(item * item, axis=1) for item in (wide_norms, small_norms)]),
        (12, 128 - 20),
    )[None]
    row_old = jnp.pad(
        jnp.stack([up_row, down_row] + [attn_row[j] for j in range(4)], axis=1), ((0, 0), (0, 122))
    )
    col_old = jnp.concatenate([up_col.reshape(-1, D), down_col.reshape(-1, D), attn_col], axis=0)
    sources = [down_rows, up_rows, attn_rows_out]
    finished = [(k, c) for k, item in enumerate(sources) for c in range(item.shape[1])]
    per_ff, per_proj = FF // SHARE // REDUCE_COLS, width // REDUCE_COLS
    down_places, up_places = finished[:per_ff], finished[per_ff : 2 * per_ff]
    attn_places = [
        finished[2 * per_ff + c * per_proj : 2 * per_ff + (c + 1) * per_proj] for c in (1, 2, 3, 0)
    ]
    row_new, results = update(
        [up_places, down_places] + attn_places,
        sources,
        [up_weight, down_weight, attn_weight],
        row_old,
        col_old,
        wide_terms,
        jnp.concatenate([gain_one[None], bias_one[None], norm_grads[2:6]], axis=0),
        moments,
        vector_squares,
    )
    (
        up_grad, down_grad, attn_grad, up_new, down_new, attn_new, up_copy, down_copy, attn_copy,
        col_new, vectors,
    ) = results
    vectors = vectors.reshape(3, -1, D)
    wide_parts = take_block(vectors[:, : 2 * WIDE].reshape(6, FF), me, wide_width, 1)
    wide_parts = wide_parts.reshape(3, 2, wide_width)
    small_parts = take_block(vectors[:, 2 * WIDE :].reshape(18, D), me, small_width, 1)
    small_parts = small_parts.reshape(3, 6, small_width)
    return (
        block_out,
        input_grad,
        attn_grad,
        up_grad,
        down_grad,
        row_new[:, 2:6].T,
        col_new[2 * WIDE :],
        row_new[:, 0],
        col_new[:WIDE].reshape(FF),
        row_new[:, 1],
        col_new[WIDE : 2 * WIDE].reshape(FF),
        attn_new,
        up_new,
        down_new,
        attn_copy,
        up_copy,
        down_copy,
        small_parts[0],
        wide_parts[0],
        small_parts[1],
        wide_parts[1],
        small_norms - small_parts[2],
        wide_norms - wide_parts[2],
    )


def solution(mesh):
    placed = (
        P("dp", None),
        P("dp", None),
        P("dp"),
        P("dp", None, None),
        P("dp", None),
        P("dp", None),
        P(None, "dp"),
        P(None, "dp"),
        P(None, "dp"),
        P(),
        P("dp"),
        P(),
        P("dp"),
        P(),
        P(None, "dp"),
        P(None, "dp"),
    )
    return jax.shard_map(
        per_device,
        mesh=mesh,
        in_specs=placed,
        out_specs=(
            P("dp", None),
            P("dp", None),
            P("dp", None, None),
            P("dp", None),
            P("dp", None),
            P(None, "dp"),
            P(),
            P("dp"),
            P(),
            P("dp"),
            P(),
            P("dp", None, None),
            P("dp", None),
            P("dp", None),
            P("dp", None, None),
            P("dp", None),
            P("dp", None),
            P(None, "dp"),
            P(None, "dp"),
            P(None, "dp"),
            P(None, "dp"),
            P(None, "dp"),
            P(None, "dp"),
        ),
        check_vma=False,
    )
```

```python
from functools import partial
import math

import jax
import jax.numpy as jnp
from jax import lax
from jax.experimental import pallas as pl
from jax.experimental.pallas import tpu as pltpu
from jax.sharding import PartitionSpec as P

D = 2048
FF = 8192
HEADS = 32
L = 128
IMG = 64
SHARE = 4


EPS_NORM = 1e-05
EPS_SQUARE = 1e-30
EPS_SCALE = 0.001
DECAY_RATE = 0.5
CLIP_LEVEL = 0.5
LEARN_RATE = 0.8
SCALE_BASE = 512.0
MASK_FILL = -1e30

BF = jnp.bfloat16
F32 = jnp.float32


def dot_f32(left, right, left_dim, right_dim):
    return lax.dot_general(
        left, right, (((left_dim,), (right_dim,)), ((), ())), preferred_element_type=F32
    )


def group_masks():
    count = lax.axis_size("dp")
    masks = []
    mask = 2 * SHARE
    while mask < count:
        masks.append(mask)
        mask *= 2
    if count > SHARE:
        masks.append(SHARE)
    return masks


def take_block(value, index, width, axis):
    return lax.dynamic_slice_in_dim(value, index * width, width, axis)


def xpos_tables(head_size, head_count):
    slot_pos = jnp.arange(L, dtype=F32)[:, None]
    pair_idx = jnp.arange(head_size // 2, dtype=F32)[None, :]
    theta = jnp.exp(-(2.0 * pair_idx / head_size) * jnp.log(10000.0))
    angle = slot_pos * theta
    zeta = (2.0 * pair_idx / head_size + 0.4) / 1.4
    power_table = jnp.exp(jnp.log(zeta) * slot_pos / SCALE_BASE)

    def widen(table):
        return jnp.tile(jnp.repeat(table, 2, axis=1), (1, head_count))

    cosine, sine, power = widen(jnp.cos(angle)), widen(jnp.sin(angle)), widen(power_table)
    return cosine * power, sine * power, cosine / power, sine / power


def quarter_turn(values):
    width = values.shape[1]
    lane = lax.broadcasted_iota(jnp.int32, values.shape, 1)
    return jnp.where(
        lane % 2 == 0, -pltpu.roll(values, width - 1, 1), pltpu.roll(values, 1, 1)
    )


def masked_probs(query, key, caption, head_size):
    scores = dot_f32(query, key, 1, 1) * (1.0 / math.sqrt(head_size))
    row = lax.broadcasted_iota(jnp.int32, scores.shape, 0)
    col = lax.broadcasted_iota(jnp.int32, scores.shape, 1)
    scores = jnp.where((col <= row) & (col < IMG + caption), scores, MASK_FILL)
    terms = jnp.exp(scores - jnp.max(scores, axis=-1, keepdims=True))
    return terms / jnp.sum(terms, axis=-1, keepdims=True)


def attention_back_block(head_size, caption, q_low, k_low, v_low, g_low, tables):
    cq, sq, ck, sk = tables
    grads_q, grads_k, grads_v = [], [], []
    for head in range(q_low.shape[1] // head_size):
        at = slice(head * head_size, (head + 1) * head_size)
        probs = masked_probs(q_low[:, at], k_low[:, at], caption, head_size)
        grads_v.append(dot_f32(probs.astype(BF), g_low[:, at], 0, 0))
        prob_grad = dot_f32(g_low[:, at], v_low[:, at], 1, 1)
        score_grad = probs * (prob_grad - jnp.sum(probs * prob_grad, axis=-1, keepdims=True))
        score_low = (score_grad * (1.0 / math.sqrt(head_size))).astype(BF)
        grads_q.append(dot_f32(score_low, k_low[:, at], 1, 0))
        grads_k.append(dot_f32(score_low, q_low[:, at], 0, 0))
    grad_q = jnp.concatenate(grads_q, axis=1)
    grad_k = jnp.concatenate(grads_k, axis=1)
    return (
        (grad_q * cq - quarter_turn(grad_q) * sq).astype(BF),
        (grad_k * ck - quarter_turn(grad_k) * sk).astype(BF),
        jnp.concatenate(grads_v, axis=1).astype(BF),
    )


MESH = pl.DeviceIdType.MESH
KERNEL_VMEM = 62 * 1024 * 1024


def flipped(index, mask):
    bit = 1
    while bit <= mask:
        if mask & bit:
            index = index + bit - 2 * bit * ((index // bit) % 2)
        bit *= 2
    return index


def partner_masks():
    return list(range(1, SHARE)) + group_masks()


class Wire:
    def __init__(self):
        self.me = lax.axis_index("dp")
        self.member = self.me % SHARE

    def meet(self, more=()):
        barrier = pltpu.get_barrier_semaphore()
        masks = partner_masks() + list(more)
        for mask in masks:
            pl.semaphore_signal(
                barrier, inc=1, device_id=(flipped(self.me, mask),), device_id_type=MESH
            )
        pl.semaphore_wait(barrier, len(masks))

    def copy(self, source, target, send_sem, recv_sem, mask):
        return pltpu.make_async_remote_copy(
            src_ref=source,
            dst_ref=target,
            send_sem=send_sem,
            recv_sem=recv_sem,
            device_id=(flipped(self.me, mask),),
            device_id_type=MESH,
        )


def row_tiles(rows, body, tile=256):
    tile = min(tile, rows)

    @pl.loop(0, rows // tile)
    def _(index):
        body(pl.multiple_of(index * tile, tile), tile)


class Reducer:
    @staticmethod
    def plan(count, resumed, stopped):
        stages = len(group_masks())
        carried = min(2, stages - 1)
        resume, stop = [0] * count, [stages] * count
        if resumed:
            resume = list(range(carried, 0, -1)) + [0] * count
        stop = [stages] * len(resume)
        if stopped:
            stop[len(stop) - carried :] = range(carried, 0, -1)
        return resume, stop

    @staticmethod
    def carry_shapes(cols):
        carried = min(2, len(group_masks()) - 1)
        return [jax.ShapeDtypeStruct((D >> at, cols), F32) for at in range(carried, 0, -1)]

    @staticmethod
    def scratch(plan, cols):
        resume, stop = plan
        stages = len(group_masks())
        halves = [D >> (stage + 1) for stage in range(stages)]
        block = D >> stages
        count = len(resume)
        used = [
            sum(first <= stage < last for first, last in zip(resume, stop))
            for stage in range(stages)
        ]
        return (
            [
                pltpu.VMEM((2 if stage else REDUCE_AHEAD, half, cols), BF)
                for stage, half in enumerate(halves)
            ]
            + [pltpu.VMEM((number, half, cols), BF) for number, half in zip(used, halves)]
            + [
                pltpu.VMEM((min(stages, count), D // 2, cols), F32),
                pltpu.VMEM((2, block, cols), BF),
                pltpu.SemaphoreType.DMA((count, stages)),
                pltpu.SemaphoreType.DMA((count, stages)),
                pltpu.SemaphoreType.DMA((count, SHARE)),
                pltpu.SemaphoreType.DMA((count, SHARE)),
                pltpu.SemaphoreType.DMA((count,)),
            ]
        )

    @staticmethod
    def out_shape(plan, cols):
        stages = len(group_masks())
        block = D >> stages
        finished = sum(last == stages for last in plan[1])
        return jax.ShapeDtypeStruct((SHARE, finished, block // SHARE, cols), BF)

    def __init__(self, wire, plan, terms, out, refs, carry_in=(), carry_out=()):
        self.wire, self.out = wire, out
        self.resume, self.stop = plan
        self.count = len(self.resume)
        self.terms = [None] * (self.count - len(terms)) + list(terms)
        self.carry_in, self.carry_out = carry_in, carry_out
        self.masks = group_masks()[::-1]
        self.stages = len(self.masks)
        self.slots = min(self.stages, self.count)
        self.sends, refs = refs[: self.stages], refs[self.stages :]
        self.recvs, refs = refs[: self.stages], refs[self.stages :]
        (
            self.kept, self.done, self.send_sem, self.recv_sem, self.out_send, self.out_recv,
            self.carry_sem,
        ) = refs
        self.block = D >> self.stages
        self.low = (wire.me // SHARE) % 2

    def goes(self, chunk, stage):
        return 0 <= chunk < self.count and self.resume[chunk] <= stage < self.stop[chunk]

    def got(self, chunk, stage):
        first = min(c for c in range(self.count) if self.goes(c, stage))
        return self.recvs[stage].at[chunk - first]

    def finishes(self, chunk):
        return 0 <= chunk < self.count and self.stop[chunk] == self.stages

    def carry_load(self, chunk):
        ref = self.carry_in[chunk]
        return pltpu.make_async_copy(
            ref,
            self.kept.at[chunk % self.slots, pl.ds(0, ref.shape[0]), :],
            self.carry_sem.at[chunk],
        )

    def carry_store(self, chunk):
        ref = self.carry_out[chunk - (self.count - len(self.carry_out))]
        return pltpu.make_async_copy(
            self.kept.at[chunk % self.slots, pl.ds(0, ref.shape[0]), :],
            ref,
            self.carry_sem.at[chunk],
        )

    def load(self):
        for chunk in range(len(self.carry_in)):
            self.carry_load(chunk).start()

    def begin(self):
        first = self.resume.index(0)
        for chunk in range(first, first + REDUCE_AHEAD):
            self.start(chunk)
            if chunk == first:
                for at in range(first):
                    self.tick(at, start=False)
        if first == 0:
            self.keep(0)

    def half_bit(self, stage):
        return (self.wire.me // self.masks[stage]) % 2

    def lhs_row(self, row, tile, low):
        block = row // self.block
        return pl.multiple_of((2 * block + low) * self.block + row % self.block, tile)

    def copy(self, chunk, stage):
        return self.wire.copy(
            self.sends[stage].at[chunk % self.sends[stage].shape[0]],
            self.got(chunk, stage),
            self.send_sem.at[chunk, stage],
            self.recv_sem.at[chunk, stage],
            self.masks[stage],
        )

    def start(self, chunk):
        if not self.goes(chunk, 0):
            return
        slot = chunk % REDUCE_AHEAD
        if self.goes(chunk - REDUCE_AHEAD, 0):
            self.copy(chunk - REDUCE_AHEAD, 0).wait_send()
        lhs, rhs, cols = self.terms[chunk]
        half = D // 2

        def body(row, tile):
            at = pl.ds(self.lhs_row(row, tile, 1 - self.low), tile)
            self.sends[0][slot, pl.ds(row, tile), :] = dot_f32(
                lhs[at, :], rhs[:, cols], 1, 0
            ).astype(BF)

        row_tiles(half, body, self.block)
        self.copy(chunk, 0).start()

    def keep(self, chunk):
        if not self.goes(chunk, 0):
            return
        lhs, rhs, cols = self.terms[chunk]

        def body(row, tile):
            at = pl.ds(self.lhs_row(row, tile, self.low), tile)
            self.kept[chunk % self.slots, pl.ds(row, tile), :] = dot_f32(
                lhs[at, :], rhs[:, cols], 1, 0
            )

        row_tiles(D // 2, body, self.block)

    def step(self, chunk, stage):
        if not 0 <= chunk < self.count or not self.resume[chunk] <= stage <= self.stop[chunk]:
            return
        half = D >> (stage + 1)
        kept = self.kept
        slot = chunk % self.slots
        got = None
        if stage > self.resume[chunk]:
            self.copy(chunk, stage - 1).wait_recv()
            got = self.got(chunk, stage - 1)
        else:
            self.carry_load(chunk).wait()

        def value(at):
            if got is None:
                return kept[slot, at, :]
            return kept[slot, at, :] + got[at, :].astype(F32)

        if stage == self.stop[chunk]:

            def whole(row, tile):
                at = pl.ds(row, tile)
                kept[slot, at, :] = value(at)

            row_tiles(2 * half, whole)
            self.carry_store(chunk).start()
            return
        if self.goes(chunk - 2, stage):
            self.copy(chunk - 2, stage).wait_send()
        send = self.sends[stage]
        bit = self.half_bit(stage)

        def out_half(row, tile):
            at = pl.ds(pl.multiple_of((1 - bit) * half + row, tile), tile)
            send[chunk % 2, pl.ds(row, tile), :] = value(at).astype(BF)

        def own_half(row, tile):
            at = pl.ds(pl.multiple_of(bit * half + row, tile), tile)
            kept[slot, pl.ds(row, tile), :] = value(at)

        row_tiles(half, out_half)
        self.copy(chunk, stage).start()
        row_tiles(half, own_half)

    def place(self, chunk):
        return sum(self.finishes(c) for c in range(chunk))

    def give(self, chunk):
        part = self.block // SHARE
        slot = chunk % 2
        copies = []
        for j in range(1, SHARE):
            to = flipped(self.wire.member, j)
            copies.append(
                self.wire.copy(
                    self.done.at[slot, pl.ds(pl.multiple_of(to * part, part), part), :],
                    self.out.at[j, self.place(chunk)],
                    self.out_send.at[chunk, j],
                    self.out_recv.at[chunk, j],
                    j,
                )
            )
        own = pltpu.make_async_copy(
            self.done.at[slot, pl.ds(pl.multiple_of(self.wire.member * part, part), part), :],
            self.out.at[0, self.place(chunk)],
            self.out_send.at[chunk, 0],
        )
        return own, copies

    def given(self, chunk):
        own, copies = self.give(chunk)
        own.wait()
        for item in copies:
            item.wait_send()

    def finish(self, chunk):
        if not self.finishes(chunk):
            return
        self.copy(chunk, self.stages - 1).wait_recv()
        if self.finishes(chunk - 2):
            self.given(chunk - 2)
        got = self.got(chunk, self.stages - 1)
        slot = chunk % self.slots

        def body(row, tile):
            at = pl.ds(row, tile)
            self.done[chunk % 2, at, :] = (
                self.kept[slot, at, :] + got[at, :].astype(F32)
            ).astype(BF)

        row_tiles(self.block, body)
        own, copies = self.give(chunk)
        own.start()
        for item in copies:
            item.start()

    def tick(self, at, start=True):
        for stage in range(1, self.stages):
            self.step(at - stage + 1, stage)
            if stage == 1 and start:
                self.start(at + REDUCE_AHEAD)
        if self.stages == 1:
            self.start(at + REDUCE_AHEAD)
        self.finish(at - self.stages + 1)
        self.keep(at + 1)

    def ticks(self):
        return self.count + self.stages - 1

    def close(self):
        for stage in range(self.stages):
            slots = self.sends[stage].shape[0]
            for chunk in [c for c in range(self.count) if self.goes(c, stage)][-slots:]:
                self.copy(chunk, stage).wait_send()
        finished = [c for c in range(self.count) if self.finishes(c)]
        for chunk in finished[-2:]:
            self.given(chunk)
        for chunk in finished:
            for item in self.give(chunk)[1]:
                item.wait_recv()
        for chunk in range(self.count - len(self.carry_out), self.count):
            self.carry_store(chunk).wait()


class OwnerSum:
    @staticmethod
    def scratch(own):
        return [
            pltpu.VMEM((2 * own, D), BF),
            pltpu.VMEM((own, D), BF),
            pltpu.SemaphoreType.DMA((4,)),
        ]

    def __init__(self, wire, own, send, kept, refs):
        self.wire, self.own, self.send, self.kept = wire, own, send, kept
        self.near, self.far, self.sems = refs

    def core_copy(self):
        return self.wire.copy(
            self.send.at[pl.ds(0, 2 * self.own), :],
            self.near,
            self.sems.at[0],
            self.sems.at[1],
            1,
        )

    def far_copy(self):
        return self.wire.copy(
            self.send.at[pl.ds(2 * self.own, self.own), :],
            self.far,
            self.sems.at[2],
            self.sems.at[3],
            2,
        )

    def first(self, term):
        for place, block in enumerate((3, 1)):

            def body(row, tile, place=place, block=block):
                self.send[pl.ds(place * self.own + row, tile), :] = term(block, row, tile).astype(BF)

            row_tiles(self.own, body)
        self.core_copy().start()

    def second(self, term):
        for place, block in enumerate((2, 0)):

            def body(row, tile, place=place, block=block):
                self.kept[pl.ds((1 - place) * self.own + row, tile), :] = term(block, row, tile)

            row_tiles(self.own, body)

    def third(self):
        self.core_copy().wait_recv()
        own = self.own

        def far(row, tile):
            self.send[pl.ds(2 * own + row, tile), :] = (
                self.kept[pl.ds(own + row, tile), :] + self.near[pl.ds(row, tile), :].astype(F32)
            ).astype(BF)

        def near(row, tile):
            at = pl.ds(row, tile)
            self.kept[at, :] = self.kept[at, :] + self.near[pl.ds(own + row, tile), :].astype(F32)

        row_tiles(own, far)
        self.far_copy().start()
        row_tiles(own, near)

    def last(self):
        self.far_copy().wait_recv()

        def body(row, tile):
            at = pl.ds(row, tile)
            self.kept[at, :] = self.kept[at, :] + self.far[at, :].astype(F32)

        row_tiles(self.own, body)
        self.core_copy().wait_send()
        self.far_copy().wait_send()


REDUCE_CHUNKS = 4
REDUCE_COLS = 256
REDUCE_AHEAD = 4


def ffn_back_kernel(own, back, back_t, mid, down, up, unit_in, slope_in, gain, rstd, *refs):
    width = mid.shape[1]
    tokens = SHARE * own
    cols = width // REDUCE_CHUNKS
    chunks = width // REDUCE_COLS
    pieces = len(down)
    out, up_low_out, wide_out, sum_out = refs[:4]
    refs = refs[4:]
    plan = Reducer.plan(chunks, False, True)
    carried = len(Reducer.carry_shapes(REDUCE_COLS))
    carry_out, refs = refs[:carried], refs[carried:]
    wire = Wire()
    count = len(Reducer.scratch(plan, REDUCE_COLS))
    reducer_refs, refs = refs[:count], refs[count:]
    sum_refs, refs = refs[:3], refs[3:]
    (
        back_v, back_tv, mid_v, weight, unit, slope, grad, sums, stat_send, stat_recv,
        load_sem, stat_sems, store_sem,
    ) = refs

    def weight_copies(parts, first):
        step = width // pieces
        return [
            pltpu.make_async_copy(
                part, weight.at[:, pl.ds(k * step, step)], load_sem.at[first + k]
            )
            for k, part in enumerate(parts)
        ]

    loads = [
        pltpu.make_async_copy(source, target, load_sem.at[k])
        for k, (source, target) in enumerate(
            [(back_t, back_tv), (mid, mid_v), (back, back_v), (unit_in, unit), (slope_in, slope)]
        )
    ]
    down_loads = weight_copies(down, 5)
    up_loads = weight_copies(up, 5 + pieces)
    for item in loads[:3] + down_loads + loads[3:]:
        item.start()
    wire.meet()
    reducer = Reducer(
        wire,
        plan,
        [(back_tv, mid_v, pl.ds(c * REDUCE_COLS, REDUCE_COLS)) for c in range(chunks)],
        out,
        reducer_refs,
        carry_out=carry_out,
    )
    loads[0].wait()
    loads[1].wait()
    reducer.begin()

    wide_out[...] = jnp.zeros_like(wide_out)
    sums[...] = jnp.zeros_like(sums)

    def token_tiles(body):
        row_tiles(tokens, body, own)

    def first_pass(k):
        at_cols = pl.ds(k * cols, cols)

        def body(row, tile):
            at = pl.ds(row, tile)
            value = dot_f32(back_v[at, :], weight[:, at_cols], 1, 0)
            grad[at, at_cols] = value
            part = unit[at, at_cols].astype(F32)
            scaled = value * gain[:, at_cols]
            lane = lax.broadcasted_iota(jnp.int32, (tile, sums.shape[1]), 1)
            sums[at, :] += jnp.where(
                lane == 0,
                jnp.sum(scaled, axis=1, keepdims=True),
                jnp.sum(scaled * part, axis=1, keepdims=True),
            )
            wide_out[0:1, at_cols] += jnp.sum(value * part, axis=0, keepdims=True)
            wide_out[1:2, at_cols] += jnp.sum(value, axis=0, keepdims=True)

        token_tiles(body)

    loads[2].wait()
    for item in down_loads:
        item.wait()
    loads[3].wait()
    loads[4].wait()
    for k in range(REDUCE_CHUNKS):
        first_pass(k)
    for item in up_loads:
        item.start()

    stats = [
        wire.copy(
            stat_send, stat_recv.at[j - 1], stat_sems.at[0, j - 1], stat_sems.at[1, j - 1], j
        )
        for j in range(1, SHARE)
    ]
    for j in range(SHARE):
        stat_send[j] = sums[pl.ds(j * own, own), :].T[0:8, :]
    for item in stats:
        item.start()
    reducer.tick(0)
    reducer.tick(1)
    for item in stats:
        item.wait_recv()
    for j in range(SHARE):
        total = stat_send[j]
        for k in range(1, SHARE):
            total = total + stat_recv[k - 1, j ^ k]
        total = total * (1.0 / (SHARE * width))
        sums[pl.ds(j * own, own), :] = jnp.concatenate([total] * (sums.shape[1] // 8), axis=0).T
    for item in stats:
        item.wait_send()

    def second_pass(k):
        at_cols = pl.ds(k * cols, cols)

        def body(row, tile):
            at = pl.ds(row, tile)
            act_grad = rstd[at, 0:1] * (
                grad[at, at_cols] * gain[:, at_cols]
                - sums[at, 0:1]
                - unit[at, at_cols].astype(F32) * sums[at, 1:2]
            )
            unit[at, at_cols] = (act_grad * slope[at, at_cols].astype(F32)).astype(BF)

        token_tiles(body)

    for k in range(REDUCE_CHUNKS):
        second_pass(k)
    store = pltpu.make_async_copy(unit, up_low_out, store_sem.at[0])
    store.start()
    reducer.tick(2)
    reducer.tick(3)
    for item in up_loads:
        item.wait()

    def term(block, row, tile):
        return dot_f32(unit[pl.ds(block * own + row, tile), :], weight[...], 1, 1)

    owner = OwnerSum(wire, own, slope, grad, sum_refs)
    owner.first(term)
    owner.second(term)
    owner.third()
    for at in range(4, reducer.ticks()):
        reducer.tick(at)
    owner.last()
    result = pltpu.make_async_copy(grad.at[pl.ds(0, own), :], sum_out, store_sem.at[1])
    result.start()
    reducer.close()
    store.wait()
    result.wait()


def ffn_back(back, back_t, mid, down, up, unit, slope, gain, rstd):
    tokens, width = mid.shape
    own = tokens // SHARE
    cols = REDUCE_COLS
    lanes = 128
    any_spec = pl.BlockSpec(memory_space=pl.ANY)
    vmem = pl.BlockSpec(memory_space=pltpu.VMEM)
    pieces = len(down)
    plan = Reducer.plan(width // cols, False, True)
    carry = Reducer.carry_shapes(cols)

    def kernel(back, back_t, mid, *refs):
        down, up, refs = refs[:pieces], refs[pieces : 2 * pieces], refs[2 * pieces :]
        ffn_back_kernel(own, back, back_t, mid, down, up, *refs)

    return pl.pallas_call(
        kernel,
        in_specs=[any_spec] * (5 + 2 * pieces) + [vmem] * 2,
        out_specs=[any_spec, any_spec, vmem, any_spec] + [any_spec] * len(carry),
        out_shape=[
            Reducer.out_shape(plan, cols),
            jax.ShapeDtypeStruct((tokens, width), BF),
            jax.ShapeDtypeStruct((8, width), F32),
            jax.ShapeDtypeStruct((own, D), F32),
        ]
        + carry,
        scratch_shapes=Reducer.scratch(plan, cols)
        + OwnerSum.scratch(own)
        + [
            pltpu.VMEM((tokens, D), BF),
            pltpu.VMEM((D, tokens), BF),
            pltpu.VMEM((tokens, width), BF),
            pltpu.VMEM((D, width), BF),
            pltpu.VMEM((tokens, width), BF),
            pltpu.VMEM((tokens, width), BF),
            pltpu.VMEM((tokens, width), F32),
            pltpu.VMEM((tokens, lanes), F32),
            pltpu.VMEM((SHARE, 8, own), F32),
            pltpu.VMEM((SHARE - 1, SHARE, 8, own), F32),
            pltpu.SemaphoreType.DMA((5 + 2 * pieces,)),
            pltpu.SemaphoreType.DMA((2, SHARE - 1)),
            pltpu.SemaphoreType.DMA((2,)),
        ],
        compiler_params=pltpu.CompilerParams(
            collective_id=1, has_side_effects=True, vmem_limit_bytes=KERNEL_VMEM
        ),
        name="ffn_back",
    )(
        back,
        back_t,
        mid,
        *down,
        *up,
        unit,
        slope,
        gain[None],
        rstd,
    )


def attention_back_kernel(
    head_size, own, left_t, right, q_in, k_in, v_in, ffn_grad, hidden, back, mixed_in, out_full,
    small, cap, cq, sq, ck, sk, *refs
):
    width = q_in.shape[1]
    chunks = right.shape[1] // REDUCE_COLS
    plan = Reducer.plan(chunks, True, True)
    carried = len(Reducer.carry_shapes(REDUCE_COLS))
    carry_in, refs = refs[:carried], refs[carried:]
    out, q_out, k_out, v_out, hidden_out, grad_out, norm_out = refs[:7]
    refs = refs[7:]
    carry_out, refs = refs[:carried], refs[carried:]
    wire = Wire()
    count = len(Reducer.scratch(plan, REDUCE_COLS))
    reducer_refs, refs = refs[:count], refs[count:]
    (
        left_v, right_v, q_v, k_v, v_v, mixed_cols, hidden_cols, grad, state, back_v, mixed_v,
        weight, low, mixed, load_sem, turn_sem, weight_sem, store_sem,
    ) = refs
    loads = [
        pltpu.make_async_copy(source, target, load_sem.at[k])
        for k, (source, target) in enumerate(
            [
                (left_t, left_v),
                (right, right_v),
                (ffn_grad, grad),
                (hidden, state),
                (back.at[pl.ds(0, own), :], back_v),
                (mixed_in, mixed_v),
                (q_in, q_v),
                (k_in, k_v),
                (v_in, v_v),
            ]
        )
    ]
    for item in loads:
        item.start()
    wire.meet()
    reducer = Reducer(
        wire,
        plan,
        [(left_v, right_v, pl.ds(c * REDUCE_COLS, REDUCE_COLS)) for c in range(chunks)],
        out,
        reducer_refs,
        carry_in,
        carry_out,
    )
    reducer.load()
    loads[0].wait()
    loads[1].wait()
    reducer.begin()

    def fetch(t):
        return pltpu.make_async_copy(out_full.at[t], weight.at[t % 2], weight_sem.at[t % 2])

    fetch(0).start()
    for item in loads[2:6]:
        item.wait()
    norm_out[...] = jnp.zeros_like(norm_out)

    def norm_back_rows(value, upstream, gain_row):
        center = value - jnp.mean(value, axis=-1, keepdims=True)
        rstd = lax.rsqrt(jnp.mean(center * center, axis=-1, keepdims=True) + EPS_NORM)
        unit = center * rstd
        scaled = upstream * small[gain_row : gain_row + 1, :]
        lean = jnp.mean(scaled, axis=-1, keepdims=True)
        slope = jnp.mean(scaled * unit, axis=-1, keepdims=True)
        norm_out[gain_row : gain_row + 1, :] += jnp.sum(upstream * unit, axis=0, keepdims=True)
        norm_out[gain_row + 1 : gain_row + 2, :] += jnp.sum(upstream, axis=0, keepdims=True)
        return rstd * (scaled - lean - unit * slope)

    def hidden_rows(row, tile):
        at = pl.ds(row, tile)
        value = back_v[at, :].astype(F32) + norm_back_rows(state[at, :], grad[at, :], 4)
        grad[at, :] = value
        low[at, :] = value.astype(BF)

    row_tiles(own, hidden_rows, 64)
    grad_store = pltpu.make_async_copy(grad, grad_out, store_sem.at[0])
    grad_store.start()

    def turn(source, target, sems):
        copies = []
        for j in range(1, SHARE):
            to = pl.multiple_of(flipped(wire.member, j) * width, width)
            copies.append(
                wire.copy(
                    source.at[:, pl.ds(to, width)],
                    target.at[pl.ds(j * own, own), :],
                    sems.at[0, j],
                    sems.at[1, j],
                    j,
                )
            )
        here = pl.multiple_of(wire.member * width, width)
        local = pltpu.make_async_copy(
            source.at[:, pl.ds(here, width)], target.at[pl.ds(0, own), :], sems.at[0, 0]
        )
        for item in copies + [local]:
            item.start()
        return copies, local

    def turned(copies, local):
        local.wait()
        for item in copies:
            item.wait_recv()

    for t in range(SHARE):
        fetch(t).wait()
        if t + 1 < SHARE:
            fetch(t + 1).start()
        part = dot_f32(
            low[:, pl.ds(t * width, width)], weight[t % 2].reshape(D, width), 1, 1
        )
        state[...] = part if t == 0 else state[...] + part

    reducer.tick(carried)

    def mixed_rows(row, tile):
        at = pl.ds(row, tile)
        value = jnp.concatenate([mixed_v[t, at, :].astype(F32) for t in range(SHARE)], axis=1)
        mixed[at, :] = norm_back_rows(value, state[at, :], 2).astype(BF)

    row_tiles(own, mixed_rows, 64)
    mixed_turn = turn(mixed, mixed_cols, turn_sem.at[0])
    hidden_turn = turn(low, hidden_cols, turn_sem.at[1])
    reducer.tick(carried + 1)
    turned(*mixed_turn)
    for item in loads[6:]:
        item.wait()
    row_count = SHARE * own // L

    def rows(first, last):
        @pl.loop(first, last)
        def _(row):
            at = pl.ds(pl.multiple_of(row * L, L), L)
            got = attention_back_block(
                head_size,
                cap[row],
                q_v[at, :],
                k_v[at, :],
                v_v[at, :],
                mixed_cols[at, :],
                (cq[...], sq[...], ck[...], sk[...]),
            )
            q_v[at, :], k_v[at, :], v_v[at, :] = got

    parts = 4
    for part in range(parts):
        rows(part * row_count // parts, (part + 1) * row_count // parts)
        if part < parts - 1:
            reducer.tick(carried + 2 + part)
    stores = [
        pltpu.make_async_copy(source, target, load_sem.at[k])
        for k, (source, target) in enumerate([(q_v, q_out), (k_v, k_out), (v_v, v_out)])
    ]
    for item in stores:
        item.start()
    turned(*hidden_turn)
    stores.append(pltpu.make_async_copy(hidden_cols, hidden_out, load_sem.at[3]))
    stores[-1].start()
    for at in range(carried + 1 + parts, reducer.ticks()):
        reducer.tick(at)
    reducer.close()
    for item in stores + [grad_store]:
        item.wait()
    for item in mixed_turn[0] + hidden_turn[0]:
        item.wait_send()


def attention_back(
    left_t, right, queries, keys, values, ffn_grad, hidden, back, mixed, out_full, small, captions,
    tables, carry_in,
):
    tokens, width = queries.shape
    own = tokens // SHARE
    cols = REDUCE_COLS
    any_spec = pl.BlockSpec(memory_space=pl.ANY)
    vmem = pl.BlockSpec(memory_space=pltpu.VMEM)
    part = jax.ShapeDtypeStruct((tokens, width), BF)
    plan = Reducer.plan(right.shape[1] // cols, True, True)
    carry = Reducer.carry_shapes(cols)
    return pl.pallas_call(
        partial(attention_back_kernel, D // HEADS, own),
        in_specs=[any_spec] * 10
        + [vmem]
        + [pl.BlockSpec(memory_space=pltpu.SMEM)]
        + [vmem] * 4
        + [any_spec] * len(carry),
        out_specs=[any_spec] * 6 + [vmem] + [any_spec] * len(carry),
        out_shape=[Reducer.out_shape(plan, cols)]
        + [part] * 4
        + [jax.ShapeDtypeStruct((own, D), F32), jax.ShapeDtypeStruct((8, D), F32)]
        + carry,
        scratch_shapes=Reducer.scratch(plan, cols)
        + [pltpu.VMEM((D, tokens), BF), pltpu.VMEM(right.shape, BF)]
        + [pltpu.VMEM((tokens, width), BF)] * 5
        + [pltpu.VMEM((own, D), F32)] * 2
        + [
            pltpu.VMEM((own, D), BF),
            pltpu.VMEM(mixed.shape, BF),
            pltpu.VMEM((2,) + out_full.shape[1:], BF),
            pltpu.VMEM((own, D), BF),
            pltpu.VMEM((own, D), BF),
            pltpu.SemaphoreType.DMA((9,)),
            pltpu.SemaphoreType.DMA((2, 2, SHARE)),
            pltpu.SemaphoreType.DMA((2,)),
            pltpu.SemaphoreType.DMA((1,)),
        ],
        compiler_params=pltpu.CompilerParams(
            collective_id=2, has_side_effects=True, vmem_limit_bytes=KERNEL_VMEM
        ),
        name="attention_back",
    )(
        left_t,
        right,
        queries,
        keys,
        values,
        ffn_grad,
        hidden,
        back,
        mixed,
        out_full,
        small,
        captions,
        *tables,
        *carry_in,
    )


def project_back_kernel(own, normed_t, context_t, *refs):
    parts, refs = refs[:4], refs[4:]
    mid, weights, refs = refs[0], refs[1:4], refs[4:]
    pieces = REDUCE_CHUNKS
    down, refs = refs[:pieces], refs[pieces:]
    width = parts[0].shape[1]
    split = width // REDUCE_COLS
    plan = Reducer.plan(4 * split, True, False)
    carried = len(Reducer.carry_shapes(REDUCE_COLS))
    carry_in, refs = refs[:carried], refs[carried:]
    tokens, small, grad_in, hidden, refs = refs[0], refs[1], refs[2], refs[3], refs[4:]
    out, grad_out, block_out, norm_out = refs[:4]
    refs = refs[4:]
    wire = Wire()
    count = len(Reducer.scratch(plan, REDUCE_COLS))
    reducer_refs, refs = refs[:count], refs[count:]
    grad_refs, refs = refs[:3], refs[3:]
    block_refs, refs = refs[:3], refs[3:]
    normed_v, context_v, parts_v, mid_v, weight, send, kept, state, load_sem, store_sem = refs
    state_loads = [
        pltpu.make_async_copy(source, state, store_sem.at[2 + k])
        for k, source in enumerate((grad_in, hidden))
    ]
    state_loads[0].start()
    loads = [
        pltpu.make_async_copy(source, target, load_sem.at[k])
        for k, (source, target) in enumerate(
            [
                (context_t, context_v),
                (parts[0], parts_v.at[0]),
                (normed_t, normed_v),
                (parts[1], parts_v.at[1]),
                (parts[2], parts_v.at[2]),
                (parts[3], parts_v.at[3]),
                (mid, mid_v),
            ]
            + [(item, weight.at[:, pl.ds(k * width, width)]) for k, item in enumerate(weights)]
        )
    ]
    for item in loads:
        item.start()
    wire.meet()
    reducer = Reducer(
        wire,
        plan,
        [
            (normed_v if k else context_v, parts_v.at[k], pl.ds(c * REDUCE_COLS, REDUCE_COLS))
            for k in range(4)
            for c in range(split)
        ],
        out,
        reducer_refs,
        carry_in,
    )
    reducer.load()
    for item in loads[:4]:
        item.wait()
    reducer.begin()
    for item in loads[4:]:
        item.wait()

    def grad_term(block, row, tile):
        at = pl.ds(block * own + row, tile)
        return sum(
            dot_f32(parts_v[1 + k, at, :], weight[:, pl.ds(k * width, width)], 1, 1)
            for k in range(3)
        )

    grad_sum = OwnerSum(wire, own, send, kept, grad_refs)
    grad_sum.first(grad_term)
    grad_sum.second(grad_term)
    step = mid.shape[1] // pieces
    down_loads = [
        pltpu.make_async_copy(part, weight.at[:, pl.ds(k * step, step)], load_sem.at[10 + k])
        for k, part in enumerate(down)
    ]
    for item in down_loads:
        item.start()
    reducer.tick(carried)
    reducer.tick(carried + 1)
    grad_sum.third()
    for item in down_loads:
        item.wait()
    reducer.tick(carried + 2)
    reducer.tick(carried + 3)
    grad_sum.last()
    state_loads[0].wait()
    norm_out[...] = jnp.zeros_like(norm_out)

    def input_rows(row, tile):
        at = pl.ds(row, tile)
        value, upstream = tokens[at, :].astype(F32), kept[at, :]
        center = value - jnp.mean(value, axis=-1, keepdims=True)
        rstd = lax.rsqrt(jnp.mean(center * center, axis=-1, keepdims=True) + EPS_NORM)
        unit = center * rstd
        scaled = upstream * small[0:1, :]
        lean = jnp.mean(scaled, axis=-1, keepdims=True)
        slope = jnp.mean(scaled * unit, axis=-1, keepdims=True)
        norm_out[0:1, :] += jnp.sum(upstream * unit, axis=0, keepdims=True)
        norm_out[1:2, :] += jnp.sum(upstream, axis=0, keepdims=True)
        kept[at, :] = state[at, :] + rstd * (scaled - lean - unit * slope)

    row_tiles(own, input_rows, 64)
    state_loads[1].start()
    grad_store = pltpu.make_async_copy(kept.at[pl.ds(0, own), :], grad_out, store_sem.at[0])
    grad_store.start()

    def block_term(block, row, tile):
        at = pl.ds(block * own + row, tile)
        return dot_f32(mid_v[at, :], weight[...], 1, 1)

    block_sum = OwnerSum(wire, own, send, kept, block_refs)
    block_sum.first(block_term)
    reducer.tick(carried + 4)
    grad_store.wait()
    block_sum.second(block_term)
    block_sum.third()
    late = reducer.ticks() - 3
    for at in range(carried + 5, late):
        reducer.tick(at)
    block_sum.last()
    state_loads[1].wait()

    def block_rows(row, tile):
        at = pl.ds(row, tile)
        send[at, :] = (kept[at, :] + state[at, :]).astype(BF)

    row_tiles(own, block_rows, 64)
    block_store = pltpu.make_async_copy(send.at[pl.ds(0, own), :], block_out, store_sem.at[1])
    block_store.start()
    for at in range(late, reducer.ticks()):
        reducer.tick(at)
    reducer.close()
    block_store.wait()


def project_back(
    normed_t, context_t, parts, mid, weights, down, carry_in, inputs, small, grad, hidden
):
    tokens, width = parts[0].shape
    own = tokens // SHARE
    any_spec = pl.BlockSpec(memory_space=pl.ANY)
    vmem = pl.BlockSpec(memory_space=pltpu.VMEM)
    part = jax.ShapeDtypeStruct((own, D), F32)
    plan = Reducer.plan(4 * width // REDUCE_COLS, True, False)
    return pl.pallas_call(
        partial(project_back_kernel, own),
        in_specs=[any_spec] * (10 + len(down) + len(carry_in)) + [vmem] * 2 + [any_spec] * 2,
        out_specs=[any_spec] * 3 + [vmem],
        out_shape=[
            Reducer.out_shape(plan, REDUCE_COLS),
            part,
            jax.ShapeDtypeStruct((own, D), BF),
            jax.ShapeDtypeStruct((8, D), F32),
        ],
        scratch_shapes=Reducer.scratch(plan, REDUCE_COLS)
        + OwnerSum.scratch(own)
        + OwnerSum.scratch(own)
        + [
            pltpu.VMEM((D, tokens), BF),
            pltpu.VMEM((D, tokens), BF),
            pltpu.VMEM((4, tokens, width), BF),
            pltpu.VMEM(mid.shape, BF),
            pltpu.VMEM((D, mid.shape[1]), BF),
            pltpu.VMEM((3 * own, D), BF),
            pltpu.VMEM((2 * own, D), F32),
            pltpu.VMEM((own, D), F32),
            pltpu.SemaphoreType.DMA((10 + len(down),)),
            pltpu.SemaphoreType.DMA((4,)),
        ],
        compiler_params=pltpu.CompilerParams(
            collective_id=3, has_side_effects=True, vmem_limit_bytes=KERNEL_VMEM
        ),
        name="project_back",
    )(
        normed_t, context_t, *parts, mid, *weights, *down, *carry_in, inputs, small, grad, hidden
    )


def sum_over_devices(wire, total, whole, got, send_sem, recv_sem):
    rows, cols = total.shape
    row, col = 0, 0
    regions = []
    for stage in range(len(got)):
        mask = 1 << stage
        bit = (wire.me // mask) % 2
        regions.append((row, col, rows, cols))
        if rows > 8:
            rows //= 2
            away = (pl.multiple_of(row + (1 - bit) * rows, 8), col)
            row = pl.multiple_of(row + bit * rows, 8)
        else:
            cols //= 2
            away = (row, pl.multiple_of(col + (1 - bit) * cols, 128))
            col = pl.multiple_of(col + bit * cols, 128)
        copy = wire.copy(
            total.at[pl.ds(away[0], rows), pl.ds(away[1], cols)],
            got[stage],
            send_sem.at[0, stage],
            recv_sem.at[0, stage],
            mask,
        )
        copy.start()
        copy.wait()
        total[pl.ds(row, rows), pl.ds(col, cols)] += got[stage][...]
    whole[pl.ds(row, rows), pl.ds(col, cols)] = total[pl.ds(row, rows), pl.ds(col, cols)]
    for stage in reversed(range(len(got))):
        part = whole.at[pl.ds(row, rows), pl.ds(col, cols)]
        copy = wire.copy(part, part, send_sem.at[1, stage], recv_sem.at[1, stage], 1 << stage)
        copy.start()
        copy.wait()
        row, col, rows, cols = regions[stage]


WIDE = FF // D
SUM_COLS, SUM_WEIGHTED = 0, 2 * WIDE + 4
SUM_NORMS = 2 * SUM_WEIGHTED
SUM_MOMENTS = SUM_NORMS + 2 * WIDE + 6
SUM_SCALARS = SUM_MOMENTS + 2 * WIDE + 6
SUM_ROWS = 64


def update_matrices(places, tile):
    matrices = []
    for index in range(2):
        pieces = [
            (index * WIDE + t, c * tile, t * D + c * tile, t, place)
            for t in range(SHARE)
            for c, place in enumerate(places[index])
        ]
        matrices.append((index, FF, pieces, tile))
    for j in range(4):
        width = len(places[2 + j]) * tile
        pieces = [
            (2 * WIDE + j, t * width + c * tile, t * width + c * tile, t, place)
            for t in range(SHARE)
            for c, place in enumerate(places[2 + j])
        ]
        matrices.append((2 + j, D, pieces, tile))
    return matrices


def matrix_cols(refs, index, col, size):
    if index < 2:
        return refs[index][:, pl.ds(col, size)]
    return refs[2][:, index - 2, pl.ds(col, size)]


def put_matrix_cols(refs, index, col, size, value):
    if index < 2:
        refs[index][:, pl.ds(col, size)] = value
    else:
        refs[2][:, index - 2, pl.ds(col, size)] = value


def update_sums_kernel(
    places, sources, row_old, wide_terms, small_terms, moments, squares, *refs
):
    row_new, whole, total = refs[:3]
    got, send_sem, recv_sem = refs[3:-2], refs[-2], refs[-1]
    wire = Wire()
    barrier = pltpu.get_barrier_semaphore()
    for stage in range(len(got)):
        pl.semaphore_signal(
            barrier, inc=1, device_id=(flipped(wire.me, 1 << stage),), device_id_type=MESH
        )
    width = sources[0].shape[3]

    def piece_of(member, place):
        return sources[place[0]][flipped(wire.member, member), place[1]].astype(F32)

    total[...] = jnp.zeros_like(total)
    lane = lax.broadcasted_iota(jnp.int32, (1, 128), 1)
    scalars = squares[0:1, :]
    row_lane = lax.broadcasted_iota(jnp.int32, row_new.shape, 1)
    row_all = jnp.zeros(row_new.shape, F32)
    for index, size, pieces, tile in update_matrices(places, width):
        row_sum = jnp.zeros((row_new.shape[0], 1), F32)
        for at, sum_col, col, member, place in pieces:
            value = piece_of(member, place)
            square = value * value
            row_sum += jnp.sum(square, axis=1, keepdims=True)
            total[SUM_COLS + at : SUM_COLS + at + 1, sum_col : sum_col + tile] = jnp.sum(
                square, axis=0, keepdims=True
            )
        moment = DECAY_RATE * row_old[:, index : index + 1] + (1.0 - DECAY_RATE) * (
            row_sum * (1.0 / size) + EPS_SQUARE
        )
        row_all = jnp.where(row_lane == index, moment, row_all)
        inverse = 1.0 / moment
        for at, sum_col, col, member, place in pieces:
            value = piece_of(member, place)
            total[SUM_WEIGHTED + at : SUM_WEIGHTED + at + 1, sum_col : sum_col + tile] = jnp.sum(
                value * value * inverse, axis=0, keepdims=True
            )
        scalars = jnp.where(lane == index, jnp.sum(moment, keepdims=True), scalars)
    row_new[...] = row_all
    for r in range(2):
        for t in range(SHARE):
            at = SUM_NORMS + r * WIDE + t
            total[at : at + 1, :] = jnp.where(wire.member == t, wide_terms[r : r + 1, :], 0.0)
    total[SUM_NORMS + 2 * WIDE : SUM_MOMENTS, :] = small_terms[...]
    total[SUM_MOMENTS:SUM_SCALARS, :] = moments[...]
    total[SUM_SCALARS : SUM_SCALARS + 1, 0:128] = scalars

    pl.semaphore_wait(barrier, len(got))
    sum_over_devices(wire, total, whole, got, send_sem, recv_sem)


def update_kernel(
    places, sources, up_old, down_old, attn_old, row_new, col_old, whole, up_grad, down_grad,
    attn_grad, up_new, down_new, attn_new, up_copy, down_copy, attn_copy, col_new, vectors, scale
):
    mine = lax.axis_index("dp") % SHARE
    width = sources[0].shape[3]
    old, grad = (up_old, down_old, attn_old), (up_grad, down_grad, attn_grad)
    new, low = (up_new, down_new, attn_new), (up_copy, down_copy, attn_copy)
    columns = DECAY_RATE * col_old[...] + (1.0 - DECAY_RATE) * (
        whole[SUM_COLS:SUM_WEIGHTED, :] * (1.0 / D) + EPS_SQUARE
    )
    col_new[...] = columns
    scale[...] = lax.rsqrt(columns)
    ratio = whole[SUM_WEIGHTED:SUM_NORMS, :] / columns

    def scalar(index):
        return whole[SUM_SCALARS : SUM_SCALARS + 1, index : index + 1]

    def step_size(square, weight_square, size):
        upd_rms = jnp.sqrt(square * (1.0 / size))
        weight_rms = jnp.sqrt(weight_square * (1.0 / size))
        return (
            LEARN_RATE
            * jnp.maximum(EPS_SCALE, weight_rms)
            / jnp.maximum(1.0, upd_rms * (1.0 / CLIP_LEVEL))
        )

    for index, size, pieces, tile in update_matrices(places, width):
        first, last = pieces[0][0], pieces[-1][0] + 1
        row_mean = scalar(index) * (1.0 / D)
        square = row_mean * jnp.sum(ratio[first:last, :], keepdims=True)
        factor = step_size(square, scalar(6 + index), D * size)
        row_scale = lax.rsqrt(row_new[:, index : index + 1] / row_mean) * factor
        for at, sum_col, col, member, place in pieces:
            value = sources[place[0]][flipped(mine, member), place[1]].astype(F32)
            put_matrix_cols(grad, index, col, tile, value)
            value = matrix_cols(old, index, col, tile) - value * row_scale * scale[
                at : at + 1, sum_col : sum_col + tile
            ]
            put_matrix_cols(new, index, col, tile, value)
            put_matrix_cols(low, index, col, tile, value.astype(BF))

    count = 2 * WIDE + 6
    grads = whole[SUM_NORMS:SUM_MOMENTS, :]
    moment = DECAY_RATE * whole[SUM_MOMENTS:SUM_SCALARS, :] + (1.0 - DECAY_RATE) * (
        grads * grads + EPS_SQUARE
    )
    scaled = grads * lax.rsqrt(moment)
    vectors[0:count, :] = grads
    vectors[count : 2 * count, :] = moment
    spans = [(r * WIDE, (r + 1) * WIDE) for r in range(2)]
    spans += [(2 * WIDE + r, 2 * WIDE + r + 1) for r in range(6)]
    for r, (first, last) in enumerate(spans):
        part = scaled[first:last, :]
        size = (last - first) * D
        factor = step_size(jnp.sum(part * part, keepdims=True), scalar(12 + r), size)
        vectors[2 * count + first : 2 * count + last, :] = part * factor


def update(places, sources, weights, row_old, col_old, wide_terms, small_terms, moments, squares):
    count = lax.axis_size("dp")
    stages = count.bit_length() - 1
    rows = weights[0].shape[0]
    parts = []
    size = [SUM_ROWS, D]
    for _ in range(stages):
        size[0 if size[0] > 8 else 1] //= 2
        parts.append(pltpu.VMEM(tuple(size), F32))
    vmem = pl.BlockSpec(memory_space=pltpu.VMEM)
    number = len(sources)
    whole_shape = jax.ShapeDtypeStruct((SUM_ROWS, D), F32)

    def sums_kernel(*refs):
        update_sums_kernel(places, refs[:number], *refs[number:])

    def kernel(*refs):
        update_kernel(places, refs[:number], *refs[number:])

    row_new, whole = pl.pallas_call(
        sums_kernel,
        in_specs=[vmem] * (number + 5),
        out_specs=[vmem] * 2,
        out_shape=[jax.ShapeDtypeStruct((rows, 128), F32), whole_shape],
        scratch_shapes=[pltpu.VMEM((SUM_ROWS, D), F32)]
        + parts
        + [pltpu.SemaphoreType.DMA((2, stages)), pltpu.SemaphoreType.DMA((2, stages))],
        compiler_params=pltpu.CompilerParams(
            collective_id=4, has_side_effects=True, vmem_limit_bytes=KERNEL_VMEM
        ),
        name="update_sums",
    )(*sources, row_old, wide_terms, small_terms, moments, squares)
    shapes = [jax.ShapeDtypeStruct(item.shape, kind) for kind in (F32, F32, BF) for item in weights]
    shapes += [
        jax.ShapeDtypeStruct((SUM_WEIGHTED, D), F32),
        jax.ShapeDtypeStruct((3 * (2 * WIDE + 6), D), F32),
    ]
    results = pl.pallas_call(
        kernel,
        in_specs=[vmem] * (number + 6),
        out_specs=[vmem] * len(shapes),
        out_shape=shapes,
        scratch_shapes=[pltpu.VMEM((SUM_WEIGHTED, D), F32)],
        compiler_params=pltpu.CompilerParams(vmem_limit_bytes=KERNEL_VMEM),
        name="update",
    )(*sources, *weights, row_new, col_old, whole)
    return row_new, results


class Share:
    def __init__(self, wire, source, target, sems):
        self.wire, self.source, self.target, self.sems = wire, source, target, sems

    def copies(self):
        parts = [
            (self.source, self.target.at[2], 2),
            (self.source, self.target.at[1], 1),
            (self.target.at[2], self.target.at[3], 1),
        ]
        return [
            self.wire.copy(source, target, self.sems.at[0, k], self.sems.at[1, k], mask)
            for k, (source, target, mask) in enumerate(parts)
        ]

    def start(self):
        far, near, unused = self.copies()
        far.start()
        near.start()

    def forward(self):
        far, unused, last = self.copies()
        far.wait_recv()
        last.start()

    def done(self):
        unused, near, last = self.copies()
        near.wait_recv()
        last.wait_recv()

    def close(self):
        for item in self.copies():
            item.wait_send()


def normalized(value):
    center = value - jnp.mean(value, axis=-1, keepdims=True)
    return center * lax.rsqrt(jnp.mean(center * center, axis=-1, keepdims=True) + EPS_NORM)


def attention_block(head_size, caption, q_low, k_low, v_low):
    mixed = []
    for head in range(q_low.shape[1] // head_size):
        at = slice(head * head_size, (head + 1) * head_size)
        probs = masked_probs(q_low[:, at], k_low[:, at], caption, head_size).astype(BF)
        mixed.append(dot_f32(probs, v_low[:, at], 1, 0))
    return jnp.concatenate(mixed, axis=1).astype(BF)


def vector_rows(count):
    wide = FF // count
    return max(1, wide // 128), min(wide, 128)


GATHERED = 4 + 2 * REDUCE_CHUNKS


def forward_kernel(
    own, tokens, cotangent, live, attn_in, up_in, down_in, vectors, cq, sq, ck, sk, *refs
):
    gathered, refs = refs[:GATHERED], refs[GATHERED:]
    (
        out_full, normed_out, back_out, back_t_out, context_out, ffn_out, mid_out, unit_out,
        slope_out, q_out, k_out, v_out, mixed_out, hidden_out, small, wide, rstd_out, captions, squares,
    ) = refs[:19]
    (
        attn_v, up_v, down_v, pieces, normed, back_v, weight, q_v, k_v, v_v, mixed, mixed_own,
        context, ffn, act, unit, mid, slope, norms, sums, stat_send, stat_recv, load_sem,
        piece_sems, gather_sems, norm_sems, share_sems, turn_sems, stat_sems, weight_sem, store_sem,
        turned, turned_sem,
    ) = refs[19:]
    wire = Wire()
    count = lax.axis_size("dp")
    member, group = wire.member, wire.me // SHARE
    low, high = group % 2, group // 2
    masks = group_masks()
    width = q_v.shape[1]
    step = width
    ff_width = act.shape[1]
    local = attn_v.shape[0]
    head_size = D // HEADS
    rows_each = L

    loads = [
        pltpu.make_async_copy(source, target, load_sem.at[k])
        for k, (source, target) in enumerate(
            [(attn_in, attn_v), (up_in, up_v), (down_in, down_v)]
        )
    ]
    for item in loads:
        item.start()
    norms[wire.me] = vectors[...].astype(BF).astype(F32)
    chain = count == 8 * SHARE
    wire.meet([6 * SHARE] if chain else [])

    def piece_copies(chunk):
        place = gathered[chunk].at[high, low, pl.ds(pl.multiple_of(member * local, local), local), :]
        here = pltpu.make_async_copy(pieces.at[0, chunk], place, piece_sems.at[0, chunk, 0])
        away = [
            wire.copy(
                pieces.at[j, chunk], place, piece_sems.at[0, chunk, j], piece_sems.at[1, chunk, j], j
            )
            for j in range(1, SHARE)
        ]
        return here, away

    def send_pieces(chunk):
        for j in range(SHARE):
            to = flipped(member, j)
            if chunk < 4:
                value = attn_v[:, chunk, pl.ds(pl.multiple_of(to * width, width), width)]
            else:
                source = up_v if chunk < 4 + REDUCE_CHUNKS else down_v
                k = (chunk - 4) % REDUCE_CHUNKS
                value = source[:, pl.ds(pl.multiple_of(to * ff_width + k * step, step), step)]
            pieces[j, chunk] = value.astype(BF)
        here, away = piece_copies(chunk)
        here.start()
        for item in away:
            item.start()

    always = None
    nearby = flipped(wire.me, 1)

    def doubling(chunk):
        buf = gathered[chunk]
        route = []
        for stage, mask in enumerate(masks):
            if stage == len(masks) - 1:
                part = buf.at[:, low]
            else:
                size = 1 << stage
                part = buf.at[pl.ds((high // size) * size, size), low]
            to = flipped(wire.me, mask)
            route.append(([(always, part, to, stage)], [(always, part, stage)]))
        return route

    def chained(chunk):
        buf = gathered[chunk]
        y_first = chunk % 6 == 5
        neighbour = 2 * SHARE

        def part(z):
            return buf.at[z] if y_first else buf.at[z, low]

        hops = []
        for hop in range(1, 4):
            hops.append(
                (
                    [
                        (
                            jnp.logical_and(high >= hop - 1, high < 3),
                            part(high - hop + 1),
                            wire.me + neighbour,
                            hop - 1,
                        ),
                        (
                            jnp.logical_and(high <= 4 - hop, high > 0),
                            part(high + hop - 1),
                            wire.me - neighbour,
                            hop + 2,
                        ),
                    ],
                    [
                        (high >= hop, part(high - hop), hop - 1),
                        (high <= 3 - hop, part(high + hop), hop + 2),
                    ],
                )
            )
        own_part = buf.at[high, low] if y_first else buf.at[:, low]
        across = ([(always, own_part, flipped(wire.me, SHARE), 6)], [(always, own_part, 6)])
        return [across] + hops if y_first else hops + [across]

    route_of = chained if chain else doubling
    stages = 4 if chain else len(masks)
    ahead = stages + 1 if chain else stages

    def where(condition, action):
        if condition is always:
            action()
        else:
            pl.when(condition)(action)

    def moved(chunk, part, to, index):
        return pltpu.make_async_remote_copy(
            src_ref=part,
            dst_ref=part,
            send_sem=gather_sems.at[0, chunk, index],
            recv_sem=gather_sems.at[1, chunk, index],
            device_id=(to,),
            device_id_type=MESH,
        )

    def expect(chunk, stage):
        for condition, part, index in route_of(chunk)[stage][1]:
            where(condition, lambda: moved(chunk, part, nearby, index).wait_recv())

    def launch(chunk, stage):
        if not 0 <= chunk < GATHERED:
            return
        if stage == 0:
            here, away = piece_copies(chunk)
            here.wait()
            for item in away:
                item.wait_recv()
        else:
            expect(chunk, stage - 1)
        for condition, part, to, index in route_of(chunk)[stage][0]:
            where(condition, lambda: moved(chunk, part, to, index).start())

    def advance(at):
        for stage in range(stages):
            launch(at - stage, stage)

    def tick(chunk):
        advance(chunk + ahead)
        expect(chunk, stages - 1)

    norm_stages = count.bit_length() - 1

    def norm_copy(stage):
        size = 1 << stage
        part = norms.at[pl.ds((wire.me // size) * size, size)]
        return wire.copy(part, part, norm_sems.at[0, stage], norm_sems.at[1, stage], size)

    norm_copy(0).start()
    loads[0].wait()
    send_pieces(0)
    for stage in range(1, norm_stages):
        norm_copy(stage - 1).wait_recv()
        norm_copy(stage).start()
        if stage == 1:
            advance(0)
            for chunk in range(1, 4):
                send_pieces(chunk)
        if stage == 3:
            advance(1)
    norm_copy(norm_stages - 1).wait_recv()
    small_cols = D // count
    join = max(1, 128 // small_cols)
    small[...] = jnp.concatenate(
        [
            jnp.concatenate([norms[p * join + i][0:8, 0:small_cols] for i in range(join)], axis=1)
            for p in range(count // join)
        ],
        axis=1,
    )
    wide[...] = jnp.zeros_like(wide)
    per_row, row_cols = vector_rows(count)
    per_quarter = count // SHARE
    for r in range(2):
        got = [
            norms[member * per_quarter + i][8 + r * per_row + k : 9 + r * per_row + k, 0:row_cols]
            for i in range(per_quarter)
            for k in range(per_row)
        ]
        wide[r : r + 1, :] = jnp.concatenate(got, axis=1)
    row_count = SHARE * own // rows_each
    own_count = own // rows_each
    advance(2)
    lane = lax.broadcasted_iota(jnp.int32, (8, 128), 1)
    sub = lax.broadcasted_iota(jnp.int32, (8, 128), 0)
    table = jnp.zeros((8, 128), F32)
    for row in range(row_count):
        j, i = row // own_count, row % own_count
        at = 8 + 2 * per_row
        value = norms[flipped(wire.me, j)][at : at + 1, i : i + 1]
        table = jnp.where((sub == row % 8) & (lane == row // 8), value, table)
    captions[...] = table

    def norm_rows(read, at_gain, write, tile=64):
        def body(row, tile):
            at = pl.ds(row, tile)
            scaled = normalized(read(at)) * small[at_gain : at_gain + 1, :]
            write(at, scaled + small[at_gain + 1 : at_gain + 2, :])

        row_tiles(own, body, tile)

    def write_normed(at, value):
        normed[0, at, :] = value.astype(BF)

    norm_rows(lambda at: tokens[at, :].astype(F32), 0, write_normed)
    share_normed = Share(wire, normed.at[0], normed, share_sems.at[0])
    share_normed.start()
    for at in range(3, stages):
        advance(at)

    def back_rows(row, tile):
        at = pl.ds(row, tile)
        back_v[at, :] = (cotangent[at, :].astype(F32) * live[at, 0:1]).astype(BF)

    row_tiles(own, back_rows, 64)
    back_here = pltpu.make_async_copy(back_v, mid.at[0], store_sem.at[0])
    back_here.start()

    def store_turned(source, target):
        tile = turned.shape[1]

        def copy(row, slot):
            return pltpu.make_async_copy(
                turned.at[slot], target.at[pl.ds(row, tile), :], turned_sem.at[slot]
            )

        @pl.loop(0, D // tile // 2)
        def _(pair):
            for slot in range(2):
                row = pl.multiple_of((2 * pair + slot) * tile, tile)

                @pl.when(pair > 0)
                def _():
                    copy(row, slot).wait()

                for j in range(SHARE):
                    turned[slot, :, pl.ds(j * own, own)] = source[j, :, pl.ds(row, tile)].T
                copy(row, slot).start()

        for slot in range(2):
            copy(0, slot).wait()

    for item in loads[1:]:
        item.wait()
    for chunk in range(4, 4 + REDUCE_CHUNKS):
        send_pieces(chunk)
    for at in range(stages, ahead):
        advance(at)
    share_normed.forward()
    share_back = Share(wire, back_v, mid, share_sems.at[1])
    share_back.start()
    for chunk in range(4 + REDUCE_CHUNKS, GATHERED):
        send_pieces(chunk)

    def fetch(source, slot):
        return pltpu.make_async_copy(source, weight.at[slot], weight_sem.at[slot])

    def block_of(chunk):
        return gathered[chunk]

    def weights_of(slot):
        return weight[slot].reshape(D, step)

    def project(slot, target, cosine, sine):
        @pl.loop(0, SHARE)
        def _(j):
            value = dot_f32(normed[j], weights_of(slot), 1, 0)
            for i in range(own_count):
                part = value[i * rows_each : (i + 1) * rows_each]
                if cosine is not None:
                    part = part * cosine[...] + quarter_turn(part) * sine[...]
                at = pl.ds(pl.multiple_of(j * own + i * rows_each, rows_each), rows_each)
                target[at, :] = part.astype(BF)

    tick(0)
    fetch(block_of(0), 0).start()
    share_normed.done()
    fetch(block_of(0), 0).wait()
    project(0, q_v, cq, sq)
    store_turned(normed, normed_out)
    found = jnp.zeros((8, 128), F32)
    for index in range(6):
        weights = (up_v, down_v)[index][...] if index < 2 else attn_v[:, index - 2, :]
        found = jnp.where(
            (sub == 0) & (lane == 6 + index), jnp.sum(weights * weights, keepdims=True), found
        )
    squares[...] = found
    tick(1)
    fetch(block_of(1), 1).start()
    fetch(block_of(1), 1).wait()
    project(1, k_v, ck, sk)
    share_back.forward()
    tick(2)
    fetch(block_of(2), 0).start()
    fetch(block_of(2), 0).wait()
    project(0, v_v, None, None)

    def attend_loop(first, last):
        @pl.loop(first, last)
        def _(row):
            at = pl.ds(pl.multiple_of(row * rows_each, rows_each), rows_each)
            caption = captions[pl.ds(row, 1), 0:1]
            mixed[at, :] = attention_block(
                head_size, caption, q_v[at, :], k_v[at, :], v_v[at, :]
            )

    attend_loop(0, row_count // 2)
    tick(3)

    def out_copies():
        mine = out_full.at[member]
        far = flipped(member, 2)
        parts = [
            (gathered[3], mine, 2),
            (gathered[3], mine, 1),
            (out_full.at[far], out_full.at[far], 1),
        ]
        return [
            wire.copy(source, target, share_sems.at[4, 0, k], share_sems.at[4, 1, k], mask)
            for k, (source, target, mask) in enumerate(parts)
        ]

    out_here = pltpu.make_async_copy(gathered[3], out_full.at[member], store_sem.at[2])
    out_here.start()
    out_moves = out_copies()
    out_moves[0].start()
    out_moves[1].start()
    attend_loop(row_count // 2, row_count)

    def mixed_copies():
        here = pltpu.make_async_copy(
            mixed.at[pl.ds(0, own), :], mixed_own.at[member], turn_sems.at[0, 0]
        )
        away = [
            wire.copy(
                mixed.at[pl.ds(j * own, own), :],
                mixed_own.at[member],
                turn_sems.at[0, j],
                turn_sems.at[1, j],
                j,
            )
            for j in range(1, SHARE)
        ]
        return here, away

    mixed_here, mixed_away = mixed_copies()
    mixed_here.start()
    for item in mixed_away:
        item.start()
    stores = [
        pltpu.make_async_copy(source, target, store_sem.at[3 + k])
        for k, (source, target) in enumerate([(q_v, q_out), (k_v, k_out), (v_v, v_out)])
    ]
    for item in stores:
        item.start()
    tick(4)
    mixed_here.wait()
    for item in mixed_away:
        item.wait_recv()

    def write_context(at, value):
        context[at, :] = value.astype(BF)

    norm_rows(
        lambda at: jnp.concatenate(
            [mixed_own[t, at, :].astype(F32) for t in range(SHARE)], axis=1
        ),
        2,
        write_context,
    )
    stores.append(pltpu.make_async_copy(mixed_own, mixed_out, store_sem.at[6]))
    stores[-1].start()
    context_here = pltpu.make_async_copy(context, unit.at[0], store_sem.at[7])
    context_here.start()
    back_here.wait()
    share_back.done()
    back_store = pltpu.make_async_copy(mid, back_out, store_sem.at[1])
    back_store.start()
    store_turned(mid, back_t_out)
    tick(5)
    out_moves[0].wait_recv()
    out_moves[2].start()
    share_context = Share(wire, context, unit, share_sems.at[3])
    share_context.start()
    tick(6)
    out_here.wait()
    out_moves[1].wait_recv()
    out_moves[2].wait_recv()
    fetch(out_full.at[0], 0).start()
    for t in range(SHARE):
        fetch(out_full.at[t], t % 2).wait()
        if t + 1 < SHARE:
            fetch(out_full.at[t + 1], (t + 1) % 2).start()
        at = pl.ds(t * width, width)
        hidden_out[:, at] = tokens[:, at].astype(F32) + dot_f32(
            context[...], weights_of(t % 2), 1, 0
        )

    def write_ffn(at, value):
        ffn[0, at, :] = value.astype(BF)

    norm_rows(lambda at: hidden_out[at, :], 4, write_ffn)
    share_ffn = Share(wire, ffn.at[0], ffn, share_sems.at[2])
    share_ffn.start()
    share_context.forward()
    context_here.wait()
    share_context.done()
    store_turned(unit, context_out)
    tick(7)
    share_ffn.forward()
    fetch(block_of(4), 0).start()
    share_ffn.done()
    sums[...] = jnp.zeros_like(sums)

    def widen(k):
        slot = k % 2
        fetch(block_of(4 + k), slot).wait()
        if k + 1 < REDUCE_CHUNKS:
            fetch(block_of(5 + k), 1 - slot).start()
        at_cols = pl.ds(k * step, step)

        @pl.loop(0, SHARE)
        def _(j):
            at = pl.ds(pl.multiple_of(j * own, own), own)
            value = dot_f32(ffn[j], weights_of(slot), 1, 0)
            cdf, density = gelu_parts(value)
            active = value * cdf
            act[at, at_cols] = active
            slope[at, at_cols] = (cdf + value * density).astype(BF)
            sums[at, :] += jnp.broadcast_to(
                jnp.sum(active, axis=1, keepdims=True), (own, sums.shape[1])
            )

    widen(0)
    widen(1)
    tick(8)
    widen(2)
    widen(3)

    def spread_body(row, tile):
        at = pl.ds(row, tile)
        mean = sums[at, 0:1] * (1.0 / ff_width)
        square = jnp.zeros((tile, 1), F32)
        for k in range(REDUCE_CHUNKS):
            center = act[at, pl.ds(k * step, step)] - mean
            square += jnp.sum(center * center, axis=1, keepdims=True)
        lane = lax.broadcasted_iota(jnp.int32, (tile, sums.shape[1]), 1)
        sums[at, :] = jnp.where(lane == 0, mean, square)

    row_tiles(SHARE * own, spread_body)
    for j in range(SHARE):
        stat_send[j] = sums[pl.ds(j * own, own), :].T[0:8, :]
    stats = [
        wire.copy(
            stat_send, stat_recv.at[j - 1], stat_sems.at[0, j - 1], stat_sems.at[1, j - 1], j
        )
        for j in range(1, SHARE)
    ]
    for item in stats:
        item.start()
    stores.append(pltpu.make_async_copy(slope, slope_out, store_sem.at[9]))
    stores[-1].start()
    back_store.wait()
    share_back.close()
    share_context.close()
    tick(9)
    for item in stats:
        item.wait_recv()
    for j in range(SHARE):
        parts = [stat_send[j]] + [stat_recv[k - 1, j ^ k] for k in range(1, SHARE)]
        mean = sum(part[0:1, :] for part in parts) * (1.0 / SHARE)
        square = sum(
            part[1:2, :] + ff_width * (part[0:1, :] - mean) ** 2 for part in parts
        )
        rstd = lax.rsqrt(square * (1.0 / (SHARE * ff_width)) + EPS_NORM)
        sub_all = lax.broadcasted_iota(jnp.int32, (128, own), 0)
        both = jnp.where(sub_all == 0, mean, rstd).T
        sums[pl.ds(j * own, own), :] = both
    rstd_out[...] = jnp.broadcast_to(sums[:, 1:2], rstd_out.shape)

    def finish(k):
        at_cols = pl.ds(k * step, step)

        @pl.loop(0, SHARE)
        def _(j):
            at = pl.ds(pl.multiple_of(j * own, own), own)
            value = (act[at, at_cols] - sums[at, 0:1]) * sums[at, 1:2]
            unit[j, :, at_cols] = value.astype(BF)
            mid[j, :, at_cols] = (value * wide[0:1, at_cols] + wide[1:2, at_cols]).astype(BF)

    finish(0)
    finish(1)
    tick(10)
    finish(2)
    finish(3)
    stores += [
        pltpu.make_async_copy(unit, unit_out, store_sem.at[10]),
        pltpu.make_async_copy(mid, mid_out, store_sem.at[11]),
    ]
    for item in stores[-2:]:
        item.start()
    store_turned(ffn, ffn_out)
    for chunk in range(11, GATHERED):
        tick(chunk)
    for item in stores:
        item.wait()
    for chunk in range(GATHERED):
        for item in piece_copies(chunk)[1]:
            item.wait_send()
        for starts, unused in route_of(chunk):
            for condition, part, to, index in starts:
                where(condition, lambda: moved(chunk, part, to, index).wait_send())
    for stage in range(norm_stages):
        norm_copy(stage).wait_send()
    for item in [share_normed, share_ffn]:
        item.close()
    for item in out_moves + mixed_away + stats:
        item.wait_send()


def forward(tokens, cotangent, live, attn_weight, up_weight, down_weight, vectors, tables):
    count = lax.axis_size("dp")
    own = tokens.shape[0]
    all_tokens = SHARE * own
    width, ff_width = D // SHARE, FF // SHARE
    groups = count // SHARE
    local = D // count
    chunk = (groups // 2, 2, D // groups, width)
    stages = len(group_masks())
    any_spec = pl.BlockSpec(memory_space=pl.ANY)
    vmem = pl.BlockSpec(memory_space=pltpu.VMEM)
    shared = jax.ShapeDtypeStruct((SHARE, own, D), BF)
    across = jax.ShapeDtypeStruct((D, all_tokens), BF)
    wide = jax.ShapeDtypeStruct((SHARE, own, ff_width), BF)
    flat = jax.ShapeDtypeStruct((all_tokens, ff_width), BF)
    part = jax.ShapeDtypeStruct((all_tokens, width), BF)
    norm_stages = count.bit_length() - 1
    return pl.pallas_call(
        partial(forward_kernel, own),
        in_specs=[vmem] * 3 + [any_spec] * 3 + [vmem] * 5,
        out_specs=[any_spec] * (GATHERED + 13) + [vmem] * 6,
        out_shape=[jax.ShapeDtypeStruct(chunk, BF)] * GATHERED
        + [jax.ShapeDtypeStruct((SHARE,) + chunk, BF)]
        + [across, shared, across, across, across]
        + [wide, wide, flat]
        + [part] * 3
        + [
            jax.ShapeDtypeStruct((SHARE, own, width), BF),
            jax.ShapeDtypeStruct((own, D), F32),
            jax.ShapeDtypeStruct((8, D), F32),
            jax.ShapeDtypeStruct((8, ff_width), F32),
            jax.ShapeDtypeStruct((all_tokens, 128), F32),
            jax.ShapeDtypeStruct((8, 128), F32),
            jax.ShapeDtypeStruct((8, 128), F32),
        ],
        scratch_shapes=[
            pltpu.VMEM((local, 4, D), F32),
            pltpu.VMEM((local, FF), F32),
            pltpu.VMEM((local, FF), F32),
            pltpu.VMEM((SHARE, GATHERED, local, width), BF),
            pltpu.VMEM((SHARE, own, D), BF),
            pltpu.VMEM((own, D), BF),
            pltpu.VMEM((2,) + chunk, BF),
            pltpu.VMEM((all_tokens, width), BF),
            pltpu.VMEM((all_tokens, width), BF),
            pltpu.VMEM((all_tokens, width), BF),
            pltpu.VMEM((all_tokens, width), BF),
            pltpu.VMEM((SHARE, own, width), BF),
            pltpu.VMEM((own, D), BF),
            pltpu.VMEM((SHARE, own, D), BF),
            pltpu.VMEM((all_tokens, ff_width), F32),
            pltpu.VMEM((SHARE, own, ff_width), BF),
            pltpu.VMEM((SHARE, own, ff_width), BF),
            pltpu.VMEM((all_tokens, ff_width), BF),
            pltpu.VMEM((count, 16, 128), F32),
            pltpu.VMEM((all_tokens, 128), F32),
            pltpu.VMEM((SHARE, 8, own), F32),
            pltpu.VMEM((SHARE - 1, SHARE, 8, own), F32),
            pltpu.SemaphoreType.DMA((3,)),
            pltpu.SemaphoreType.DMA((2, GATHERED, SHARE)),
            pltpu.SemaphoreType.DMA((2, GATHERED, max(stages, 7))),
            pltpu.SemaphoreType.DMA((2, norm_stages)),
            pltpu.SemaphoreType.DMA((5, 2, 3)),
            pltpu.SemaphoreType.DMA((2, SHARE)),
            pltpu.SemaphoreType.DMA((2, SHARE - 1)),
            pltpu.SemaphoreType.DMA((2,)),
            pltpu.SemaphoreType.DMA((12,)),
            pltpu.VMEM((2, 256, all_tokens), BF),
            pltpu.SemaphoreType.DMA((2,)),
        ],
        compiler_params=pltpu.CompilerParams(
            collective_id=5, has_side_effects=True, vmem_limit_bytes=KERNEL_VMEM
        ),
        name="forward",
    )(tokens, cotangent, live, attn_weight, up_weight, down_weight, vectors, *tables)


def gelu_parts(value):
    cdf = 0.5 * (1.0 + lax.erf(value * math.sqrt(0.5)))
    density = jnp.exp(-0.5 * value * value) * (1.0 / math.sqrt(2.0 * math.pi))
    return cdf, density


def per_device(
    tokens,
    cotangent,
    caption_len,
    attn_weight,
    up_weight,
    down_weight,
    small_norms,
    wide_norms,
    attn_row,
    attn_col,
    up_row,
    up_col,
    down_row,
    down_col,
    small_moment,
    wide_moment,
):
    count = lax.axis_size("dp")
    me = lax.axis_index("dp")
    head_size = D // HEADS
    width = D // SHARE
    own = tokens.shape[0]
    own_rows = caption_len.shape[0]

    small_width = D // count
    wide_width = FF // count
    per_row, row_cols = vector_rows(count)
    vectors = jnp.concatenate(
        [
            jnp.pad(small_norms, ((0, 2), (0, 128 - small_width))),
            jnp.pad(
                wide_norms.reshape(2 * per_row, row_cols),
                ((0, 0), (0, 128 - row_cols)),
            ),
            jnp.pad(caption_len.astype(F32), (0, 128 - own_rows))[None],
            jnp.zeros((7 - 2 * per_row, 128), F32),
        ],
        axis=0,
    )
    slot_index = jnp.arange(L)
    live_mask = (slot_index[None, :] < IMG + caption_len[:, None]).astype(F32).reshape(own)
    tables = xpos_tables(head_size, width // head_size)
    results = forward(
        tokens,
        cotangent,
        jnp.broadcast_to(live_mask[:, None], (own, 128)),
        attn_weight,
        up_weight,
        down_weight,
        vectors,
        tables,
    )
    full = [item.reshape(D, width) for item in results[:GATHERED]]
    query_full, key_full, value_full = full[:3]
    up_full, down_full = full[4 : 4 + REDUCE_CHUNKS], full[4 + REDUCE_CHUNKS :]
    (
        out_full, normed_turned, back_all, back_turned, context_turned, ffn_turned, ffn_mid, unit,
        slope, queries, keys_low, values_low, mixed_own, hidden, small_vals, wide_own, rstd, captions,
        weight_squares,
    ) = results[GATHERED:]
    all_tokens = SHARE * own
    back_all = back_all.reshape(all_tokens, D)
    ffn_mid, unit = ffn_mid.reshape(all_tokens, -1), unit.reshape(all_tokens, -1)
    captions = captions[:, 0].astype(jnp.int32)

    down_rows, up_grad_low, wide_terms, ffn_in_grad, *carry = ffn_back(
        back_all, back_turned, ffn_mid, down_full, up_full, unit, slope, wide_own[0], rstd
    )

    up_rows, grad_q, grad_k, grad_v, hidden_cols, hidden_grad, norm_grads, *carry = attention_back(
        ffn_turned,
        up_grad_low,
        queries,
        keys_low,
        values_low,
        ffn_in_grad,
        hidden,
        back_all,
        mixed_own,
        out_full,
        small_vals,
        captions,
        tables,
        carry,
    )
    attn_rows_out, input_grad, block_out, input_norms = project_back(
        normed_turned,
        context_turned,
        [hidden_cols, grad_q, grad_k, grad_v],
        ffn_mid,
        [query_full, key_full, value_full],
        down_full,
        carry,
        tokens,
        small_vals,
        hidden_grad,
        hidden,
    )

    def spread_columns(value, whole):
        return lax.dynamic_update_slice(
            jnp.zeros((value.shape[0], whole), F32), value, (0, me * value.shape[1])
        ).reshape(-1, D)

    moments = jnp.concatenate(
        [spread_columns(wide_moment, FF), spread_columns(small_moment, D)], axis=0
    )
    vector_squares = jnp.pad(
        jnp.concatenate([jnp.sum(item * item, axis=1) for item in (wide_norms, small_norms)]),
        (12, 128 - 20),
    )[None]
    row_old = jnp.pad(
        jnp.stack([up_row, down_row] + [attn_row[j] for j in range(4)], axis=1), ((0, 0), (0, 122))
    )
    col_old = jnp.concatenate([up_col.reshape(-1, D), down_col.reshape(-1, D), attn_col], axis=0)
    sources = [down_rows, up_rows, attn_rows_out]
    finished = [(k, c) for k, item in enumerate(sources) for c in range(item.shape[1])]
    per_ff, per_proj = FF // SHARE // REDUCE_COLS, width // REDUCE_COLS
    down_places, up_places = finished[:per_ff], finished[per_ff : 2 * per_ff]
    attn_places = [
        finished[2 * per_ff + c * per_proj : 2 * per_ff + (c + 1) * per_proj] for c in (1, 2, 3, 0)
    ]
    row_new, results = update(
        [up_places, down_places] + attn_places,
        sources,
        [up_weight, down_weight, attn_weight],
        row_old,
        col_old,
        wide_terms,
        jnp.concatenate([input_norms[0:2], norm_grads[2:6]], axis=0),
        moments,
        weight_squares + vector_squares,
    )
    (
        up_grad, down_grad, attn_grad, up_new, down_new, attn_new, up_copy, down_copy, attn_copy,
        col_new, vectors,
    ) = results
    vectors = vectors.reshape(3, -1, D)
    wide_parts = take_block(vectors[:, : 2 * WIDE].reshape(6, FF), me, wide_width, 1)
    wide_parts = wide_parts.reshape(3, 2, wide_width)
    small_parts = take_block(vectors[:, 2 * WIDE :].reshape(18, D), me, small_width, 1)
    small_parts = small_parts.reshape(3, 6, small_width)
    return (
        block_out,
        input_grad,
        attn_grad,
        up_grad,
        down_grad,
        row_new[:, 2:6].T,
        col_new[2 * WIDE :],
        row_new[:, 0],
        col_new[:WIDE].reshape(FF),
        row_new[:, 1],
        col_new[WIDE : 2 * WIDE].reshape(FF),
        attn_new,
        up_new,
        down_new,
        attn_copy,
        up_copy,
        down_copy,
        small_parts[0],
        wide_parts[0],
        small_parts[1],
        wide_parts[1],
        small_norms - small_parts[2],
        wide_norms - wide_parts[2],
    )


def solution(mesh):
    placed = (
        P("dp", None),
        P("dp", None),
        P("dp"),
        P("dp", None, None),
        P("dp", None),
        P("dp", None),
        P(None, "dp"),
        P(None, "dp"),
        P(None, "dp"),
        P(),
        P("dp"),
        P(),
        P("dp"),
        P(),
        P(None, "dp"),
        P(None, "dp"),
    )
    return jax.shard_map(
        per_device,
        mesh=mesh,
        in_specs=placed,
        out_specs=(
            P("dp", None),
            P("dp", None),
            P("dp", None, None),
            P("dp", None),
            P("dp", None),
            P(None, "dp"),
            P(),
            P("dp"),
            P(),
            P("dp"),
            P(),
            P("dp", None, None),
            P("dp", None),
            P("dp", None),
            P("dp", None, None),
            P("dp", None),
            P("dp", None),
            P(None, "dp"),
            P(None, "dp"),
            P(None, "dp"),
            P(None, "dp"),
            P(None, "dp"),
            P(None, "dp"),
        ),
        check_vma=False,
    )
```

```python
from functools import partial
import math

import jax
import jax.numpy as jnp
from jax import lax
from jax.experimental import pallas as pl
from jax.experimental.pallas import tpu as pltpu
from jax.sharding import PartitionSpec as P
import numpy as np

D = 2048
FF = 8192
HEADS = 32
L = 128
IMG = 64
SHARE = 4


EPS_NORM = 1e-05
EPS_SQUARE = 1e-30
EPS_SCALE = 0.001
DECAY_RATE = 0.5
CLIP_LEVEL = 0.5
LEARN_RATE = 0.8
SCALE_BASE = 512.0
MASK_FILL = -1e30

BF = jnp.bfloat16
F32 = jnp.float32


def dot_f32(left, right, left_dim, right_dim):
    return lax.dot_general(
        left, right, (((left_dim,), (right_dim,)), ((), ())), preferred_element_type=F32
    )


def group_masks():
    count = lax.axis_size("dp")
    masks = []
    mask = 2 * SHARE
    while mask < count:
        masks.append(mask)
        mask *= 2
    if count > SHARE:
        masks.append(SHARE)
    return masks


def take_block(value, index, width, axis):
    return lax.dynamic_slice_in_dim(value, index * width, width, axis)


def xpos_tables(head_size, head_count):
    slot_pos = np.arange(L, dtype=np.float64)[:, None]
    pair_idx = np.arange(head_size // 2, dtype=np.float64)[None, :]
    angle = slot_pos * 10000.0 ** (-2.0 * pair_idx / head_size)
    zeta = (2.0 * pair_idx / head_size + 0.4) / 1.4
    power = zeta ** (slot_pos / SCALE_BASE)

    def widen(table):
        wide = np.tile(np.repeat(table, 2, axis=1), (1, head_count))
        return jnp.asarray(wide.astype(np.float32))

    cosine, sine = np.cos(angle), np.sin(angle)
    return tuple(
        widen(table) for table in (cosine * power, sine * power, cosine / power, sine / power)
    )


def quarter_turn(values):
    width = values.shape[1]
    lane = lax.broadcasted_iota(jnp.int32, values.shape, 1)
    return jnp.where(
        lane % 2 == 0, -pltpu.roll(values, width - 1, 1), pltpu.roll(values, 1, 1)
    )


def masked_probs(query, key, caption, head_size):
    scores = dot_f32(query, key, 1, 1) * (1.0 / math.sqrt(head_size))
    row = lax.broadcasted_iota(jnp.int32, scores.shape, 0)
    col = lax.broadcasted_iota(jnp.int32, scores.shape, 1)
    scores = jnp.where((col <= row) & (col < IMG + caption), scores, MASK_FILL)
    terms = jnp.exp(scores - jnp.max(scores, axis=-1, keepdims=True))
    return terms / jnp.sum(terms, axis=-1, keepdims=True)


def attention_back_block(head_size, caption, q_low, k_low, v_low, g_low, tables):
    cq, sq, ck, sk = tables
    grads_q, grads_k, grads_v = [], [], []
    for head in range(q_low.shape[1] // head_size):
        at = slice(head * head_size, (head + 1) * head_size)
        probs = masked_probs(q_low[:, at], k_low[:, at], caption, head_size)
        grads_v.append(dot_f32(probs.astype(BF), g_low[:, at], 0, 0))
        prob_grad = dot_f32(g_low[:, at], v_low[:, at], 1, 1)
        score_grad = probs * (prob_grad - jnp.sum(probs * prob_grad, axis=-1, keepdims=True))
        score_low = (score_grad * (1.0 / math.sqrt(head_size))).astype(BF)
        grads_q.append(dot_f32(score_low, k_low[:, at], 1, 0))
        grads_k.append(dot_f32(score_low, q_low[:, at], 0, 0))
    grad_q = jnp.concatenate(grads_q, axis=1)
    grad_k = jnp.concatenate(grads_k, axis=1)
    return (
        (grad_q * cq - quarter_turn(grad_q) * sq).astype(BF),
        (grad_k * ck - quarter_turn(grad_k) * sk).astype(BF),
        jnp.concatenate(grads_v, axis=1).astype(BF),
    )


MESH = pl.DeviceIdType.MESH
KERNEL_VMEM = 62 * 1024 * 1024


def flipped(index, mask):
    bit = 1
    while bit <= mask:
        if mask & bit:
            index = index + bit - 2 * bit * ((index // bit) % 2)
        bit *= 2
    return index


def partner_masks():
    return list(range(1, SHARE)) + group_masks()


class Wire:
    def __init__(self):
        self.me = lax.axis_index("dp")
        self.member = self.me % SHARE

    def meet(self, more=()):
        barrier = pltpu.get_barrier_semaphore()
        masks = partner_masks() + list(more)
        for mask in masks:
            pl.semaphore_signal(
                barrier, inc=1, device_id=(flipped(self.me, mask),), device_id_type=MESH
            )
        pl.semaphore_wait(barrier, len(masks))

    def copy(self, source, target, send_sem, recv_sem, mask):
        return pltpu.make_async_remote_copy(
            src_ref=source,
            dst_ref=target,
            send_sem=send_sem,
            recv_sem=recv_sem,
            device_id=(flipped(self.me, mask),),
            device_id_type=MESH,
        )


def row_tiles(rows, body, tile=256):
    tile = min(tile, rows)

    @pl.loop(0, rows // tile)
    def _(index):
        body(pl.multiple_of(index * tile, tile), tile)


class Reducer:
    @staticmethod
    def plan(count, resumed, stopped):
        stages = len(group_masks())
        carried = min(2, stages - 1)
        resume, stop = [0] * count, [stages] * count
        if resumed:
            resume = list(range(carried, 0, -1)) + [0] * count
        stop = [stages] * len(resume)
        if stopped:
            stop[len(stop) - carried :] = range(carried, 0, -1)
        return resume, stop

    @staticmethod
    def carry_shapes(cols):
        carried = min(2, len(group_masks()) - 1)
        return [jax.ShapeDtypeStruct((D >> at, cols), F32) for at in range(carried, 0, -1)]

    @staticmethod
    def scratch(plan, cols):
        resume, stop = plan
        stages = len(group_masks())
        halves = [D >> (stage + 1) for stage in range(stages)]
        block = D >> stages
        count = len(resume)
        used = [
            sum(first <= stage < last for first, last in zip(resume, stop))
            for stage in range(stages)
        ]
        return (
            [
                pltpu.VMEM((2 if stage else REDUCE_AHEAD, half, cols), BF)
                for stage, half in enumerate(halves)
            ]
            + [pltpu.VMEM((number, half, cols), BF) for number, half in zip(used, halves)]
            + [
                pltpu.VMEM((min(stages, count), D // 2, cols), F32),
                pltpu.VMEM((2, block, cols), BF),
                pltpu.SemaphoreType.DMA((count, stages)),
                pltpu.SemaphoreType.DMA((count, stages)),
                pltpu.SemaphoreType.DMA((count, SHARE)),
                pltpu.SemaphoreType.DMA((count, SHARE)),
                pltpu.SemaphoreType.DMA((count,)),
            ]
        )

    @staticmethod
    def out_shape(plan, cols):
        stages = len(group_masks())
        block = D >> stages
        finished = sum(last == stages for last in plan[1])
        return jax.ShapeDtypeStruct((SHARE, finished, block // SHARE, cols), BF)

    def __init__(self, wire, plan, terms, out, refs, carry_in=(), carry_out=()):
        self.wire, self.out = wire, out
        self.resume, self.stop = plan
        self.count = len(self.resume)
        self.terms = [None] * (self.count - len(terms)) + list(terms)
        self.carry_in, self.carry_out = carry_in, carry_out
        self.masks = group_masks()[::-1]
        self.stages = len(self.masks)
        self.slots = min(self.stages, self.count)
        self.sends, refs = refs[: self.stages], refs[self.stages :]
        self.recvs, refs = refs[: self.stages], refs[self.stages :]
        (
            self.kept, self.done, self.send_sem, self.recv_sem, self.out_send, self.out_recv,
            self.carry_sem,
        ) = refs
        self.block = D >> self.stages
        self.low = (wire.me // SHARE) % 2

    def goes(self, chunk, stage):
        return 0 <= chunk < self.count and self.resume[chunk] <= stage < self.stop[chunk]

    def got(self, chunk, stage):
        first = min(c for c in range(self.count) if self.goes(c, stage))
        return self.recvs[stage].at[chunk - first]

    def finishes(self, chunk):
        return 0 <= chunk < self.count and self.stop[chunk] == self.stages

    def carry_load(self, chunk):
        ref = self.carry_in[chunk]
        return pltpu.make_async_copy(
            ref,
            self.kept.at[chunk % self.slots, pl.ds(0, ref.shape[0]), :],
            self.carry_sem.at[chunk],
        )

    def carry_store(self, chunk):
        ref = self.carry_out[chunk - (self.count - len(self.carry_out))]
        return pltpu.make_async_copy(
            self.kept.at[chunk % self.slots, pl.ds(0, ref.shape[0]), :],
            ref,
            self.carry_sem.at[chunk],
        )

    def load(self):
        for chunk in range(len(self.carry_in)):
            self.carry_load(chunk).start()

    def begin(self):
        first = self.resume.index(0)
        for chunk in range(first, first + REDUCE_AHEAD):
            self.start(chunk)
            if chunk == first:
                for at in range(first):
                    self.tick(at, start=False)
        if first == 0:
            self.keep(0)

    def half_bit(self, stage):
        return (self.wire.me // self.masks[stage]) % 2

    def lhs_row(self, row, tile, low):
        block = row // self.block
        return pl.multiple_of((2 * block + low) * self.block + row % self.block, tile)

    def copy(self, chunk, stage):
        return self.wire.copy(
            self.sends[stage].at[chunk % self.sends[stage].shape[0]],
            self.got(chunk, stage),
            self.send_sem.at[chunk, stage],
            self.recv_sem.at[chunk, stage],
            self.masks[stage],
        )

    def start(self, chunk):
        if not self.goes(chunk, 0):
            return
        slot = chunk % REDUCE_AHEAD
        if self.goes(chunk - REDUCE_AHEAD, 0):
            self.copy(chunk - REDUCE_AHEAD, 0).wait_send()
        lhs, rhs, cols = self.terms[chunk]
        half = D // 2

        def body(row, tile):
            at = pl.ds(self.lhs_row(row, tile, 1 - self.low), tile)
            self.sends[0][slot, pl.ds(row, tile), :] = dot_f32(
                lhs[at, :], rhs[:, cols], 1, 0
            ).astype(BF)

        row_tiles(half, body, self.block)
        self.copy(chunk, 0).start()

    def keep(self, chunk):
        if not self.goes(chunk, 0):
            return
        lhs, rhs, cols = self.terms[chunk]

        def body(row, tile):
            at = pl.ds(self.lhs_row(row, tile, self.low), tile)
            self.kept[chunk % self.slots, pl.ds(row, tile), :] = dot_f32(
                lhs[at, :], rhs[:, cols], 1, 0
            )

        row_tiles(D // 2, body, self.block)

    def step(self, chunk, stage):
        if not 0 <= chunk < self.count or not self.resume[chunk] <= stage <= self.stop[chunk]:
            return
        half = D >> (stage + 1)
        kept = self.kept
        slot = chunk % self.slots
        got = None
        if stage > self.resume[chunk]:
            self.copy(chunk, stage - 1).wait_recv()
            got = self.got(chunk, stage - 1)
        else:
            self.carry_load(chunk).wait()

        def value(at):
            if got is None:
                return kept[slot, at, :]
            return kept[slot, at, :] + got[at, :].astype(F32)

        if stage == self.stop[chunk]:

            def whole(row, tile):
                at = pl.ds(row, tile)
                kept[slot, at, :] = value(at)

            row_tiles(2 * half, whole)
            self.carry_store(chunk).start()
            return
        if self.goes(chunk - 2, stage):
            self.copy(chunk - 2, stage).wait_send()
        send = self.sends[stage]
        bit = self.half_bit(stage)

        def out_half(row, tile):
            at = pl.ds(pl.multiple_of((1 - bit) * half + row, tile), tile)
            send[chunk % 2, pl.ds(row, tile), :] = value(at).astype(BF)

        def own_half(row, tile):
            at = pl.ds(pl.multiple_of(bit * half + row, tile), tile)
            kept[slot, pl.ds(row, tile), :] = value(at)

        row_tiles(half, out_half)
        self.copy(chunk, stage).start()
        row_tiles(half, own_half)

    def place(self, chunk):
        return sum(self.finishes(c) for c in range(chunk))

    def give(self, chunk):
        part = self.block // SHARE
        slot = chunk % 2
        copies = []
        for j in range(1, SHARE):
            to = flipped(self.wire.member, j)
            copies.append(
                self.wire.copy(
                    self.done.at[slot, pl.ds(pl.multiple_of(to * part, part), part), :],
                    self.out.at[j, self.place(chunk)],
                    self.out_send.at[chunk, j],
                    self.out_recv.at[chunk, j],
                    j,
                )
            )
        own = pltpu.make_async_copy(
            self.done.at[slot, pl.ds(pl.multiple_of(self.wire.member * part, part), part), :],
            self.out.at[0, self.place(chunk)],
            self.out_send.at[chunk, 0],
        )
        return own, copies

    def given(self, chunk):
        own, copies = self.give(chunk)
        own.wait()
        for item in copies:
            item.wait_send()

    def finish(self, chunk):
        if not self.finishes(chunk):
            return
        self.copy(chunk, self.stages - 1).wait_recv()
        if self.finishes(chunk - 2):
            self.given(chunk - 2)
        got = self.got(chunk, self.stages - 1)
        slot = chunk % self.slots

        def body(row, tile):
            at = pl.ds(row, tile)
            self.done[chunk % 2, at, :] = (
                self.kept[slot, at, :] + got[at, :].astype(F32)
            ).astype(BF)

        row_tiles(self.block, body)
        own, copies = self.give(chunk)
        own.start()
        for item in copies:
            item.start()

    def tick(self, at, start=True):
        for stage in range(1, self.stages):
            self.step(at - stage + 1, stage)
            if stage == 1 and start:
                self.start(at + REDUCE_AHEAD)
        if self.stages == 1:
            self.start(at + REDUCE_AHEAD)
        self.finish(at - self.stages + 1)
        self.keep(at + 1)

    def ticks(self):
        return self.count + self.stages - 1

    def close(self):
        for stage in range(self.stages):
            slots = self.sends[stage].shape[0]
            for chunk in [c for c in range(self.count) if self.goes(c, stage)][-slots:]:
                self.copy(chunk, stage).wait_send()
        finished = [c for c in range(self.count) if self.finishes(c)]
        for chunk in finished[-2:]:
            self.given(chunk)
        for chunk in finished:
            for item in self.give(chunk)[1]:
                item.wait_recv()
        for chunk in range(self.count - len(self.carry_out), self.count):
            self.carry_store(chunk).wait()


class OwnerSum:
    @staticmethod
    def scratch(own):
        return [
            pltpu.VMEM((2 * own, D), BF),
            pltpu.VMEM((own, D), BF),
            pltpu.SemaphoreType.DMA((4,)),
        ]

    def __init__(self, wire, own, send, kept, refs):
        self.wire, self.own, self.send, self.kept = wire, own, send, kept
        self.near, self.far, self.sems = refs

    def core_copy(self):
        return self.wire.copy(
            self.send.at[pl.ds(0, 2 * self.own), :],
            self.near,
            self.sems.at[0],
            self.sems.at[1],
            1,
        )

    def far_copy(self):
        return self.wire.copy(
            self.send.at[pl.ds(2 * self.own, self.own), :],
            self.far,
            self.sems.at[2],
            self.sems.at[3],
            2,
        )

    def first(self, term):
        for place, block in enumerate((3, 1)):

            def body(row, tile, place=place, block=block):
                self.send[pl.ds(place * self.own + row, tile), :] = term(block, row, tile).astype(BF)

            row_tiles(self.own, body)
        self.core_copy().start()

    def second(self, term):
        for place, block in enumerate((2, 0)):

            def body(row, tile, place=place, block=block):
                self.kept[pl.ds((1 - place) * self.own + row, tile), :] = term(block, row, tile)

            row_tiles(self.own, body)

    def third(self):
        self.core_copy().wait_recv()
        own = self.own

        def far(row, tile):
            self.send[pl.ds(2 * own + row, tile), :] = (
                self.kept[pl.ds(own + row, tile), :] + self.near[pl.ds(row, tile), :].astype(F32)
            ).astype(BF)

        def near(row, tile):
            at = pl.ds(row, tile)
            self.kept[at, :] = self.kept[at, :] + self.near[pl.ds(own + row, tile), :].astype(F32)

        row_tiles(own, far)
        self.far_copy().start()
        row_tiles(own, near)

    def last(self):
        self.far_copy().wait_recv()

        def body(row, tile):
            at = pl.ds(row, tile)
            self.kept[at, :] = self.kept[at, :] + self.far[at, :].astype(F32)

        row_tiles(self.own, body)
        self.core_copy().wait_send()
        self.far_copy().wait_send()


REDUCE_CHUNKS = 4
REDUCE_COLS = 256
REDUCE_AHEAD = 4


def ffn_back_kernel(own, back, back_t, mid, down, up, unit_in, slope_in, gain, rstd, *refs):
    width = mid.shape[1]
    tokens = SHARE * own
    cols = width // REDUCE_CHUNKS
    chunks = width // REDUCE_COLS
    pieces = len(down)
    out, up_low_out, wide_out, sum_out = refs[:4]
    refs = refs[4:]
    plan = Reducer.plan(chunks, False, True)
    carried = len(Reducer.carry_shapes(REDUCE_COLS))
    carry_out, refs = refs[:carried], refs[carried:]
    wire = Wire()
    count = len(Reducer.scratch(plan, REDUCE_COLS))
    reducer_refs, refs = refs[:count], refs[count:]
    sum_refs, refs = refs[:3], refs[3:]
    (
        back_v, back_tv, mid_v, weight, unit, slope, grad, sums, stat_send, stat_recv,
        load_sem, stat_sems, store_sem,
    ) = refs

    def weight_copies(parts, first):
        step = width // pieces
        return [
            pltpu.make_async_copy(
                part, weight.at[:, pl.ds(k * step, step)], load_sem.at[first + k]
            )
            for k, part in enumerate(parts)
        ]

    loads = [
        pltpu.make_async_copy(source, target, load_sem.at[k])
        for k, (source, target) in enumerate(
            [(back_t, back_tv), (mid, mid_v), (back, back_v), (unit_in, unit), (slope_in, slope)]
        )
    ]
    down_loads = weight_copies(down, 5)
    up_loads = weight_copies(up, 5 + pieces)
    for item in loads[:3] + down_loads + loads[3:]:
        item.start()
    wire.meet()
    reducer = Reducer(
        wire,
        plan,
        [(back_tv, mid_v, pl.ds(c * REDUCE_COLS, REDUCE_COLS)) for c in range(chunks)],
        out,
        reducer_refs,
        carry_out=carry_out,
    )
    loads[0].wait()
    loads[1].wait()
    reducer.begin()

    wide_out[...] = jnp.zeros_like(wide_out)
    sums[...] = jnp.zeros_like(sums)

    def token_tiles(body):
        row_tiles(tokens, body, own)

    def first_pass(k):
        at_cols = pl.ds(k * cols, cols)

        def body(row, tile):
            at = pl.ds(row, tile)
            value = dot_f32(back_v[at, :], weight[:, at_cols], 1, 0)
            grad[at, at_cols] = value
            part = unit[at, at_cols].astype(F32)
            scaled = value * gain[0:1, at_cols]
            lane = lax.broadcasted_iota(jnp.int32, (tile, sums.shape[1]), 1)
            sums[at, :] += jnp.where(
                lane == 0,
                jnp.sum(scaled, axis=1, keepdims=True),
                jnp.sum(scaled * part, axis=1, keepdims=True),
            )
            wide_out[0:1, at_cols] += jnp.sum(value * part, axis=0, keepdims=True)
            wide_out[1:2, at_cols] += jnp.sum(value, axis=0, keepdims=True)

        token_tiles(body)

    loads[2].wait()
    for item in down_loads:
        item.wait()
    loads[3].wait()
    loads[4].wait()
    for k in range(REDUCE_CHUNKS):
        first_pass(k)
    for item in up_loads:
        item.start()

    stats = [
        wire.copy(
            stat_send, stat_recv.at[j - 1], stat_sems.at[0, j - 1], stat_sems.at[1, j - 1], j
        )
        for j in range(1, SHARE)
    ]
    for j in range(SHARE):
        stat_send[j] = sums[pl.ds(j * own, own), :].T[0:8, :]
    for item in stats:
        item.start()
    reducer.tick(0)
    reducer.tick(1)
    for item in stats:
        item.wait_recv()
    for j in range(SHARE):
        total = stat_send[j]
        for k in range(1, SHARE):
            total = total + stat_recv[k - 1, j ^ k]
        total = total * (1.0 / (SHARE * width))
        sums[pl.ds(j * own, own), :] = jnp.concatenate([total] * (sums.shape[1] // 8), axis=0).T
    for item in stats:
        item.wait_send()

    def second_pass(k):
        at_cols = pl.ds(k * cols, cols)

        def body(row, tile):
            at = pl.ds(row, tile)
            act_grad = rstd[at, 0:1] * (
                grad[at, at_cols] * gain[0:1, at_cols]
                - sums[at, 0:1]
                - unit[at, at_cols].astype(F32) * sums[at, 1:2]
            )
            unit[at, at_cols] = (act_grad * slope[at, at_cols].astype(F32)).astype(BF)

        token_tiles(body)

    for k in range(REDUCE_CHUNKS):
        second_pass(k)
    store = pltpu.make_async_copy(unit, up_low_out, store_sem.at[0])
    store.start()
    reducer.tick(2)
    reducer.tick(3)
    for item in up_loads:
        item.wait()

    def term(block, row, tile):
        return dot_f32(unit[pl.ds(block * own + row, tile), :], weight[...], 1, 1)

    owner = OwnerSum(wire, own, slope, grad, sum_refs)
    owner.first(term)
    owner.second(term)
    owner.third()
    for at in range(4, reducer.ticks()):
        reducer.tick(at)
    owner.last()
    result = pltpu.make_async_copy(grad.at[pl.ds(0, own), :], sum_out, store_sem.at[1])
    result.start()
    reducer.close()
    store.wait()
    result.wait()


def ffn_back(back, back_t, mid, down, up, unit, slope, gain, rstd):
    tokens, width = mid.shape
    own = tokens // SHARE
    cols = REDUCE_COLS
    lanes = 128
    any_spec = pl.BlockSpec(memory_space=pl.ANY)
    vmem = pl.BlockSpec(memory_space=pltpu.VMEM)
    pieces = len(down)
    plan = Reducer.plan(width // cols, False, True)
    carry = Reducer.carry_shapes(cols)

    def kernel(back, back_t, mid, *refs):
        down, up, refs = refs[:pieces], refs[pieces : 2 * pieces], refs[2 * pieces :]
        ffn_back_kernel(own, back, back_t, mid, down, up, *refs)

    return pl.pallas_call(
        kernel,
        in_specs=[any_spec] * (5 + 2 * pieces) + [vmem] * 2,
        out_specs=[any_spec, any_spec, vmem, any_spec] + [any_spec] * len(carry),
        out_shape=[
            Reducer.out_shape(plan, cols),
            jax.ShapeDtypeStruct((tokens, width), BF),
            jax.ShapeDtypeStruct((8, width), F32),
            jax.ShapeDtypeStruct((own, D), F32),
        ]
        + carry,
        scratch_shapes=Reducer.scratch(plan, cols)
        + OwnerSum.scratch(own)
        + [
            pltpu.VMEM((tokens, D), BF),
            pltpu.VMEM((D, tokens), BF),
            pltpu.VMEM((tokens, width), BF),
            pltpu.VMEM((D, width), BF),
            pltpu.VMEM((tokens, width), BF),
            pltpu.VMEM((tokens, width), BF),
            pltpu.VMEM((tokens, width), F32),
            pltpu.VMEM((tokens, lanes), F32),
            pltpu.VMEM((SHARE, 8, own), F32),
            pltpu.VMEM((SHARE - 1, SHARE, 8, own), F32),
            pltpu.SemaphoreType.DMA((5 + 2 * pieces,)),
            pltpu.SemaphoreType.DMA((2, SHARE - 1)),
            pltpu.SemaphoreType.DMA((2,)),
        ],
        compiler_params=pltpu.CompilerParams(
            collective_id=1, has_side_effects=True, vmem_limit_bytes=KERNEL_VMEM
        ),
        name="ffn_back",
    )(
        back,
        back_t,
        mid,
        *down,
        *up,
        unit,
        slope,
        gain,
        rstd,
    )


def attention_back_kernel(
    head_size, own, left_t, right, q_in, k_in, v_in, ffn_grad, hidden, back, mixed_in, out_full,
    small, cap, cq, sq, ck, sk, *refs
):
    width = q_in.shape[1]
    chunks = right.shape[1] // REDUCE_COLS
    plan = Reducer.plan(chunks, True, True)
    carried = len(Reducer.carry_shapes(REDUCE_COLS))
    carry_in, refs = refs[:carried], refs[carried:]
    out, q_out, k_out, v_out, hidden_out, grad_out, norm_out = refs[:7]
    refs = refs[7:]
    carry_out, refs = refs[:carried], refs[carried:]
    wire = Wire()
    count = len(Reducer.scratch(plan, REDUCE_COLS))
    reducer_refs, refs = refs[:count], refs[count:]
    (
        left_v, right_v, q_v, k_v, v_v, mixed_cols, hidden_cols, grad, state, back_v, mixed_v,
        weight, low, mixed, load_sem, turn_sem, weight_sem, store_sem,
    ) = refs
    loads = [
        pltpu.make_async_copy(source, target, load_sem.at[k])
        for k, (source, target) in enumerate(
            [
                (left_t, left_v),
                (right, right_v),
                (ffn_grad, grad),
                (hidden, state),
                (back.at[pl.ds(0, own), :], back_v),
                (mixed_in, mixed_v),
                (q_in, q_v),
                (k_in, k_v),
                (v_in, v_v),
            ]
        )
    ]
    for item in loads:
        item.start()
    wire.meet()
    reducer = Reducer(
        wire,
        plan,
        [(left_v, right_v, pl.ds(c * REDUCE_COLS, REDUCE_COLS)) for c in range(chunks)],
        out,
        reducer_refs,
        carry_in,
        carry_out,
    )
    reducer.load()
    loads[0].wait()
    loads[1].wait()
    reducer.begin()

    def fetch(t):
        return pltpu.make_async_copy(out_full.at[t], weight.at[t % 2], weight_sem.at[t % 2])

    fetch(0).start()
    for item in loads[2:6]:
        item.wait()
    norm_out[...] = jnp.zeros_like(norm_out)

    def norm_back_rows(value, upstream, gain_row):
        center = value - jnp.mean(value, axis=-1, keepdims=True)
        rstd = lax.rsqrt(jnp.mean(center * center, axis=-1, keepdims=True) + EPS_NORM)
        unit = center * rstd
        scaled = upstream * small[gain_row : gain_row + 1, :]
        lean = jnp.mean(scaled, axis=-1, keepdims=True)
        slope = jnp.mean(scaled * unit, axis=-1, keepdims=True)
        norm_out[gain_row : gain_row + 1, :] += jnp.sum(upstream * unit, axis=0, keepdims=True)
        norm_out[gain_row + 1 : gain_row + 2, :] += jnp.sum(upstream, axis=0, keepdims=True)
        return rstd * (scaled - lean - unit * slope)

    def hidden_rows(row, tile):
        at = pl.ds(row, tile)
        value = back_v[at, :].astype(F32) + norm_back_rows(state[at, :], grad[at, :], 4)
        grad[at, :] = value
        low[at, :] = value.astype(BF)

    row_tiles(own, hidden_rows, 64)
    grad_store = pltpu.make_async_copy(grad, grad_out, store_sem.at[0])
    grad_store.start()

    def turn(source, target, sems):
        copies = []
        for j in range(1, SHARE):
            to = pl.multiple_of(flipped(wire.member, j) * width, width)
            copies.append(
                wire.copy(
                    source.at[:, pl.ds(to, width)],
                    target.at[pl.ds(j * own, own), :],
                    sems.at[0, j],
                    sems.at[1, j],
                    j,
                )
            )
        here = pl.multiple_of(wire.member * width, width)
        local = pltpu.make_async_copy(
            source.at[:, pl.ds(here, width)], target.at[pl.ds(0, own), :], sems.at[0, 0]
        )
        for item in copies + [local]:
            item.start()
        return copies, local

    def turned(copies, local):
        local.wait()
        for item in copies:
            item.wait_recv()

    for t in range(SHARE):
        fetch(t).wait()
        if t + 1 < SHARE:
            fetch(t + 1).start()
        part = dot_f32(
            low[:, pl.ds(t * width, width)], weight[t % 2].reshape(D, width), 1, 1
        )
        state[...] = part if t == 0 else state[...] + part

    reducer.tick(carried)

    def mixed_rows(row, tile):
        at = pl.ds(row, tile)
        value = jnp.concatenate([mixed_v[t, at, :].astype(F32) for t in range(SHARE)], axis=1)
        mixed[at, :] = norm_back_rows(value, state[at, :], 2).astype(BF)

    row_tiles(own, mixed_rows, 64)
    mixed_turn = turn(mixed, mixed_cols, turn_sem.at[0])
    hidden_turn = turn(low, hidden_cols, turn_sem.at[1])
    reducer.tick(carried + 1)
    turned(*mixed_turn)
    for item in loads[6:]:
        item.wait()
    row_count = SHARE * own // L

    def rows(first, last):
        @pl.loop(first, last)
        def _(row):
            at = pl.ds(pl.multiple_of(row * L, L), L)
            got = attention_back_block(
                head_size,
                cap[row],
                q_v[at, :],
                k_v[at, :],
                v_v[at, :],
                mixed_cols[at, :],
                (cq[...], sq[...], ck[...], sk[...]),
            )
            q_v[at, :], k_v[at, :], v_v[at, :] = got

    parts = 4
    for part in range(parts):
        rows(part * row_count // parts, (part + 1) * row_count // parts)
        if part < parts - 1:
            reducer.tick(carried + 2 + part)
    stores = [
        pltpu.make_async_copy(source, target, load_sem.at[k])
        for k, (source, target) in enumerate([(q_v, q_out), (k_v, k_out), (v_v, v_out)])
    ]
    for item in stores:
        item.start()
    turned(*hidden_turn)
    stores.append(pltpu.make_async_copy(hidden_cols, hidden_out, load_sem.at[3]))
    stores[-1].start()
    for at in range(carried + 1 + parts, reducer.ticks()):
        reducer.tick(at)
    reducer.close()
    for item in stores + [grad_store]:
        item.wait()
    for item in mixed_turn[0] + hidden_turn[0]:
        item.wait_send()


def attention_back(
    left_t, right, queries, keys, values, ffn_grad, hidden, back, mixed, out_full, small, captions,
    tables, carry_in,
):
    tokens, width = queries.shape
    own = tokens // SHARE
    cols = REDUCE_COLS
    any_spec = pl.BlockSpec(memory_space=pl.ANY)
    vmem = pl.BlockSpec(memory_space=pltpu.VMEM)
    part = jax.ShapeDtypeStruct((tokens, width), BF)
    plan = Reducer.plan(right.shape[1] // cols, True, True)
    carry = Reducer.carry_shapes(cols)
    return pl.pallas_call(
        partial(attention_back_kernel, D // HEADS, own),
        in_specs=[any_spec] * 10
        + [vmem]
        + [pl.BlockSpec(memory_space=pltpu.SMEM)]
        + [vmem] * 4
        + [any_spec] * len(carry),
        out_specs=[any_spec] * 6 + [vmem] + [any_spec] * len(carry),
        out_shape=[Reducer.out_shape(plan, cols)]
        + [part] * 4
        + [jax.ShapeDtypeStruct((own, D), F32), jax.ShapeDtypeStruct((8, D), F32)]
        + carry,
        scratch_shapes=Reducer.scratch(plan, cols)
        + [pltpu.VMEM((D, tokens), BF), pltpu.VMEM(right.shape, BF)]
        + [pltpu.VMEM((tokens, width), BF)] * 5
        + [pltpu.VMEM((own, D), F32)] * 2
        + [
            pltpu.VMEM((own, D), BF),
            pltpu.VMEM(mixed.shape, BF),
            pltpu.VMEM((2,) + out_full.shape[1:], BF),
            pltpu.VMEM((own, D), BF),
            pltpu.VMEM((own, D), BF),
            pltpu.SemaphoreType.DMA((9,)),
            pltpu.SemaphoreType.DMA((2, 2, SHARE)),
            pltpu.SemaphoreType.DMA((2,)),
            pltpu.SemaphoreType.DMA((1,)),
        ],
        compiler_params=pltpu.CompilerParams(
            collective_id=2, has_side_effects=True, vmem_limit_bytes=KERNEL_VMEM
        ),
        name="attention_back",
    )(
        left_t,
        right,
        queries,
        keys,
        values,
        ffn_grad,
        hidden,
        back,
        mixed,
        out_full,
        small,
        captions,
        *tables,
        *carry_in,
    )


def project_back_kernel(own, normed_t, context_t, *refs):
    parts, refs = refs[:4], refs[4:]
    mid, weights, refs = refs[0], refs[1:4], refs[4:]
    pieces = REDUCE_CHUNKS
    down, refs = refs[:pieces], refs[pieces:]
    width = parts[0].shape[1]
    split = width // REDUCE_COLS
    plan = Reducer.plan(4 * split, True, False)
    carried = len(Reducer.carry_shapes(REDUCE_COLS))
    carry_in, refs = refs[:carried], refs[carried:]
    tokens, small, grad_in, hidden, refs = refs[0], refs[1], refs[2], refs[3], refs[4:]
    out, grad_out, block_out, norm_out = refs[:4]
    refs = refs[4:]
    wire = Wire()
    count = len(Reducer.scratch(plan, REDUCE_COLS))
    reducer_refs, refs = refs[:count], refs[count:]
    grad_refs, refs = refs[:3], refs[3:]
    block_refs, refs = refs[:3], refs[3:]
    normed_v, context_v, parts_v, mid_v, weight, send, kept, state, load_sem, store_sem = refs
    state_loads = [
        pltpu.make_async_copy(source, state, store_sem.at[2 + k])
        for k, source in enumerate((grad_in, hidden))
    ]
    state_loads[0].start()
    loads = [
        pltpu.make_async_copy(source, target, load_sem.at[k])
        for k, (source, target) in enumerate(
            [
                (context_t, context_v),
                (parts[0], parts_v.at[0]),
                (normed_t, normed_v),
                (parts[1], parts_v.at[1]),
                (parts[2], parts_v.at[2]),
                (parts[3], parts_v.at[3]),
                (mid, mid_v),
            ]
            + [(item, weight.at[:, pl.ds(k * width, width)]) for k, item in enumerate(weights)]
        )
    ]
    for item in loads:
        item.start()
    wire.meet()
    reducer = Reducer(
        wire,
        plan,
        [
            (normed_v if k else context_v, parts_v.at[k], pl.ds(c * REDUCE_COLS, REDUCE_COLS))
            for k in range(4)
            for c in range(split)
        ],
        out,
        reducer_refs,
        carry_in,
    )
    reducer.load()
    for item in loads[:4]:
        item.wait()
    reducer.begin()
    for item in loads[4:]:
        item.wait()

    def grad_term(block, row, tile):
        at = pl.ds(block * own + row, tile)
        return sum(
            dot_f32(parts_v[1 + k, at, :], weight[:, pl.ds(k * width, width)], 1, 1)
            for k in range(3)
        )

    grad_sum = OwnerSum(wire, own, send, kept, grad_refs)
    grad_sum.first(grad_term)
    grad_sum.second(grad_term)
    step = mid.shape[1] // pieces
    down_loads = [
        pltpu.make_async_copy(part, weight.at[:, pl.ds(k * step, step)], load_sem.at[10 + k])
        for k, part in enumerate(down)
    ]
    for item in down_loads:
        item.start()
    reducer.tick(carried)
    reducer.tick(carried + 1)
    grad_sum.third()
    for item in down_loads:
        item.wait()
    reducer.tick(carried + 2)
    reducer.tick(carried + 3)
    grad_sum.last()
    state_loads[0].wait()
    norm_out[...] = jnp.zeros_like(norm_out)

    def input_rows(row, tile):
        at = pl.ds(row, tile)
        value, upstream = tokens[at, :].astype(F32), kept[at, :]
        center = value - jnp.mean(value, axis=-1, keepdims=True)
        rstd = lax.rsqrt(jnp.mean(center * center, axis=-1, keepdims=True) + EPS_NORM)
        unit = center * rstd
        scaled = upstream * small[0:1, :]
        lean = jnp.mean(scaled, axis=-1, keepdims=True)
        slope = jnp.mean(scaled * unit, axis=-1, keepdims=True)
        norm_out[0:1, :] += jnp.sum(upstream * unit, axis=0, keepdims=True)
        norm_out[1:2, :] += jnp.sum(upstream, axis=0, keepdims=True)
        kept[at, :] = state[at, :] + rstd * (scaled - lean - unit * slope)

    row_tiles(own, input_rows, 64)
    state_loads[1].start()
    grad_store = pltpu.make_async_copy(kept.at[pl.ds(0, own), :], grad_out, store_sem.at[0])
    grad_store.start()

    def block_term(block, row, tile):
        at = pl.ds(block * own + row, tile)
        return dot_f32(mid_v[at, :], weight[...], 1, 1)

    block_sum = OwnerSum(wire, own, send, kept, block_refs)
    block_sum.first(block_term)
    reducer.tick(carried + 4)
    grad_store.wait()
    block_sum.second(block_term)
    block_sum.third()
    late = reducer.ticks() - 3
    for at in range(carried + 5, late):
        reducer.tick(at)
    block_sum.last()
    state_loads[1].wait()

    def block_rows(row, tile):
        at = pl.ds(row, tile)
        send[at, :] = (kept[at, :] + state[at, :]).astype(BF)

    row_tiles(own, block_rows, 64)
    block_store = pltpu.make_async_copy(send.at[pl.ds(0, own), :], block_out, store_sem.at[1])
    block_store.start()
    for at in range(late, reducer.ticks()):
        reducer.tick(at)
    reducer.close()
    block_store.wait()


def project_back(
    normed_t, context_t, parts, mid, weights, down, carry_in, inputs, small, grad, hidden
):
    tokens, width = parts[0].shape
    own = tokens // SHARE
    any_spec = pl.BlockSpec(memory_space=pl.ANY)
    vmem = pl.BlockSpec(memory_space=pltpu.VMEM)
    part = jax.ShapeDtypeStruct((own, D), F32)
    plan = Reducer.plan(4 * width // REDUCE_COLS, True, False)
    return pl.pallas_call(
        partial(project_back_kernel, own),
        in_specs=[any_spec] * (10 + len(down) + len(carry_in)) + [vmem] * 2 + [any_spec] * 2,
        out_specs=[any_spec] * 3 + [vmem],
        out_shape=[
            Reducer.out_shape(plan, REDUCE_COLS),
            part,
            jax.ShapeDtypeStruct((own, D), BF),
            jax.ShapeDtypeStruct((8, D), F32),
        ],
        scratch_shapes=Reducer.scratch(plan, REDUCE_COLS)
        + OwnerSum.scratch(own)
        + OwnerSum.scratch(own)
        + [
            pltpu.VMEM((D, tokens), BF),
            pltpu.VMEM((D, tokens), BF),
            pltpu.VMEM((4, tokens, width), BF),
            pltpu.VMEM(mid.shape, BF),
            pltpu.VMEM((D, mid.shape[1]), BF),
            pltpu.VMEM((3 * own, D), BF),
            pltpu.VMEM((2 * own, D), F32),
            pltpu.VMEM((own, D), F32),
            pltpu.SemaphoreType.DMA((10 + len(down),)),
            pltpu.SemaphoreType.DMA((4,)),
        ],
        compiler_params=pltpu.CompilerParams(
            collective_id=3, has_side_effects=True, vmem_limit_bytes=KERNEL_VMEM
        ),
        name="project_back",
    )(
        normed_t, context_t, *parts, mid, *weights, *down, *carry_in, inputs, small, grad, hidden
    )


def sum_over_devices(wire, total, whole, got, send_sem, recv_sem):
    rows, cols = total.shape
    row, col = 0, 0
    regions = []
    for stage in range(len(got)):
        mask = 1 << stage
        bit = (wire.me // mask) % 2
        regions.append((row, col, rows, cols))
        if rows > 8:
            rows //= 2
            away = (pl.multiple_of(row + (1 - bit) * rows, 8), col)
            row = pl.multiple_of(row + bit * rows, 8)
        else:
            cols //= 2
            away = (row, pl.multiple_of(col + (1 - bit) * cols, 128))
            col = pl.multiple_of(col + bit * cols, 128)
        copy = wire.copy(
            total.at[pl.ds(away[0], rows), pl.ds(away[1], cols)],
            got[stage],
            send_sem.at[0, stage],
            recv_sem.at[0, stage],
            mask,
        )
        copy.start()
        copy.wait()
        total[pl.ds(row, rows), pl.ds(col, cols)] += got[stage][...]
    whole[pl.ds(row, rows), pl.ds(col, cols)] = total[pl.ds(row, rows), pl.ds(col, cols)]
    for stage in reversed(range(len(got))):
        part = whole.at[pl.ds(row, rows), pl.ds(col, cols)]
        copy = wire.copy(part, part, send_sem.at[1, stage], recv_sem.at[1, stage], 1 << stage)
        copy.start()
        copy.wait()
        row, col, rows, cols = regions[stage]


WIDE = FF // D
SUM_COLS, SUM_WEIGHTED = 0, 2 * WIDE + 4
SUM_NORMS = 2 * SUM_WEIGHTED
SUM_MOMENTS = SUM_NORMS + 2 * WIDE + 6
SUM_SCALARS = SUM_MOMENTS + 2 * WIDE + 6
SUM_ROWS = 64


def update_matrices(places, tile):
    matrices = []
    for index in range(2):
        pieces = [
            (index * WIDE + t, c * tile, t * D + c * tile, t, place)
            for t in range(SHARE)
            for c, place in enumerate(places[index])
        ]
        matrices.append((index, FF, pieces, tile))
    for j in range(4):
        width = len(places[2 + j]) * tile
        pieces = [
            (2 * WIDE + j, t * width + c * tile, t * width + c * tile, t, place)
            for t in range(SHARE)
            for c, place in enumerate(places[2 + j])
        ]
        matrices.append((2 + j, D, pieces, tile))
    return matrices


def matrix_cols(refs, index, col, size):
    if index < 2:
        return refs[index][:, pl.ds(col, size)]
    return refs[2][:, index - 2, pl.ds(col, size)]


def put_matrix_cols(refs, index, col, size, value):
    if index < 2:
        refs[index][:, pl.ds(col, size)] = value
    else:
        refs[2][:, index - 2, pl.ds(col, size)] = value


def update_sums_kernel(
    places, sources, row_old, wide_terms, first_norms, other_norms, moments, squares,
    vector_squares, *refs
):
    row_new, whole, total = refs[:3]
    got, send_sem, recv_sem = refs[3:-2], refs[-2], refs[-1]
    wire = Wire()
    barrier = pltpu.get_barrier_semaphore()
    for stage in range(len(got)):
        pl.semaphore_signal(
            barrier, inc=1, device_id=(flipped(wire.me, 1 << stage),), device_id_type=MESH
        )
    width = sources[0].shape[3]

    def piece_of(member, place):
        return sources[place[0]][flipped(wire.member, member), place[1]].astype(F32)

    total[...] = jnp.zeros_like(total)
    lane = lax.broadcasted_iota(jnp.int32, (1, 128), 1)
    scalars = squares[0:1, :] + vector_squares[0:1, :]
    row_lane = lax.broadcasted_iota(jnp.int32, row_new.shape, 1)
    row_all = jnp.zeros(row_new.shape, F32)
    for index, size, pieces, tile in update_matrices(places, width):
        row_sum = jnp.zeros((row_new.shape[0], 1), F32)
        for at, sum_col, col, member, place in pieces:
            value = piece_of(member, place)
            square = value * value
            row_sum += jnp.sum(square, axis=1, keepdims=True)
            total[SUM_COLS + at : SUM_COLS + at + 1, sum_col : sum_col + tile] = jnp.sum(
                square, axis=0, keepdims=True
            )
        moment = DECAY_RATE * row_old[:, index : index + 1] + (1.0 - DECAY_RATE) * (
            row_sum * (1.0 / size) + EPS_SQUARE
        )
        row_all = jnp.where(row_lane == index, moment, row_all)
        inverse = 1.0 / moment
        for at, sum_col, col, member, place in pieces:
            value = piece_of(member, place)
            total[SUM_WEIGHTED + at : SUM_WEIGHTED + at + 1, sum_col : sum_col + tile] = jnp.sum(
                value * value * inverse, axis=0, keepdims=True
            )
        scalars = jnp.where(lane == index, jnp.sum(moment, keepdims=True), scalars)
    row_new[...] = row_all
    for r in range(2):
        for t in range(SHARE):
            at = SUM_NORMS + r * WIDE + t
            total[at : at + 1, :] = jnp.where(wire.member == t, wide_terms[r : r + 1, :], 0.0)
    first = SUM_NORMS + 2 * WIDE
    total[first : first + 2, :] = first_norms[0:2, :]
    total[first + 2 : SUM_MOMENTS, :] = other_norms[2:6, :]
    total[SUM_MOMENTS:SUM_SCALARS, :] = moments[...]
    total[SUM_SCALARS : SUM_SCALARS + 1, 0:128] = scalars

    pl.semaphore_wait(barrier, len(got))
    sum_over_devices(wire, total, whole, got, send_sem, recv_sem)


def update_kernel(
    places, sources, up_old, down_old, attn_old, row_new, col_old, whole, up_grad, down_grad,
    attn_grad, up_new, down_new, attn_new, up_copy, down_copy, attn_copy, up_cols, down_cols,
    attn_cols, wide_all, small_all, scale
):
    mine = lax.axis_index("dp") % SHARE
    width = sources[0].shape[3]
    old, grad = (up_old, down_old, attn_old), (up_grad, down_grad, attn_grad)
    new, low = (up_new, down_new, attn_new), (up_copy, down_copy, attn_copy)
    columns = DECAY_RATE * col_old[...] + (1.0 - DECAY_RATE) * (
        whole[SUM_COLS:SUM_WEIGHTED, :] * (1.0 / D) + EPS_SQUARE
    )
    up_cols[...] = columns[0:WIDE]
    down_cols[...] = columns[WIDE : 2 * WIDE]
    attn_cols[...] = columns[2 * WIDE :]
    scale[...] = lax.rsqrt(columns)
    ratio = whole[SUM_WEIGHTED:SUM_NORMS, :] / columns

    def scalar(index):
        return whole[SUM_SCALARS : SUM_SCALARS + 1, index : index + 1]

    def step_size(square, weight_square, size):
        upd_rms = jnp.sqrt(square * (1.0 / size))
        weight_rms = jnp.sqrt(weight_square * (1.0 / size))
        return (
            LEARN_RATE
            * jnp.maximum(EPS_SCALE, weight_rms)
            / jnp.maximum(1.0, upd_rms * (1.0 / CLIP_LEVEL))
        )

    for index, size, pieces, tile in update_matrices(places, width):
        first, last = pieces[0][0], pieces[-1][0] + 1
        row_mean = scalar(index) * (1.0 / D)
        square = row_mean * jnp.sum(ratio[first:last, :], keepdims=True)
        factor = step_size(square, scalar(6 + index), D * size)
        row_scale = lax.rsqrt(row_new[:, index : index + 1] / row_mean) * factor
        for at, sum_col, col, member, place in pieces:
            value = sources[place[0]][flipped(mine, member), place[1]].astype(F32)
            put_matrix_cols(grad, index, col, tile, value)
            value = matrix_cols(old, index, col, tile) - value * row_scale * scale[
                at : at + 1, sum_col : sum_col + tile
            ]
            put_matrix_cols(new, index, col, tile, value)
            put_matrix_cols(low, index, col, tile, value.astype(BF))

    grads = whole[SUM_NORMS:SUM_MOMENTS, :]
    moment = DECAY_RATE * whole[SUM_MOMENTS:SUM_SCALARS, :] + (1.0 - DECAY_RATE) * (
        grads * grads + EPS_SQUARE
    )
    scaled = grads * lax.rsqrt(moment)
    wide = 2 * WIDE
    small_all[...] = jnp.zeros_like(small_all)
    for k, value in enumerate((grads, moment)):
        wide_all[k * wide : (k + 1) * wide, :] = value[0:wide]
        small_all[k * 8 : k * 8 + 6, :] = value[wide:]
    for r in range(8):
        first, last = (r * WIDE, (r + 1) * WIDE) if r < 2 else (wide + r - 2, wide + r - 1)
        part = scaled[first:last, :]
        factor = step_size(
            jnp.sum(part * part, keepdims=True), scalar(12 + r), (last - first) * D
        )
        if r < 2:
            wide_all[2 * wide + first : 2 * wide + last, :] = part * factor
        else:
            small_all[14 + r : 15 + r, :] = part * factor


def update(places, sources, weights, row_old, col_old, wide_terms, norms, moments, squares):
    count = lax.axis_size("dp")
    stages = count.bit_length() - 1
    rows = weights[0].shape[0]
    parts = []
    size = [SUM_ROWS, D]
    for _ in range(stages):
        size[0 if size[0] > 8 else 1] //= 2
        parts.append(pltpu.VMEM(tuple(size), F32))
    vmem = pl.BlockSpec(memory_space=pltpu.VMEM)
    number = len(sources)
    whole_shape = jax.ShapeDtypeStruct((SUM_ROWS, D), F32)

    def sums_kernel(*refs):
        update_sums_kernel(places, refs[:number], *refs[number:])

    def kernel(*refs):
        update_kernel(places, refs[:number], *refs[number:])

    row_new, whole = pl.pallas_call(
        sums_kernel,
        in_specs=[vmem] * (number + 7),
        out_specs=[vmem] * 2,
        out_shape=[jax.ShapeDtypeStruct((rows, 128), F32), whole_shape],
        scratch_shapes=[pltpu.VMEM((SUM_ROWS, D), F32)]
        + parts
        + [pltpu.SemaphoreType.DMA((2, stages)), pltpu.SemaphoreType.DMA((2, stages))],
        compiler_params=pltpu.CompilerParams(
            collective_id=4, has_side_effects=True, vmem_limit_bytes=KERNEL_VMEM
        ),
        name="update_sums",
    )(*sources, row_old, wide_terms, *norms, moments, *squares)
    shapes = [jax.ShapeDtypeStruct(item.shape, kind) for kind in (F32, F32, BF) for item in weights]
    shapes += [
        jax.ShapeDtypeStruct((count, D), F32) for count in (WIDE, WIDE, 4, 6 * WIDE, 24)
    ]
    results = pl.pallas_call(
        kernel,
        in_specs=[vmem] * (number + 6),
        out_specs=[vmem] * len(shapes),
        out_shape=shapes,
        scratch_shapes=[pltpu.VMEM((SUM_WEIGHTED, D), F32)],
        compiler_params=pltpu.CompilerParams(vmem_limit_bytes=KERNEL_VMEM),
        name="update",
    )(*sources, *weights, row_new, col_old, whole)
    return row_new, results


class Share:
    def __init__(self, wire, source, target, sems):
        self.wire, self.source, self.target, self.sems = wire, source, target, sems

    def copies(self):
        parts = [
            (self.source, self.target.at[2], 2),
            (self.source, self.target.at[1], 1),
            (self.target.at[2], self.target.at[3], 1),
        ]
        return [
            self.wire.copy(source, target, self.sems.at[0, k], self.sems.at[1, k], mask)
            for k, (source, target, mask) in enumerate(parts)
        ]

    def start(self):
        far, near, unused = self.copies()
        far.start()
        near.start()

    def forward(self):
        far, unused, last = self.copies()
        far.wait_recv()
        last.start()

    def done(self):
        unused, near, last = self.copies()
        near.wait_recv()
        last.wait_recv()

    def close(self):
        for item in self.copies():
            item.wait_send()


def normalized(value):
    center = value - jnp.mean(value, axis=-1, keepdims=True)
    return center * lax.rsqrt(jnp.mean(center * center, axis=-1, keepdims=True) + EPS_NORM)


def attention_block(head_size, caption, q_low, k_low, v_low):
    mixed = []
    for head in range(q_low.shape[1] // head_size):
        at = slice(head * head_size, (head + 1) * head_size)
        probs = masked_probs(q_low[:, at], k_low[:, at], caption, head_size).astype(BF)
        mixed.append(dot_f32(probs, v_low[:, at], 1, 0))
    return jnp.concatenate(mixed, axis=1).astype(BF)


def vector_rows(count):
    wide = FF // count
    return max(1, wide // 128), min(wide, 128)


GATHERED = 4 + 2 * REDUCE_CHUNKS


def forward_kernel(
    own, tokens, cotangent, live, attn_in, up_in, down_in, vectors, cq, sq, ck, sk, *refs
):
    gathered, refs = refs[:GATHERED], refs[GATHERED:]
    (
        out_full, normed_out, back_out, back_t_out, context_out, ffn_out, mid_out, unit_out,
        slope_out, q_out, k_out, v_out, mixed_out, hidden_out, small, wide, rstd_out, captions, squares,
    ) = refs[:19]
    (
        attn_v, up_v, down_v, pieces, normed, back_v, weight, q_v, k_v, v_v, mixed, mixed_own,
        context, ffn, act, unit, mid, slope, norms, sums, stat_send, stat_recv, load_sem,
        piece_sems, gather_sems, norm_sems, share_sems, turn_sems, stat_sems, weight_sem, store_sem,
        turned, turned_sem,
    ) = refs[19:]
    wire = Wire()
    count = lax.axis_size("dp")
    member, group = wire.member, wire.me // SHARE
    low, high = group % 2, group // 2
    masks = group_masks()
    width = q_v.shape[1]
    step = width
    ff_width = act.shape[1]
    local = attn_v.shape[0]
    head_size = D // HEADS
    rows_each = L

    loads = [
        pltpu.make_async_copy(source, target, load_sem.at[k])
        for k, (source, target) in enumerate(
            [(attn_in, attn_v), (up_in, up_v), (down_in, down_v)]
        )
    ]
    for item in loads:
        item.start()
    norms[wire.me] = vectors[...].astype(BF).astype(F32)
    chain = count == 8 * SHARE
    wire.meet([6 * SHARE] if chain else [])

    def piece_copies(chunk):
        place = gathered[chunk].at[high, low, pl.ds(pl.multiple_of(member * local, local), local), :]
        here = pltpu.make_async_copy(pieces.at[0, chunk], place, piece_sems.at[0, chunk, 0])
        away = [
            wire.copy(
                pieces.at[j, chunk], place, piece_sems.at[0, chunk, j], piece_sems.at[1, chunk, j], j
            )
            for j in range(1, SHARE)
        ]
        return here, away

    def send_pieces(chunk):
        for j in range(SHARE):
            to = flipped(member, j)
            if chunk < 4:
                value = attn_v[:, chunk, pl.ds(pl.multiple_of(to * width, width), width)]
            else:
                source = up_v if chunk < 4 + REDUCE_CHUNKS else down_v
                k = (chunk - 4) % REDUCE_CHUNKS
                value = source[:, pl.ds(pl.multiple_of(to * ff_width + k * step, step), step)]
            pieces[j, chunk] = value.astype(BF)
        here, away = piece_copies(chunk)
        here.start()
        for item in away:
            item.start()

    always = None
    nearby = flipped(wire.me, 1)

    def doubling(chunk):
        buf = gathered[chunk]
        route = []
        for stage, mask in enumerate(masks):
            if stage == len(masks) - 1:
                part = buf.at[:, low]
            else:
                size = 1 << stage
                part = buf.at[pl.ds((high // size) * size, size), low]
            to = flipped(wire.me, mask)
            route.append(([(always, part, to, stage)], [(always, part, stage)]))
        return route

    def chained(chunk):
        buf = gathered[chunk]
        y_first = chunk % 6 == 5
        neighbour = 2 * SHARE

        def part(z):
            return buf.at[z] if y_first else buf.at[z, low]

        hops = []
        for hop in range(1, 4):
            hops.append(
                (
                    [
                        (
                            jnp.logical_and(high >= hop - 1, high < 3),
                            part(high - hop + 1),
                            wire.me + neighbour,
                            hop - 1,
                        ),
                        (
                            jnp.logical_and(high <= 4 - hop, high > 0),
                            part(high + hop - 1),
                            wire.me - neighbour,
                            hop + 2,
                        ),
                    ],
                    [
                        (high >= hop, part(high - hop), hop - 1),
                        (high <= 3 - hop, part(high + hop), hop + 2),
                    ],
                )
            )
        own_part = buf.at[high, low] if y_first else buf.at[:, low]
        across = ([(always, own_part, flipped(wire.me, SHARE), 6)], [(always, own_part, 6)])
        return [across] + hops if y_first else hops + [across]

    route_of = chained if chain else doubling
    stages = 4 if chain else len(masks)
    ahead = stages + 1 if chain else stages

    def where(condition, action):
        if condition is always:
            action()
        else:
            pl.when(condition)(action)

    def moved(chunk, part, to, index):
        return pltpu.make_async_remote_copy(
            src_ref=part,
            dst_ref=part,
            send_sem=gather_sems.at[0, chunk, index],
            recv_sem=gather_sems.at[1, chunk, index],
            device_id=(to,),
            device_id_type=MESH,
        )

    def expect(chunk, stage):
        for condition, part, index in route_of(chunk)[stage][1]:
            where(condition, lambda: moved(chunk, part, nearby, index).wait_recv())

    def launch(chunk, stage):
        if not 0 <= chunk < GATHERED:
            return
        if stage == 0:
            here, away = piece_copies(chunk)
            here.wait()
            for item in away:
                item.wait_recv()
        else:
            expect(chunk, stage - 1)
        for condition, part, to, index in route_of(chunk)[stage][0]:
            where(condition, lambda: moved(chunk, part, to, index).start())

    def advance(at):
        for stage in range(stages):
            launch(at - stage, stage)

    def tick(chunk):
        advance(chunk + ahead)
        expect(chunk, stages - 1)

    norm_stages = count.bit_length() - 1

    def norm_copy(stage):
        size = 1 << stage
        part = norms.at[pl.ds((wire.me // size) * size, size)]
        return wire.copy(part, part, norm_sems.at[0, stage], norm_sems.at[1, stage], size)

    norm_copy(0).start()
    loads[0].wait()
    send_pieces(0)
    for stage in range(1, norm_stages):
        norm_copy(stage - 1).wait_recv()
        norm_copy(stage).start()
        if stage == 1:
            advance(0)
            for chunk in range(1, 4):
                send_pieces(chunk)
        if stage == 3:
            advance(1)
    norm_copy(norm_stages - 1).wait_recv()
    small_cols = D // count
    join = max(1, 128 // small_cols)
    small[...] = jnp.concatenate(
        [
            jnp.concatenate([norms[p * join + i][0:8, 0:small_cols] for i in range(join)], axis=1)
            for p in range(count // join)
        ],
        axis=1,
    )
    wide[...] = jnp.zeros_like(wide)
    per_row, row_cols = vector_rows(count)
    per_quarter = count // SHARE
    for r in range(2):
        got = [
            norms[member * per_quarter + i][8 + r * per_row + k : 9 + r * per_row + k, 0:row_cols]
            for i in range(per_quarter)
            for k in range(per_row)
        ]
        wide[r : r + 1, :] = jnp.concatenate(got, axis=1)
    row_count = SHARE * own // rows_each
    own_count = own // rows_each
    advance(2)
    lane = lax.broadcasted_iota(jnp.int32, (8, 128), 1)
    sub = lax.broadcasted_iota(jnp.int32, (8, 128), 0)
    table = jnp.zeros((8, 128), F32)
    for row in range(row_count):
        j, i = row // own_count, row % own_count
        at = 8 + 2 * per_row
        value = norms[flipped(wire.me, j)][at : at + 1, i : i + 1]
        table = jnp.where((sub == row % 8) & (lane == row // 8), value, table)
    captions[...] = table

    def norm_rows(read, at_gain, write, tile=64):
        def body(row, tile):
            at = pl.ds(row, tile)
            scaled = normalized(read(at)) * small[at_gain : at_gain + 1, :]
            write(at, scaled + small[at_gain + 1 : at_gain + 2, :])

        row_tiles(own, body, tile)

    def write_normed(at, value):
        normed[0, at, :] = value.astype(BF)

    norm_rows(lambda at: tokens[at, :].astype(F32), 0, write_normed)
    share_normed = Share(wire, normed.at[0], normed, share_sems.at[0])
    share_normed.start()
    for at in range(3, stages):
        advance(at)

    def back_rows(row, tile):
        at = pl.ds(row, tile)
        back_v[at, :] = (cotangent[at, :].astype(F32) * live[at, 0:1]).astype(BF)

    row_tiles(own, back_rows, 64)
    back_here = pltpu.make_async_copy(back_v, mid.at[0], store_sem.at[0])
    back_here.start()

    def store_turned(source, target):
        tile = turned.shape[1]

        def copy(row, slot):
            return pltpu.make_async_copy(
                turned.at[slot], target.at[pl.ds(row, tile), :], turned_sem.at[slot]
            )

        @pl.loop(0, D // tile // 2)
        def _(pair):
            for slot in range(2):
                row = pl.multiple_of((2 * pair + slot) * tile, tile)

                @pl.when(pair > 0)
                def _():
                    copy(row, slot).wait()

                for j in range(SHARE):
                    turned[slot, :, pl.ds(j * own, own)] = source[j, :, pl.ds(row, tile)].T
                copy(row, slot).start()

        for slot in range(2):
            copy(0, slot).wait()

    for item in loads[1:]:
        item.wait()
    for chunk in range(4, 4 + REDUCE_CHUNKS):
        send_pieces(chunk)
    for at in range(stages, ahead):
        advance(at)
    share_normed.forward()
    share_back = Share(wire, back_v, mid, share_sems.at[1])
    share_back.start()
    for chunk in range(4 + REDUCE_CHUNKS, GATHERED):
        send_pieces(chunk)

    def fetch(source, slot):
        return pltpu.make_async_copy(source, weight.at[slot], weight_sem.at[slot])

    def block_of(chunk):
        return gathered[chunk]

    def weights_of(slot):
        return weight[slot].reshape(D, step)

    def project(slot, target, cosine, sine):
        @pl.loop(0, SHARE)
        def _(j):
            value = dot_f32(normed[j], weights_of(slot), 1, 0)
            for i in range(own_count):
                part = value[i * rows_each : (i + 1) * rows_each]
                if cosine is not None:
                    part = part * cosine[...] + quarter_turn(part) * sine[...]
                at = pl.ds(pl.multiple_of(j * own + i * rows_each, rows_each), rows_each)
                target[at, :] = part.astype(BF)

    tick(0)
    fetch(block_of(0), 0).start()
    share_normed.done()
    fetch(block_of(0), 0).wait()
    project(0, q_v, cq, sq)
    store_turned(normed, normed_out)
    found = jnp.zeros((8, 128), F32)
    for index in range(6):
        weights = (up_v, down_v)[index][...] if index < 2 else attn_v[:, index - 2, :]
        found = jnp.where(
            (sub == 0) & (lane == 6 + index), jnp.sum(weights * weights, keepdims=True), found
        )
    squares[...] = found
    tick(1)
    fetch(block_of(1), 1).start()
    fetch(block_of(1), 1).wait()
    project(1, k_v, ck, sk)
    share_back.forward()
    tick(2)
    fetch(block_of(2), 0).start()
    fetch(block_of(2), 0).wait()
    project(0, v_v, None, None)

    def attend_loop(first, last):
        @pl.loop(first, last)
        def _(row):
            at = pl.ds(pl.multiple_of(row * rows_each, rows_each), rows_each)
            caption = captions[pl.ds(row, 1), 0:1]
            mixed[at, :] = attention_block(
                head_size, caption, q_v[at, :], k_v[at, :], v_v[at, :]
            )

    attend_loop(0, row_count // 2)
    tick(3)

    def out_copies():
        mine = out_full.at[member]
        far = flipped(member, 2)
        parts = [
            (gathered[3], mine, 2),
            (gathered[3], mine, 1),
            (out_full.at[far], out_full.at[far], 1),
        ]
        return [
            wire.copy(source, target, share_sems.at[4, 0, k], share_sems.at[4, 1, k], mask)
            for k, (source, target, mask) in enumerate(parts)
        ]

    out_here = pltpu.make_async_copy(gathered[3], out_full.at[member], store_sem.at[2])
    out_here.start()
    out_moves = out_copies()
    out_moves[0].start()
    out_moves[1].start()
    attend_loop(row_count // 2, row_count)

    def mixed_copies():
        here = pltpu.make_async_copy(
            mixed.at[pl.ds(0, own), :], mixed_own.at[member], turn_sems.at[0, 0]
        )
        away = [
            wire.copy(
                mixed.at[pl.ds(j * own, own), :],
                mixed_own.at[member],
                turn_sems.at[0, j],
                turn_sems.at[1, j],
                j,
            )
            for j in range(1, SHARE)
        ]
        return here, away

    mixed_here, mixed_away = mixed_copies()
    mixed_here.start()
    for item in mixed_away:
        item.start()
    stores = [
        pltpu.make_async_copy(source, target, store_sem.at[3 + k])
        for k, (source, target) in enumerate([(q_v, q_out), (k_v, k_out), (v_v, v_out)])
    ]
    for item in stores:
        item.start()
    tick(4)
    mixed_here.wait()
    for item in mixed_away:
        item.wait_recv()

    def write_context(at, value):
        context[at, :] = value.astype(BF)

    norm_rows(
        lambda at: jnp.concatenate(
            [mixed_own[t, at, :].astype(F32) for t in range(SHARE)], axis=1
        ),
        2,
        write_context,
    )
    stores.append(pltpu.make_async_copy(mixed_own, mixed_out, store_sem.at[6]))
    stores[-1].start()
    context_here = pltpu.make_async_copy(context, unit.at[0], store_sem.at[7])
    context_here.start()
    back_here.wait()
    share_back.done()
    back_store = pltpu.make_async_copy(mid, back_out, store_sem.at[1])
    back_store.start()
    store_turned(mid, back_t_out)
    tick(5)
    out_moves[0].wait_recv()
    out_moves[2].start()
    share_context = Share(wire, context, unit, share_sems.at[3])
    share_context.start()
    tick(6)
    out_here.wait()
    out_moves[1].wait_recv()
    out_moves[2].wait_recv()
    fetch(out_full.at[0], 0).start()
    for t in range(SHARE):
        fetch(out_full.at[t], t % 2).wait()
        if t + 1 < SHARE:
            fetch(out_full.at[t + 1], (t + 1) % 2).start()
        at = pl.ds(t * width, width)
        hidden_out[:, at] = tokens[:, at].astype(F32) + dot_f32(
            context[...], weights_of(t % 2), 1, 0
        )

    def write_ffn(at, value):
        ffn[0, at, :] = value.astype(BF)

    norm_rows(lambda at: hidden_out[at, :], 4, write_ffn)
    share_ffn = Share(wire, ffn.at[0], ffn, share_sems.at[2])
    share_ffn.start()
    share_context.forward()
    context_here.wait()
    share_context.done()
    store_turned(unit, context_out)
    tick(7)
    share_ffn.forward()
    fetch(block_of(4), 0).start()
    share_ffn.done()
    sums[...] = jnp.zeros_like(sums)

    def widen(k):
        slot = k % 2
        fetch(block_of(4 + k), slot).wait()
        if k + 1 < REDUCE_CHUNKS:
            fetch(block_of(5 + k), 1 - slot).start()
        at_cols = pl.ds(k * step, step)

        @pl.loop(0, SHARE)
        def _(j):
            at = pl.ds(pl.multiple_of(j * own, own), own)
            value = dot_f32(ffn[j], weights_of(slot), 1, 0)
            cdf, density = gelu_parts(value)
            active = value * cdf
            act[at, at_cols] = active
            slope[at, at_cols] = (cdf + value * density).astype(BF)
            sums[at, :] += jnp.broadcast_to(
                jnp.sum(active, axis=1, keepdims=True), (own, sums.shape[1])
            )

    widen(0)
    widen(1)
    tick(8)
    widen(2)
    widen(3)

    def spread_body(row, tile):
        at = pl.ds(row, tile)
        mean = sums[at, 0:1] * (1.0 / ff_width)
        square = jnp.zeros((tile, 1), F32)
        for k in range(REDUCE_CHUNKS):
            center = act[at, pl.ds(k * step, step)] - mean
            square += jnp.sum(center * center, axis=1, keepdims=True)
        lane = lax.broadcasted_iota(jnp.int32, (tile, sums.shape[1]), 1)
        sums[at, :] = jnp.where(lane == 0, mean, square)

    row_tiles(SHARE * own, spread_body)
    for j in range(SHARE):
        stat_send[j] = sums[pl.ds(j * own, own), :].T[0:8, :]
    stats = [
        wire.copy(
            stat_send, stat_recv.at[j - 1], stat_sems.at[0, j - 1], stat_sems.at[1, j - 1], j
        )
        for j in range(1, SHARE)
    ]
    for item in stats:
        item.start()
    stores.append(pltpu.make_async_copy(slope, slope_out, store_sem.at[9]))
    stores[-1].start()
    back_store.wait()
    share_back.close()
    share_context.close()
    tick(9)
    for item in stats:
        item.wait_recv()
    for j in range(SHARE):
        parts = [stat_send[j]] + [stat_recv[k - 1, j ^ k] for k in range(1, SHARE)]
        mean = sum(part[0:1, :] for part in parts) * (1.0 / SHARE)
        square = sum(
            part[1:2, :] + ff_width * (part[0:1, :] - mean) ** 2 for part in parts
        )
        rstd = lax.rsqrt(square * (1.0 / (SHARE * ff_width)) + EPS_NORM)
        sub_all = lax.broadcasted_iota(jnp.int32, (128, own), 0)
        both = jnp.where(sub_all == 0, mean, rstd).T
        sums[pl.ds(j * own, own), :] = both
    rstd_out[...] = jnp.broadcast_to(sums[:, 1:2], rstd_out.shape)

    def finish(k):
        at_cols = pl.ds(k * step, step)

        @pl.loop(0, SHARE)
        def _(j):
            at = pl.ds(pl.multiple_of(j * own, own), own)
            value = (act[at, at_cols] - sums[at, 0:1]) * sums[at, 1:2]
            unit[j, :, at_cols] = value.astype(BF)
            mid[j, :, at_cols] = (value * wide[0:1, at_cols] + wide[1:2, at_cols]).astype(BF)

    finish(0)
    finish(1)
    tick(10)
    finish(2)
    finish(3)
    stores += [
        pltpu.make_async_copy(unit, unit_out, store_sem.at[10]),
        pltpu.make_async_copy(mid, mid_out, store_sem.at[11]),
    ]
    for item in stores[-2:]:
        item.start()
    store_turned(ffn, ffn_out)
    for chunk in range(11, GATHERED):
        tick(chunk)
    for item in stores:
        item.wait()
    for chunk in range(GATHERED):
        for item in piece_copies(chunk)[1]:
            item.wait_send()
        for starts, unused in route_of(chunk):
            for condition, part, to, index in starts:
                where(condition, lambda: moved(chunk, part, to, index).wait_send())
    for stage in range(norm_stages):
        norm_copy(stage).wait_send()
    for item in [share_normed, share_ffn]:
        item.close()
    for item in out_moves + mixed_away + stats:
        item.wait_send()


def forward(tokens, cotangent, live, attn_weight, up_weight, down_weight, vectors, tables):
    count = lax.axis_size("dp")
    own = tokens.shape[0]
    all_tokens = SHARE * own
    width, ff_width = D // SHARE, FF // SHARE
    groups = count // SHARE
    local = D // count
    chunk = (groups // 2, 2, D // groups, width)
    stages = len(group_masks())
    any_spec = pl.BlockSpec(memory_space=pl.ANY)
    vmem = pl.BlockSpec(memory_space=pltpu.VMEM)
    shared = jax.ShapeDtypeStruct((SHARE, own, D), BF)
    across = jax.ShapeDtypeStruct((D, all_tokens), BF)
    wide = jax.ShapeDtypeStruct((SHARE, own, ff_width), BF)
    flat = jax.ShapeDtypeStruct((all_tokens, ff_width), BF)
    part = jax.ShapeDtypeStruct((all_tokens, width), BF)
    norm_stages = count.bit_length() - 1
    return pl.pallas_call(
        partial(forward_kernel, own),
        in_specs=[vmem] * 3 + [any_spec] * 3 + [vmem] * 5,
        out_specs=[any_spec] * (GATHERED + 13) + [vmem] * 6,
        out_shape=[jax.ShapeDtypeStruct(chunk, BF)] * GATHERED
        + [jax.ShapeDtypeStruct((SHARE,) + chunk, BF)]
        + [across, shared, across, across, across]
        + [wide, wide, flat]
        + [part] * 3
        + [
            jax.ShapeDtypeStruct((SHARE, own, width), BF),
            jax.ShapeDtypeStruct((own, D), F32),
            jax.ShapeDtypeStruct((8, D), F32),
            jax.ShapeDtypeStruct((8, ff_width), F32),
            jax.ShapeDtypeStruct((all_tokens, 128), F32),
            jax.ShapeDtypeStruct((8, 128), F32),
            jax.ShapeDtypeStruct((8, 128), F32),
        ],
        scratch_shapes=[
            pltpu.VMEM((local, 4, D), F32),
            pltpu.VMEM((local, FF), F32),
            pltpu.VMEM((local, FF), F32),
            pltpu.VMEM((SHARE, GATHERED, local, width), BF),
            pltpu.VMEM((SHARE, own, D), BF),
            pltpu.VMEM((own, D), BF),
            pltpu.VMEM((2,) + chunk, BF),
            pltpu.VMEM((all_tokens, width), BF),
            pltpu.VMEM((all_tokens, width), BF),
            pltpu.VMEM((all_tokens, width), BF),
            pltpu.VMEM((all_tokens, width), BF),
            pltpu.VMEM((SHARE, own, width), BF),
            pltpu.VMEM((own, D), BF),
            pltpu.VMEM((SHARE, own, D), BF),
            pltpu.VMEM((all_tokens, ff_width), F32),
            pltpu.VMEM((SHARE, own, ff_width), BF),
            pltpu.VMEM((SHARE, own, ff_width), BF),
            pltpu.VMEM((all_tokens, ff_width), BF),
            pltpu.VMEM((count, 16, 128), F32),
            pltpu.VMEM((all_tokens, 128), F32),
            pltpu.VMEM((SHARE, 8, own), F32),
            pltpu.VMEM((SHARE - 1, SHARE, 8, own), F32),
            pltpu.SemaphoreType.DMA((3,)),
            pltpu.SemaphoreType.DMA((2, GATHERED, SHARE)),
            pltpu.SemaphoreType.DMA((2, GATHERED, max(stages, 7))),
            pltpu.SemaphoreType.DMA((2, norm_stages)),
            pltpu.SemaphoreType.DMA((5, 2, 3)),
            pltpu.SemaphoreType.DMA((2, SHARE)),
            pltpu.SemaphoreType.DMA((2, SHARE - 1)),
            pltpu.SemaphoreType.DMA((2,)),
            pltpu.SemaphoreType.DMA((12,)),
            pltpu.VMEM((2, 256, all_tokens), BF),
            pltpu.SemaphoreType.DMA((2,)),
        ],
        compiler_params=pltpu.CompilerParams(
            collective_id=5, has_side_effects=True, vmem_limit_bytes=KERNEL_VMEM
        ),
        name="forward",
    )(tokens, cotangent, live, attn_weight, up_weight, down_weight, vectors, *tables)


def gelu_parts(value):
    cdf = 0.5 * (1.0 + lax.erf(value * math.sqrt(0.5)))
    density = jnp.exp(-0.5 * value * value) * (1.0 / math.sqrt(2.0 * math.pi))
    return cdf, density


def per_device(
    tokens,
    cotangent,
    caption_len,
    attn_weight,
    up_weight,
    down_weight,
    small_norms,
    wide_norms,
    attn_row,
    attn_col,
    up_row,
    up_col,
    down_row,
    down_col,
    small_moment,
    wide_moment,
):
    count = lax.axis_size("dp")
    me = lax.axis_index("dp")
    head_size = D // HEADS
    width = D // SHARE
    own = tokens.shape[0]
    own_rows = caption_len.shape[0]

    small_width = D // count
    wide_width = FF // count
    per_row, row_cols = vector_rows(count)
    vectors = jnp.concatenate(
        [
            jnp.pad(small_norms, ((0, 2), (0, 128 - small_width))),
            jnp.pad(
                wide_norms.reshape(2 * per_row, row_cols),
                ((0, 0), (0, 128 - row_cols)),
            ),
            jnp.pad(caption_len.astype(F32), (0, 128 - own_rows))[None],
            jnp.zeros((7 - 2 * per_row, 128), F32),
        ],
        axis=0,
    )
    slot_index = jnp.arange(L)
    live_mask = (slot_index[None, :] < IMG + caption_len[:, None]).astype(F32).reshape(own)
    tables = xpos_tables(head_size, width // head_size)
    results = forward(
        tokens,
        cotangent,
        jnp.broadcast_to(live_mask[:, None], (own, 128)),
        attn_weight,
        up_weight,
        down_weight,
        vectors,
        tables,
    )
    full = [item.reshape(D, width) for item in results[:GATHERED]]
    query_full, key_full, value_full = full[:3]
    up_full, down_full = full[4 : 4 + REDUCE_CHUNKS], full[4 + REDUCE_CHUNKS :]
    (
        out_full, normed_turned, back_all, back_turned, context_turned, ffn_turned, ffn_mid, unit,
        slope, queries, keys_low, values_low, mixed_own, hidden, small_vals, wide_own, rstd, captions,
        weight_squares,
    ) = results[GATHERED:]
    all_tokens = SHARE * own
    back_all = back_all.reshape(all_tokens, D)
    ffn_mid, unit = ffn_mid.reshape(all_tokens, -1), unit.reshape(all_tokens, -1)
    captions = captions[:, 0].astype(jnp.int32)

    down_rows, up_grad_low, wide_terms, ffn_in_grad, *carry = ffn_back(
        back_all, back_turned, ffn_mid, down_full, up_full, unit, slope, wide_own, rstd
    )

    up_rows, grad_q, grad_k, grad_v, hidden_cols, hidden_grad, norm_grads, *carry = attention_back(
        ffn_turned,
        up_grad_low,
        queries,
        keys_low,
        values_low,
        ffn_in_grad,
        hidden,
        back_all,
        mixed_own,
        out_full,
        small_vals,
        captions,
        tables,
        carry,
    )
    attn_rows_out, input_grad, block_out, input_norms = project_back(
        normed_turned,
        context_turned,
        [hidden_cols, grad_q, grad_k, grad_v],
        ffn_mid,
        [query_full, key_full, value_full],
        down_full,
        carry,
        tokens,
        small_vals,
        hidden_grad,
        hidden,
    )

    def spread_columns(value, whole):
        return lax.dynamic_update_slice(
            jnp.zeros((value.shape[0], whole), F32), value, (0, me * value.shape[1])
        ).reshape(-1, D)

    moments = jnp.concatenate(
        [spread_columns(wide_moment, FF), spread_columns(small_moment, D)], axis=0
    )
    vector_squares = jnp.pad(
        jnp.concatenate([jnp.sum(item * item, axis=1) for item in (wide_norms, small_norms)]),
        (12, 128 - 20),
    )[None]
    row_old = jnp.pad(
        jnp.stack([up_row, down_row] + [attn_row[j] for j in range(4)], axis=1), ((0, 0), (0, 122))
    )
    col_old = jnp.concatenate([up_col.reshape(-1, D), down_col.reshape(-1, D), attn_col], axis=0)
    sources = [down_rows, up_rows, attn_rows_out]
    finished = [(k, c) for k, item in enumerate(sources) for c in range(item.shape[1])]
    per_ff, per_proj = FF // SHARE // REDUCE_COLS, width // REDUCE_COLS
    down_places, up_places = finished[:per_ff], finished[per_ff : 2 * per_ff]
    attn_places = [
        finished[2 * per_ff + c * per_proj : 2 * per_ff + (c + 1) * per_proj] for c in (1, 2, 3, 0)
    ]
    row_new, results = update(
        [up_places, down_places] + attn_places,
        sources,
        [up_weight, down_weight, attn_weight],
        row_old,
        col_old,
        wide_terms,
        (input_norms, norm_grads),
        moments,
        (weight_squares, vector_squares),
    )
    (
        up_grad, down_grad, attn_grad, up_new, down_new, attn_new, up_copy, down_copy, attn_copy,
        up_cols, down_cols, attn_cols, wide_all, small_all,
    ) = results
    small_parts = take_block(small_all, me, small_width, 1)
    start = me * wide_width

    def wide_part(k):
        rows = [
            lax.dynamic_slice(
                wide_all, ((2 * k + r) * WIDE + start // D, start % D), (1, wide_width)
            )
            for r in range(2)
        ]
        return jnp.concatenate(rows, axis=0)

    return (
        block_out,
        input_grad,
        attn_grad,
        up_grad,
        down_grad,
        row_new[:, 2:6].T,
        attn_cols,
        row_new[:, 0],
        up_cols.reshape(FF),
        row_new[:, 1],
        down_cols.reshape(FF),
        attn_new,
        up_new,
        down_new,
        attn_copy,
        up_copy,
        down_copy,
        small_parts[0:6],
        wide_part(0),
        small_parts[8:14],
        wide_part(1),
        small_norms - small_parts[16:22],
        wide_norms - wide_part(2),
    )


def solution(mesh):
    placed = (
        P("dp", None),
        P("dp", None),
        P("dp"),
        P("dp", None, None),
        P("dp", None),
        P("dp", None),
        P(None, "dp"),
        P(None, "dp"),
        P(None, "dp"),
        P(),
        P("dp"),
        P(),
        P("dp"),
        P(),
        P(None, "dp"),
        P(None, "dp"),
    )
    return jax.shard_map(
        per_device,
        mesh=mesh,
        in_specs=placed,
        out_specs=(
            P("dp", None),
            P("dp", None),
            P("dp", None, None),
            P("dp", None),
            P("dp", None),
            P(None, "dp"),
            P(),
            P("dp"),
            P(),
            P("dp"),
            P(),
            P("dp", None, None),
            P("dp", None),
            P("dp", None),
            P("dp", None, None),
            P("dp", None),
            P("dp", None),
            P(None, "dp"),
            P(None, "dp"),
            P(None, "dp"),
            P(None, "dp"),
            P(None, "dp"),
            P(None, "dp"),
        ),
        check_vma=False,
    )
```
